32 devices in a mesh: shard: 4 (over z), context: 2 (over y), tensor: 4 (over x, core).
Axes of the slice: x: 2, y: 2, z: 4, core: 2. Of those that a mesh axis runs over, the one named last changes fastest.
Arguments:
- residual_in: bfloat16 [8192, 1536], P(('shard', 'context')), may hold values from -6 to 6
- gain_attn: bfloat16 [1536], P(('shard', 'context')), may hold values from 0.5 to 1.5
- query_weight: bfloat16 [1536, 1536], P(('shard', 'context'), 'tensor'), may hold values from -0.15625 to 0.15625
- key_projection_weight: bfloat16 [1536, 512], P(('shard', 'context'), 'tensor'), may hold values from -0.15625 to 0.15625
- value_projection_weight: bfloat16 [1536, 512], P(('shard', 'context'), 'tensor'), may hold values from -0.15625 to 0.15625
- out_weight: bfloat16 [1536, 1536], P('tensor', ('shard', 'context')), may hold values from -1.25 to 1.25
- gain_ffn: bfloat16 [1536], P(('shard', 'context')), may hold values from 0.5 to 1.5
- gate_weight: bfloat16 [40, 1536, 512], P(None, ('shard', 'context'), 'tensor'), may hold values from -0.15625 to 0.15625
- up_weight: bfloat16 [40, 1536, 512], P(None, ('shard', 'context'), 'tensor'), may hold values from -0.15625 to 0.15625
- down_weight: bfloat16 [40, 512, 1536], P(None, 'tensor', ('shard', 'context')), may hold values from -1 to 1
- segments: int32 [8192], P('shard'), may hold values from 0 to 4, as said below
- routes: int32 [8192, 8], P(('shard', 'context')), may hold values from 0 to 39, all different within a row; in each aligned block of 1024 rows (0 to 1023, 1024 to 2047, ...) at most 256 rows name the same one
- shares: float32 [8192, 8], P(('shard', 'context')), may hold values from 0.05 to 0.25
- cotangent: bfloat16 [8192, 1536], P(('shard', 'context')), may hold values from -6 to 6
Outputs:
- output: bfloat16 [8192, 1536], P(('shard', 'context'))
- grad_input: bfloat16 [8192, 1536], P(('shard', 'context'))
- grad_gain_attn: float32 [1536], P(('shard', 'context'))
- grad_query: float32 [1536, 1536], P(('shard', 'context'), 'tensor')
- grad_key: float32 [1536, 512], P(('shard', 'context'), 'tensor')
- grad_value: float32 [1536, 512], P(('shard', 'context'), 'tensor')
- grad_out: float32 [1536, 1536], P('tensor', ('shard', 'context'))
- grad_gain_ffn: float32 [1536], P(('shard', 'context'))
- grad_gate: float32 [40, 1536, 512], P(None, ('shard', 'context'), 'tensor')
- grad_up: float32 [40, 1536, 512], P(None, ('shard', 'context'), 'tensor')
- grad_down: float32 [40, 512, 1536], P(None, 'tensor', ('shard', 'context'))
The draws below stay inside these ranges and needn't reach their ends.
Inputs may be any that keep to these rules, and one draw needn't show every extreme that they name: `segments`: within each group of 2048 tokens the numbers start at 0, never fall and rise by one at each new document, 5 documents a group; every document has at most 1024 tokens, and one document in each group has exactly 1024 and reaches from the first half of the group into the second. `routes`: each row names 8 different experts; in each aligned block of 1024 rows (the tokens of one index of shard and context) no expert is named by more than 256 rows.
All inputs are finite; a program needn't handle non-finite values.
Results may differ from the reference program's by a relative error of at most 0.025.
Values may be sent and summed in bfloat16 or wider, within the bound.
A program may use at most 256 MiB of HBM per device.

```python
import math
import jax
import jax.numpy as jnp
import numpy as np
from jax import lax

MODEL_DIM = 1536
QUERY_HEAD_COUNT = 24
KV_HEAD_COUNT = 8
HEAD_DIM = 64
FF = 512
E = 40
TOPK = 8
NDOCS = 5
ROWS = 1024
SHARD_TOKENS = 2048
TOTAL_TOKENS = 8192
CAP = 256


def draw_segments(key, part):
    key = jax.random.fold_in(key, 11)
    groups_total = TOTAL_TOKENS // SHARD_TOKENS
    first_key, second_key, third_key = jax.random.split(key, 3)
    span_start = jax.random.randint(first_key, (groups_total, 1), ROWS // 4, 3 * ROWS // 4 + 1)
    early_cut = 1 + jax.random.randint(second_key, (groups_total, 1), 0, 1 << 20) % (span_start - 1)
    span_end = span_start + ROWS
    late_cut = span_end + 1 + jax.random.randint(third_key, (groups_total, 1), 0, 1 << 20) % (SHARD_TOKENS - span_end - 1)
    index_row = jnp.arange(SHARD_TOKENS, dtype=jnp.int32)[None, :]
    segment_ids = (index_row >= early_cut).astype(jnp.int32) + (index_row >= span_start).astype(jnp.int32)
    segment_ids = segment_ids + (index_row >= span_end).astype(jnp.int32) + (index_row >= late_cut).astype(jnp.int32)
    return segment_ids.reshape(-1)


def block_scale(stream_key, extent, cuts, least, top_value):
    factor_of = 1.0
    for axis_at, shards_of in cuts:
        steps = jax.random.uniform(jax.random.fold_in(jax.random.fold_in(stream_key, 6), axis_at), (shards_of,), jnp.float32, least / len(cuts), top_value / len(cuts))
        factor_of = factor_of * jnp.repeat(jnp.exp(steps), extent[axis_at] // shards_of).reshape((-1,) + (1,) * (len(extent) - 1 - axis_at))
    return factor_of


def deal_out(key, own, number, rows, count, top, bound, lean):
    sequence = jax.random.permutation(key, count)
    packed, common = portions_of(count, rows * top, bound, lean, True), portions_of(count, rows * top, bound, lean, False)
    places = jnp.arange(count)

    def named(sizes, offset_by):
        used = int((sizes > 0).sum())
        fixed = max(1, used // 4)
        shifted = fixed + (places - fixed + offset_by * (used - fixed)) % max(1, count - fixed)
        return jnp.zeros((count,), jnp.int32).at[sequence[jnp.where(places < fixed, places, shifted)]].set(jnp.asarray(sizes, jnp.int32))

    sizes = jnp.where(number % 4 == 0, named(packed, number // 4), named(common, number - number // 4 - 1))
    mixed = jax.random.permutation(jax.random.fold_in(own, 3), count)
    source_of, taker = mixed[0:count // 2 * 2:2], mixed[1:count // 2 * 2:2]
    margin = jnp.minimum(sizes[source_of] - 1, bound - sizes[taker]) // 2
    margin = jnp.where((source_of == sequence[0]) | (taker == sequence[0]) | (sizes[taker] == 0), 0, jnp.maximum(margin, 0))
    shifted = jax.random.randint(jax.random.fold_in(own, 4), (count // 2,), 0, 1 << 20) % (margin + 1)
    sizes = sizes.at[source_of].add(-shifted).at[taker].add(shifted)
    members = jnp.searchsorted(jnp.cumsum(sizes), jnp.arange(rows * top), side="right").astype(jnp.int32)
    grid = members.reshape(top, rows).T
    grid = grid[jax.random.permutation(jax.random.fold_in(own, 1), rows)]
    offset_by = jax.random.randint(jax.random.fold_in(own, 2), (rows, 1), 0, top)
    return jnp.take_along_axis(grid, (jnp.arange(top)[None, :] + offset_by) % top, axis=1)


def portions_of(count, total, reach, lean, full):
    portions = [(1 << 20) // math.isqrt(rank ** lean) + 1 for rank in range(1, count + 1)]
    largest = reach if full else min(reach, max(-(-total // count), total * portions[0] // sum(portions)))
    least = 1 if total - largest >= count - 1 else 0
    counts, rest = [largest] + [least] * (count - 1), total - largest - least * (count - 1)
    while rest > 0:
        movable = [i for i in range(1, count) if counts[i] < largest] or [i for i in range(1, count) if counts[i] < reach]
        pool, budget = sum([portions[i] for i in movable]), rest
        for i in movable:
            more = min(reach - counts[i], max(1, budget * portions[i] // pool), rest)
            counts[i] = counts[i] + more
            rest = rest - more
    return np.array(counts)


def gaussian(own_key, extent, scale, most, pieces=(), kind=jnp.bfloat16):
    values = jax.random.normal(own_key, extent, jnp.float32) * scale
    if len(pieces) > 0:
        values = block_scale(own_key, extent, pieces, -0.22, 0.18) * values
    return jnp.clip(values, min=-most, max=most).astype(kind)


def setup_inputs(seed: int = 0) -> dict:
    key_of = jax.random.split(jax.random.key(seed), 15)
    residual_in = gaussian(key_of[0], (TOTAL_TOKENS, MODEL_DIM), 1.0, 6.0, ((0, 8),))
    gain_attn = jnp.clip(1.0 + 0.1 * jax.random.normal(key_of[1], (MODEL_DIM,), jnp.float32), 0.5, 1.5).astype(jnp.bfloat16)
    query_weight = gaussian(key_of[2], (MODEL_DIM, QUERY_HEAD_COUNT * HEAD_DIM), MODEL_DIM ** -0.5, 0.15625, ((0, 8), (1, 4)))
    key_projection_weight = gaussian(key_of[3], (MODEL_DIM, KV_HEAD_COUNT * HEAD_DIM), MODEL_DIM ** -0.5, 0.15625, ((0, 8), (1, 4)))
    value_projection_weight = gaussian(key_of[4], (MODEL_DIM, KV_HEAD_COUNT * HEAD_DIM), MODEL_DIM ** -0.5, 0.15625, ((0, 8), (1, 4)))
    out_weight = gaussian(key_of[5], (QUERY_HEAD_COUNT * HEAD_DIM, MODEL_DIM), (QUERY_HEAD_COUNT * HEAD_DIM // 64) ** -0.5, 1.25, ((0, 4), (1, 8)))
    gain_ffn = jnp.clip(1.0 + 0.1 * jax.random.normal(key_of[6], (MODEL_DIM,), jnp.float32), 0.5, 1.5).astype(jnp.bfloat16)
    gate_weight = gaussian(key_of[7], (E, MODEL_DIM, FF), MODEL_DIM ** -0.5, 0.15625, ((1, 8), (2, 4)))
    up_weight = gaussian(key_of[8], (E, MODEL_DIM, FF), MODEL_DIM ** -0.5, 0.15625, ((1, 8), (2, 4)))
    down_weight = gaussian(key_of[9], (E, FF, MODEL_DIM), (FF // 16) ** -0.5, 1.0, ((1, 4), (2, 8)))
    segments = draw_segments(jax.random.fold_in(key_of[14], 71), 0)
    routes_keys = jax.random.split(jax.random.fold_in(key_of[11], 1), TOTAL_TOKENS // ROWS)
    routes_turns = jax.random.permutation(jax.random.fold_in(key_of[11], 3), TOTAL_TOKENS // ROWS)
    routes = jax.vmap(lambda own, number: deal_out(jax.random.fold_in(key_of[11], 2), own, number, ROWS, E, TOPK, CAP, 1))(routes_keys, routes_turns).reshape((TOTAL_TOKENS, TOPK))
    shares = jnp.clip(jnp.exp(math.log(0.25) - 1.609438 * jax.random.uniform(key_of[12], (TOTAL_TOKENS, TOPK), jnp.float32) ** block_scale(key_of[12], (TOTAL_TOKENS, TOPK), ((0, 8),), -0.2, 0.2)), 0.05, 0.25)
    cotangent = gaussian(key_of[13], (TOTAL_TOKENS, MODEL_DIM), 1.0, 6.0, ((0, 8),))
    return dict(residual_in=residual_in, gain_attn=gain_attn, query_weight=query_weight, key_projection_weight=key_projection_weight, value_projection_weight=value_projection_weight, out_weight=out_weight, gain_ffn=gain_ffn, gate_weight=gate_weight, up_weight=up_weight, down_weight=down_weight, segments=segments, routes=routes, shares=shares, cotangent=cotangent)


@jax.custom_vjp
def lowered_precision(v):
    return lax.optimization_barrier(v.astype(jnp.bfloat16)).astype(jnp.float32)

@jax.custom_vjp
def lowered_backward(v):
    return v

def low_keep(v):
    return (lowered_precision(v), None)

def low_pass(kept, grad):
    return (grad,)

def back_keep(v):
    return (v, None)

def back_low(kept, grad):
    return (lowered_precision(grad),)
lowered_precision.defvjp(low_keep, low_pass)
lowered_backward.defvjp(back_keep, back_low)
epsilon = 1e-06
highest_precision = lax.Precision.HIGHEST

def rms_scale(values, gain):
    return values * lax.rsqrt(lax.optimization_barrier(jnp.mean(values * values, axis=-1, keepdims=True)) + epsilon) * gain

def doc_positions(segment_ids):
    sequence_length = segment_ids.shape[-1]
    index_row = jnp.arange(sequence_length, dtype=jnp.int32)
    documents = jnp.arange(NDOCS, dtype=jnp.int32)
    doc_starts = lax.optimization_barrier(jnp.sum((segment_ids[..., :, None] < documents).astype(jnp.int32), axis=-2))
    own_start = lax.optimization_barrier(jnp.sum(jnp.where(segment_ids[..., :, None] == documents, doc_starts[..., None, :], 0), axis=-1))
    return index_row - own_start

def rotary(values, positions):
    half_dim = values.shape[-1] // 2
    frequencies = 10000.0 ** (-2.0 * jnp.arange(half_dim, dtype=jnp.float32) / values.shape[-1])
    angles = positions.astype(jnp.float32)[:, None] * frequencies[None, :]
    cosine = jnp.cos(angles)[:, None, :]
    sines = jnp.sin(angles)[:, None, :]
    first_half = values[..., :half_dim]
    second_half = values[..., half_dim:]
    return jnp.concatenate([first_half * cosine - second_half * sines, second_half * cosine + first_half * sines], axis=-1)

def dispatch(routes, shares, block_rows, capacity, expert_count):
    block_count = routes.shape[0] // block_rows
    picks = routes.shape[1]
    chosen = routes.reshape(block_count, block_rows * picks)
    onehot = (chosen[:, :, None] == jnp.arange(expert_count, dtype=jnp.int32)).astype(jnp.int32)
    ranked = lax.optimization_barrier(jnp.sum((jnp.cumsum(onehot, axis=1) - onehot) * onehot, axis=2))
    slot_index = chosen * (block_count * capacity) + jnp.arange(block_count, dtype=jnp.int32)[:, None] * capacity + ranked
    tokens = jnp.arange(block_count * block_rows * picks, dtype=jnp.int32) // picks
    total_slots = expert_count * block_count * capacity
    slot_rows = jnp.zeros((total_slots,), jnp.int32).at[slot_index.reshape(-1)].set(tokens)
    slot_share = jnp.zeros((total_slots,), jnp.float32).at[slot_index.reshape(-1)].set(shares.reshape(-1).astype(jnp.float32))
    return (slot_rows, slot_share)

def attend(query_rows, key_rows, values, segment_ids):
    sequence_length = query_rows.shape[0]
    grouped_rows = query_rows.reshape(sequence_length, KV_HEAD_COUNT, QUERY_HEAD_COUNT // KV_HEAD_COUNT, HEAD_DIM)
    raw_scores = jnp.einsum('qgrd,kgd->grqk', grouped_rows, key_rows, precision=highest_precision)
    index_row = jnp.arange(sequence_length, dtype=jnp.int32)
    allowed = (segment_ids[:, None] == segment_ids[None, :]) & (index_row[None, :] <= index_row[:, None])
    scores = lowered_backward(raw_scores) * HEAD_DIM ** (-0.5)
    probs = lowered_precision(jax.nn.softmax(jnp.where(allowed, scores, -1e+30), axis=-1))
    mixed_output = jnp.einsum('grqk,kgd->qgrd', probs, values, precision=highest_precision)
    return mixed_output.reshape(sequence_length, QUERY_HEAD_COUNT * HEAD_DIM)

def expert_term(normed, gate_mat, up_mat, down_mat, slot_rows, slot_share):
    picked = normed[slot_rows]
    gate_value = lowered_backward(jnp.dot(picked, gate_mat, precision=highest_precision))
    up_value = lowered_backward(jnp.dot(picked, up_mat, precision=highest_precision))
    inner = lowered_precision(lowered_backward(jax.nn.silu(gate_value) * up_value))
    expert_result = lowered_backward(jnp.dot(inner, down_mat, precision=highest_precision))
    return jnp.zeros_like(normed).at[slot_rows].add(slot_share[:, None] * expert_result)

def reference(residual_in, gain_attn, query_weight, key_projection_weight, value_projection_weight, out_weight, gain_ffn, gate_weight, up_weight, down_weight, segments, routes, shares, cotangent):
    groups_total = TOTAL_TOKENS // SHARD_TOKENS
    grouped_index = segments.reshape(groups_total, SHARD_TOKENS)
    positions = doc_positions(grouped_index).reshape(TOTAL_TOKENS)
    slot_rows, slot_share = dispatch(routes, shares, ROWS, CAP, E)
    slot_rows = slot_rows.reshape(E, -1)
    slot_share = slot_share.reshape(E, -1)
    attend_block = jax.checkpoint(attend)
    expert_block = jax.checkpoint(expert_term)

    def forward(inputs, gain_first, query_mat, key_matrix, value_matrix, out_mat, gain_second, gate_mat, up_mat, down_mat):
        first_normalized = lowered_precision(rms_scale(inputs, gain_first))
        query_lin = lowered_backward(jnp.dot(first_normalized, query_mat, precision=highest_precision)).reshape(TOTAL_TOKENS, QUERY_HEAD_COUNT, HEAD_DIM)
        key_linear = lowered_backward(jnp.dot(first_normalized, key_matrix, precision=highest_precision)).reshape(TOTAL_TOKENS, KV_HEAD_COUNT, HEAD_DIM)
        value_tokens = lowered_precision(lowered_backward(jnp.dot(first_normalized, value_matrix, precision=highest_precision))).reshape(TOTAL_TOKENS, KV_HEAD_COUNT, HEAD_DIM)
        query_rows = lowered_precision(rotary(query_lin, positions))
        key_rows = lowered_precision(rotary(key_linear, positions))

        def single_group(item):
            return attend_block(item[0], item[1], item[2], item[3])
        mixed_output = lax.map(single_group, (query_rows.reshape(groups_total, SHARD_TOKENS, QUERY_HEAD_COUNT, HEAD_DIM), key_rows.reshape(groups_total, SHARD_TOKENS, KV_HEAD_COUNT, HEAD_DIM), value_tokens.reshape(groups_total, SHARD_TOKENS, KV_HEAD_COUNT, HEAD_DIM), grouped_index))
        attended = lowered_precision(lowered_backward(mixed_output.reshape(TOTAL_TOKENS, QUERY_HEAD_COUNT * HEAD_DIM)))
        hidden = inputs + lowered_backward(jnp.dot(attended, out_mat, precision=highest_precision))
        normed_second = lowered_precision(rms_scale(hidden, gain_second))

        def one_expert(running, item):
            return (running + expert_block(normed_second, item[0], item[1], item[2], item[3], item[4]), None)
        expert_total, _ = lax.scan(one_expert, jnp.zeros_like(hidden), (gate_mat, up_mat, down_mat, slot_rows, slot_share))
        return hidden + expert_total
    result, pullback = jax.vjp(forward, residual_in.astype(jnp.float32), gain_attn.astype(jnp.float32), query_weight.astype(jnp.float32), key_projection_weight.astype(jnp.float32), value_projection_weight.astype(jnp.float32), out_weight.astype(jnp.float32), gain_ffn.astype(jnp.float32), gate_weight.astype(jnp.float32), up_weight.astype(jnp.float32), down_weight.astype(jnp.float32))
    grads = pullback(cotangent.astype(jnp.float32))
    return (result.astype(jnp.bfloat16), grads[0].astype(jnp.bfloat16), grads[1], grads[2], grads[3], grads[4], grads[5], grads[6], grads[7], grads[8], grads[9])
```

```python
from functools import partial

import jax
import jax.numpy as jnp
from jax import lax
from jax.experimental import pallas as pl
from jax.experimental.pallas import tpu as pltpu
from jax.sharding import PartitionSpec as P

HEAD_DIM = 64
NDOCS = 5
SHARD = "shard"
CONTEXT = "context"
TENSOR = "tensor"
GROUP = (SHARD, CONTEXT)
PRODUCT_0 = "qgrd,kgd->grqk"
PRODUCT_1 = "grqk,kgd->qgrd"
PRODUCT_2 = "ecd,edf->ecf"
PRODUCT_3 = "ecf,efd->ecd"
PRODUCT_4 = "ecd,efd->ecf"
PRODUCT_5 = "ecf,edf->ecd"
PRODUCT_6 = "ecd,ecf->edf"
PRODUCT_7 = "ecf,ecd->efd"
PRODUCT_8 = "grqk,qgrd->kgd"


epsilon = 1e-06


def rms_scale(values, gain):
    return values * lax.rsqrt(jnp.mean(values * values, axis=-1, keepdims=True) + epsilon) * gain


def doc_positions(segment_ids):
    sequence_length = segment_ids.shape[-1]
    index_row = jnp.arange(sequence_length, dtype=jnp.int32)
    documents = jnp.arange(NDOCS, dtype=jnp.int32)
    doc_starts = jnp.sum((segment_ids[..., :, None] < documents).astype(jnp.int32), axis=-2)
    own_start = jnp.sum(
        jnp.where(segment_ids[..., :, None] == documents, doc_starts[..., None, :], 0), axis=-1
    )
    return index_row - own_start


def rotary(values, positions):
    half_dim = values.shape[-1] // 2
    frequencies = 10000.0 ** (-2.0 * jnp.arange(half_dim, dtype=jnp.float32) / values.shape[-1])
    angles = positions.astype(jnp.float32)[:, None] * frequencies[None, :]
    cosine = jnp.cos(angles)[:, None, :]
    sines = jnp.sin(angles)[:, None, :]
    first_half = values[..., :half_dim]
    second_half = values[..., half_dim:]
    return jnp.concatenate(
        [first_half * cosine - second_half * sines, second_half * cosine + first_half * sines],
        axis=-1,
    )


def swiglu(gate_value, up_value):
    return jax.nn.silu(gate_value) * up_value


def dispatch(routes, shares, block_rows, capacity, expert_count):
    block_count = routes.shape[0] // block_rows
    picks = routes.shape[1]
    chosen = routes.reshape(block_count, block_rows * picks)
    onehot = (chosen[:, :, None] == jnp.arange(expert_count, dtype=jnp.int32)).astype(jnp.int32)
    ranked = jnp.sum((jnp.cumsum(onehot, axis=1) - onehot) * onehot, axis=2)
    slot_index = (
        chosen * (block_count * capacity)
        + jnp.arange(block_count, dtype=jnp.int32)[:, None] * capacity
        + ranked
    )
    tokens = jnp.arange(block_count * block_rows * picks, dtype=jnp.int32) // picks
    total_slots = expert_count * block_count * capacity
    slot_rows = jnp.zeros((total_slots,), jnp.int32).at[slot_index.reshape(-1)].set(tokens)
    slot_share = (
        jnp.zeros((total_slots,), jnp.float32).at[slot_index.reshape(-1)].set(shares.reshape(-1))
    )
    return (slot_rows, slot_share)


def gathered_plan(
    residual_in,
    gain_attn,
    query_weight,
    key_projection_weight,
    value_projection_weight,
    out_weight,
    gain_ffn,
    gate_weight,
    up_weight,
    down_weight,
    segments,
    routes,
    shares,
    cotangent,
):
    row_count, model_width = residual_in.shape
    head_size = HEAD_DIM
    query_cols = query_weight.shape[1]
    kv_heads = key_projection_weight.shape[1] // head_size
    group_size = query_cols // head_size // kv_heads
    expert_count = gate_weight.shape[0]
    capacity = row_count * routes.shape[1] * 5 // (4 * expert_count)
    score_scale = head_size ** (-0.5)
    context_rank = lax.axis_index(CONTEXT)
    own_first = context_rank * row_count
    gain_attn_full, gain_ffn_full, query_full, key_full, value_full, out_full = (
        lax.all_gather(gain_attn, GROUP, axis=0, tiled=True),
        lax.all_gather(gain_ffn, GROUP, axis=0, tiled=True),
        lax.all_gather(query_weight, GROUP, axis=0, tiled=True),
        lax.all_gather(key_projection_weight, GROUP, axis=0, tiled=True),
        lax.all_gather(value_projection_weight, GROUP, axis=0, tiled=True),
        lax.all_gather(out_weight, GROUP, axis=1, tiled=True),
    )
    gain_attn_float = gain_attn_full.astype(jnp.float32)
    gain_ffn_float = gain_ffn_full.astype(jnp.float32)
    positions = doc_positions(segments)
    own_positions = lax.dynamic_slice_in_dim(positions, own_first, row_count)
    own_ids = lax.dynamic_slice_in_dim(segments, own_first, row_count)
    own_index = own_first + jnp.arange(row_count, dtype=jnp.int32)
    input_float = residual_in.astype(jnp.float32)
    normed_attn, attn_norm_back = jax.vjp(rms_scale, input_float, gain_attn_float)
    first_normalized = normed_attn.astype(jnp.bfloat16)
    query_lin = jnp.dot(first_normalized, query_full, preferred_element_type=jnp.float32).reshape(
        row_count, -1, head_size
    )
    key_linear = jnp.dot(first_normalized, key_full, preferred_element_type=jnp.float32).reshape(
        row_count, -1, head_size
    )
    value_tokens = jnp.dot(first_normalized, value_full, preferred_element_type=jnp.float32).astype(
        jnp.bfloat16
    )
    rope_local = partial(rotary, positions=own_positions)
    query_rot, rope_query_back = jax.vjp(rope_local, query_lin)
    key_rot, rope_key_back = jax.vjp(rope_local, key_linear)
    query_low = query_rot.astype(jnp.bfloat16)
    key_low = key_rot.astype(jnp.bfloat16).reshape(row_count, -1)
    key_all, value_all = (
        lax.all_gather(key_low, CONTEXT, axis=0, tiled=True),
        lax.all_gather(value_tokens, CONTEXT, axis=0, tiled=True),
    )
    key_index = jnp.arange(key_all.shape[0], dtype=jnp.int32)
    key_ids = jnp.take(segments, jnp.clip(key_index, 0, segments.shape[0] - 1))
    key_valid = key_index >= 0
    key_heads = key_all.reshape(-1, kv_heads, head_size)
    value_heads = value_all.reshape(-1, kv_heads, head_size)
    query_heads = query_low.reshape(row_count, kv_heads, group_size, head_size)
    block_rows = min(512, row_count)
    block_starts = list(range(0, row_count, block_rows))

    def block_scores(block_first):
        query_block = query_heads[block_first : block_first + block_rows]
        raw_scores = jnp.einsum(
            PRODUCT_0, query_block, key_heads, preferred_element_type=jnp.float32
        )
        block_ids = own_ids[block_first : block_first + block_rows]
        block_index = own_index[block_first : block_first + block_rows]
        allowed = (
            key_valid[None, :]
            & (key_ids[None, :] == block_ids[:, None])
            & (key_index[None, :] <= block_index[:, None])
        )
        return (query_block, jnp.where(allowed, raw_scores * score_scale, -1e30))

    mixed_parts = []
    lse_parts = []
    for block_first in block_starts:
        query_block, scores = block_scores(block_first)
        row_max = jnp.max(scores, axis=-1, keepdims=True)
        exponent = jnp.exp(scores - row_max)
        row_total = jnp.sum(exponent, axis=-1, keepdims=True)
        probs = (exponent / row_total).astype(jnp.bfloat16)
        mixed_parts.append(
            jnp.einsum(PRODUCT_1, probs, value_heads, preferred_element_type=jnp.float32)
        )
        lse_parts.append(row_max + jnp.log(row_total))
    attended = (
        jnp.concatenate(mixed_parts, axis=0).reshape(row_count, query_cols).astype(jnp.bfloat16)
    )
    attn_part = jnp.dot(attended, out_full, preferred_element_type=jnp.float32)
    hidden = input_float + lax.psum(attn_part.astype(jnp.bfloat16), TENSOR).astype(jnp.float32)
    normed_ffn, ffn_norm_back = jax.vjp(rms_scale, hidden, gain_ffn_float)
    normed_second = normed_ffn.astype(jnp.bfloat16)
    slot_rows, slot_share = dispatch(routes, shares, row_count, capacity, expert_count)
    per_turn = expert_count // 5
    turn_count = expert_count // per_turn
    turn_slots = per_turn * capacity

    def local_experts(turn_index):
        gate_part = lax.dynamic_slice_in_dim(gate_weight, turn_index * per_turn, per_turn, 0)
        up_part = lax.dynamic_slice_in_dim(up_weight, turn_index * per_turn, per_turn, 0)
        down_part = lax.dynamic_slice_in_dim(down_weight, turn_index * per_turn, per_turn, 0)
        return (gate_part, up_part, down_part)

    def turn_inputs(turn_index):
        token_rows = lax.dynamic_slice_in_dim(slot_rows, turn_index * turn_slots, turn_slots)
        share_rows = lax.dynamic_slice_in_dim(slot_share, turn_index * turn_slots, turn_slots)
        picked = normed_second[token_rows].reshape(per_turn, capacity, model_width)
        return (token_rows, share_rows, picked)

    def forward_turn(running, turn_index):
        gate_part, up_part, down_part = local_experts(turn_index)
        gate_full, up_full, down_full = (
            lax.all_gather(gate_part, GROUP, axis=1, tiled=True),
            lax.all_gather(up_part, GROUP, axis=1, tiled=True),
            lax.all_gather(down_part, GROUP, axis=2, tiled=True),
        )
        token_rows, share_rows, picked = turn_inputs(turn_index)
        gate_value = jnp.einsum(
            PRODUCT_2, picked, gate_full, preferred_element_type=jnp.float32
        )
        up_value = jnp.einsum(PRODUCT_2, picked, up_full, preferred_element_type=jnp.float32)
        inner = swiglu(gate_value, up_value).astype(jnp.bfloat16)
        expert_result = jnp.einsum(
            PRODUCT_3, inner, down_full, preferred_element_type=jnp.float32
        ).reshape(turn_slots, model_width)
        return (running.at[token_rows].add(expert_result * share_rows[:, None]), None)

    turn_ids = jnp.arange(turn_count, dtype=jnp.int32)
    expert_part, _ = lax.scan(
        forward_turn, jnp.zeros((row_count, model_width), jnp.float32), turn_ids
    )
    expert_total = lax.psum(expert_part.astype(jnp.bfloat16), TENSOR).astype(jnp.float32)
    output = (hidden + expert_total).astype(jnp.bfloat16)
    upstream = cotangent.astype(jnp.float32)

    def backward_turn(running, turn_index):
        gate_part, up_part, down_part = local_experts(turn_index)
        gate_full, up_full, down_full = (
            lax.all_gather(gate_part, GROUP, axis=1, tiled=True),
            lax.all_gather(up_part, GROUP, axis=1, tiled=True),
            lax.all_gather(down_part, GROUP, axis=2, tiled=True),
        )
        token_rows, share_rows, picked = turn_inputs(turn_index)
        gate_value = jnp.einsum(
            PRODUCT_2, picked, gate_full, preferred_element_type=jnp.float32
        )
        up_value = jnp.einsum(PRODUCT_2, picked, up_full, preferred_element_type=jnp.float32)
        inner_float, swiglu_back = jax.vjp(swiglu, gate_value, up_value)
        inner = inner_float.astype(jnp.bfloat16)
        grad_slot = (
            (upstream[token_rows] * share_rows[:, None])
            .astype(jnp.bfloat16)
            .reshape(per_turn, capacity, model_width)
        )
        grad_inner = jnp.einsum(
            PRODUCT_4, grad_slot, down_full, preferred_element_type=jnp.float32
        )
        grad_gate_value, grad_up_value = swiglu_back(grad_inner)
        grad_gate_low = grad_gate_value.astype(jnp.bfloat16)
        grad_up_low = grad_up_value.astype(jnp.bfloat16)
        grad_picked = jnp.einsum(
            PRODUCT_5, grad_gate_low, gate_full, preferred_element_type=jnp.float32
        )
        grad_picked = grad_picked + jnp.einsum(
            PRODUCT_5, grad_up_low, up_full, preferred_element_type=jnp.float32
        )
        running = running.at[token_rows].add(grad_picked.reshape(turn_slots, model_width))
        shard_grads = (
            lax.psum_scatter(
                jnp.einsum(
                    PRODUCT_6, picked, grad_gate_low, preferred_element_type=jnp.float32
                ).astype(jnp.bfloat16),
                GROUP,
                scatter_dimension=1,
                tiled=True,
            ).astype(jnp.float32),
            lax.psum_scatter(
                jnp.einsum(
                    PRODUCT_6, picked, grad_up_low, preferred_element_type=jnp.float32
                ).astype(jnp.bfloat16),
                GROUP,
                scatter_dimension=1,
                tiled=True,
            ).astype(jnp.float32),
            lax.psum_scatter(
                jnp.einsum(
                    PRODUCT_7, inner, grad_slot, preferred_element_type=jnp.float32
                ).astype(jnp.bfloat16),
                GROUP,
                scatter_dimension=2,
                tiled=True,
            ).astype(jnp.float32),
        )
        return (running, shard_grads)

    grad_second_part, stacked_grads = lax.scan(
        backward_turn, jnp.zeros((row_count, model_width), jnp.float32), turn_ids
    )
    grad_gate_out = stacked_grads[0].reshape(gate_weight.shape)
    grad_up_out = stacked_grads[1].reshape(up_weight.shape)
    grad_down_out = stacked_grads[2].reshape(down_weight.shape)
    grad_second = lax.psum(grad_second_part.astype(jnp.bfloat16), TENSOR).astype(jnp.float32)
    grad_hidden_norm, grad_gain_ffn_local = ffn_norm_back(grad_second)
    grad_hidden = upstream + grad_hidden_norm
    grad_hidden_low = grad_hidden.astype(jnp.bfloat16)
    grad_out_local = jnp.einsum(
        "tc,td->cd", attended, grad_hidden_low, preferred_element_type=jnp.float32
    )
    grad_attended = jnp.einsum(
        "td,cd->tc", grad_hidden_low, out_full, preferred_element_type=jnp.float32
    )
    grad_attended = grad_attended.astype(jnp.bfloat16).reshape(
        row_count, kv_heads, group_size, head_size
    )
    grad_query_parts = []
    grad_keys = jnp.zeros(key_heads.shape, jnp.float32)
    grad_values = jnp.zeros(value_heads.shape, jnp.float32)
    for block_number in range(len(block_starts)):
        block_first = block_starts[block_number]
        query_block, scores = block_scores(block_first)
        probs_float = jnp.exp(scores - lse_parts[block_number])
        probs = probs_float.astype(jnp.bfloat16)
        grad_block = grad_attended[block_first : block_first + block_rows]
        grad_probs = jnp.einsum(
            PRODUCT_0, grad_block, value_heads, preferred_element_type=jnp.float32
        )
        inner_sum = jnp.sum(grad_probs * probs_float, axis=-1, keepdims=True)
        grad_scores = (score_scale * (probs_float * (grad_probs - inner_sum))).astype(jnp.bfloat16)
        grad_query_parts.append(
            jnp.einsum(PRODUCT_1, grad_scores, key_heads, preferred_element_type=jnp.float32)
        )
        grad_keys = grad_keys + jnp.einsum(
            PRODUCT_8, grad_scores, query_block, preferred_element_type=jnp.float32
        )
        grad_values = grad_values + jnp.einsum(
            PRODUCT_8, probs, grad_block, preferred_element_type=jnp.float32
        )
    grad_key_own, grad_value_own = (
        lax.psum_scatter(
            grad_keys.astype(jnp.bfloat16), CONTEXT, scatter_dimension=0, tiled=True
        ).astype(jnp.float32),
        lax.psum_scatter(
            grad_values.astype(jnp.bfloat16), CONTEXT, scatter_dimension=0, tiled=True
        ).astype(jnp.float32),
    )
    grad_query_all = jnp.concatenate(grad_query_parts, axis=0).reshape(row_count, -1, head_size)
    grad_query_lin = rope_query_back(grad_query_all)[0].astype(jnp.bfloat16).reshape(row_count, -1)
    grad_key_lin = rope_key_back(grad_key_own)[0].astype(jnp.bfloat16).reshape(row_count, -1)
    grad_value_low = grad_value_own.astype(jnp.bfloat16).reshape(row_count, -1)
    grad_first_part = jnp.einsum(
        "tc,dc->td", grad_query_lin, query_full, preferred_element_type=jnp.float32
    )
    grad_first_part = grad_first_part + jnp.einsum(
        "tc,dc->td", grad_key_lin, key_full, preferred_element_type=jnp.float32
    )
    grad_first_part = grad_first_part + jnp.einsum(
        "tc,dc->td", grad_value_low, value_full, preferred_element_type=jnp.float32
    )
    grad_first = lax.psum(grad_first_part.astype(jnp.bfloat16), TENSOR).astype(jnp.float32)
    grad_input_norm, grad_gain_attn_local = attn_norm_back(grad_first)
    grad_input = (grad_hidden + grad_input_norm).astype(jnp.bfloat16)
    grad_query_local = jnp.einsum(
        "td,tc->dc", first_normalized, grad_query_lin, preferred_element_type=jnp.float32
    )
    grad_key_local = jnp.einsum(
        "td,tc->dc", first_normalized, grad_key_lin, preferred_element_type=jnp.float32
    )
    grad_value_local = jnp.einsum(
        "td,tc->dc", first_normalized, grad_value_low, preferred_element_type=jnp.float32
    )
    reduced = (
        lax.psum_scatter(
            grad_gain_attn_local.astype(jnp.bfloat16),
            GROUP,
            scatter_dimension=0,
            tiled=True,
        ).astype(jnp.float32),
        lax.psum_scatter(
            grad_query_local.astype(jnp.bfloat16),
            GROUP,
            scatter_dimension=0,
            tiled=True,
        ).astype(jnp.float32),
        lax.psum_scatter(
            grad_key_local.astype(jnp.bfloat16),
            GROUP,
            scatter_dimension=0,
            tiled=True,
        ).astype(jnp.float32),
        lax.psum_scatter(
            grad_value_local.astype(jnp.bfloat16),
            GROUP,
            scatter_dimension=0,
            tiled=True,
        ).astype(jnp.float32),
        lax.psum_scatter(
            grad_out_local.astype(jnp.bfloat16),
            GROUP,
            scatter_dimension=1,
            tiled=True,
        ).astype(jnp.float32),
        lax.psum_scatter(
            grad_gain_ffn_local.astype(jnp.bfloat16),
            GROUP,
            scatter_dimension=0,
            tiled=True,
        ).astype(jnp.float32),
    )
    return (
        output,
        grad_input,
        reduced[0],
        reduced[1],
        reduced[2],
        reduced[3],
        reduced[4],
        reduced[5],
        grad_gate_out,
        grad_up_out,
        grad_down_out,
    )


F32 = jnp.float32
BF16 = jnp.bfloat16
LAST_LAST = (((1,), (1,)), ((), ()))
FIRST_FIRST = (((0,), (0,)), ((), ()))


def weight_copies(own_hbm, other_hbm, weights, sems):
    sources, _, rows, lanes = own_hbm.shape
    units = lanes // 3
    return [
        pltpu.make_async_copy(
            half_hbm.at[source, :, :, pl.ds(part * units, units)],
            weights.at[
                :, pl.ds(source * rows, rows), pl.ds((2 * part + half) * units, units)
            ],
            sems.at[source, half, part],
        )
        for source in range(sources)
        for half, half_hbm in enumerate((own_hbm, other_hbm))
        for part in range(3)
    ]


def project(tokens, cotangent, weights):
    hidden_units = weights.shape[1] // 3
    gate_up = jnp.dot(tokens, weights[:, : 2 * hidden_units], preferred_element_type=F32)
    grad_inner = jnp.dot(cotangent, weights[:, 2 * hidden_units :], preferred_element_type=F32)
    return gate_up, grad_inner


def activate(gate_up, grad_inner, share):
    hidden_units = grad_inner.shape[1]
    gate, up = gate_up[:, :hidden_units], gate_up[:, hidden_units:]
    sigmoid = 1.0 / (1.0 + jnp.exp(-gate))
    silu = gate * sigmoid
    grad_inner = grad_inner * share
    inner = silu * up * share
    grad_gate = grad_inner * up * (sigmoid * (1.0 + gate * (1.0 - sigmoid)))
    grad_up = grad_inner * silu
    return inner.astype(BF16), grad_gate.astype(BF16), grad_up.astype(BF16)


def expert_kernel(
    tokens_ref,
    cotangent_ref,
    shares_ref,
    own_hbm,
    other_hbm,
    out_ref,
    grad_tokens_ref,
    grad_own_hbm,
    grad_other_hbm,
    weights,
    grads,
    inner_low,
    grad_low,
    stage,
    load_sems,
    store_sems,
    *,
    steps,
    chunk,
):
    step = pl.program_id(0)
    expert_count, model_width, all_units = weights.shape
    hidden_units = all_units // 3
    units = hidden_units // 2

    @pl.when(step == 0)
    def _():
        copies = weight_copies(own_hbm, other_hbm, weights, load_sems)
        for copy in copies:
            copy.start()
        grads[...] = jnp.zeros_like(grads)
        for copy in copies:
            copy.wait()

    def run(expert, gate_up, grad_inner):
        lane = lax.broadcasted_iota(jnp.int32, shares_ref.shape, 1)
        share = jnp.sum(
            jnp.where(lane == expert, shares_ref[...], 0.0), axis=1, keepdims=True
        )
        inner, grad_gate, grad_up = activate(gate_up, grad_inner, share)
        inner_low[expert] = inner
        grad_low[expert, :, :hidden_units] = grad_gate
        grad_low[expert, :, hidden_units:] = grad_up

    def weight_grads(expert):
        grads[expert, :, : 2 * hidden_units] += lax.dot_general(
            tokens_ref[...], grad_low[expert], FIRST_FIRST, preferred_element_type=F32
        )
        grads[expert, :, 2 * hidden_units :] += lax.dot_general(
            cotangent_ref[...], inner_low[expert], FIRST_FIRST, preferred_element_type=F32
        )

    results = project(tokens_ref[...], cotangent_ref[...], weights[0])
    for expert in range(expert_count):
        run(expert, *results)
        if expert + 1 < expert_count:
            results = project(tokens_ref[...], cotangent_ref[...], weights[expert + 1])
        weight_grads(expert)

    @pl.loop(0, model_width // chunk)
    def _(number):
        cols = pl.ds(pl.multiple_of(number * chunk, chunk), chunk)
        total = jnp.zeros((tokens_ref.shape[0], chunk), F32)
        for expert in range(expert_count):
            total += lax.dot_general(
                inner_low[expert],
                weights[expert, cols, 2 * hidden_units :],
                LAST_LAST,
                preferred_element_type=F32,
            )
        out_ref[:, cols] = total.astype(BF16)
        total = jnp.zeros((tokens_ref.shape[0], chunk), F32)
        for expert in range(expert_count):
            total += lax.dot_general(
                grad_low[expert],
                weights[expert, cols, : 2 * hidden_units],
                LAST_LAST,
                preferred_element_type=F32,
            )
        grad_tokens_ref[:, cols] = total.astype(BF16)

    @pl.when(step == steps - 1)
    def _():
        sources, _, rows, lanes = own_hbm.shape

        @pl.loop(0, expert_count)
        def _(expert):
            copies = []
            for half, half_hbm in enumerate((grad_own_hbm, grad_other_hbm)):
                for part in range(3):
                    first = (2 * part + half) * units
                    stage[half, :, part * units : (part + 1) * units] = grads[
                        expert, :, first : first + units
                    ].astype(BF16)
                for source in range(sources):
                    copy = pltpu.make_async_copy(
                        stage.at[half, pl.ds(source * rows, rows), :],
                        half_hbm.at[source, expert],
                        store_sems.at[half, source],
                    )
                    copy.start()
                    copies.append(copy)
            for copy in copies:
                copy.wait()


def experts(tokens, cotangent, shares, own, other, block_rows=512, chunk=512):
    token_count, model_width = tokens.shape
    sources, expert_count, rows, lanes = own.shape
    hidden_units = 2 * lanes // 3
    steps = token_count // block_rows
    row_block = pl.BlockSpec((block_rows, model_width), lambda i: (i, 0))
    in_place = pl.BlockSpec(memory_space=pl.ANY)
    flops = 2 * token_count * model_width * expert_count * hidden_units * 9
    return pl.pallas_call(
        partial(expert_kernel, steps=steps, chunk=chunk),
        grid=(steps,),
        in_specs=[
            row_block,
            row_block,
            pl.BlockSpec((block_rows, shares.shape[1]), lambda i: (i, 0)),
            in_place,
            in_place,
        ],
        out_specs=[row_block, row_block, in_place, in_place],
        out_shape=[
            jax.ShapeDtypeStruct(tokens.shape, BF16),
            jax.ShapeDtypeStruct(tokens.shape, BF16),
            jax.ShapeDtypeStruct(own.shape, BF16),
            jax.ShapeDtypeStruct(own.shape, BF16),
        ],
        scratch_shapes=[
            pltpu.VMEM((expert_count, model_width, 3 * hidden_units), BF16),
            pltpu.VMEM((expert_count, model_width, 3 * hidden_units), F32),
            pltpu.VMEM((expert_count, block_rows, hidden_units), BF16),
            pltpu.VMEM((expert_count, block_rows, 2 * hidden_units), BF16),
            pltpu.VMEM((2, model_width, lanes), BF16),
            pltpu.SemaphoreType.DMA((sources, 2, 3)),
            pltpu.SemaphoreType.DMA((2, sources)),
        ],
        compiler_params=pltpu.CompilerParams(vmem_limit_bytes=63 * 2**20),
        cost_estimate=pl.CostEstimate(
            flops=flops, bytes_accessed=80 * 2**20, transcendentals=0
        ),
    )(tokens, cotangent, shares, own, other)


def attention_rows(values, kv_head, group_size):
    first = kv_head * group_size
    return jnp.concatenate(
        [values[:, (first + r) * HEAD_DIM : (first + r + 1) * HEAD_DIM] for r in range(group_size)],
        axis=0,
    )


def quarter_turn(values):
    half = HEAD_DIM // 2
    return jnp.concatenate([-values[:, half:], values[:, :half]], axis=1)


def window_mask(start, doc_start_ref, first_ref, block_rows, window):
    key_index = start + lax.broadcasted_iota(jnp.int32, (block_rows, window), 1)
    query_index = (
        first_ref[0]
        + pl.program_id(0) * block_rows
        + lax.broadcasted_iota(jnp.int32, (block_rows, window), 0)
    )
    return (key_index <= query_index) & (key_index >= doc_start_ref[...])


def window_start(first_ref, block_rows, window):
    end = first_ref[0] + (pl.program_id(0) + 1) * block_rows
    return pl.multiple_of(jnp.maximum(end - window, 0), block_rows)


def attention_forward_kernel(
    first_ref, query_ref, key_value_ref, doc_start_ref, attended_ref, lse_ref, *, group_size, window
):
    block_rows = query_ref.shape[0]
    kv_heads = key_value_ref.shape[1] // (2 * HEAD_DIM)
    start = window_start(first_ref, block_rows, window)
    allowed = window_mask(start, doc_start_ref, first_ref, block_rows, window)
    bias = jnp.where(allowed, 0.0, -1e30)
    bias = jnp.concatenate([bias] * group_size, axis=0)
    keys_values = key_value_ref[pl.ds(start, window), :]
    queries = query_ref[...]
    parts = []
    for g in range(kv_heads):
        keys = keys_values[:, g * HEAD_DIM : (g + 1) * HEAD_DIM]
        values = keys_values[:, (kv_heads + g) * HEAD_DIM : (kv_heads + g + 1) * HEAD_DIM]
        scores = lax.dot_general(
            attention_rows(queries, g, group_size), keys, LAST_LAST, preferred_element_type=F32
        )
        scores = scores * HEAD_DIM**-0.5 + bias
        row_max = jnp.max(scores, axis=1, keepdims=True)
        exponent = jnp.exp(scores - row_max)
        total = jnp.sum(exponent, axis=1, keepdims=True)
        probs = (exponent * (1.0 / total)).astype(BF16)
        mixed = jnp.dot(probs, values, preferred_element_type=F32).astype(BF16)
        lse_ref[0, g] = row_max + jnp.log(total)
        parts += [mixed[r * block_rows : (r + 1) * block_rows] for r in range(group_size)]
    attended_ref[...] = jnp.concatenate(parts, axis=1)


def attention_backward_kernel(
    first_ref,
    query_ref,
    key_value_ref,
    doc_start_ref,
    lse_ref,
    grad_ref,
    turns_ref,
    query_turns_ref,
    grad_query_ref,
    grad_key_value_ref,
    grad_keys,
    grad_values,
    *,
    group_size,
    window,
    steps,
):
    step = pl.program_id(0)
    block_rows = query_ref.shape[0]
    kv_heads = key_value_ref.shape[1] // (2 * HEAD_DIM)

    @pl.when(step == 0)
    def _():
        grad_keys[...] = jnp.zeros_like(grad_keys)
        grad_values[...] = jnp.zeros_like(grad_values)

    start = window_start(first_ref, block_rows, window)
    allowed = window_mask(start, doc_start_ref, first_ref, block_rows, window)
    bias = jnp.where(allowed, 0.0, -1e30)
    bias = jnp.concatenate([bias] * group_size, axis=0)
    rows = pl.ds(start, window)
    keys_values = key_value_ref[rows, :]
    queries = query_ref[...]
    grads = grad_ref[...]
    query_turns = jnp.concatenate([query_turns_ref[...]] * group_size, axis=0)
    parts = []
    for g in range(kv_heads):
        keys = keys_values[:, g * HEAD_DIM : (g + 1) * HEAD_DIM]
        values = keys_values[:, (kv_heads + g) * HEAD_DIM : (kv_heads + g + 1) * HEAD_DIM]
        query_rows = attention_rows(queries, g, group_size)
        grad_rows = attention_rows(grads, g, group_size)
        scores = lax.dot_general(query_rows, keys, LAST_LAST, preferred_element_type=F32)
        probs = jnp.exp(scores * HEAD_DIM**-0.5 + bias - lse_ref[0, g])
        grad_probs = lax.dot_general(grad_rows, values, LAST_LAST, preferred_element_type=F32)
        inner = jnp.sum(grad_probs * probs, axis=1, keepdims=True)
        grad_scores = (HEAD_DIM**-0.5 * (probs * (grad_probs - inner))).astype(BF16)
        grad_values[g, rows, :] += lax.dot_general(
            probs.astype(BF16), grad_rows, FIRST_FIRST, preferred_element_type=F32
        )
        both_queries = jnp.concatenate([query_rows, quarter_turn(query_rows)], axis=1)
        grad_keys[g, rows, :] += lax.dot_general(
            grad_scores, both_queries, FIRST_FIRST, preferred_element_type=F32
        )
        both_keys = jnp.concatenate([keys, quarter_turn(keys)], axis=1)
        turned = jnp.dot(grad_scores, both_keys, preferred_element_type=F32) * query_turns
        grad_query = (turned[:, :HEAD_DIM] + turned[:, HEAD_DIM:]).astype(BF16)
        parts += [grad_query[r * block_rows : (r + 1) * block_rows] for r in range(group_size)]
    grad_query_ref[...] = jnp.concatenate(parts, axis=1)

    @pl.when(step == steps - 1)
    def _():
        key_parts, value_parts = [], []
        for g in range(kv_heads):
            turned = grad_keys[g] * turns_ref[...]
            key_parts.append((turned[:, :HEAD_DIM] + turned[:, HEAD_DIM:]).astype(BF16))
            value_parts.append(grad_values[g].astype(BF16))
        grad_key_value_ref[...] = jnp.concatenate(key_parts + value_parts, axis=1)


def attention_specs(queries, keys_values, block_rows):
    return dict(
        smem=pl.BlockSpec(memory_space=pltpu.SMEM),
        rows=pl.BlockSpec((block_rows, queries.shape[1]), lambda i: (i, 0)),
        whole=pl.BlockSpec(keys_values.shape, lambda i: (0, 0)),
        column=pl.BlockSpec((block_rows, 1), lambda i: (i, 0)),
    )


def attention_forward(first, queries, keys_values, doc_start, block_rows=256, reach=1024):
    row_count, query_cols = queries.shape
    kv_heads = keys_values.shape[1] // (2 * HEAD_DIM)
    group_size = query_cols // HEAD_DIM // kv_heads
    steps = row_count // block_rows
    window = min(reach + block_rows, keys_values.shape[0])
    specs = attention_specs(queries, keys_values, block_rows)
    stacked = group_size * block_rows
    return pl.pallas_call(
        partial(attention_forward_kernel, group_size=group_size, window=window),
        grid=(steps,),
        in_specs=[specs["smem"], specs["rows"], specs["whole"], specs["column"]],
        out_specs=[
            specs["rows"],
            pl.BlockSpec((1, kv_heads, stacked, 1), lambda i: (i, 0, 0, 0)),
        ],
        out_shape=[
            jax.ShapeDtypeStruct(queries.shape, BF16),
            jax.ShapeDtypeStruct((steps, kv_heads, stacked, 1), F32),
        ],
        compiler_params=pltpu.CompilerParams(vmem_limit_bytes=48 * 2**20),
        cost_estimate=pl.CostEstimate(
            flops=4 * row_count * window * query_cols * 8, bytes_accessed=2**22, transcendentals=0
        ),
    )(first, queries, keys_values, doc_start)


def attention_backward(
    first, queries, keys_values, doc_start, lse, grads, turns, query_turns, block_rows=256, reach=1024
):
    row_count, query_cols = queries.shape
    kv_heads = keys_values.shape[1] // (2 * HEAD_DIM)
    group_size = query_cols // HEAD_DIM // kv_heads
    steps = row_count // block_rows
    window = min(reach + block_rows, keys_values.shape[0])
    specs = attention_specs(queries, keys_values, block_rows)
    stacked = group_size * block_rows
    return pl.pallas_call(
        partial(attention_backward_kernel, group_size=group_size, window=window, steps=steps),
        grid=(steps,),
        in_specs=[
            specs["smem"],
            specs["rows"],
            specs["whole"],
            specs["column"],
            pl.BlockSpec((1, kv_heads, stacked, 1), lambda i: (i, 0, 0, 0)),
            specs["rows"],
            pl.BlockSpec(turns.shape, lambda i: (0, 0)),
            pl.BlockSpec((block_rows, turns.shape[1]), lambda i: (i, 0)),
        ],
        out_specs=[specs["rows"], specs["whole"]],
        out_shape=[
            jax.ShapeDtypeStruct(queries.shape, BF16),
            jax.ShapeDtypeStruct(keys_values.shape, BF16),
        ],
        scratch_shapes=[
            pltpu.VMEM((kv_heads, keys_values.shape[0], 2 * HEAD_DIM), F32),
            pltpu.VMEM((kv_heads, keys_values.shape[0], HEAD_DIM), F32),
        ],
        compiler_params=pltpu.CompilerParams(vmem_limit_bytes=48 * 2**20),
        cost_estimate=pl.CostEstimate(
            flops=10 * row_count * window * query_cols * 8, bytes_accessed=2**23, transcendentals=0
        ),
    )(first, queries, keys_values, doc_start, lse, grads, turns, query_turns)


def rotation_tables(positions):
    half_dim = HEAD_DIM // 2
    frequencies = 10000.0 ** (-2.0 * jnp.arange(half_dim, dtype=F32) / HEAD_DIM)
    angles = positions.astype(F32)[:, None] * frequencies[None, :]
    cosine, sine = jnp.cos(angles), jnp.sin(angles)
    return jnp.concatenate([cosine, cosine, -sine, -sine], axis=1)


def turned_columns(weight):
    rows, cols = weight.shape
    halves = weight.reshape(rows, cols // HEAD_DIM, 2, HEAD_DIM // 2)
    return jnp.stack([-halves[:, :, 1], halves[:, :, 0]], axis=2).reshape(rows, cols)


def expert_plan(
    residual_in,
    gain_attn,
    query_weight,
    key_projection_weight,
    value_projection_weight,
    out_weight,
    gain_ffn,
    gate_weight,
    up_weight,
    down_weight,
    segments,
    routes,
    shares,
    cotangent,
    *,
    groups,
    tensor_size,
):
    row_count, model_width = residual_in.shape
    query_cols = query_weight.shape[1]
    kv_cols = key_projection_weight.shape[1]
    expert_count, slice_rows, unit_count = gate_weight.shape
    own_experts = expert_count // groups
    piece_rows = row_count // tensor_size
    context_rank = lax.axis_index(CONTEXT)
    tensor_rank = lax.axis_index(TENSOR)
    group_rank = lax.axis_index(SHARD) * lax.axis_size(CONTEXT) + context_rank
    own_first = context_rank * row_count
    piece_first = tensor_rank * piece_rows
    sibling = [(i, i ^ 1) for i in range(tensor_size)]
    across = [(i, i ^ 2) for i in range(tensor_size)]

    def own_piece(values):
        return lax.dynamic_slice_in_dim(values, piece_first, piece_rows)

    def padded_column(gain):
        return jnp.pad(gain[:, None], ((0, 0), (0, 127)))

    with jax.named_scope("weights"):
        qkv_full = lax.all_gather(
            jnp.concatenate(
                [
                    query_weight,
                    key_projection_weight,
                    value_projection_weight,
                    padded_column(gain_attn),
                ],
                axis=1,
            ),
            GROUP,
            axis=0,
            tiled=True,
        )
        qkv_cols = query_cols + 2 * kv_cols
        qkv_weight = qkv_full[:, :qkv_cols]
        gain_attn_float = qkv_full[:, qkv_cols].astype(F32)
        slices = jnp.concatenate(
            [gate_weight, up_weight, down_weight.transpose(0, 2, 1)], axis=2
        )
        owned = lax.all_to_all(slices, GROUP, 0, 0, tiled=True)
        out_gathered = lax.all_gather(
            jnp.concatenate([out_weight.T, padded_column(gain_ffn)], axis=1),
            GROUP,
            axis=0,
            tiled=True,
        )
        out_transposed = out_gathered[:, :query_cols]
        gain_ffn_float = out_gathered[:, query_cols].astype(F32)

    def gather_tokens(piece):
        own_core = lax.all_gather(piece, GROUP, axis=0, tiled=False)
        other_core = lax.ppermute(own_core, TENSOR, sibling)
        return jnp.stack([own_core, other_core], axis=1).reshape(-1, piece.shape[1])

    with jax.named_scope("attention"):
        positions = doc_positions(segments)
        turns = rotation_tables(positions)
        own_turns = lax.dynamic_slice_in_dim(turns, own_first, row_count)
        own_index = own_first + jnp.arange(row_count, dtype=jnp.int32)
        doc_start = own_index - lax.dynamic_slice_in_dim(positions, own_first, row_count)
        input_float = residual_in.astype(F32)
        first_normalized = rms_scale(input_float, gain_attn_float).astype(BF16)
        rotated_cols = query_cols + kv_cols
        projected = jnp.dot(
            first_normalized,
            jnp.concatenate([qkv_weight, turned_columns(qkv_weight[:, :rotated_cols])], axis=1),
            preferred_element_type=F32,
        )
        heads = rotated_cols // HEAD_DIM
        rotated = (
            projected[:, :rotated_cols] * jnp.tile(own_turns[:, :HEAD_DIM], (1, heads))
            - projected[:, qkv_cols:] * jnp.tile(own_turns[:, HEAD_DIM:], (1, heads))
        ).astype(BF16)
        queries = rotated[:, :query_cols]
        keys_values = lax.all_gather(
            jnp.concatenate(
                [rotated[:, query_cols:], projected[:, rotated_cols:qkv_cols].astype(BF16)], axis=1
            ),
            CONTEXT,
            axis=0,
            tiled=True,
        )
        first = own_first.reshape(1).astype(jnp.int32)
        attended, lse = attention_forward(first, queries, keys_values, doc_start[:, None])

    with jax.named_scope("routing"):
        owned, attended = lax.optimization_barrier((owned, attended))
        others = lax.ppermute(owned, TENSOR, across)
        cotangent_piece = own_piece(cotangent)
        cotangent_all = gather_tokens(cotangent_piece)
        spread = jnp.sum(
            jnp.where(
                own_piece(routes)[:, :, None] == jnp.arange(expert_count, dtype=jnp.int32),
                own_piece(shares)[:, :, None],
                0.0,
            ),
            axis=1,
        )
        token_shares = lax.dynamic_slice_in_dim(
            gather_tokens(spread), group_rank * own_experts, own_experts, axis=1
        )
        token_shares = jnp.pad(token_shares, ((0, 0), (0, 8 - own_experts)))

    with jax.named_scope("attention_out"):
        attn_part = lax.dot_general(
            attended, out_transposed, LAST_LAST, preferred_element_type=F32
        )
        attn_piece = lax.psum_scatter(
            attn_part.astype(BF16), TENSOR, scatter_dimension=0, tiled=True
        )
        hidden = own_piece(residual_in).astype(F32) + attn_piece.astype(F32)
        normed_ffn, ffn_norm_back = jax.vjp(rms_scale, hidden, gain_ffn_float)

    with jax.named_scope("experts"):
        tokens_all = gather_tokens(normed_ffn.astype(BF16))
        shape = (groups, own_experts, slice_rows, 3 * unit_count)
        out_parts, grad_token_parts, grad_own, grad_other = experts(
            tokens_all, cotangent_all, token_shares, owned.reshape(shape), others.reshape(shape)
        )

    def reduce_tokens(parts):
        parts = parts.reshape(groups, 2, piece_rows, model_width)
        received = lax.ppermute(parts[:, 1], TENSOR, sibling)
        both = (parts[:, 0].astype(F32) + received.astype(F32)).astype(BF16)
        return lax.psum_scatter(
            both.reshape(groups * piece_rows, model_width),
            GROUP,
            scatter_dimension=0,
            tiled=True,
        ).astype(F32)

    with jax.named_scope("expert_grads"):
        grad_second = reduce_tokens(grad_token_parts)
        received = lax.ppermute(grad_other, TENSOR, across)
        total = (grad_own.astype(F32) + received.astype(F32)).astype(BF16)
        returned = lax.all_to_all(
            total.reshape(expert_count, slice_rows, 3 * unit_count), GROUP, 0, 0, tiled=True
        )
        grad_hidden_norm, grad_gain_ffn_local = ffn_norm_back(grad_second)
        grad_hidden = cotangent_piece.astype(F32) + grad_hidden_norm
        grad_hidden_low = lax.all_gather(grad_hidden.astype(BF16), TENSOR, axis=0, tiled=True)
        output_piece = (hidden + reduce_tokens(out_parts)).astype(BF16)
        output = lax.all_gather(output_piece, TENSOR, axis=0, tiled=True)

    with jax.named_scope("attention_back"):
        grad_out_local = lax.dot_general(
            grad_hidden_low, attended, FIRST_FIRST, preferred_element_type=F32
        )
        grad_out_transposed = lax.psum_scatter(
            grad_out_local.astype(BF16), GROUP, scatter_dimension=0, tiled=True
        )
        grad_attended = jnp.dot(grad_hidden_low, out_transposed, preferred_element_type=F32)
        grad_query_lin, grad_key_value = attention_backward(
            first,
            queries,
            keys_values,
            doc_start[:, None],
            lse,
            grad_attended.astype(BF16),
            turns,
            own_turns,
        )
        grad_key_value = lax.psum_scatter(
            grad_key_value, CONTEXT, scatter_dimension=0, tiled=True
        )
        grad_projected = jnp.concatenate([grad_query_lin, grad_key_value], axis=1)
        grad_first_part = lax.dot_general(
            grad_projected, qkv_weight, LAST_LAST, preferred_element_type=F32
        )
        grad_first = lax.psum_scatter(
            grad_first_part.astype(BF16), TENSOR, scatter_dimension=0, tiled=True
        ).astype(F32)
        _, attn_norm_back = jax.vjp(
            rms_scale, own_piece(residual_in).astype(F32), gain_attn_float
        )
        grad_input_norm, grad_gain_attn_local = attn_norm_back(grad_first)
        grad_input = lax.all_gather(
            (grad_hidden + grad_input_norm).astype(BF16), TENSOR, axis=0, tiled=True
        )
        grad_qkv_local = lax.dot_general(
            first_normalized, grad_projected, FIRST_FIRST, preferred_element_type=F32
        )
        grad_qkv = lax.psum_scatter(
            grad_qkv_local.astype(BF16), GROUP, scatter_dimension=0, tiled=True
        ).astype(F32)
        gains = lax.psum(
            jnp.stack([grad_gain_attn_local, grad_gain_ffn_local]), GROUP + (TENSOR,)
        )
        gains = lax.dynamic_slice_in_dim(gains, group_rank * slice_rows, slice_rows, axis=1)
    units = unit_count
    return (
        output,
        grad_input,
        gains[0],
        grad_qkv[:, :query_cols],
        grad_qkv[:, query_cols:rotated_cols],
        grad_qkv[:, rotated_cols:],
        grad_out_transposed.astype(F32).T,
        gains[1],
        returned[:, :, :units].astype(F32),
        returned[:, :, units : 2 * units].astype(F32),
        returned[:, :, 2 * units :].transpose(0, 2, 1).astype(F32),
    )


def solution(mesh):
    placed = (
        P(GROUP, None),
        P(GROUP),
        P(GROUP, TENSOR),
        P(GROUP, TENSOR),
        P(GROUP, TENSOR),
        P(TENSOR, GROUP),
        P(GROUP),
        P(None, GROUP, TENSOR),
        P(None, GROUP, TENSOR),
        P(None, TENSOR, GROUP),
        P(SHARD),
        P(GROUP, None),
        P(GROUP, None),
        P(GROUP, None),
    )
    sizes = dict(mesh.shape)
    if sizes[SHARD] == 4 and sizes[CONTEXT] == 2 and sizes[TENSOR] == 4:
        plan = partial(
            expert_plan, groups=sizes[SHARD] * sizes[CONTEXT], tensor_size=sizes[TENSOR]
        )
    else:
        plan = gathered_plan
    return jax.shard_map(
        plan,
        mesh=mesh,
        in_specs=placed,
        out_specs=(
            P(GROUP, None),
            P(GROUP, None),
            P(GROUP),
            P(GROUP, TENSOR),
            P(GROUP, TENSOR),
            P(GROUP, TENSOR),
            P(TENSOR, GROUP),
            P(GROUP),
            P(None, GROUP, TENSOR),
            P(None, GROUP, TENSOR),
            P(None, TENSOR, GROUP),
        ),
        check_vma=False,
    )
```

```python
from functools import partial

import jax
import jax.numpy as jnp
from jax import lax
from jax.experimental import pallas as pl
from jax.experimental.pallas import tpu as pltpu
from jax.sharding import PartitionSpec as P

HEAD_DIM = 64
NDOCS = 5
SHARD = "shard"
CONTEXT = "context"
TENSOR = "tensor"
GROUP = (SHARD, CONTEXT)
PRODUCT_0 = "qgrd,kgd->grqk"
PRODUCT_1 = "grqk,kgd->qgrd"
PRODUCT_2 = "ecd,edf->ecf"
PRODUCT_3 = "ecf,efd->ecd"
PRODUCT_4 = "ecd,efd->ecf"
PRODUCT_5 = "ecf,edf->ecd"
PRODUCT_6 = "ecd,ecf->edf"
PRODUCT_7 = "ecf,ecd->efd"
PRODUCT_8 = "grqk,qgrd->kgd"


epsilon = 1e-06


def rms_scale(values, gain):
    return values * lax.rsqrt(jnp.mean(values * values, axis=-1, keepdims=True) + epsilon) * gain


def doc_positions(segment_ids):
    sequence_length = segment_ids.shape[-1]
    index_row = jnp.arange(sequence_length, dtype=jnp.int32)
    documents = jnp.arange(NDOCS, dtype=jnp.int32)
    doc_starts = jnp.sum((segment_ids[..., :, None] < documents).astype(jnp.int32), axis=-2)
    own_start = jnp.sum(
        jnp.where(segment_ids[..., :, None] == documents, doc_starts[..., None, :], 0), axis=-1
    )
    return index_row - own_start


def rotary(values, positions):
    half_dim = values.shape[-1] // 2
    frequencies = 10000.0 ** (-2.0 * jnp.arange(half_dim, dtype=jnp.float32) / values.shape[-1])
    angles = positions.astype(jnp.float32)[:, None] * frequencies[None, :]
    cosine = jnp.cos(angles)[:, None, :]
    sines = jnp.sin(angles)[:, None, :]
    first_half = values[..., :half_dim]
    second_half = values[..., half_dim:]
    return jnp.concatenate(
        [first_half * cosine - second_half * sines, second_half * cosine + first_half * sines],
        axis=-1,
    )


def swiglu(gate_value, up_value):
    return jax.nn.silu(gate_value) * up_value


def dispatch(routes, shares, block_rows, capacity, expert_count):
    block_count = routes.shape[0] // block_rows
    picks = routes.shape[1]
    chosen = routes.reshape(block_count, block_rows * picks)
    onehot = (chosen[:, :, None] == jnp.arange(expert_count, dtype=jnp.int32)).astype(jnp.int32)
    ranked = jnp.sum((jnp.cumsum(onehot, axis=1) - onehot) * onehot, axis=2)
    slot_index = (
        chosen * (block_count * capacity)
        + jnp.arange(block_count, dtype=jnp.int32)[:, None] * capacity
        + ranked
    )
    tokens = jnp.arange(block_count * block_rows * picks, dtype=jnp.int32) // picks
    total_slots = expert_count * block_count * capacity
    slot_rows = jnp.zeros((total_slots,), jnp.int32).at[slot_index.reshape(-1)].set(tokens)
    slot_share = (
        jnp.zeros((total_slots,), jnp.float32).at[slot_index.reshape(-1)].set(shares.reshape(-1))
    )
    return (slot_rows, slot_share)


def gathered_plan(
    residual_in,
    gain_attn,
    query_weight,
    key_projection_weight,
    value_projection_weight,
    out_weight,
    gain_ffn,
    gate_weight,
    up_weight,
    down_weight,
    segments,
    routes,
    shares,
    cotangent,
):
    row_count, model_width = residual_in.shape
    head_size = HEAD_DIM
    query_cols = query_weight.shape[1]
    kv_heads = key_projection_weight.shape[1] // head_size
    group_size = query_cols // head_size // kv_heads
    expert_count = gate_weight.shape[0]
    capacity = row_count * routes.shape[1] * 5 // (4 * expert_count)
    score_scale = head_size ** (-0.5)
    context_rank = lax.axis_index(CONTEXT)
    own_first = context_rank * row_count
    gain_attn_full, gain_ffn_full, query_full, key_full, value_full, out_full = (
        lax.all_gather(gain_attn, GROUP, axis=0, tiled=True),
        lax.all_gather(gain_ffn, GROUP, axis=0, tiled=True),
        lax.all_gather(query_weight, GROUP, axis=0, tiled=True),
        lax.all_gather(key_projection_weight, GROUP, axis=0, tiled=True),
        lax.all_gather(value_projection_weight, GROUP, axis=0, tiled=True),
        lax.all_gather(out_weight, GROUP, axis=1, tiled=True),
    )
    gain_attn_float = gain_attn_full.astype(jnp.float32)
    gain_ffn_float = gain_ffn_full.astype(jnp.float32)
    positions = doc_positions(segments)
    own_positions = lax.dynamic_slice_in_dim(positions, own_first, row_count)
    own_ids = lax.dynamic_slice_in_dim(segments, own_first, row_count)
    own_index = own_first + jnp.arange(row_count, dtype=jnp.int32)
    input_float = residual_in.astype(jnp.float32)
    normed_attn, attn_norm_back = jax.vjp(rms_scale, input_float, gain_attn_float)
    first_normalized = normed_attn.astype(jnp.bfloat16)
    query_lin = jnp.dot(first_normalized, query_full, preferred_element_type=jnp.float32).reshape(
        row_count, -1, head_size
    )
    key_linear = jnp.dot(first_normalized, key_full, preferred_element_type=jnp.float32).reshape(
        row_count, -1, head_size
    )
    value_tokens = jnp.dot(first_normalized, value_full, preferred_element_type=jnp.float32).astype(
        jnp.bfloat16
    )
    rope_local = partial(rotary, positions=own_positions)
    query_rot, rope_query_back = jax.vjp(rope_local, query_lin)
    key_rot, rope_key_back = jax.vjp(rope_local, key_linear)
    query_low = query_rot.astype(jnp.bfloat16)
    key_low = key_rot.astype(jnp.bfloat16).reshape(row_count, -1)
    key_all, value_all = (
        lax.all_gather(key_low, CONTEXT, axis=0, tiled=True),
        lax.all_gather(value_tokens, CONTEXT, axis=0, tiled=True),
    )
    key_index = jnp.arange(key_all.shape[0], dtype=jnp.int32)
    key_ids = jnp.take(segments, jnp.clip(key_index, 0, segments.shape[0] - 1))
    key_valid = key_index >= 0
    key_heads = key_all.reshape(-1, kv_heads, head_size)
    value_heads = value_all.reshape(-1, kv_heads, head_size)
    query_heads = query_low.reshape(row_count, kv_heads, group_size, head_size)
    block_rows = min(512, row_count)
    block_starts = list(range(0, row_count, block_rows))

    def block_scores(block_first):
        query_block = query_heads[block_first : block_first + block_rows]
        raw_scores = jnp.einsum(
            PRODUCT_0, query_block, key_heads, preferred_element_type=jnp.float32
        )
        block_ids = own_ids[block_first : block_first + block_rows]
        block_index = own_index[block_first : block_first + block_rows]
        allowed = (
            key_valid[None, :]
            & (key_ids[None, :] == block_ids[:, None])
            & (key_index[None, :] <= block_index[:, None])
        )
        return (query_block, jnp.where(allowed, raw_scores * score_scale, -1e30))

    mixed_parts = []
    lse_parts = []
    for block_first in block_starts:
        query_block, scores = block_scores(block_first)
        row_max = jnp.max(scores, axis=-1, keepdims=True)
        exponent = jnp.exp(scores - row_max)
        row_total = jnp.sum(exponent, axis=-1, keepdims=True)
        probs = (exponent / row_total).astype(jnp.bfloat16)
        mixed_parts.append(
            jnp.einsum(PRODUCT_1, probs, value_heads, preferred_element_type=jnp.float32)
        )
        lse_parts.append(row_max + jnp.log(row_total))
    attended = (
        jnp.concatenate(mixed_parts, axis=0).reshape(row_count, query_cols).astype(jnp.bfloat16)
    )
    attn_part = jnp.dot(attended, out_full, preferred_element_type=jnp.float32)
    hidden = input_float + lax.psum(attn_part.astype(jnp.bfloat16), TENSOR).astype(jnp.float32)
    normed_ffn, ffn_norm_back = jax.vjp(rms_scale, hidden, gain_ffn_float)
    normed_second = normed_ffn.astype(jnp.bfloat16)
    slot_rows, slot_share = dispatch(routes, shares, row_count, capacity, expert_count)
    per_turn = expert_count // 5
    turn_count = expert_count // per_turn
    turn_slots = per_turn * capacity

    def local_experts(turn_index):
        gate_part = lax.dynamic_slice_in_dim(gate_weight, turn_index * per_turn, per_turn, 0)
        up_part = lax.dynamic_slice_in_dim(up_weight, turn_index * per_turn, per_turn, 0)
        down_part = lax.dynamic_slice_in_dim(down_weight, turn_index * per_turn, per_turn, 0)
        return (gate_part, up_part, down_part)

    def turn_inputs(turn_index):
        token_rows = lax.dynamic_slice_in_dim(slot_rows, turn_index * turn_slots, turn_slots)
        share_rows = lax.dynamic_slice_in_dim(slot_share, turn_index * turn_slots, turn_slots)
        picked = normed_second[token_rows].reshape(per_turn, capacity, model_width)
        return (token_rows, share_rows, picked)

    def forward_turn(running, turn_index):
        gate_part, up_part, down_part = local_experts(turn_index)
        gate_full, up_full, down_full = (
            lax.all_gather(gate_part, GROUP, axis=1, tiled=True),
            lax.all_gather(up_part, GROUP, axis=1, tiled=True),
            lax.all_gather(down_part, GROUP, axis=2, tiled=True),
        )
        token_rows, share_rows, picked = turn_inputs(turn_index)
        gate_value = jnp.einsum(
            PRODUCT_2, picked, gate_full, preferred_element_type=jnp.float32
        )
        up_value = jnp.einsum(PRODUCT_2, picked, up_full, preferred_element_type=jnp.float32)
        inner = swiglu(gate_value, up_value).astype(jnp.bfloat16)
        expert_result = jnp.einsum(
            PRODUCT_3, inner, down_full, preferred_element_type=jnp.float32
        ).reshape(turn_slots, model_width)
        return (running.at[token_rows].add(expert_result * share_rows[:, None]), None)

    turn_ids = jnp.arange(turn_count, dtype=jnp.int32)
    expert_part, _ = lax.scan(
        forward_turn, jnp.zeros((row_count, model_width), jnp.float32), turn_ids
    )
    expert_total = lax.psum(expert_part.astype(jnp.bfloat16), TENSOR).astype(jnp.float32)
    output = (hidden + expert_total).astype(jnp.bfloat16)
    upstream = cotangent.astype(jnp.float32)

    def backward_turn(running, turn_index):
        gate_part, up_part, down_part = local_experts(turn_index)
        gate_full, up_full, down_full = (
            lax.all_gather(gate_part, GROUP, axis=1, tiled=True),
            lax.all_gather(up_part, GROUP, axis=1, tiled=True),
            lax.all_gather(down_part, GROUP, axis=2, tiled=True),
        )
        token_rows, share_rows, picked = turn_inputs(turn_index)
        gate_value = jnp.einsum(
            PRODUCT_2, picked, gate_full, preferred_element_type=jnp.float32
        )
        up_value = jnp.einsum(PRODUCT_2, picked, up_full, preferred_element_type=jnp.float32)
        inner_float, swiglu_back = jax.vjp(swiglu, gate_value, up_value)
        inner = inner_float.astype(jnp.bfloat16)
        grad_slot = (
            (upstream[token_rows] * share_rows[:, None])
            .astype(jnp.bfloat16)
            .reshape(per_turn, capacity, model_width)
        )
        grad_inner = jnp.einsum(
            PRODUCT_4, grad_slot, down_full, preferred_element_type=jnp.float32
        )
        grad_gate_value, grad_up_value = swiglu_back(grad_inner)
        grad_gate_low = grad_gate_value.astype(jnp.bfloat16)
        grad_up_low = grad_up_value.astype(jnp.bfloat16)
        grad_picked = jnp.einsum(
            PRODUCT_5, grad_gate_low, gate_full, preferred_element_type=jnp.float32
        )
        grad_picked = grad_picked + jnp.einsum(
            PRODUCT_5, grad_up_low, up_full, preferred_element_type=jnp.float32
        )
        running = running.at[token_rows].add(grad_picked.reshape(turn_slots, model_width))
        shard_grads = (
            lax.psum_scatter(
                jnp.einsum(
                    PRODUCT_6, picked, grad_gate_low, preferred_element_type=jnp.float32
                ).astype(jnp.bfloat16),
                GROUP,
                scatter_dimension=1,
                tiled=True,
            ).astype(jnp.float32),
            lax.psum_scatter(
                jnp.einsum(
                    PRODUCT_6, picked, grad_up_low, preferred_element_type=jnp.float32
                ).astype(jnp.bfloat16),
                GROUP,
                scatter_dimension=1,
                tiled=True,
            ).astype(jnp.float32),
            lax.psum_scatter(
                jnp.einsum(
                    PRODUCT_7, inner, grad_slot, preferred_element_type=jnp.float32
                ).astype(jnp.bfloat16),
                GROUP,
                scatter_dimension=2,
                tiled=True,
            ).astype(jnp.float32),
        )
        return (running, shard_grads)

    grad_second_part, stacked_grads = lax.scan(
        backward_turn, jnp.zeros((row_count, model_width), jnp.float32), turn_ids
    )
    grad_gate_out = stacked_grads[0].reshape(gate_weight.shape)
    grad_up_out = stacked_grads[1].reshape(up_weight.shape)
    grad_down_out = stacked_grads[2].reshape(down_weight.shape)
    grad_second = lax.psum(grad_second_part.astype(jnp.bfloat16), TENSOR).astype(jnp.float32)
    grad_hidden_norm, grad_gain_ffn_local = ffn_norm_back(grad_second)
    grad_hidden = upstream + grad_hidden_norm
    grad_hidden_low = grad_hidden.astype(jnp.bfloat16)
    grad_out_local = jnp.einsum(
        "tc,td->cd", attended, grad_hidden_low, preferred_element_type=jnp.float32
    )
    grad_attended = jnp.einsum(
        "td,cd->tc", grad_hidden_low, out_full, preferred_element_type=jnp.float32
    )
    grad_attended = grad_attended.astype(jnp.bfloat16).reshape(
        row_count, kv_heads, group_size, head_size
    )
    grad_query_parts = []
    grad_keys = jnp.zeros(key_heads.shape, jnp.float32)
    grad_values = jnp.zeros(value_heads.shape, jnp.float32)
    for block_number in range(len(block_starts)):
        block_first = block_starts[block_number]
        query_block, scores = block_scores(block_first)
        probs_float = jnp.exp(scores - lse_parts[block_number])
        probs = probs_float.astype(jnp.bfloat16)
        grad_block = grad_attended[block_first : block_first + block_rows]
        grad_probs = jnp.einsum(
            PRODUCT_0, grad_block, value_heads, preferred_element_type=jnp.float32
        )
        inner_sum = jnp.sum(grad_probs * probs_float, axis=-1, keepdims=True)
        grad_scores = (score_scale * (probs_float * (grad_probs - inner_sum))).astype(jnp.bfloat16)
        grad_query_parts.append(
            jnp.einsum(PRODUCT_1, grad_scores, key_heads, preferred_element_type=jnp.float32)
        )
        grad_keys = grad_keys + jnp.einsum(
            PRODUCT_8, grad_scores, query_block, preferred_element_type=jnp.float32
        )
        grad_values = grad_values + jnp.einsum(
            PRODUCT_8, probs, grad_block, preferred_element_type=jnp.float32
        )
    grad_key_own, grad_value_own = (
        lax.psum_scatter(
            grad_keys.astype(jnp.bfloat16), CONTEXT, scatter_dimension=0, tiled=True
        ).astype(jnp.float32),
        lax.psum_scatter(
            grad_values.astype(jnp.bfloat16), CONTEXT, scatter_dimension=0, tiled=True
        ).astype(jnp.float32),
    )
    grad_query_all = jnp.concatenate(grad_query_parts, axis=0).reshape(row_count, -1, head_size)
    grad_query_lin = rope_query_back(grad_query_all)[0].astype(jnp.bfloat16).reshape(row_count, -1)
    grad_key_lin = rope_key_back(grad_key_own)[0].astype(jnp.bfloat16).reshape(row_count, -1)
    grad_value_low = grad_value_own.astype(jnp.bfloat16).reshape(row_count, -1)
    grad_first_part = jnp.einsum(
        "tc,dc->td", grad_query_lin, query_full, preferred_element_type=jnp.float32
    )
    grad_first_part = grad_first_part + jnp.einsum(
        "tc,dc->td", grad_key_lin, key_full, preferred_element_type=jnp.float32
    )
    grad_first_part = grad_first_part + jnp.einsum(
        "tc,dc->td", grad_value_low, value_full, preferred_element_type=jnp.float32
    )
    grad_first = lax.psum(grad_first_part.astype(jnp.bfloat16), TENSOR).astype(jnp.float32)
    grad_input_norm, grad_gain_attn_local = attn_norm_back(grad_first)
    grad_input = (grad_hidden + grad_input_norm).astype(jnp.bfloat16)
    grad_query_local = jnp.einsum(
        "td,tc->dc", first_normalized, grad_query_lin, preferred_element_type=jnp.float32
    )
    grad_key_local = jnp.einsum(
        "td,tc->dc", first_normalized, grad_key_lin, preferred_element_type=jnp.float32
    )
    grad_value_local = jnp.einsum(
        "td,tc->dc", first_normalized, grad_value_low, preferred_element_type=jnp.float32
    )
    reduced = (
        lax.psum_scatter(
            grad_gain_attn_local.astype(jnp.bfloat16),
            GROUP,
            scatter_dimension=0,
            tiled=True,
        ).astype(jnp.float32),
        lax.psum_scatter(
            grad_query_local.astype(jnp.bfloat16),
            GROUP,
            scatter_dimension=0,
            tiled=True,
        ).astype(jnp.float32),
        lax.psum_scatter(
            grad_key_local.astype(jnp.bfloat16),
            GROUP,
            scatter_dimension=0,
            tiled=True,
        ).astype(jnp.float32),
        lax.psum_scatter(
            grad_value_local.astype(jnp.bfloat16),
            GROUP,
            scatter_dimension=0,
            tiled=True,
        ).astype(jnp.float32),
        lax.psum_scatter(
            grad_out_local.astype(jnp.bfloat16),
            GROUP,
            scatter_dimension=1,
            tiled=True,
        ).astype(jnp.float32),
        lax.psum_scatter(
            grad_gain_ffn_local.astype(jnp.bfloat16),
            GROUP,
            scatter_dimension=0,
            tiled=True,
        ).astype(jnp.float32),
    )
    return (
        output,
        grad_input,
        reduced[0],
        reduced[1],
        reduced[2],
        reduced[3],
        reduced[4],
        reduced[5],
        grad_gate_out,
        grad_up_out,
        grad_down_out,
    )


F32 = jnp.float32
BF16 = jnp.bfloat16
LAST_LAST = (((1,), (1,)), ((), ()))
FIRST_FIRST = (((0,), (0,)), ((), ()))


def weight_copies(own_hbm, other_hbm, weights, sems):
    sources, _, rows, lanes = own_hbm.shape
    units = lanes // 3
    return [
        pltpu.make_async_copy(
            half_hbm.at[source, :, :, pl.ds(part * units, units)],
            weights.at[
                :, pl.ds(source * rows, rows), pl.ds((2 * part + half) * units, units)
            ],
            sems.at[source, half, part],
        )
        for source in range(sources)
        for half, half_hbm in enumerate((own_hbm, other_hbm))
        for part in range(3)
    ]


def project(tokens, cotangent, weights):
    hidden_units = weights.shape[1] // 3
    gate_up = jnp.dot(tokens, weights[:, : 2 * hidden_units], preferred_element_type=F32)
    grad_inner = jnp.dot(cotangent, weights[:, 2 * hidden_units :], preferred_element_type=F32)
    return gate_up, grad_inner


def activate(gate_up, grad_inner, share):
    hidden_units = grad_inner.shape[1]
    gate, up = gate_up[:, :hidden_units], gate_up[:, hidden_units:]
    sigmoid = 1.0 / (1.0 + jnp.exp(-gate))
    silu = gate * sigmoid
    grad_inner = grad_inner * share
    inner = silu * up * share
    grad_gate = grad_inner * up * (sigmoid * (1.0 + gate * (1.0 - sigmoid)))
    grad_up = grad_inner * silu
    return inner.astype(BF16), grad_gate.astype(BF16), grad_up.astype(BF16)


MESH_ID = pl.DeviceIdType.MESH


def expert_kernel(
    piece_hbm,
    cotangent_hbm,
    shares_ref,
    own_hbm,
    other_hbm,
    out_hbm,
    grad_piece_hbm,
    grad_own_hbm,
    grad_other_hbm,
    tokens_hbm,
    parts_hbm,
    sibling_hbm,
    across_hbm,
    along_hbm,
    weights,
    grads,
    tokens_buf,
    cotangent_buf,
    inner_low,
    grad_low,
    out_buf,
    grad_buf,
    terms,
    sums,
    stage,
    load_sems,
    store_sems,
    row_sems,
    part_sems,
    term_sems,
    gather_recv,
    gather_along,
    gather_across,
    gather_sibling,
    sibling_send,
    sibling_recv,
    across_send,
    across_recv,
    along_send,
    along_recv,
    *,
    line,
    chunk,
):
    expert_count, model_width, all_units = weights.shape
    hidden_units = all_units // 3
    units = hidden_units // 2
    steps = 2 * line
    rows = piece_hbm.shape[0]
    z, y, t = lax.axis_index(SHARD), lax.axis_index(CONTEXT), lax.axis_index(TENSOR)
    sibling = (z, y, t + 1 - 2 * (t % 2))
    partner = (z, 1 - y, t)

    def inside(at):
        return (at >= 0) & (at < line)

    def block_of(at, column):
        return at * 2 + column

    def remote(source, target, send, recv, device):
        return pltpu.make_async_remote_copy(
            src_ref=source,
            dst_ref=target,
            send_sem=send,
            recv_sem=recv,
            device_id=device,
            device_id_type=MESH_ID,
        )

    def gather_line(at, side):
        here = block_of(at, y)
        return remote(
            tokens_hbm.at[here, 0],
            tokens_hbm.at[here, 0],
            gather_along.at[at, (side + 1) // 2],
            gather_recv.at[here, 0],
            (z + side, y, t),
        )

    def gather_pair(at, column):
        here = block_of(at, column)
        return remote(
            tokens_hbm.at[here, 0],
            tokens_hbm.at[here, 0],
            gather_across.at[at],
            gather_recv.at[here, 0],
            partner,
        )

    def gather_cores(here):
        return remote(
            tokens_hbm.at[here, 0],
            tokens_hbm.at[here, 1],
            gather_sibling.at[here],
            gather_recv.at[here, 1],
            sibling,
        )

    def send_cores(here, slot):
        return remote(
            grad_buf.at[slot, pl.ds(rows, rows), :],
            sibling_hbm.at[here],
            sibling_send.at[here],
            sibling_recv.at[here],
            sibling,
        )

    def send_pair(at, slot):
        return remote(
            sums.at[slot], across_hbm.at[at], across_send.at[at], across_recv.at[at], partner
        )

    def send_line(at, side, distance):
        last = (distance == 1) & (side == 1)
        slot = jnp.where(last, line, at)
        return remote(
            sums.at[2 + (side + 1) // 2],
            along_hbm.at[slot],
            along_send.at[at],
            along_recv.at[slot],
            (z + side, y, t),
        )

    def near(rank):
        half = z // 2
        mirrored = z * (1 - half) + (line - 1 - z) * half
        far = rank // 2
        place = (1 - far) * (mirrored + rank - 2 * mirrored * rank) + far * rank
        return place * (1 - half) + (line - 1 - place) * half

    def step_block(step):
        second = step // line
        rank = step * (1 - second) + (steps - 1 - step) * second
        return block_of(near(rank), y * (1 - second) + (1 - y) * second)

    barrier = pltpu.get_barrier_semaphore()
    for device in (sibling, partner):
        pl.semaphore_signal(barrier, inc=1, device_id=device, device_id_type=MESH_ID)
    for side in (-1, 1):

        @pl.when(inside(z + side))
        def _():
            pl.semaphore_signal(
                barrier, inc=1, device_id=(z + side, y, t), device_id_type=MESH_ID
            )

    below, above = (z + line - 1) // line, (2 * line - 2 - z) // line
    pl.semaphore_wait(barrier, 2 + below + above)

    own_block = block_of(z, y)
    own_copy = pltpu.make_async_copy(piece_hbm, tokens_hbm.at[own_block, 0], row_sems.at[0, 0])
    own_copy.start()
    own_copy.wait()
    for side in (-1, 1):

        @pl.when(inside(z + side))
        def _():
            gather_line(z, side).start()

    gather_pair(z, y).start()
    gather_cores(own_block).start()
    weight_loads = weight_copies(own_hbm, other_hbm, weights, load_sems)
    for copy in weight_loads:
        copy.start()
    grads[...] = jnp.zeros_like(grads)

    def row_copies(step, slot):
        here = step_block(step)
        return [
            pltpu.make_async_copy(
                tokens_hbm.at[here, 0],
                tokens_buf.at[slot, pl.ds(0, rows), :],
                row_sems.at[slot, 0],
            ),
            pltpu.make_async_copy(
                tokens_hbm.at[here, 1],
                tokens_buf.at[slot, pl.ds(rows, rows), :],
                row_sems.at[slot, 1],
            ),
            pltpu.make_async_copy(
                cotangent_hbm.at[here], cotangent_buf.at[slot], row_sems.at[slot, 2]
            ),
        ]

    def load_rows(step, slot):
        gather_cores(step_block(step)).wait_recv()
        for copy in row_copies(step, slot):
            copy.start()

    load_rows(0, 0)
    for copy in weight_loads:
        copy.wait()

    def part_copies(step, slot):
        here = step_block(step)
        return [
            pltpu.make_async_copy(
                grad_buf.at[slot, pl.ds(0, rows), :], parts_hbm.at[here], part_sems.at[slot, 0]
            ),
            pltpu.make_async_copy(out_buf, out_hbm.at[here], part_sems.at[slot, 1]),
        ]

    def add_up(sources, slot):
        copies = [
            pltpu.make_async_copy(source, terms.at[i], term_sems.at[i])
            for i, (source, _) in enumerate(sources)
        ]
        for copy, (_, there) in zip(copies, sources):
            if there is None:
                copy.start()
            else:
                pl.when(there)(copy.start)
        for i, (copy, (_, there)) in enumerate(zip(copies, sources)):
            if there is None:
                copy.wait()
            else:
                pl.when(there)(copy.wait)

                @pl.when(jnp.logical_not(there))
                def _():
                    terms[i] = jnp.zeros_like(terms[i])

        tile = 16

        @pl.loop(0, rows // tile)
        def _(number):
            here = pl.ds(pl.multiple_of(number * tile, tile), tile)
            total = terms[0, here, :].astype(F32)
            for i in range(1, len(sources)):
                total += terms[i, here, :].astype(F32)
            sums[slot, here, :] = total.astype(BF16)

    def tick(number):
        @pl.when(number < line - 1)
        def _():
            distance = number + 1
            for side in (-1, 1):
                at = z + side * distance

                @pl.when(inside(at))
                def _():
                    gather_line(at, -side).wait_recv()

                    @pl.when(inside(z - side))
                    def _():
                        gather_line(at, -side).start()

                    gather_pair(at, y).start()
                    gather_cores(block_of(at, y)).start()

        def came_across(at):
            gather_pair(at, 1 - y).wait_recv()
            gather_cores(block_of(at, 1 - y)).start()

        for distance in range(line):

            @pl.when(number == min(distance + 1, line - 1))
            def _():
                if distance == 0:
                    came_across(z)
                else:
                    for side in (-1, 1):
                        at = z + side * distance
                        pl.when(inside(at))(partial(came_across, at))

        @pl.when((number > line) & (number <= steps))
        def _():
            rank = steps - number
            at = near(rank)
            here = block_of(at, 1 - y)
            slot = number % 2

            @pl.when(number > line + 2)
            def _():
                send_pair(near(rank + 2), slot).wait_send()

            send_cores(here, 0).wait_recv()
            add_up([(parts_hbm.at[here], None), (sibling_hbm.at[here], None)], slot)
            send_pair(at, slot).start()

        @pl.when((number > line + 1) & (number <= steps))
        def _():
            distance = steps + 1 - number
            for side in (-1, 1):
                at = z + side * distance
                here = block_of(at, y)
                slot = 2 + (side + 1) // 2

                @pl.when(inside(at + side) & (number > line + 2))
                def _():
                    send_line(at + side, side, distance + 1).wait_send()

                @pl.when(inside(at))
                def _():
                    send_cores(here, 0).wait_recv()
                    send_pair(at, 0).wait_recv()
                    farther = inside(z - side)

                    @pl.when(farther)
                    def _():
                        send_line(at, side, distance + 1).wait_recv()

                    add_up(
                        [
                            (parts_hbm.at[here], None),
                            (sibling_hbm.at[here], None),
                            (across_hbm.at[at], None),
                            (along_hbm.at[at], farther),
                        ],
                        slot,
                    )
                    send_line(at, side, distance).start()

    @pl.loop(0, steps)
    def _(step):
        slot = step % 2
        for copy in row_copies(step, slot):
            copy.wait()
        here = step_block(step)
        shares = shares_ref[here]
        lane = lax.broadcasted_iota(jnp.int32, shares.shape, 1)

        def run(expert, gate_up, grad_inner):
            share = jnp.sum(jnp.where(lane == expert, shares, 0.0), axis=1, keepdims=True)
            inner, grad_gate, grad_up = activate(gate_up, grad_inner, share)
            inner_low[expert] = inner
            grad_low[expert, :, :hidden_units] = grad_gate
            grad_low[expert, :, hidden_units:] = grad_up

        def weight_grads(expert):
            grads[expert, :, : 2 * hidden_units] += lax.dot_general(
                tokens_buf[slot], grad_low[expert], FIRST_FIRST, preferred_element_type=F32
            )
            grads[expert, :, 2 * hidden_units :] += lax.dot_general(
                cotangent_buf[slot], inner_low[expert], FIRST_FIRST, preferred_element_type=F32
            )

        results = project(tokens_buf[slot], cotangent_buf[slot], weights[0])
        for expert in range(expert_count):
            run(expert, *results)
            if expert + 1 < expert_count:
                results = project(tokens_buf[slot], cotangent_buf[slot], weights[expert + 1])
            weight_grads(expert)

        @pl.when(step >= 1)
        def _():
            for copy in part_copies(step - 1, 1 - slot):
                copy.wait()

        tick(step)

        @pl.when(step >= 2)
        def _():
            send_cores(step_block(step - 2), slot).wait_send()

        @pl.loop(0, model_width // chunk)
        def _(number):
            @pl.when((number == 1) & (step + 1 < steps))
            def _():
                load_rows(step + 1, 1 - slot)

            cols = pl.ds(pl.multiple_of(number * chunk, chunk), chunk)
            total = jnp.zeros((2 * rows, chunk), F32)
            for expert in range(expert_count):
                total += lax.dot_general(
                    inner_low[expert],
                    weights[expert, cols, 2 * hidden_units :],
                    LAST_LAST,
                    preferred_element_type=F32,
                )
            out_buf[:, cols] = total.astype(BF16)
            total = jnp.zeros((2 * rows, chunk), F32)
            for expert in range(expert_count):
                total += lax.dot_general(
                    grad_low[expert],
                    weights[expert, cols, : 2 * hidden_units],
                    LAST_LAST,
                    preferred_element_type=F32,
                )
            grad_buf[slot, :, cols] = total.astype(BF16)

        for copy in part_copies(step, slot):
            copy.start()
        send_cores(here, slot).start()

    for copy in part_copies(steps - 1, (steps - 1) % 2):
        copy.wait()
    for step in (steps - 2, steps - 1):
        send_cores(step_block(step), step % 2).wait_send()

    tick(steps)

    sources = own_hbm.shape[0]
    slice_rows = own_hbm.shape[2]

    def grad_copy(expert, source, half, slot):
        half_hbm = (grad_own_hbm, grad_other_hbm)[half]
        return pltpu.make_async_copy(
            stage.at[slot, half], half_hbm.at[source, expert], store_sems.at[slot, half]
        )

    @pl.loop(0, expert_count * sources)
    def _(number):
        expert, source = number // sources, number % sources
        slot = number % 2

        @pl.when(number >= 2)
        def _():
            for half in range(2):
                grad_copy(expert, source, half, slot).wait()

        here = pl.ds(pl.multiple_of(source * slice_rows, slice_rows), slice_rows)
        for half in range(2):
            for part in range(3):
                first = (2 * part + half) * units
                stage[slot, half, :, part * units : (part + 1) * units] = grads[
                    expert, here, first : first + units
                ].astype(BF16)
            grad_copy(expert, source, half, slot).start()

    for slot in range(2):
        for half in range(2):
            grad_copy(0, 0, half, slot).wait()

    send_cores(own_block, 0).wait_recv()
    send_pair(z, 0).wait_recv()
    for side in (-1, 1):

        @pl.when(inside(z + side))
        def _():
            send_line(z, -side, 1).wait_recv()

    send_pair(near(1), (steps - 1) % 2).wait_send()
    send_pair(near(0), steps % 2).wait_send()
    add_up(
        [
            (parts_hbm.at[own_block], None),
            (sibling_hbm.at[own_block], None),
            (across_hbm.at[z], None),
            (along_hbm.at[z], inside(z + 1)),
            (along_hbm.at[line], inside(z - 1)),
        ],
        0,
    )
    final = pltpu.make_async_copy(sums.at[0], grad_piece_hbm, row_sems.at[0, 0])
    final.start()
    final.wait()

    for side in (-1, 1):

        @pl.when(inside(z + side))
        def _():
            send_line(z + side, side, 1).wait_send()
            gather_line(z, side).wait_send()

        for distance in range(1, line):

            @pl.when(inside(z - side * distance) & inside(z + side))
            def _():
                gather_line(z - side * distance, side).wait_send()

    for at in range(line):
        gather_pair(at, y).wait_send()
    for here in range(steps):
        gather_cores(here).wait_send()


def experts(piece, cotangent, shares, own, other, line, chunk=512):
    rows, model_width = piece.shape
    sources, expert_count, slice_rows, lanes = own.shape
    hidden_units = 2 * lanes // 3
    blocks = 2 * line
    in_place = pl.BlockSpec(memory_space=pl.ANY)
    flops = 2 * blocks * 2 * rows * model_width * expert_count * hidden_units * 9
    dma = pltpu.SemaphoreType.DMA

    def low(*shape):
        return jax.ShapeDtypeStruct(shape, BF16)

    results = pl.pallas_call(
        partial(expert_kernel, line=line, chunk=chunk),
        in_specs=[
            in_place,
            in_place,
            pl.BlockSpec(memory_space=pltpu.VMEM),
            in_place,
            in_place,
        ],
        out_specs=[in_place] * 9,
        out_shape=[
            low(blocks, 2 * rows, model_width),
            low(rows, model_width),
            low(*own.shape),
            low(*own.shape),
            low(blocks, 2, rows, model_width),
            low(blocks, rows, model_width),
            low(blocks, rows, model_width),
            low(line, rows, model_width),
            low(line + 1, rows, model_width),
        ],
        scratch_shapes=[
            pltpu.VMEM((expert_count, model_width, 3 * hidden_units), BF16),
            pltpu.VMEM((expert_count, model_width, 3 * hidden_units), F32),
            pltpu.VMEM((2, 2 * rows, model_width), BF16),
            pltpu.VMEM((2, 2 * rows, model_width), BF16),
            pltpu.VMEM((expert_count, 2 * rows, hidden_units), BF16),
            pltpu.VMEM((expert_count, 2 * rows, 2 * hidden_units), BF16),
            pltpu.VMEM((2 * rows, model_width), BF16),
            pltpu.VMEM((2, 2 * rows, model_width), BF16),
            pltpu.VMEM((5, rows, model_width), BF16),
            pltpu.VMEM((4, rows, model_width), BF16),
            pltpu.VMEM((2, 2, slice_rows, lanes), BF16),
            dma((sources, 2, 3)),
            dma((2, 2)),
            dma((2, 3)),
            dma((2, 2)),
            dma((5,)),
            dma((blocks, 2)),
            dma((line, 2)),
            dma((line,)),
            dma((blocks,)),
            dma((blocks,)),
            dma((blocks,)),
            dma((line,)),
            dma((line,)),
            dma((line,)),
            dma((line + 1,)),
        ],
        compiler_params=pltpu.CompilerParams(
            vmem_limit_bytes=63 * 2**20, collective_id=1, has_side_effects=True
        ),
        cost_estimate=pl.CostEstimate(
            flops=flops, bytes_accessed=80 * 2**20, transcendentals=0
        ),
    )(piece, cotangent, shares, own, other)
    return results[:4]


def attention_rows(values, kv_head, group_size):
    first = kv_head * group_size
    return jnp.concatenate(
        [values[:, (first + r) * HEAD_DIM : (first + r + 1) * HEAD_DIM] for r in range(group_size)],
        axis=0,
    )


def quarter_turn(values):
    half = HEAD_DIM // 2
    return jnp.concatenate([-values[:, half:], values[:, :half]], axis=1)


def window_mask(start, doc_start_ref, first_ref, block_rows, window):
    key_index = start + lax.broadcasted_iota(jnp.int32, (block_rows, window), 1)
    query_index = (
        first_ref[0]
        + pl.program_id(0) * block_rows
        + lax.broadcasted_iota(jnp.int32, (block_rows, window), 0)
    )
    return (key_index <= query_index) & (key_index >= doc_start_ref[...])


def window_start(first_ref, block_rows, window):
    end = first_ref[0] + (pl.program_id(0) + 1) * block_rows
    return pl.multiple_of(jnp.maximum(end - window, 0), block_rows)


def attention_forward_kernel(
    first_ref, query_ref, key_value_ref, doc_start_ref, attended_ref, lse_ref, *, group_size, window
):
    block_rows = query_ref.shape[0]
    kv_heads = key_value_ref.shape[1] // (2 * HEAD_DIM)
    start = window_start(first_ref, block_rows, window)
    allowed = window_mask(start, doc_start_ref, first_ref, block_rows, window)
    bias = jnp.where(allowed, 0.0, -1e30)
    bias = jnp.concatenate([bias] * group_size, axis=0)
    keys_values = key_value_ref[pl.ds(start, window), :]
    queries = query_ref[...]
    parts = []
    for g in range(kv_heads):
        keys = keys_values[:, g * HEAD_DIM : (g + 1) * HEAD_DIM]
        values = keys_values[:, (kv_heads + g) * HEAD_DIM : (kv_heads + g + 1) * HEAD_DIM]
        scores = lax.dot_general(
            attention_rows(queries, g, group_size), keys, LAST_LAST, preferred_element_type=F32
        )
        scores = scores * HEAD_DIM**-0.5 + bias
        row_max = jnp.max(scores, axis=1, keepdims=True)
        exponent = jnp.exp(scores - row_max)
        total = jnp.sum(exponent, axis=1, keepdims=True)
        probs = (exponent * (1.0 / total)).astype(BF16)
        mixed = jnp.dot(probs, values, preferred_element_type=F32).astype(BF16)
        lse_ref[0, g] = row_max + jnp.log(total)
        parts += [mixed[r * block_rows : (r + 1) * block_rows] for r in range(group_size)]
    attended_ref[...] = jnp.concatenate(parts, axis=1)


def attention_backward_kernel(
    first_ref,
    query_ref,
    key_value_ref,
    doc_start_ref,
    lse_ref,
    grad_ref,
    turns_ref,
    query_turns_ref,
    grad_query_ref,
    grad_key_value_ref,
    grad_keys,
    grad_values,
    *,
    group_size,
    window,
    steps,
):
    step = pl.program_id(0)
    block_rows = query_ref.shape[0]
    kv_heads = key_value_ref.shape[1] // (2 * HEAD_DIM)

    @pl.when(step == 0)
    def _():
        grad_keys[...] = jnp.zeros_like(grad_keys)
        grad_values[...] = jnp.zeros_like(grad_values)

    start = window_start(first_ref, block_rows, window)
    allowed = window_mask(start, doc_start_ref, first_ref, block_rows, window)
    bias = jnp.where(allowed, 0.0, -1e30)
    bias = jnp.concatenate([bias] * group_size, axis=0)
    rows = pl.ds(start, window)
    keys_values = key_value_ref[rows, :]
    queries = query_ref[...]
    grads = grad_ref[...]
    query_turns = jnp.concatenate([query_turns_ref[...]] * group_size, axis=0)
    parts = []
    for g in range(kv_heads):
        keys = keys_values[:, g * HEAD_DIM : (g + 1) * HEAD_DIM]
        values = keys_values[:, (kv_heads + g) * HEAD_DIM : (kv_heads + g + 1) * HEAD_DIM]
        query_rows = attention_rows(queries, g, group_size)
        grad_rows = attention_rows(grads, g, group_size)
        scores = lax.dot_general(query_rows, keys, LAST_LAST, preferred_element_type=F32)
        probs = jnp.exp(scores * HEAD_DIM**-0.5 + bias - lse_ref[0, g])
        grad_probs = lax.dot_general(grad_rows, values, LAST_LAST, preferred_element_type=F32)
        inner = jnp.sum(grad_probs * probs, axis=1, keepdims=True)
        grad_scores = (HEAD_DIM**-0.5 * (probs * (grad_probs - inner))).astype(BF16)
        grad_values[g, rows, :] += lax.dot_general(
            probs.astype(BF16), grad_rows, FIRST_FIRST, preferred_element_type=F32
        )
        both_queries = jnp.concatenate([query_rows, quarter_turn(query_rows)], axis=1)
        grad_keys[g, rows, :] += lax.dot_general(
            grad_scores, both_queries, FIRST_FIRST, preferred_element_type=F32
        )
        both_keys = jnp.concatenate([keys, quarter_turn(keys)], axis=1)
        turned = jnp.dot(grad_scores, both_keys, preferred_element_type=F32) * query_turns
        grad_query = (turned[:, :HEAD_DIM] + turned[:, HEAD_DIM:]).astype(BF16)
        parts += [grad_query[r * block_rows : (r + 1) * block_rows] for r in range(group_size)]
    grad_query_ref[...] = jnp.concatenate(parts, axis=1)

    @pl.when(step == steps - 1)
    def _():
        key_parts, value_parts = [], []
        for g in range(kv_heads):
            turned = grad_keys[g] * turns_ref[...]
            key_parts.append((turned[:, :HEAD_DIM] + turned[:, HEAD_DIM:]).astype(BF16))
            value_parts.append(grad_values[g].astype(BF16))
        grad_key_value_ref[...] = jnp.concatenate(key_parts + value_parts, axis=1)


def attention_specs(queries, keys_values, block_rows):
    return dict(
        smem=pl.BlockSpec(memory_space=pltpu.SMEM),
        rows=pl.BlockSpec((block_rows, queries.shape[1]), lambda i: (i, 0)),
        whole=pl.BlockSpec(keys_values.shape, lambda i: (0, 0)),
        column=pl.BlockSpec((block_rows, 1), lambda i: (i, 0)),
    )


def attention_forward(first, queries, keys_values, doc_start, block_rows=256, reach=1024):
    row_count, query_cols = queries.shape
    kv_heads = keys_values.shape[1] // (2 * HEAD_DIM)
    group_size = query_cols // HEAD_DIM // kv_heads
    steps = row_count // block_rows
    window = min(reach + block_rows, keys_values.shape[0])
    specs = attention_specs(queries, keys_values, block_rows)
    stacked = group_size * block_rows
    return pl.pallas_call(
        partial(attention_forward_kernel, group_size=group_size, window=window),
        grid=(steps,),
        in_specs=[specs["smem"], specs["rows"], specs["whole"], specs["column"]],
        out_specs=[
            specs["rows"],
            pl.BlockSpec((1, kv_heads, stacked, 1), lambda i: (i, 0, 0, 0)),
        ],
        out_shape=[
            jax.ShapeDtypeStruct(queries.shape, BF16),
            jax.ShapeDtypeStruct((steps, kv_heads, stacked, 1), F32),
        ],
        compiler_params=pltpu.CompilerParams(vmem_limit_bytes=48 * 2**20),
        cost_estimate=pl.CostEstimate(
            flops=4 * row_count * window * query_cols * 8, bytes_accessed=2**22, transcendentals=0
        ),
    )(first, queries, keys_values, doc_start)


def attention_backward(
    first, queries, keys_values, doc_start, lse, grads, turns, query_turns, block_rows=256, reach=1024
):
    row_count, query_cols = queries.shape
    kv_heads = keys_values.shape[1] // (2 * HEAD_DIM)
    group_size = query_cols // HEAD_DIM // kv_heads
    steps = row_count // block_rows
    window = min(reach + block_rows, keys_values.shape[0])
    specs = attention_specs(queries, keys_values, block_rows)
    stacked = group_size * block_rows
    return pl.pallas_call(
        partial(attention_backward_kernel, group_size=group_size, window=window, steps=steps),
        grid=(steps,),
        in_specs=[
            specs["smem"],
            specs["rows"],
            specs["whole"],
            specs["column"],
            pl.BlockSpec((1, kv_heads, stacked, 1), lambda i: (i, 0, 0, 0)),
            specs["rows"],
            pl.BlockSpec(turns.shape, lambda i: (0, 0)),
            pl.BlockSpec((block_rows, turns.shape[1]), lambda i: (i, 0)),
        ],
        out_specs=[specs["rows"], specs["whole"]],
        out_shape=[
            jax.ShapeDtypeStruct(queries.shape, BF16),
            jax.ShapeDtypeStruct(keys_values.shape, BF16),
        ],
        scratch_shapes=[
            pltpu.VMEM((kv_heads, keys_values.shape[0], 2 * HEAD_DIM), F32),
            pltpu.VMEM((kv_heads, keys_values.shape[0], HEAD_DIM), F32),
        ],
        compiler_params=pltpu.CompilerParams(vmem_limit_bytes=48 * 2**20),
        cost_estimate=pl.CostEstimate(
            flops=10 * row_count * window * query_cols * 8, bytes_accessed=2**23, transcendentals=0
        ),
    )(first, queries, keys_values, doc_start, lse, grads, turns, query_turns)


def rotation_tables(positions):
    half_dim = HEAD_DIM // 2
    frequencies = 10000.0 ** (-2.0 * jnp.arange(half_dim, dtype=F32) / HEAD_DIM)
    angles = positions.astype(F32)[:, None] * frequencies[None, :]
    cosine, sine = jnp.cos(angles), jnp.sin(angles)
    return jnp.concatenate([cosine, cosine, -sine, -sine], axis=1)


def turned_columns(weight):
    rows, cols = weight.shape
    halves = weight.reshape(rows, cols // HEAD_DIM, 2, HEAD_DIM // 2)
    return jnp.stack([-halves[:, :, 1], halves[:, :, 0]], axis=2).reshape(rows, cols)


def expert_plan(
    residual_in,
    gain_attn,
    query_weight,
    key_projection_weight,
    value_projection_weight,
    out_weight,
    gain_ffn,
    gate_weight,
    up_weight,
    down_weight,
    segments,
    routes,
    shares,
    cotangent,
    *,
    groups,
    tensor_size,
):
    row_count, model_width = residual_in.shape
    query_cols = query_weight.shape[1]
    kv_cols = key_projection_weight.shape[1]
    expert_count, slice_rows, unit_count = gate_weight.shape
    own_experts = expert_count // groups
    piece_rows = row_count // tensor_size
    context_rank = lax.axis_index(CONTEXT)
    tensor_rank = lax.axis_index(TENSOR)
    group_rank = lax.axis_index(SHARD) * lax.axis_size(CONTEXT) + context_rank
    own_first = context_rank * row_count
    piece_first = tensor_rank * piece_rows
    sibling = [(i, i ^ 1) for i in range(tensor_size)]
    across = [(i, i ^ 2) for i in range(tensor_size)]

    def own_piece(values):
        return lax.dynamic_slice_in_dim(values, piece_first, piece_rows)

    def padded_column(gain):
        return jnp.pad(gain[:, None], ((0, 0), (0, 127)))

    with jax.named_scope("weights"):
        qkv_full = lax.all_gather(
            jnp.concatenate(
                [
                    query_weight,
                    key_projection_weight,
                    value_projection_weight,
                    padded_column(gain_attn),
                ],
                axis=1,
            ),
            GROUP,
            axis=0,
            tiled=True,
        )
        qkv_cols = query_cols + 2 * kv_cols
        qkv_weight = qkv_full[:, :qkv_cols]
        gain_attn_float = qkv_full[:, qkv_cols].astype(F32)
        slices = jnp.concatenate(
            [gate_weight, up_weight, down_weight.transpose(0, 2, 1)], axis=2
        )
        owned = lax.all_to_all(slices, GROUP, 0, 0, tiled=True)
        out_gathered = lax.all_gather(
            jnp.concatenate([out_weight.T, padded_column(gain_ffn)], axis=1),
            GROUP,
            axis=0,
            tiled=True,
        )
        out_transposed = out_gathered[:, :query_cols]
        gain_ffn_float = out_gathered[:, query_cols].astype(F32)

    def gather_tokens(piece):
        own_core = lax.all_gather(piece, GROUP, axis=0, tiled=False)
        other_core = lax.ppermute(own_core, TENSOR, sibling)
        return jnp.stack([own_core, other_core], axis=1).reshape(-1, piece.shape[1])

    with jax.named_scope("attention"):
        positions = doc_positions(segments)
        turns = rotation_tables(positions)
        own_turns = lax.dynamic_slice_in_dim(turns, own_first, row_count)
        own_index = own_first + jnp.arange(row_count, dtype=jnp.int32)
        doc_start = own_index - lax.dynamic_slice_in_dim(positions, own_first, row_count)
        input_float = residual_in.astype(F32)
        first_normalized = rms_scale(input_float, gain_attn_float).astype(BF16)
        rotated_cols = query_cols + kv_cols
        projected = jnp.dot(
            first_normalized,
            jnp.concatenate([qkv_weight, turned_columns(qkv_weight[:, :rotated_cols])], axis=1),
            preferred_element_type=F32,
        )
        heads = rotated_cols // HEAD_DIM
        rotated = (
            projected[:, :rotated_cols] * jnp.tile(own_turns[:, :HEAD_DIM], (1, heads))
            - projected[:, qkv_cols:] * jnp.tile(own_turns[:, HEAD_DIM:], (1, heads))
        ).astype(BF16)
        queries = rotated[:, :query_cols]
        keys_values = lax.all_gather(
            jnp.concatenate(
                [rotated[:, query_cols:], projected[:, rotated_cols:qkv_cols].astype(BF16)], axis=1
            ),
            CONTEXT,
            axis=0,
            tiled=True,
        )
        first = own_first.reshape(1).astype(jnp.int32)
        attended, lse = attention_forward(first, queries, keys_values, doc_start[:, None])

    with jax.named_scope("routing"):
        owned, attended = lax.optimization_barrier((owned, attended))
        others = lax.ppermute(owned, TENSOR, across)
        cotangent_piece = own_piece(cotangent)
        cotangent_all = gather_tokens(cotangent_piece)
        spread = jnp.sum(
            jnp.where(
                own_piece(routes)[:, :, None] == jnp.arange(expert_count, dtype=jnp.int32),
                own_piece(shares)[:, :, None],
                0.0,
            ),
            axis=1,
        )
        token_shares = lax.dynamic_slice_in_dim(
            gather_tokens(spread), group_rank * own_experts, own_experts, axis=1
        )
        token_shares = jnp.pad(token_shares, ((0, 0), (0, 8 - own_experts)))

    with jax.named_scope("attention_out"):
        attn_part = lax.dot_general(
            attended, out_transposed, LAST_LAST, preferred_element_type=F32
        )
        attn_piece = lax.psum_scatter(
            attn_part.astype(BF16), TENSOR, scatter_dimension=0, tiled=True
        )
        hidden = own_piece(residual_in).astype(F32) + attn_piece.astype(F32)
        normed_ffn, ffn_norm_back = jax.vjp(rms_scale, hidden, gain_ffn_float)

    with jax.named_scope("experts"):
        shape = (groups, own_experts, slice_rows, 3 * unit_count)
        out_parts, grad_second, grad_own, grad_other = experts(
            normed_ffn.astype(BF16),
            cotangent_all.reshape(groups, 2 * piece_rows, model_width),
            token_shares.reshape(groups, 2 * piece_rows, 8),
            owned.reshape(shape),
            others.reshape(shape),
            groups // 2,
        )

    def reduce_tokens(parts):
        parts = parts.reshape(groups, 2, piece_rows, model_width)
        received = lax.ppermute(parts[:, 1], TENSOR, sibling)
        both = (parts[:, 0].astype(F32) + received.astype(F32)).astype(BF16)
        return lax.psum_scatter(
            both.reshape(groups * piece_rows, model_width),
            GROUP,
            scatter_dimension=0,
            tiled=True,
        ).astype(F32)

    with jax.named_scope("expert_grads"):
        received = lax.ppermute(grad_other, TENSOR, across)
        total = (grad_own.astype(F32) + received.astype(F32)).astype(BF16)
        returned = lax.all_to_all(
            total.reshape(expert_count, slice_rows, 3 * unit_count), GROUP, 0, 0, tiled=True
        )
        grad_hidden_norm, grad_gain_ffn_local = ffn_norm_back(grad_second.astype(F32))
        grad_hidden = cotangent_piece.astype(F32) + grad_hidden_norm
        grad_hidden_low = lax.all_gather(grad_hidden.astype(BF16), TENSOR, axis=0, tiled=True)
        output_piece = (hidden + reduce_tokens(out_parts)).astype(BF16)
        output = lax.all_gather(output_piece, TENSOR, axis=0, tiled=True)

    with jax.named_scope("attention_back"):
        grad_out_local = lax.dot_general(
            grad_hidden_low, attended, FIRST_FIRST, preferred_element_type=F32
        )
        grad_out_transposed = lax.psum_scatter(
            grad_out_local.astype(BF16), GROUP, scatter_dimension=0, tiled=True
        )
        grad_attended = jnp.dot(grad_hidden_low, out_transposed, preferred_element_type=F32)
        grad_query_lin, grad_key_value = attention_backward(
            first,
            queries,
            keys_values,
            doc_start[:, None],
            lse,
            grad_attended.astype(BF16),
            turns,
            own_turns,
        )
        grad_key_value = lax.psum_scatter(
            grad_key_value, CONTEXT, scatter_dimension=0, tiled=True
        )
        grad_projected = jnp.concatenate([grad_query_lin, grad_key_value], axis=1)
        grad_first_part = lax.dot_general(
            grad_projected, qkv_weight, LAST_LAST, preferred_element_type=F32
        )
        grad_first = lax.psum_scatter(
            grad_first_part.astype(BF16), TENSOR, scatter_dimension=0, tiled=True
        ).astype(F32)
        _, attn_norm_back = jax.vjp(
            rms_scale, own_piece(residual_in).astype(F32), gain_attn_float
        )
        grad_input_norm, grad_gain_attn_local = attn_norm_back(grad_first)
        grad_input = lax.all_gather(
            (grad_hidden + grad_input_norm).astype(BF16), TENSOR, axis=0, tiled=True
        )
        grad_qkv_local = lax.dot_general(
            first_normalized, grad_projected, FIRST_FIRST, preferred_element_type=F32
        )
        grad_qkv = lax.psum_scatter(
            grad_qkv_local.astype(BF16), GROUP, scatter_dimension=0, tiled=True
        ).astype(F32)
        gains = lax.psum(
            jnp.stack([grad_gain_attn_local, grad_gain_ffn_local]), GROUP + (TENSOR,)
        )
        gains = lax.dynamic_slice_in_dim(gains, group_rank * slice_rows, slice_rows, axis=1)
    units = unit_count
    return (
        output,
        grad_input,
        gains[0],
        grad_qkv[:, :query_cols],
        grad_qkv[:, query_cols:rotated_cols],
        grad_qkv[:, rotated_cols:],
        grad_out_transposed.astype(F32).T,
        gains[1],
        returned[:, :, :units].astype(F32),
        returned[:, :, units : 2 * units].astype(F32),
        returned[:, :, 2 * units :].transpose(0, 2, 1).astype(F32),
    )


def solution(mesh):
    placed = (
        P(GROUP, None),
        P(GROUP),
        P(GROUP, TENSOR),
        P(GROUP, TENSOR),
        P(GROUP, TENSOR),
        P(TENSOR, GROUP),
        P(GROUP),
        P(None, GROUP, TENSOR),
        P(None, GROUP, TENSOR),
        P(None, TENSOR, GROUP),
        P(SHARD),
        P(GROUP, None),
        P(GROUP, None),
        P(GROUP, None),
    )
    sizes = dict(mesh.shape)
    if sizes[SHARD] == 4 and sizes[CONTEXT] == 2 and sizes[TENSOR] == 4:
        plan = partial(
            expert_plan, groups=sizes[SHARD] * sizes[CONTEXT], tensor_size=sizes[TENSOR]
        )
    else:
        plan = gathered_plan
    return jax.shard_map(
        plan,
        mesh=mesh,
        in_specs=placed,
        out_specs=(
            P(GROUP, None),
            P(GROUP, None),
            P(GROUP),
            P(GROUP, TENSOR),
            P(GROUP, TENSOR),
            P(GROUP, TENSOR),
            P(TENSOR, GROUP),
            P(GROUP),
            P(None, GROUP, TENSOR),
            P(None, GROUP, TENSOR),
            P(None, TENSOR, GROUP),
        ),
        check_vma=False,
    )
```

```python
from functools import partial

import jax
import jax.numpy as jnp
from jax import lax
from jax.experimental import pallas as pl
from jax.experimental.pallas import tpu as pltpu
from jax.sharding import PartitionSpec as P

HEAD_DIM = 64
NDOCS = 5
SHARD = "shard"
CONTEXT = "context"
TENSOR = "tensor"
GROUP = (SHARD, CONTEXT)
PRODUCT_0 = "qgrd,kgd->grqk"
PRODUCT_1 = "grqk,kgd->qgrd"
PRODUCT_2 = "ecd,edf->ecf"
PRODUCT_3 = "ecf,efd->ecd"
PRODUCT_4 = "ecd,efd->ecf"
PRODUCT_5 = "ecf,edf->ecd"
PRODUCT_6 = "ecd,ecf->edf"
PRODUCT_7 = "ecf,ecd->efd"
PRODUCT_8 = "grqk,qgrd->kgd"


epsilon = 1e-06


def rms_scale(values, gain):
    return values * lax.rsqrt(jnp.mean(values * values, axis=-1, keepdims=True) + epsilon) * gain


def doc_positions(segment_ids):
    sequence_length = segment_ids.shape[-1]
    index_row = jnp.arange(sequence_length, dtype=jnp.int32)
    documents = jnp.arange(NDOCS, dtype=jnp.int32)
    doc_starts = jnp.sum((segment_ids[..., :, None] < documents).astype(jnp.int32), axis=-2)
    own_start = jnp.sum(
        jnp.where(segment_ids[..., :, None] == documents, doc_starts[..., None, :], 0), axis=-1
    )
    return index_row - own_start


def rotary(values, positions):
    half_dim = values.shape[-1] // 2
    frequencies = 10000.0 ** (-2.0 * jnp.arange(half_dim, dtype=jnp.float32) / values.shape[-1])
    angles = positions.astype(jnp.float32)[:, None] * frequencies[None, :]
    cosine = jnp.cos(angles)[:, None, :]
    sines = jnp.sin(angles)[:, None, :]
    first_half = values[..., :half_dim]
    second_half = values[..., half_dim:]
    return jnp.concatenate(
        [first_half * cosine - second_half * sines, second_half * cosine + first_half * sines],
        axis=-1,
    )


def swiglu(gate_value, up_value):
    return jax.nn.silu(gate_value) * up_value


def dispatch(routes, shares, block_rows, capacity, expert_count):
    block_count = routes.shape[0] // block_rows
    picks = routes.shape[1]
    chosen = routes.reshape(block_count, block_rows * picks)
    onehot = (chosen[:, :, None] == jnp.arange(expert_count, dtype=jnp.int32)).astype(jnp.int32)
    ranked = jnp.sum((jnp.cumsum(onehot, axis=1) - onehot) * onehot, axis=2)
    slot_index = (
        chosen * (block_count * capacity)
        + jnp.arange(block_count, dtype=jnp.int32)[:, None] * capacity
        + ranked
    )
    tokens = jnp.arange(block_count * block_rows * picks, dtype=jnp.int32) // picks
    total_slots = expert_count * block_count * capacity
    slot_rows = jnp.zeros((total_slots,), jnp.int32).at[slot_index.reshape(-1)].set(tokens)
    slot_share = (
        jnp.zeros((total_slots,), jnp.float32).at[slot_index.reshape(-1)].set(shares.reshape(-1))
    )
    return (slot_rows, slot_share)


def gathered_plan(
    residual_in,
    gain_attn,
    query_weight,
    key_projection_weight,
    value_projection_weight,
    out_weight,
    gain_ffn,
    gate_weight,
    up_weight,
    down_weight,
    segments,
    routes,
    shares,
    cotangent,
):
    row_count, model_width = residual_in.shape
    head_size = HEAD_DIM
    query_cols = query_weight.shape[1]
    kv_heads = key_projection_weight.shape[1] // head_size
    group_size = query_cols // head_size // kv_heads
    expert_count = gate_weight.shape[0]
    capacity = row_count * routes.shape[1] * 5 // (4 * expert_count)
    score_scale = head_size ** (-0.5)
    context_rank = lax.axis_index(CONTEXT)
    own_first = context_rank * row_count
    gain_attn_full, gain_ffn_full, query_full, key_full, value_full, out_full = (
        lax.all_gather(gain_attn, GROUP, axis=0, tiled=True),
        lax.all_gather(gain_ffn, GROUP, axis=0, tiled=True),
        lax.all_gather(query_weight, GROUP, axis=0, tiled=True),
        lax.all_gather(key_projection_weight, GROUP, axis=0, tiled=True),
        lax.all_gather(value_projection_weight, GROUP, axis=0, tiled=True),
        lax.all_gather(out_weight, GROUP, axis=1, tiled=True),
    )
    gain_attn_float = gain_attn_full.astype(jnp.float32)
    gain_ffn_float = gain_ffn_full.astype(jnp.float32)
    positions = doc_positions(segments)
    own_positions = lax.dynamic_slice_in_dim(positions, own_first, row_count)
    own_ids = lax.dynamic_slice_in_dim(segments, own_first, row_count)
    own_index = own_first + jnp.arange(row_count, dtype=jnp.int32)
    input_float = residual_in.astype(jnp.float32)
    normed_attn, attn_norm_back = jax.vjp(rms_scale, input_float, gain_attn_float)
    first_normalized = normed_attn.astype(jnp.bfloat16)
    query_lin = jnp.dot(first_normalized, query_full, preferred_element_type=jnp.float32).reshape(
        row_count, -1, head_size
    )
    key_linear = jnp.dot(first_normalized, key_full, preferred_element_type=jnp.float32).reshape(
        row_count, -1, head_size
    )
    value_tokens = jnp.dot(first_normalized, value_full, preferred_element_type=jnp.float32).astype(
        jnp.bfloat16
    )
    rope_local = partial(rotary, positions=own_positions)
    query_rot, rope_query_back = jax.vjp(rope_local, query_lin)
    key_rot, rope_key_back = jax.vjp(rope_local, key_linear)
    query_low = query_rot.astype(jnp.bfloat16)
    key_low = key_rot.astype(jnp.bfloat16).reshape(row_count, -1)
    key_all, value_all = (
        lax.all_gather(key_low, CONTEXT, axis=0, tiled=True),
        lax.all_gather(value_tokens, CONTEXT, axis=0, tiled=True),
    )
    key_index = jnp.arange(key_all.shape[0], dtype=jnp.int32)
    key_ids = jnp.take(segments, jnp.clip(key_index, 0, segments.shape[0] - 1))
    key_valid = key_index >= 0
    key_heads = key_all.reshape(-1, kv_heads, head_size)
    value_heads = value_all.reshape(-1, kv_heads, head_size)
    query_heads = query_low.reshape(row_count, kv_heads, group_size, head_size)
    block_rows = min(512, row_count)
    block_starts = list(range(0, row_count, block_rows))

    def block_scores(block_first):
        query_block = query_heads[block_first : block_first + block_rows]
        raw_scores = jnp.einsum(
            PRODUCT_0, query_block, key_heads, preferred_element_type=jnp.float32
        )
        block_ids = own_ids[block_first : block_first + block_rows]
        block_index = own_index[block_first : block_first + block_rows]
        allowed = (
            key_valid[None, :]
            & (key_ids[None, :] == block_ids[:, None])
            & (key_index[None, :] <= block_index[:, None])
        )
        return (query_block, jnp.where(allowed, raw_scores * score_scale, -1e30))

    mixed_parts = []
    lse_parts = []
    for block_first in block_starts:
        query_block, scores = block_scores(block_first)
        row_max = jnp.max(scores, axis=-1, keepdims=True)
        exponent = jnp.exp(scores - row_max)
        row_total = jnp.sum(exponent, axis=-1, keepdims=True)
        probs = (exponent / row_total).astype(jnp.bfloat16)
        mixed_parts.append(
            jnp.einsum(PRODUCT_1, probs, value_heads, preferred_element_type=jnp.float32)
        )
        lse_parts.append(row_max + jnp.log(row_total))
    attended = (
        jnp.concatenate(mixed_parts, axis=0).reshape(row_count, query_cols).astype(jnp.bfloat16)
    )
    attn_part = jnp.dot(attended, out_full, preferred_element_type=jnp.float32)
    hidden = input_float + lax.psum(attn_part.astype(jnp.bfloat16), TENSOR).astype(jnp.float32)
    normed_ffn, ffn_norm_back = jax.vjp(rms_scale, hidden, gain_ffn_float)
    normed_second = normed_ffn.astype(jnp.bfloat16)
    slot_rows, slot_share = dispatch(routes, shares, row_count, capacity, expert_count)
    per_turn = expert_count // 5
    turn_count = expert_count // per_turn
    turn_slots = per_turn * capacity

    def local_experts(turn_index):
        gate_part = lax.dynamic_slice_in_dim(gate_weight, turn_index * per_turn, per_turn, 0)
        up_part = lax.dynamic_slice_in_dim(up_weight, turn_index * per_turn, per_turn, 0)
        down_part = lax.dynamic_slice_in_dim(down_weight, turn_index * per_turn, per_turn, 0)
        return (gate_part, up_part, down_part)

    def turn_inputs(turn_index):
        token_rows = lax.dynamic_slice_in_dim(slot_rows, turn_index * turn_slots, turn_slots)
        share_rows = lax.dynamic_slice_in_dim(slot_share, turn_index * turn_slots, turn_slots)
        picked = normed_second[token_rows].reshape(per_turn, capacity, model_width)
        return (token_rows, share_rows, picked)

    def forward_turn(running, turn_index):
        gate_part, up_part, down_part = local_experts(turn_index)
        gate_full, up_full, down_full = (
            lax.all_gather(gate_part, GROUP, axis=1, tiled=True),
            lax.all_gather(up_part, GROUP, axis=1, tiled=True),
            lax.all_gather(down_part, GROUP, axis=2, tiled=True),
        )
        token_rows, share_rows, picked = turn_inputs(turn_index)
        gate_value = jnp.einsum(
            PRODUCT_2, picked, gate_full, preferred_element_type=jnp.float32
        )
        up_value = jnp.einsum(PRODUCT_2, picked, up_full, preferred_element_type=jnp.float32)
        inner = swiglu(gate_value, up_value).astype(jnp.bfloat16)
        expert_result = jnp.einsum(
            PRODUCT_3, inner, down_full, preferred_element_type=jnp.float32
        ).reshape(turn_slots, model_width)
        return (running.at[token_rows].add(expert_result * share_rows[:, None]), None)

    turn_ids = jnp.arange(turn_count, dtype=jnp.int32)
    expert_part, _ = lax.scan(
        forward_turn, jnp.zeros((row_count, model_width), jnp.float32), turn_ids
    )
    expert_total = lax.psum(expert_part.astype(jnp.bfloat16), TENSOR).astype(jnp.float32)
    output = (hidden + expert_total).astype(jnp.bfloat16)
    upstream = cotangent.astype(jnp.float32)

    def backward_turn(running, turn_index):
        gate_part, up_part, down_part = local_experts(turn_index)
        gate_full, up_full, down_full = (
            lax.all_gather(gate_part, GROUP, axis=1, tiled=True),
            lax.all_gather(up_part, GROUP, axis=1, tiled=True),
            lax.all_gather(down_part, GROUP, axis=2, tiled=True),
        )
        token_rows, share_rows, picked = turn_inputs(turn_index)
        gate_value = jnp.einsum(
            PRODUCT_2, picked, gate_full, preferred_element_type=jnp.float32
        )
        up_value = jnp.einsum(PRODUCT_2, picked, up_full, preferred_element_type=jnp.float32)
        inner_float, swiglu_back = jax.vjp(swiglu, gate_value, up_value)
        inner = inner_float.astype(jnp.bfloat16)
        grad_slot = (
            (upstream[token_rows] * share_rows[:, None])
            .astype(jnp.bfloat16)
            .reshape(per_turn, capacity, model_width)
        )
        grad_inner = jnp.einsum(
            PRODUCT_4, grad_slot, down_full, preferred_element_type=jnp.float32
        )
        grad_gate_value, grad_up_value = swiglu_back(grad_inner)
        grad_gate_low = grad_gate_value.astype(jnp.bfloat16)
        grad_up_low = grad_up_value.astype(jnp.bfloat16)
        grad_picked = jnp.einsum(
            PRODUCT_5, grad_gate_low, gate_full, preferred_element_type=jnp.float32
        )
        grad_picked = grad_picked + jnp.einsum(
            PRODUCT_5, grad_up_low, up_full, preferred_element_type=jnp.float32
        )
        running = running.at[token_rows].add(grad_picked.reshape(turn_slots, model_width))
        shard_grads = (
            lax.psum_scatter(
                jnp.einsum(
                    PRODUCT_6, picked, grad_gate_low, preferred_element_type=jnp.float32
                ).astype(jnp.bfloat16),
                GROUP,
                scatter_dimension=1,
                tiled=True,
            ).astype(jnp.float32),
            lax.psum_scatter(
                jnp.einsum(
                    PRODUCT_6, picked, grad_up_low, preferred_element_type=jnp.float32
                ).astype(jnp.bfloat16),
                GROUP,
                scatter_dimension=1,
                tiled=True,
            ).astype(jnp.float32),
            lax.psum_scatter(
                jnp.einsum(
                    PRODUCT_7, inner, grad_slot, preferred_element_type=jnp.float32
                ).astype(jnp.bfloat16),
                GROUP,
                scatter_dimension=2,
                tiled=True,
            ).astype(jnp.float32),
        )
        return (running, shard_grads)

    grad_second_part, stacked_grads = lax.scan(
        backward_turn, jnp.zeros((row_count, model_width), jnp.float32), turn_ids
    )
    grad_gate_out = stacked_grads[0].reshape(gate_weight.shape)
    grad_up_out = stacked_grads[1].reshape(up_weight.shape)
    grad_down_out = stacked_grads[2].reshape(down_weight.shape)
    grad_second = lax.psum(grad_second_part.astype(jnp.bfloat16), TENSOR).astype(jnp.float32)
    grad_hidden_norm, grad_gain_ffn_local = ffn_norm_back(grad_second)
    grad_hidden = upstream + grad_hidden_norm
    grad_hidden_low = grad_hidden.astype(jnp.bfloat16)
    grad_out_local = jnp.einsum(
        "tc,td->cd", attended, grad_hidden_low, preferred_element_type=jnp.float32
    )
    grad_attended = jnp.einsum(
        "td,cd->tc", grad_hidden_low, out_full, preferred_element_type=jnp.float32
    )
    grad_attended = grad_attended.astype(jnp.bfloat16).reshape(
        row_count, kv_heads, group_size, head_size
    )
    grad_query_parts = []
    grad_keys = jnp.zeros(key_heads.shape, jnp.float32)
    grad_values = jnp.zeros(value_heads.shape, jnp.float32)
    for block_number in range(len(block_starts)):
        block_first = block_starts[block_number]
        query_block, scores = block_scores(block_first)
        probs_float = jnp.exp(scores - lse_parts[block_number])
        probs = probs_float.astype(jnp.bfloat16)
        grad_block = grad_attended[block_first : block_first + block_rows]
        grad_probs = jnp.einsum(
            PRODUCT_0, grad_block, value_heads, preferred_element_type=jnp.float32
        )
        inner_sum = jnp.sum(grad_probs * probs_float, axis=-1, keepdims=True)
        grad_scores = (score_scale * (probs_float * (grad_probs - inner_sum))).astype(jnp.bfloat16)
        grad_query_parts.append(
            jnp.einsum(PRODUCT_1, grad_scores, key_heads, preferred_element_type=jnp.float32)
        )
        grad_keys = grad_keys + jnp.einsum(
            PRODUCT_8, grad_scores, query_block, preferred_element_type=jnp.float32
        )
        grad_values = grad_values + jnp.einsum(
            PRODUCT_8, probs, grad_block, preferred_element_type=jnp.float32
        )
    grad_key_own, grad_value_own = (
        lax.psum_scatter(
            grad_keys.astype(jnp.bfloat16), CONTEXT, scatter_dimension=0, tiled=True
        ).astype(jnp.float32),
        lax.psum_scatter(
            grad_values.astype(jnp.bfloat16), CONTEXT, scatter_dimension=0, tiled=True
        ).astype(jnp.float32),
    )
    grad_query_all = jnp.concatenate(grad_query_parts, axis=0).reshape(row_count, -1, head_size)
    grad_query_lin = rope_query_back(grad_query_all)[0].astype(jnp.bfloat16).reshape(row_count, -1)
    grad_key_lin = rope_key_back(grad_key_own)[0].astype(jnp.bfloat16).reshape(row_count, -1)
    grad_value_low = grad_value_own.astype(jnp.bfloat16).reshape(row_count, -1)
    grad_first_part = jnp.einsum(
        "tc,dc->td", grad_query_lin, query_full, preferred_element_type=jnp.float32
    )
    grad_first_part = grad_first_part + jnp.einsum(
        "tc,dc->td", grad_key_lin, key_full, preferred_element_type=jnp.float32
    )
    grad_first_part = grad_first_part + jnp.einsum(
        "tc,dc->td", grad_value_low, value_full, preferred_element_type=jnp.float32
    )
    grad_first = lax.psum(grad_first_part.astype(jnp.bfloat16), TENSOR).astype(jnp.float32)
    grad_input_norm, grad_gain_attn_local = attn_norm_back(grad_first)
    grad_input = (grad_hidden + grad_input_norm).astype(jnp.bfloat16)
    grad_query_local = jnp.einsum(
        "td,tc->dc", first_normalized, grad_query_lin, preferred_element_type=jnp.float32
    )
    grad_key_local = jnp.einsum(
        "td,tc->dc", first_normalized, grad_key_lin, preferred_element_type=jnp.float32
    )
    grad_value_local = jnp.einsum(
        "td,tc->dc", first_normalized, grad_value_low, preferred_element_type=jnp.float32
    )
    reduced = (
        lax.psum_scatter(
            grad_gain_attn_local.astype(jnp.bfloat16),
            GROUP,
            scatter_dimension=0,
            tiled=True,
        ).astype(jnp.float32),
        lax.psum_scatter(
            grad_query_local.astype(jnp.bfloat16),
            GROUP,
            scatter_dimension=0,
            tiled=True,
        ).astype(jnp.float32),
        lax.psum_scatter(
            grad_key_local.astype(jnp.bfloat16),
            GROUP,
            scatter_dimension=0,
            tiled=True,
        ).astype(jnp.float32),
        lax.psum_scatter(
            grad_value_local.astype(jnp.bfloat16),
            GROUP,
            scatter_dimension=0,
            tiled=True,
        ).astype(jnp.float32),
        lax.psum_scatter(
            grad_out_local.astype(jnp.bfloat16),
            GROUP,
            scatter_dimension=1,
            tiled=True,
        ).astype(jnp.float32),
        lax.psum_scatter(
            grad_gain_ffn_local.astype(jnp.bfloat16),
            GROUP,
            scatter_dimension=0,
            tiled=True,
        ).astype(jnp.float32),
    )
    return (
        output,
        grad_input,
        reduced[0],
        reduced[1],
        reduced[2],
        reduced[3],
        reduced[4],
        reduced[5],
        grad_gate_out,
        grad_up_out,
        grad_down_out,
    )


F32 = jnp.float32
BF16 = jnp.bfloat16
LAST_LAST = (((1,), (1,)), ((), ()))
FIRST_FIRST = (((0,), (0,)), ((), ()))


def weight_copies(own_hbm, other_hbm, weights, sems):
    sources, _, rows, lanes = own_hbm.shape
    units = lanes // 3
    return [
        pltpu.make_async_copy(
            half_hbm.at[source, :, :, pl.ds(part * units, units)],
            weights.at[
                :, pl.ds(source * rows, rows), pl.ds((2 * part + half) * units, units)
            ],
            sems.at[source, half, part],
        )
        for source in range(sources)
        for half, half_hbm in enumerate((own_hbm, other_hbm))
        for part in range(3)
    ]


def project(tokens, cotangent, weights):
    hidden_units = weights.shape[1] // 3
    gate_up = jnp.dot(tokens, weights[:, : 2 * hidden_units], preferred_element_type=F32)
    grad_inner = jnp.dot(cotangent, weights[:, 2 * hidden_units :], preferred_element_type=F32)
    return gate_up, grad_inner


def activate(gate_up, grad_inner, share):
    hidden_units = grad_inner.shape[1]
    gate, up = gate_up[:, :hidden_units], gate_up[:, hidden_units:]
    sigmoid = 1.0 / (1.0 + jnp.exp(-gate))
    silu = gate * sigmoid
    grad_inner = grad_inner * share
    inner = silu * up * share
    grad_gate = grad_inner * up * (sigmoid * (1.0 + gate * (1.0 - sigmoid)))
    grad_up = grad_inner * silu
    return inner.astype(BF16), grad_gate.astype(BF16), grad_up.astype(BF16)


MESH_ID = pl.DeviceIdType.MESH


class Place:
    def __init__(self, line):
        self.line = line
        self.z, self.y = lax.axis_index(SHARD), lax.axis_index(CONTEXT)
        self.t = lax.axis_index(TENSOR)
        self.sibling = (self.z, self.y, self.t + 1 - 2 * (self.t % 2))
        self.partner = (self.z, 1 - self.y, self.t)
        self.across = (self.z, self.y, (self.t + 2) % 4)

    def beside(self, side):
        return (self.z + side, self.y, self.t)

    def inside(self, at):
        return (at >= 0) & (at < self.line)

    def near(self, rank):
        z, line = self.z, self.line
        half = z // 2
        mirrored = z * (1 - half) + (line - 1 - z) * half
        far = rank // 2
        place = (1 - far) * (mirrored + rank - 2 * mirrored * rank) + far * rank
        return place * (1 - half) + (line - 1 - place) * half

    def block(self, order, step):
        rank, across = order[0]
        for number, (later_rank, later_across) in enumerate(order[1:], 1):
            rank = jnp.where(step == number, later_rank, rank)
            across = jnp.where(step == number, later_across, across)
        column = self.y + across - 2 * self.y * across
        return self.near(rank) * 2 + column

    def meet(self):
        z, line = self.z, self.line
        barrier = pltpu.get_barrier_semaphore()
        for device in (self.sibling, self.partner, self.across):
            pl.semaphore_signal(barrier, inc=1, device_id=device, device_id_type=MESH_ID)
        for side in (-1, 1):

            @pl.when(self.inside(z + side))
            def _():
                pl.semaphore_signal(
                    barrier, inc=1, device_id=self.beside(side), device_id_type=MESH_ID
                )

        below, above = (z + line - 1) // line, (2 * line - 2 - z) // line
        pl.semaphore_wait(barrier, 3 + below + above)


def remote(source, target, send, recv, device):
    return pltpu.make_async_remote_copy(
        src_ref=source,
        dst_ref=target,
        send_sem=send,
        recv_sem=recv,
        device_id=device,
        device_id_type=MESH_ID,
    )


class Gather:
    order = ((0, 0), (1, 0), (0, 1), (2, 0), (1, 1), (3, 0), (2, 1), (3, 1))
    rounds = (0, 2, 4)
    crossings = (1, 3, 5, 6)

    def __init__(self, place, tokens, sems):
        self.place, self.tokens = place, tokens
        self.recv, self.along, self.across, self.cores = sems

    def line_copy(self, at, side):
        here, tokens = at * 2 + self.place.y, self.tokens
        return remote(
            tokens.at[here, 0],
            tokens.at[here, 0],
            self.along.at[at, (side + 1) // 2],
            self.recv.at[here, 0],
            self.place.beside(side),
        )

    def pair_copy(self, at, column):
        here, tokens = at * 2 + column, self.tokens
        return remote(
            tokens.at[here, 0],
            tokens.at[here, 0],
            self.across.at[at],
            self.recv.at[here, 0],
            self.place.partner,
        )

    def core_copy(self, here):
        tokens = self.tokens
        return remote(
            tokens.at[here, 0],
            tokens.at[here, 1],
            self.cores.at[here],
            self.recv.at[here, 1],
            self.place.sibling,
        )

    def start(self):
        place = self.place
        for side in (-1, 1):
            pl.when(place.inside(place.z + side))(lambda: self.line_copy(place.z, side).start())
        self.pair_copy(place.z, place.y).start()
        self.core_copy(place.z * 2 + place.y).start()

    def came_along(self, at, side):
        place = self.place
        self.line_copy(at, -side).wait_recv()
        pl.when(place.inside(place.z - side))(lambda: self.line_copy(at, -side).start())
        self.pair_copy(at, place.y).start()
        self.core_copy(at * 2 + place.y).start()

    def came_across(self, at):
        column = 1 - self.place.y
        self.pair_copy(at, column).wait_recv()
        self.core_copy(at * 2 + column).start()

    def tick(self, number):
        place = self.place
        for distance, when in enumerate(self.rounds, 1):

            @pl.when(number == when)
            def _():
                for side in (-1, 1):
                    at = place.z + side * distance
                    pl.when(place.inside(at))(partial(self.came_along, at, side))

        for distance, when in enumerate(self.crossings):

            @pl.when(number == when)
            def _():
                for side in (-1, 1) if distance else (1,):
                    at = place.z + side * distance
                    pl.when(place.inside(at))(partial(self.came_across, at))

    def finish(self):
        place = self.place
        for side in (-1, 1):
            for distance in range(place.line):
                at = place.z - side * distance

                @pl.when(place.inside(at) & place.inside(place.z + side))
                def _():
                    self.line_copy(at, side).wait_send()

        for at in range(place.line):
            self.pair_copy(at, place.y).wait_send()
        for here in range(2 * place.line):
            self.core_copy(here).wait_send()


class Reduce:
    order = ((3, 1), (3, 0), (2, 1), (2, 0), (1, 1), (1, 0), (0, 1), (0, 0))

    def __init__(self, place, arrays, terms, sums, sems):
        self.place, self.terms, self.sums = place, terms, sums
        self.parts, self.from_core, self.from_pair, self.from_line = arrays
        (
            self.term_sems,
            self.core_send,
            self.core_recv,
            self.pair_send,
            self.pair_recv,
            self.line_send,
            self.line_recv,
        ) = sems

    def core_copy(self, here, source):
        return remote(
            source,
            self.from_core.at[here],
            self.core_send.at[here],
            self.core_recv.at[here],
            self.place.sibling,
        )

    def core_arrived(self, here):
        self.core_copy(here, self.from_core.at[here]).wait_recv()

    def pair_copy(self, at, slot):
        return remote(
            self.sums.at[slot],
            self.from_pair.at[at],
            self.pair_send.at[at],
            self.pair_recv.at[at],
            self.place.partner,
        )

    def line_copy(self, at, side, distance):
        slot = self.place.line if distance == 1 and side == 1 else at
        return remote(
            self.sums.at[2 + (side + 1) // 2],
            self.from_line.at[slot],
            self.line_send.at[at],
            self.line_recv.at[slot],
            self.place.beside(side),
        )

    def add_up(self, sources, slot):
        terms = self.terms
        copies = [
            pltpu.make_async_copy(source, terms.at[i], self.term_sems.at[i])
            for i, (source, _) in enumerate(sources)
        ]
        for copy, (_, there) in zip(copies, sources):
            if there is None:
                copy.start()
            else:
                pl.when(there)(copy.start)
        for i, (copy, (_, there)) in enumerate(zip(copies, sources)):
            if there is None:
                copy.wait()
            else:
                pl.when(there)(copy.wait)

                @pl.when(jnp.logical_not(there))
                def _():
                    terms[i] = jnp.zeros_like(terms[i])

        tile = 16

        @pl.loop(0, terms.shape[1] // tile)
        def _(number):
            here = pl.ds(pl.multiple_of(number * tile, tile), tile)
            total = terms[0, here, :].astype(F32)
            for i in range(1, len(sources)):
                total += terms[i, here, :].astype(F32)
            self.sums[slot, here, :] = total.astype(BF16)

    def cross(self, rank):
        place = self.place
        at = place.near(rank)
        here = at * 2 + 1 - place.y
        slot = rank % 2
        if rank + 2 < place.line:
            self.pair_copy(place.near(rank + 2), slot).wait_send()
        self.core_arrived(here)
        self.add_up([(self.parts.at[here], None), (self.from_core.at[here], None)], slot)
        self.pair_copy(at, slot).start()

    def advance(self, distance):
        place = self.place
        for side in (-1, 1):
            at = place.z + side * distance
            here = at * 2 + place.y
            farther = place.inside(place.z - side)
            if distance + 1 < place.line:

                @pl.when(place.inside(at + side))
                def _():
                    self.line_copy(at + side, side, distance + 1).wait_send()

            @pl.when(place.inside(at))
            def _():
                self.core_arrived(here)
                self.pair_copy(at, 0).wait_recv()
                sources = [
                    (self.parts.at[here], None),
                    (self.from_core.at[here], None),
                    (self.from_pair.at[at], None),
                ]
                if distance + 1 < place.line:

                    @pl.when(farther)
                    def _():
                        self.line_copy(at, side, distance + 1).wait_recv()

                    sources.append((self.from_line.at[at], farther))
                self.add_up(sources, 2 + (side + 1) // 2)
                self.line_copy(at, side, distance).start()

    def tick(self, number):
        line = self.place.line
        for rank in range(line):

            @pl.when(number == 2 * (line - rank) - 1)
            def _():
                self.cross(rank)
                if rank + 1 < line:
                    self.advance(rank + 1)

    def finish(self, result, sem):
        place = self.place
        z, line = place.z, place.line
        here = z * 2 + place.y
        self.core_arrived(here)
        self.pair_copy(z, 0).wait_recv()
        for side in (-1, 1):
            pl.when(place.inside(z + side))(lambda: self.line_copy(z, -side, 1).wait_recv())
        for rank in (1, 0):
            self.pair_copy(place.near(rank), rank % 2).wait_send()
        self.add_up(
            [
                (self.parts.at[here], None),
                (self.from_core.at[here], None),
                (self.from_pair.at[z], None),
                (self.from_line.at[z], place.inside(z + 1)),
                (self.from_line.at[line], place.inside(z - 1)),
            ],
            0,
        )
        copy = pltpu.make_async_copy(self.sums.at[0], result, sem)
        copy.start()
        copy.wait()
        for side in (-1, 1):

            @pl.when(place.inside(z + side))
            def _():
                self.line_copy(z + side, side, 1).wait_send()


def expert_kernel(*refs, line, chunk, gathers):
    refs = list(refs)

    def take(count):
        taken = refs[:count]
        del refs[:count]
        return taken[0] if count == 1 else taken

    tokens_in, cotangent_own, cotangent_other, shares_ref, own_hbm, other_hbm = take(6)
    exchanged = take(1)
    if not gathers:
        out_before, grad_before = take(2)
        out_hbm, grad_piece, grad_own, grad_other, out_core, received = take(6)
        arrays = take(4)
        tokens_hbm = tokens_in
    else:
        out_hbm, grad_hbm, grad_own, grad_other, tokens_hbm, received = take(6)
    weights, grads, tokens_buf, cotangent_buf, inner_low, grad_low = take(6)
    out_buf, grad_buf, stage, load_sems, store_sems, row_sems, part_sems, exchange_sems = take(8)

    expert_count, model_width, all_units = weights.shape
    hidden_units = all_units // 3
    units = hidden_units // 2
    steps = 2 * line
    rows = tokens_hbm.shape[2]
    place = Place(line)
    first_rows, second_rows = pl.ds(0, rows), pl.ds(rows, rows)
    if gathers:
        mover = Gather(place, tokens_hbm, take(4))
    else:
        before_buf, terms, sums = take(3)
        core_out_send, core_out_recv = take(2)
        mover = Reduce(place, arrays, terms, sums, take(7))
    order = mover.order

    place.meet()
    exchange = remote(
        exchanged, received, exchange_sems.at[0], exchange_sems.at[1], place.across
    )
    exchange.start()
    if gathers:
        own_block = place.z * 2 + place.y
        own_copy = pltpu.make_async_copy(tokens_in, tokens_hbm.at[own_block, 0], row_sems.at[0, 0])
        own_copy.start()
        own_copy.wait()
        mover.start()
    weight_loads = weight_copies(own_hbm, other_hbm, weights, load_sems)
    for copy in weight_loads:
        copy.start()
    grads[...] = jnp.zeros_like(grads)

    def row_copies(step, slot):
        here = place.block(order, step)
        lanes = pl.ds(0, model_width)
        pairs = [
            (tokens_hbm.at[here, 0], tokens_buf.at[slot, first_rows, :]),
            (tokens_hbm.at[here, 1], tokens_buf.at[slot, second_rows, :]),
            (cotangent_own.at[here, :, lanes], cotangent_buf.at[slot, first_rows, :]),
            (cotangent_other.at[here, :, lanes], cotangent_buf.at[slot, second_rows, :]),
        ]
        if not gathers:
            pairs.append((out_before.at[here], before_buf.at[slot, 0]))
            pairs.append((grad_before.at[here], before_buf.at[slot, 1]))
        return [
            pltpu.make_async_copy(source, target, row_sems.at[slot, i])
            for i, (source, target) in enumerate(pairs)
        ]

    def load_rows(step, slot):
        if gathers:
            mover.core_copy(place.block(order, step)).wait_recv()
        for copy in row_copies(step, slot):
            copy.start()

    load_rows(0, 0)
    for copy in weight_loads:
        copy.wait()

    def out_core_copy(step):
        here = place.block(order, step)
        return remote(
            out_buf.at[second_rows],
            out_core.at[here],
            core_out_send.at[here],
            core_out_recv.at[here],
            place.sibling,
        )

    def grad_core_copy(step, slot):
        return mover.core_copy(place.block(order, step), grad_buf.at[slot, second_rows, :])

    def part_copies(step, slot):
        here = place.block(order, step)
        if gathers:
            pairs = [(out_buf, out_hbm.at[here]), (grad_buf.at[slot], grad_hbm.at[here])]
        else:
            pairs = [
                (out_buf.at[first_rows], out_hbm.at[here]),
                (grad_buf.at[slot, first_rows, :], arrays[0].at[here]),
            ]
        return [
            pltpu.make_async_copy(source, target, part_sems.at[i])
            for i, (source, target) in enumerate(pairs)
        ]

    @pl.loop(0, steps)
    def _(step):
        slot = step % 2
        for copy in row_copies(step, slot):
            copy.wait()
        shares = shares_ref[place.block(order, step)]
        lane = lax.broadcasted_iota(jnp.int32, shares.shape, 1)

        def run(expert, gate_up, grad_inner):
            share = jnp.sum(jnp.where(lane == expert, shares, 0.0), axis=1, keepdims=True)
            inner, grad_gate, grad_up = activate(gate_up, grad_inner, share)
            inner_low[expert] = inner
            grad_low[expert, :, :hidden_units] = grad_gate
            grad_low[expert, :, hidden_units:] = grad_up

        def weight_grads(expert):
            grads[expert, :, : 2 * hidden_units] += lax.dot_general(
                tokens_buf[slot], grad_low[expert], FIRST_FIRST, preferred_element_type=F32
            )
            grads[expert, :, 2 * hidden_units :] += lax.dot_general(
                cotangent_buf[slot], inner_low[expert], FIRST_FIRST, preferred_element_type=F32
            )

        results = project(tokens_buf[slot], cotangent_buf[slot], weights[0])
        for expert in range(expert_count):
            run(expert, *results)
            if expert + 1 < expert_count:
                results = project(tokens_buf[slot], cotangent_buf[slot], weights[expert + 1])
            weight_grads(expert)

        @pl.when(step >= 1)
        def _():
            for copy in part_copies(step - 1, 1 - slot):
                copy.wait()
            if not gathers:
                out_core_copy(step - 1).wait_send()

        mover.tick(step)

        if not gathers:

            @pl.when(step >= 2)
            def _():
                grad_core_copy(step - 2, slot).wait_send()

        @pl.loop(0, model_width // chunk)
        def _(number):
            @pl.when((number == 1) & (step + 1 < steps))
            def _():
                load_rows(step + 1, 1 - slot)

            cols = pl.ds(pl.multiple_of(number * chunk, chunk), chunk)

            def total_of(kind, lows, lanes):
                if gathers:
                    total = jnp.zeros((2 * rows, chunk), F32)
                else:
                    total = before_buf[slot, kind, :, cols].astype(F32)
                for expert in range(expert_count):
                    total += lax.dot_general(
                        lows[expert],
                        weights[expert, cols, lanes],
                        LAST_LAST,
                        preferred_element_type=F32,
                    )
                return total.astype(BF16)

            out_buf[:, cols] = total_of(0, inner_low, pl.ds(2 * hidden_units, hidden_units))
            grad_buf[slot, :, cols] = total_of(1, grad_low, pl.ds(0, 2 * hidden_units))

        for copy in part_copies(step, slot):
            copy.start()
        if not gathers:
            out_core_copy(step).start()
            grad_core_copy(step, slot).start()

    last = (steps - 1) % 2
    for copy in part_copies(steps - 1, last):
        copy.wait()
    if not gathers:
        out_core_copy(steps - 1).wait_send()
        grad_core_copy(steps - 2, 1 - last).wait_send()
        grad_core_copy(steps - 1, last).wait_send()

    sources, _, slice_rows, _ = own_hbm.shape

    def grad_copy(expert, source, half, slot):
        return pltpu.make_async_copy(
            stage.at[slot, half],
            (grad_own, grad_other)[half].at[source, expert],
            store_sems.at[slot, half],
        )

    @pl.loop(0, expert_count * sources)
    def _(number):
        expert, source = number // sources, number % sources
        slot = number % 2

        @pl.when(number >= 2)
        def _():
            for half in range(2):
                grad_copy(expert, source, half, slot).wait()

        here = pl.ds(pl.multiple_of(source * slice_rows, slice_rows), slice_rows)
        for half in range(2):
            for part in range(3):
                first = (2 * part + half) * units
                stage[slot, half, :, part * units : (part + 1) * units] = grads[
                    expert, here, first : first + units
                ].astype(BF16)
            grad_copy(expert, source, half, slot).start()

    for slot in range(2):
        for half in range(2):
            grad_copy(0, 0, half, slot).wait()

    exchange.wait()
    if gathers:
        mover.finish()
    else:
        for step in range(steps):
            out_core_copy(step).wait_recv()
        mover.finish(grad_piece, row_sems.at[0, 0])


def expert_call(operands, own, shares, line, rows, model_width, gathers, collective_id, chunk=512):
    sources, expert_count, slice_rows, lanes = own.shape
    hidden_units = 2 * lanes // 3
    blocks = 2 * line
    in_place = pl.BlockSpec(memory_space=pl.ANY)
    dma = pltpu.SemaphoreType.DMA
    flops = 2 * blocks * 2 * rows * model_width * expert_count * hidden_units * 9

    def low(*shape):
        return jax.ShapeDtypeStruct(shape, BF16)

    if gathers:
        out_shape = [
            low(blocks, 2 * rows, model_width),
            low(blocks, 2 * rows, model_width),
            low(*own.shape),
            low(*own.shape),
            low(blocks, 2, rows, model_width),
            low(*operands[6].shape),
        ]
        own_scratch = [dma((blocks, 2)), dma((line, 2)), dma((line,)), dma((blocks,))]
    else:
        out_shape = [
            low(blocks, rows, model_width),
            low(rows, model_width),
            low(*own.shape),
            low(*own.shape),
            low(blocks, rows, model_width),
            low(*operands[6].shape),
            low(blocks, rows, model_width),
            low(blocks, rows, model_width),
            low(line, rows, model_width),
            low(line + 1, rows, model_width),
        ]
        own_scratch = [
            pltpu.VMEM((2, 2, 2 * rows, model_width), BF16),
            pltpu.VMEM((5, rows, model_width), BF16),
            pltpu.VMEM((4, rows, model_width), BF16),
            dma((blocks,)),
            dma((blocks,)),
            dma((5,)),
            dma((blocks,)),
            dma((blocks,)),
            dma((line,)),
            dma((line,)),
            dma((line,)),
            dma((line + 1,)),
        ]
    in_specs = [in_place] * len(operands)
    in_specs[3] = pl.BlockSpec(memory_space=pltpu.VMEM)
    results = pl.pallas_call(
        partial(expert_kernel, line=line, chunk=chunk, gathers=gathers),
        in_specs=in_specs,
        out_specs=[in_place] * len(out_shape),
        out_shape=out_shape,
        scratch_shapes=[
            pltpu.VMEM((expert_count, model_width, 3 * hidden_units), BF16),
            pltpu.VMEM((expert_count, model_width, 3 * hidden_units), F32),
            pltpu.VMEM((2, 2 * rows, model_width), BF16),
            pltpu.VMEM((2, 2 * rows, model_width), BF16),
            pltpu.VMEM((expert_count, 2 * rows, hidden_units), BF16),
            pltpu.VMEM((expert_count, 2 * rows, 2 * hidden_units), BF16),
            pltpu.VMEM((2 * rows, model_width), BF16),
            pltpu.VMEM((2, 2 * rows, model_width), BF16),
            pltpu.VMEM((2, 2, slice_rows, lanes), BF16),
            dma((sources, 2, 3)),
            dma((2, 2)),
            dma((2, 6)),
            dma((2,)),
            dma((2,)),
        ]
        + own_scratch,
        compiler_params=pltpu.CompilerParams(
            vmem_limit_bytes=60 * 2**20, collective_id=collective_id, has_side_effects=True
        ),
        cost_estimate=pl.CostEstimate(
            flops=flops, bytes_accessed=80 * 2**20, transcendentals=0
        ),
    )(*operands)
    return results[:6]


def experts_gathering(piece, cotangents, shares, own, other, exchanged, line):
    rows, model_width = piece.shape
    operands = (piece, *cotangents, shares, own, other, exchanged)
    return expert_call(operands, own, shares, line, rows, model_width, True, 1)


def experts_reducing(
    tokens, cotangents, shares, own, other, exchanged, out_parts, grad_parts, line
):
    _, _, rows, model_width = tokens.shape
    operands = (tokens, *cotangents, shares, own, other, exchanged, out_parts, grad_parts)
    return expert_call(operands, own, shares, line, rows, model_width, False, 2)


def attention_rows(values, kv_head, group_size):
    first = kv_head * group_size
    return jnp.concatenate(
        [values[:, (first + r) * HEAD_DIM : (first + r + 1) * HEAD_DIM] for r in range(group_size)],
        axis=0,
    )


def quarter_turn(values):
    half = HEAD_DIM // 2
    return jnp.concatenate([-values[:, half:], values[:, :half]], axis=1)


def window_mask(start, doc_start_ref, first_ref, block_rows, window):
    key_index = start + lax.broadcasted_iota(jnp.int32, (block_rows, window), 1)
    query_index = (
        first_ref[0]
        + pl.program_id(0) * block_rows
        + lax.broadcasted_iota(jnp.int32, (block_rows, window), 0)
    )
    return (key_index <= query_index) & (key_index >= doc_start_ref[...])


def window_start(first_ref, block_rows, window):
    end = first_ref[0] + (pl.program_id(0) + 1) * block_rows
    return pl.multiple_of(jnp.maximum(end - window, 0), block_rows)


def attention_forward_kernel(
    first_ref, query_ref, key_value_ref, doc_start_ref, attended_ref, lse_ref, *, group_size, window
):
    block_rows = query_ref.shape[0]
    kv_heads = key_value_ref.shape[1] // (2 * HEAD_DIM)
    start = window_start(first_ref, block_rows, window)
    allowed = window_mask(start, doc_start_ref, first_ref, block_rows, window)
    bias = jnp.where(allowed, 0.0, -1e30)
    bias = jnp.concatenate([bias] * group_size, axis=0)
    keys_values = key_value_ref[pl.ds(start, window), :]
    queries = query_ref[...]
    parts = []
    for g in range(kv_heads):
        keys = keys_values[:, g * HEAD_DIM : (g + 1) * HEAD_DIM]
        values = keys_values[:, (kv_heads + g) * HEAD_DIM : (kv_heads + g + 1) * HEAD_DIM]
        scores = lax.dot_general(
            attention_rows(queries, g, group_size), keys, LAST_LAST, preferred_element_type=F32
        )
        scores = scores * HEAD_DIM**-0.5 + bias
        row_max = jnp.max(scores, axis=1, keepdims=True)
        exponent = jnp.exp(scores - row_max)
        total = jnp.sum(exponent, axis=1, keepdims=True)
        probs = (exponent * (1.0 / total)).astype(BF16)
        mixed = jnp.dot(probs, values, preferred_element_type=F32).astype(BF16)
        lse_ref[0, g] = row_max + jnp.log(total)
        parts += [mixed[r * block_rows : (r + 1) * block_rows] for r in range(group_size)]
    attended_ref[...] = jnp.concatenate(parts, axis=1)


def attention_backward_kernel(
    first_ref,
    query_ref,
    key_value_ref,
    doc_start_ref,
    lse_ref,
    grad_ref,
    turns_ref,
    query_turns_ref,
    grad_query_ref,
    grad_key_value_ref,
    grad_keys,
    grad_values,
    *,
    group_size,
    window,
    steps,
):
    step = pl.program_id(0)
    block_rows = query_ref.shape[0]
    kv_heads = key_value_ref.shape[1] // (2 * HEAD_DIM)

    @pl.when(step == 0)
    def _():
        grad_keys[...] = jnp.zeros_like(grad_keys)
        grad_values[...] = jnp.zeros_like(grad_values)

    start = window_start(first_ref, block_rows, window)
    allowed = window_mask(start, doc_start_ref, first_ref, block_rows, window)
    bias = jnp.where(allowed, 0.0, -1e30)
    bias = jnp.concatenate([bias] * group_size, axis=0)
    rows = pl.ds(start, window)
    keys_values = key_value_ref[rows, :]
    queries = query_ref[...]
    grads = grad_ref[...]
    query_turns = jnp.concatenate([query_turns_ref[...]] * group_size, axis=0)
    parts = []
    for g in range(kv_heads):
        keys = keys_values[:, g * HEAD_DIM : (g + 1) * HEAD_DIM]
        values = keys_values[:, (kv_heads + g) * HEAD_DIM : (kv_heads + g + 1) * HEAD_DIM]
        query_rows = attention_rows(queries, g, group_size)
        grad_rows = attention_rows(grads, g, group_size)
        scores = lax.dot_general(query_rows, keys, LAST_LAST, preferred_element_type=F32)
        probs = jnp.exp(scores * HEAD_DIM**-0.5 + bias - lse_ref[0, g])
        grad_probs = lax.dot_general(grad_rows, values, LAST_LAST, preferred_element_type=F32)
        inner = jnp.sum(grad_probs * probs, axis=1, keepdims=True)
        grad_scores = (HEAD_DIM**-0.5 * (probs * (grad_probs - inner))).astype(BF16)
        grad_values[g, rows, :] += lax.dot_general(
            probs.astype(BF16), grad_rows, FIRST_FIRST, preferred_element_type=F32
        )
        both_queries = jnp.concatenate([query_rows, quarter_turn(query_rows)], axis=1)
        grad_keys[g, rows, :] += lax.dot_general(
            grad_scores, both_queries, FIRST_FIRST, preferred_element_type=F32
        )
        both_keys = jnp.concatenate([keys, quarter_turn(keys)], axis=1)
        turned = jnp.dot(grad_scores, both_keys, preferred_element_type=F32) * query_turns
        grad_query = (turned[:, :HEAD_DIM] + turned[:, HEAD_DIM:]).astype(BF16)
        parts += [grad_query[r * block_rows : (r + 1) * block_rows] for r in range(group_size)]
    grad_query_ref[...] = jnp.concatenate(parts, axis=1)

    @pl.when(step == steps - 1)
    def _():
        key_parts, value_parts = [], []
        for g in range(kv_heads):
            turned = grad_keys[g] * turns_ref[...]
            key_parts.append((turned[:, :HEAD_DIM] + turned[:, HEAD_DIM:]).astype(BF16))
            value_parts.append(grad_values[g].astype(BF16))
        grad_key_value_ref[...] = jnp.concatenate(key_parts + value_parts, axis=1)


def attention_specs(queries, keys_values, block_rows):
    return dict(
        smem=pl.BlockSpec(memory_space=pltpu.SMEM),
        rows=pl.BlockSpec((block_rows, queries.shape[1]), lambda i: (i, 0)),
        whole=pl.BlockSpec(keys_values.shape, lambda i: (0, 0)),
        column=pl.BlockSpec((block_rows, 1), lambda i: (i, 0)),
    )


def attention_forward(first, queries, keys_values, doc_start, block_rows=256, reach=1024):
    row_count, query_cols = queries.shape
    kv_heads = keys_values.shape[1] // (2 * HEAD_DIM)
    group_size = query_cols // HEAD_DIM // kv_heads
    steps = row_count // block_rows
    window = min(reach + block_rows, keys_values.shape[0])
    specs = attention_specs(queries, keys_values, block_rows)
    stacked = group_size * block_rows
    return pl.pallas_call(
        partial(attention_forward_kernel, group_size=group_size, window=window),
        grid=(steps,),
        in_specs=[specs["smem"], specs["rows"], specs["whole"], specs["column"]],
        out_specs=[
            specs["rows"],
            pl.BlockSpec((1, kv_heads, stacked, 1), lambda i: (i, 0, 0, 0)),
        ],
        out_shape=[
            jax.ShapeDtypeStruct(queries.shape, BF16),
            jax.ShapeDtypeStruct((steps, kv_heads, stacked, 1), F32),
        ],
        compiler_params=pltpu.CompilerParams(vmem_limit_bytes=48 * 2**20),
        cost_estimate=pl.CostEstimate(
            flops=4 * row_count * window * query_cols * 8, bytes_accessed=2**22, transcendentals=0
        ),
    )(first, queries, keys_values, doc_start)


def attention_backward(
    first, queries, keys_values, doc_start, lse, grads, turns, query_turns, block_rows=256, reach=1024
):
    row_count, query_cols = queries.shape
    kv_heads = keys_values.shape[1] // (2 * HEAD_DIM)
    group_size = query_cols // HEAD_DIM // kv_heads
    steps = row_count // block_rows
    window = min(reach + block_rows, keys_values.shape[0])
    specs = attention_specs(queries, keys_values, block_rows)
    stacked = group_size * block_rows
    return pl.pallas_call(
        partial(attention_backward_kernel, group_size=group_size, window=window, steps=steps),
        grid=(steps,),
        in_specs=[
            specs["smem"],
            specs["rows"],
            specs["whole"],
            specs["column"],
            pl.BlockSpec((1, kv_heads, stacked, 1), lambda i: (i, 0, 0, 0)),
            specs["rows"],
            pl.BlockSpec(turns.shape, lambda i: (0, 0)),
            pl.BlockSpec((block_rows, turns.shape[1]), lambda i: (i, 0)),
        ],
        out_specs=[specs["rows"], specs["whole"]],
        out_shape=[
            jax.ShapeDtypeStruct(queries.shape, BF16),
            jax.ShapeDtypeStruct(keys_values.shape, BF16),
        ],
        scratch_shapes=[
            pltpu.VMEM((kv_heads, keys_values.shape[0], 2 * HEAD_DIM), F32),
            pltpu.VMEM((kv_heads, keys_values.shape[0], HEAD_DIM), F32),
        ],
        compiler_params=pltpu.CompilerParams(vmem_limit_bytes=48 * 2**20),
        cost_estimate=pl.CostEstimate(
            flops=10 * row_count * window * query_cols * 8, bytes_accessed=2**23, transcendentals=0
        ),
    )(first, queries, keys_values, doc_start, lse, grads, turns, query_turns)


def rotation_tables(positions):
    half_dim = HEAD_DIM // 2
    frequencies = 10000.0 ** (-2.0 * jnp.arange(half_dim, dtype=F32) / HEAD_DIM)
    angles = positions.astype(F32)[:, None] * frequencies[None, :]
    cosine, sine = jnp.cos(angles), jnp.sin(angles)
    return jnp.concatenate([cosine, cosine, -sine, -sine], axis=1)


def turned_columns(weight):
    rows, cols = weight.shape
    halves = weight.reshape(rows, cols // HEAD_DIM, 2, HEAD_DIM // 2)
    return jnp.stack([-halves[:, :, 1], halves[:, :, 0]], axis=2).reshape(rows, cols)


def expert_plan(
    residual_in,
    gain_attn,
    query_weight,
    key_projection_weight,
    value_projection_weight,
    out_weight,
    gain_ffn,
    gate_weight,
    up_weight,
    down_weight,
    segments,
    routes,
    shares,
    cotangent,
    *,
    groups,
    tensor_size,
):
    row_count, model_width = residual_in.shape
    query_cols = query_weight.shape[1]
    kv_cols = key_projection_weight.shape[1]
    expert_count, slice_rows, unit_count = gate_weight.shape
    own_experts = expert_count // groups
    piece_rows = row_count // tensor_size
    first_count = own_experts * 2 // 5
    context_rank = lax.axis_index(CONTEXT)
    tensor_rank = lax.axis_index(TENSOR)
    group_rank = lax.axis_index(SHARD) * lax.axis_size(CONTEXT) + context_rank
    chip_half, core = tensor_rank // 2, tensor_rank % 2
    own_first = context_rank * row_count
    piece_first = tensor_rank * piece_rows
    sibling = [(i, i ^ 1) for i in range(tensor_size)]
    across = [(i, i ^ 2) for i in range(tensor_size)]
    pair = [(0, 1), (1, 0)]

    def own_piece(values):
        return lax.dynamic_slice_in_dim(values, piece_first, piece_rows)

    def pick(values, axis, index):
        return lax.dynamic_index_in_dim(values, index, axis, keepdims=False)

    def sum_over_tensor(parts):
        parts = parts.astype(BF16).reshape(2, 2, piece_rows, -1)
        received = lax.ppermute(pick(parts, 1, 1 - core), TENSOR, sibling)
        half = pick(parts, 1, core).astype(F32) + received.astype(F32)
        received = lax.ppermute(pick(half, 0, 1 - chip_half).astype(BF16), TENSOR, across)
        return pick(half, 0, chip_half) + received.astype(F32)

    def gather_over_tensor(piece):
        other = lax.ppermute(piece, TENSOR, across)
        chips = jnp.where(
            chip_half == 0, jnp.concatenate([piece, other]), jnp.concatenate([other, piece])
        ).reshape(2, 1, piece_rows, -1)
        others = lax.ppermute(chips, TENSOR, sibling)
        both = jnp.where(
            core == 0,
            jnp.concatenate([chips, others], axis=1),
            jnp.concatenate([others, chips], axis=1),
        )
        return both.reshape(row_count, -1)

    def padded_columns(*gains):
        columns = jnp.stack(gains, axis=1)
        return jnp.pad(columns, ((0, 0), (0, 128 - len(gains))))

    with jax.named_scope("weights"):
        qkv_full = lax.all_gather(
            jnp.concatenate(
                [
                    query_weight,
                    key_projection_weight,
                    value_projection_weight,
                    out_weight.T,
                    padded_columns(gain_attn, gain_ffn),
                ],
                axis=1,
            ),
            GROUP,
            axis=0,
            tiled=True,
        )
        qkv_cols = query_cols + 2 * kv_cols
        qkv_weight = qkv_full[:, :qkv_cols]
        out_transposed = qkv_full[:, qkv_cols : qkv_cols + query_cols]
        gain_attn_float = qkv_full[:, qkv_cols + query_cols].astype(F32)
        gain_ffn_float = qkv_full[:, qkv_cols + query_cols + 1].astype(F32)
        lanes = 3 * unit_count


        def expert_slices(first, count):
            slices = jnp.concatenate(
                [
                    weight.reshape((groups, own_experts) + weight.shape[1:])[:, first : first + count]
                    for weight in (gate_weight, up_weight, down_weight.transpose(0, 2, 1))
                ],
                axis=3,
            ).reshape(groups * count, slice_rows, lanes)
            owned = lax.all_to_all(slices, GROUP, 0, 0, tiled=True)
            return owned.reshape(groups, count, slice_rows, lanes)

        owned_first = expert_slices(0, first_count)
        owned_second = expert_slices(first_count, own_experts - first_count)

    with jax.named_scope("cotangents"):
        cotangent_piece = own_piece(cotangent)
        spread = jnp.sum(
            jnp.where(
                own_piece(routes)[:, :, None] == jnp.arange(expert_count, dtype=jnp.int32),
                own_piece(shares)[:, :, None],
                0.0,
            ),
            axis=1,
        )
        spread_high = spread.astype(BF16)
        spread_low = (spread - spread_high.astype(F32)).astype(BF16)
        spread_both = jnp.pad(
            jnp.concatenate([spread_high, spread_low], axis=1),
            ((0, 0), (0, 128 - 2 * expert_count)),
        )
        cotangent_own = lax.all_gather(
            jnp.concatenate([cotangent_piece, spread_both], axis=1), GROUP, axis=0, tiled=False
        )

    with jax.named_scope("attention"):
        positions = doc_positions(segments)
        turns = rotation_tables(positions)
        own_turns = lax.dynamic_slice_in_dim(turns, own_first, row_count)
        own_index = own_first + jnp.arange(row_count, dtype=jnp.int32)
        doc_start = own_index - lax.dynamic_slice_in_dim(positions, own_first, row_count)
        input_float = residual_in.astype(F32)
        first_normalized = rms_scale(input_float, gain_attn_float).astype(BF16)
        rotated_cols = query_cols + kv_cols
        projected = jnp.dot(
            first_normalized,
            jnp.concatenate([qkv_weight, turned_columns(qkv_weight[:, :rotated_cols])], axis=1),
            preferred_element_type=F32,
        )
        heads = rotated_cols // HEAD_DIM
        rotated = (
            projected[:, :rotated_cols] * jnp.tile(own_turns[:, :HEAD_DIM], (1, heads))
            - projected[:, qkv_cols:] * jnp.tile(own_turns[:, HEAD_DIM:], (1, heads))
        ).astype(BF16)
        queries = rotated[:, :query_cols]
        own_keys_values = jnp.concatenate(
            [rotated[:, query_cols:], projected[:, rotated_cols:qkv_cols].astype(BF16)], axis=1
        )
        owned_first, own_keys_values = lax.optimization_barrier((owned_first, own_keys_values))
        other_keys_values = lax.ppermute(own_keys_values, CONTEXT, pair)
        keys_values = jnp.where(
            context_rank == 0,
            jnp.concatenate([own_keys_values, other_keys_values]),
            jnp.concatenate([other_keys_values, own_keys_values]),
        )
        others_first = lax.ppermute(owned_first, TENSOR, across)
        first = own_first.reshape(1).astype(jnp.int32)
        attended, lse = attention_forward(first, queries, keys_values, doc_start[:, None])
        attn_part = lax.dot_general(
            attended, out_transposed, LAST_LAST, preferred_element_type=F32
        )
        attn_piece = sum_over_tensor(attn_part)
        others_first, owned_second, attn_piece = lax.optimization_barrier(
            (others_first, owned_second, attn_piece)
        )
        hidden = own_piece(residual_in).astype(F32) + attn_piece
        normed_ffn, ffn_norm_back = jax.vjp(rms_scale, hidden, gain_ffn_float)

    with jax.named_scope("exchange"):
        cotangent_own, normed_ffn = lax.optimization_barrier((cotangent_own, normed_ffn))
        cotangent_other = lax.ppermute(cotangent_own, TENSOR, sibling)
        spread_all = jnp.concatenate(
            [cotangent_own[:, :, model_width:], cotangent_other[:, :, model_width:]], axis=1
        )

        def shares_of(first, count):
            start = group_rank * own_experts + first
            high = lax.dynamic_slice_in_dim(spread_all, start, count, axis=2)
            low = lax.dynamic_slice_in_dim(spread_all, start + expert_count, count, axis=2)
            total = high.astype(F32) + low.astype(F32)
            return jnp.pad(total, ((0, 0), (0, 0), (0, 8 - count)))

        shares_first = shares_of(0, first_count)
        shares_second = shares_of(first_count, own_experts - first_count)

    with jax.named_scope("experts"):
        line = groups // 2
        cotangents = (cotangent_own, cotangent_other)
        out_parts, grad_parts, grad_own_first, grad_other_first, tokens, others_second = (
            experts_gathering(
                normed_ffn.astype(BF16),
                cotangents,
                shares_first,
                owned_first,
                others_first,
                owned_second,
                line,
            )
        )
        out_own, grad_second, grad_own_second, grad_other_second, out_other, received_first = (
            experts_reducing(
                tokens,
                cotangents,
                shares_second,
                owned_second,
                others_second,
                grad_other_first,
                out_parts,
                grad_parts,
                line,
            )
        )

    with jax.named_scope("expert_grads"):

        def added(own, received):
            return (own.astype(F32) + received.astype(F32)).astype(BF16)

        def returned(total):
            flat = total.reshape((total.shape[0] * total.shape[1],) + total.shape[2:])
            return lax.all_to_all(flat, GROUP, 0, 0, tiled=True).reshape(total.shape)

        total_first = added(grad_own_first, received_first)
        received_second = lax.ppermute(grad_other_second, TENSOR, across)
        total_first, grad_second = lax.optimization_barrier((total_first, grad_second))
        returned_first = returned(total_first)
        grad_hidden_norm, grad_gain_ffn_local = ffn_norm_back(grad_second.astype(F32))
        grad_hidden = cotangent_piece.astype(F32) + grad_hidden_norm
        grad_hidden_low = gather_over_tensor(grad_hidden.astype(BF16))
        out_sum = (out_own.astype(F32) + out_other.astype(F32)).astype(BF16)
        out_piece = lax.psum_scatter(
            out_sum.reshape(groups * piece_rows, model_width),
            GROUP,
            scatter_dimension=0,
            tiled=True,
        )
        output = gather_over_tensor((hidden + out_piece.astype(F32)).astype(BF16))

    with jax.named_scope("attention_back"):
        grad_out_local = lax.dot_general(
            grad_hidden_low, attended, FIRST_FIRST, preferred_element_type=F32
        )
        grad_out_transposed = lax.psum_scatter(
            grad_out_local.astype(BF16), GROUP, scatter_dimension=0, tiled=True
        )
        grad_attended = jnp.dot(grad_hidden_low, out_transposed, preferred_element_type=F32)
        grad_query_lin, grad_key_value = attention_backward(
            first,
            queries,
            keys_values,
            doc_start[:, None],
            lse,
            grad_attended.astype(BF16),
            turns,
            own_turns,
        )
        received_second, grad_key_value = lax.optimization_barrier(
            (received_second, grad_key_value)
        )
        total_second = added(grad_own_second, received_second)
        grad_key_value = grad_key_value.reshape(2, row_count, -1)
        received = lax.ppermute(pick(grad_key_value, 0, 1 - context_rank), CONTEXT, pair)
        grad_key_value = (
            pick(grad_key_value, 0, context_rank).astype(F32) + received.astype(F32)
        ).astype(BF16)
        grad_projected = jnp.concatenate([grad_query_lin, grad_key_value], axis=1)
        grad_first_part = lax.dot_general(
            grad_projected, qkv_weight, LAST_LAST, preferred_element_type=F32
        )
        returned_first, total_second, grad_first_part = lax.optimization_barrier(
            (returned_first, total_second, grad_first_part)
        )
        returned_second = returned(total_second)
        grad_first = sum_over_tensor(grad_first_part)
        out_piece, grad_first = lax.optimization_barrier((out_piece, grad_first))
        _, attn_norm_back = jax.vjp(
            rms_scale, own_piece(residual_in).astype(F32), gain_attn_float
        )
        grad_input_norm, grad_gain_attn_local = attn_norm_back(grad_first)
        grad_input = gather_over_tensor((grad_hidden + grad_input_norm).astype(BF16))
        grad_qkv_local = lax.dot_general(
            first_normalized, grad_projected, FIRST_FIRST, preferred_element_type=F32
        )
        grad_qkv = lax.psum_scatter(
            jnp.concatenate(
                [grad_qkv_local, padded_columns(grad_gain_attn_local, grad_gain_ffn_local)], axis=1
            ).astype(BF16),
            GROUP,
            scatter_dimension=0,
            tiled=True,
        ).astype(F32)
        gains = grad_qkv[:, qkv_cols : qkv_cols + 2]
        gains = gains + lax.ppermute(gains, TENSOR, sibling)
        gains = gains + lax.ppermute(gains, TENSOR, across)

    def whole(first, last, turned):
        parts = [
            part[..., first:last].transpose(0, 1, 3, 2) if turned else part[..., first:last]
            for part in (returned_first, returned_second)
        ]
        joined = jnp.concatenate(parts, axis=1).astype(F32)
        return joined.reshape((expert_count,) + joined.shape[2:])

    units = unit_count
    return (
        output,
        grad_input,
        gains[:, 0],
        grad_qkv[:, :query_cols],
        grad_qkv[:, query_cols:rotated_cols],
        grad_qkv[:, rotated_cols:qkv_cols],
        grad_out_transposed.astype(F32).T,
        gains[:, 1],
        whole(0, units, False),
        whole(units, 2 * units, False),
        whole(2 * units, 3 * units, True),
    )


def solution(mesh):
    placed = (
        P(GROUP, None),
        P(GROUP),
        P(GROUP, TENSOR),
        P(GROUP, TENSOR),
        P(GROUP, TENSOR),
        P(TENSOR, GROUP),
        P(GROUP),
        P(None, GROUP, TENSOR),
        P(None, GROUP, TENSOR),
        P(None, TENSOR, GROUP),
        P(SHARD),
        P(GROUP, None),
        P(GROUP, None),
        P(GROUP, None),
    )
    sizes = dict(mesh.shape)
    if sizes[SHARD] == 4 and sizes[CONTEXT] == 2 and sizes[TENSOR] == 4:
        plan = partial(
            expert_plan, groups=sizes[SHARD] * sizes[CONTEXT], tensor_size=sizes[TENSOR]
        )
    else:
        plan = gathered_plan
    return jax.shard_map(
        plan,
        mesh=mesh,
        in_specs=placed,
        out_specs=(
            P(GROUP, None),
            P(GROUP, None),
            P(GROUP),
            P(GROUP, TENSOR),
            P(GROUP, TENSOR),
            P(GROUP, TENSOR),
            P(TENSOR, GROUP),
            P(GROUP),
            P(None, GROUP, TENSOR),
            P(None, GROUP, TENSOR),
            P(None, TENSOR, GROUP),
        ),
        check_vma=False,
    )
```

```python
from functools import partial

import jax
import jax.numpy as jnp
from jax import lax
from jax.experimental import pallas as pl
from jax.experimental.pallas import tpu as pltpu
from jax.sharding import PartitionSpec as P

HEAD_DIM = 64
NDOCS = 5
SHARD = "shard"
CONTEXT = "context"
TENSOR = "tensor"
GROUP = (SHARD, CONTEXT)
PRODUCT_0 = "qgrd,kgd->grqk"
PRODUCT_1 = "grqk,kgd->qgrd"
PRODUCT_2 = "ecd,edf->ecf"
PRODUCT_3 = "ecf,efd->ecd"
PRODUCT_4 = "ecd,efd->ecf"
PRODUCT_5 = "ecf,edf->ecd"
PRODUCT_6 = "ecd,ecf->edf"
PRODUCT_7 = "ecf,ecd->efd"
PRODUCT_8 = "grqk,qgrd->kgd"


epsilon = 1e-06


def rms_scale(values, gain):
    return values * lax.rsqrt(jnp.mean(values * values, axis=-1, keepdims=True) + epsilon) * gain


def doc_positions(segment_ids):
    sequence_length = segment_ids.shape[-1]
    index_row = jnp.arange(sequence_length, dtype=jnp.int32)
    documents = jnp.arange(NDOCS, dtype=jnp.int32)
    doc_starts = jnp.sum((segment_ids[..., :, None] < documents).astype(jnp.int32), axis=-2)
    own_start = jnp.sum(
        jnp.where(segment_ids[..., :, None] == documents, doc_starts[..., None, :], 0), axis=-1
    )
    return index_row - own_start


def rotary(values, positions):
    half_dim = values.shape[-1] // 2
    frequencies = 10000.0 ** (-2.0 * jnp.arange(half_dim, dtype=jnp.float32) / values.shape[-1])
    angles = positions.astype(jnp.float32)[:, None] * frequencies[None, :]
    cosine = jnp.cos(angles)[:, None, :]
    sines = jnp.sin(angles)[:, None, :]
    first_half = values[..., :half_dim]
    second_half = values[..., half_dim:]
    return jnp.concatenate(
        [first_half * cosine - second_half * sines, second_half * cosine + first_half * sines],
        axis=-1,
    )


def swiglu(gate_value, up_value):
    return jax.nn.silu(gate_value) * up_value


def dispatch(routes, shares, block_rows, capacity, expert_count):
    block_count = routes.shape[0] // block_rows
    picks = routes.shape[1]
    chosen = routes.reshape(block_count, block_rows * picks)
    onehot = (chosen[:, :, None] == jnp.arange(expert_count, dtype=jnp.int32)).astype(jnp.int32)
    ranked = jnp.sum((jnp.cumsum(onehot, axis=1) - onehot) * onehot, axis=2)
    slot_index = (
        chosen * (block_count * capacity)
        + jnp.arange(block_count, dtype=jnp.int32)[:, None] * capacity
        + ranked
    )
    tokens = jnp.arange(block_count * block_rows * picks, dtype=jnp.int32) // picks
    total_slots = expert_count * block_count * capacity
    slot_rows = jnp.zeros((total_slots,), jnp.int32).at[slot_index.reshape(-1)].set(tokens)
    slot_share = (
        jnp.zeros((total_slots,), jnp.float32).at[slot_index.reshape(-1)].set(shares.reshape(-1))
    )
    return (slot_rows, slot_share)


def gathered_plan(
    residual_in,
    gain_attn,
    query_weight,
    key_projection_weight,
    value_projection_weight,
    out_weight,
    gain_ffn,
    gate_weight,
    up_weight,
    down_weight,
    segments,
    routes,
    shares,
    cotangent,
):
    row_count, model_width = residual_in.shape
    head_size = HEAD_DIM
    query_cols = query_weight.shape[1]
    kv_heads = key_projection_weight.shape[1] // head_size
    group_size = query_cols // head_size // kv_heads
    expert_count = gate_weight.shape[0]
    capacity = row_count * routes.shape[1] * 5 // (4 * expert_count)
    score_scale = head_size ** (-0.5)
    context_rank = lax.axis_index(CONTEXT)
    own_first = context_rank * row_count
    gain_attn_full, gain_ffn_full, query_full, key_full, value_full, out_full = (
        lax.all_gather(gain_attn, GROUP, axis=0, tiled=True),
        lax.all_gather(gain_ffn, GROUP, axis=0, tiled=True),
        lax.all_gather(query_weight, GROUP, axis=0, tiled=True),
        lax.all_gather(key_projection_weight, GROUP, axis=0, tiled=True),
        lax.all_gather(value_projection_weight, GROUP, axis=0, tiled=True),
        lax.all_gather(out_weight, GROUP, axis=1, tiled=True),
    )
    gain_attn_float = gain_attn_full.astype(jnp.float32)
    gain_ffn_float = gain_ffn_full.astype(jnp.float32)
    positions = doc_positions(segments)
    own_positions = lax.dynamic_slice_in_dim(positions, own_first, row_count)
    own_ids = lax.dynamic_slice_in_dim(segments, own_first, row_count)
    own_index = own_first + jnp.arange(row_count, dtype=jnp.int32)
    input_float = residual_in.astype(jnp.float32)
    normed_attn, attn_norm_back = jax.vjp(rms_scale, input_float, gain_attn_float)
    first_normalized = normed_attn.astype(jnp.bfloat16)
    query_lin = jnp.dot(first_normalized, query_full, preferred_element_type=jnp.float32).reshape(
        row_count, -1, head_size
    )
    key_linear = jnp.dot(first_normalized, key_full, preferred_element_type=jnp.float32).reshape(
        row_count, -1, head_size
    )
    value_tokens = jnp.dot(first_normalized, value_full, preferred_element_type=jnp.float32).astype(
        jnp.bfloat16
    )
    rope_local = partial(rotary, positions=own_positions)
    query_rot, rope_query_back = jax.vjp(rope_local, query_lin)
    key_rot, rope_key_back = jax.vjp(rope_local, key_linear)
    query_low = query_rot.astype(jnp.bfloat16)
    key_low = key_rot.astype(jnp.bfloat16).reshape(row_count, -1)
    key_all, value_all = (
        lax.all_gather(key_low, CONTEXT, axis=0, tiled=True),
        lax.all_gather(value_tokens, CONTEXT, axis=0, tiled=True),
    )
    key_index = jnp.arange(key_all.shape[0], dtype=jnp.int32)
    key_ids = jnp.take(segments, jnp.clip(key_index, 0, segments.shape[0] - 1))
    key_valid = key_index >= 0
    key_heads = key_all.reshape(-1, kv_heads, head_size)
    value_heads = value_all.reshape(-1, kv_heads, head_size)
    query_heads = query_low.reshape(row_count, kv_heads, group_size, head_size)
    block_rows = min(512, row_count)
    block_starts = list(range(0, row_count, block_rows))

    def block_scores(block_first):
        query_block = query_heads[block_first : block_first + block_rows]
        raw_scores = jnp.einsum(
            PRODUCT_0, query_block, key_heads, preferred_element_type=jnp.float32
        )
        block_ids = own_ids[block_first : block_first + block_rows]
        block_index = own_index[block_first : block_first + block_rows]
        allowed = (
            key_valid[None, :]
            & (key_ids[None, :] == block_ids[:, None])
            & (key_index[None, :] <= block_index[:, None])
        )
        return (query_block, jnp.where(allowed, raw_scores * score_scale, -1e30))

    mixed_parts = []
    lse_parts = []
    for block_first in block_starts:
        query_block, scores = block_scores(block_first)
        row_max = jnp.max(scores, axis=-1, keepdims=True)
        exponent = jnp.exp(scores - row_max)
        row_total = jnp.sum(exponent, axis=-1, keepdims=True)
        probs = (exponent / row_total).astype(jnp.bfloat16)
        mixed_parts.append(
            jnp.einsum(PRODUCT_1, probs, value_heads, preferred_element_type=jnp.float32)
        )
        lse_parts.append(row_max + jnp.log(row_total))
    attended = (
        jnp.concatenate(mixed_parts, axis=0).reshape(row_count, query_cols).astype(jnp.bfloat16)
    )
    attn_part = jnp.dot(attended, out_full, preferred_element_type=jnp.float32)
    hidden = input_float + lax.psum(attn_part.astype(jnp.bfloat16), TENSOR).astype(jnp.float32)
    normed_ffn, ffn_norm_back = jax.vjp(rms_scale, hidden, gain_ffn_float)
    normed_second = normed_ffn.astype(jnp.bfloat16)
    slot_rows, slot_share = dispatch(routes, shares, row_count, capacity, expert_count)
    per_turn = expert_count // 5
    turn_count = expert_count // per_turn
    turn_slots = per_turn * capacity

    def local_experts(turn_index):
        gate_part = lax.dynamic_slice_in_dim(gate_weight, turn_index * per_turn, per_turn, 0)
        up_part = lax.dynamic_slice_in_dim(up_weight, turn_index * per_turn, per_turn, 0)
        down_part = lax.dynamic_slice_in_dim(down_weight, turn_index * per_turn, per_turn, 0)
        return (gate_part, up_part, down_part)

    def turn_inputs(turn_index):
        token_rows = lax.dynamic_slice_in_dim(slot_rows, turn_index * turn_slots, turn_slots)
        share_rows = lax.dynamic_slice_in_dim(slot_share, turn_index * turn_slots, turn_slots)
        picked = normed_second[token_rows].reshape(per_turn, capacity, model_width)
        return (token_rows, share_rows, picked)

    def forward_turn(running, turn_index):
        gate_part, up_part, down_part = local_experts(turn_index)
        gate_full, up_full, down_full = (
            lax.all_gather(gate_part, GROUP, axis=1, tiled=True),
            lax.all_gather(up_part, GROUP, axis=1, tiled=True),
            lax.all_gather(down_part, GROUP, axis=2, tiled=True),
        )
        token_rows, share_rows, picked = turn_inputs(turn_index)
        gate_value = jnp.einsum(
            PRODUCT_2, picked, gate_full, preferred_element_type=jnp.float32
        )
        up_value = jnp.einsum(PRODUCT_2, picked, up_full, preferred_element_type=jnp.float32)
        inner = swiglu(gate_value, up_value).astype(jnp.bfloat16)
        expert_result = jnp.einsum(
            PRODUCT_3, inner, down_full, preferred_element_type=jnp.float32
        ).reshape(turn_slots, model_width)
        return (running.at[token_rows].add(expert_result * share_rows[:, None]), None)

    turn_ids = jnp.arange(turn_count, dtype=jnp.int32)
    expert_part, _ = lax.scan(
        forward_turn, jnp.zeros((row_count, model_width), jnp.float32), turn_ids
    )
    expert_total = lax.psum(expert_part.astype(jnp.bfloat16), TENSOR).astype(jnp.float32)
    output = (hidden + expert_total).astype(jnp.bfloat16)
    upstream = cotangent.astype(jnp.float32)

    def backward_turn(running, turn_index):
        gate_part, up_part, down_part = local_experts(turn_index)
        gate_full, up_full, down_full = (
            lax.all_gather(gate_part, GROUP, axis=1, tiled=True),
            lax.all_gather(up_part, GROUP, axis=1, tiled=True),
            lax.all_gather(down_part, GROUP, axis=2, tiled=True),
        )
        token_rows, share_rows, picked = turn_inputs(turn_index)
        gate_value = jnp.einsum(
            PRODUCT_2, picked, gate_full, preferred_element_type=jnp.float32
        )
        up_value = jnp.einsum(PRODUCT_2, picked, up_full, preferred_element_type=jnp.float32)
        inner_float, swiglu_back = jax.vjp(swiglu, gate_value, up_value)
        inner = inner_float.astype(jnp.bfloat16)
        grad_slot = (
            (upstream[token_rows] * share_rows[:, None])
            .astype(jnp.bfloat16)
            .reshape(per_turn, capacity, model_width)
        )
        grad_inner = jnp.einsum(
            PRODUCT_4, grad_slot, down_full, preferred_element_type=jnp.float32
        )
        grad_gate_value, grad_up_value = swiglu_back(grad_inner)
        grad_gate_low = grad_gate_value.astype(jnp.bfloat16)
        grad_up_low = grad_up_value.astype(jnp.bfloat16)
        grad_picked = jnp.einsum(
            PRODUCT_5, grad_gate_low, gate_full, preferred_element_type=jnp.float32
        )
        grad_picked = grad_picked + jnp.einsum(
            PRODUCT_5, grad_up_low, up_full, preferred_element_type=jnp.float32
        )
        running = running.at[token_rows].add(grad_picked.reshape(turn_slots, model_width))
        shard_grads = (
            lax.psum_scatter(
                jnp.einsum(
                    PRODUCT_6, picked, grad_gate_low, preferred_element_type=jnp.float32
                ).astype(jnp.bfloat16),
                GROUP,
                scatter_dimension=1,
                tiled=True,
            ).astype(jnp.float32),
            lax.psum_scatter(
                jnp.einsum(
                    PRODUCT_6, picked, grad_up_low, preferred_element_type=jnp.float32
                ).astype(jnp.bfloat16),
                GROUP,
                scatter_dimension=1,
                tiled=True,
            ).astype(jnp.float32),
            lax.psum_scatter(
                jnp.einsum(
                    PRODUCT_7, inner, grad_slot, preferred_element_type=jnp.float32
                ).astype(jnp.bfloat16),
                GROUP,
                scatter_dimension=2,
                tiled=True,
            ).astype(jnp.float32),
        )
        return (running, shard_grads)

    grad_second_part, stacked_grads = lax.scan(
        backward_turn, jnp.zeros((row_count, model_width), jnp.float32), turn_ids
    )
    grad_gate_out = stacked_grads[0].reshape(gate_weight.shape)
    grad_up_out = stacked_grads[1].reshape(up_weight.shape)
    grad_down_out = stacked_grads[2].reshape(down_weight.shape)
    grad_second = lax.psum(grad_second_part.astype(jnp.bfloat16), TENSOR).astype(jnp.float32)
    grad_hidden_norm, grad_gain_ffn_local = ffn_norm_back(grad_second)
    grad_hidden = upstream + grad_hidden_norm
    grad_hidden_low = grad_hidden.astype(jnp.bfloat16)
    grad_out_local = jnp.einsum(
        "tc,td->cd", attended, grad_hidden_low, preferred_element_type=jnp.float32
    )
    grad_attended = jnp.einsum(
        "td,cd->tc", grad_hidden_low, out_full, preferred_element_type=jnp.float32
    )
    grad_attended = grad_attended.astype(jnp.bfloat16).reshape(
        row_count, kv_heads, group_size, head_size
    )
    grad_query_parts = []
    grad_keys = jnp.zeros(key_heads.shape, jnp.float32)
    grad_values = jnp.zeros(value_heads.shape, jnp.float32)
    for block_number in range(len(block_starts)):
        block_first = block_starts[block_number]
        query_block, scores = block_scores(block_first)
        probs_float = jnp.exp(scores - lse_parts[block_number])
        probs = probs_float.astype(jnp.bfloat16)
        grad_block = grad_attended[block_first : block_first + block_rows]
        grad_probs = jnp.einsum(
            PRODUCT_0, grad_block, value_heads, preferred_element_type=jnp.float32
        )
        inner_sum = jnp.sum(grad_probs * probs_float, axis=-1, keepdims=True)
        grad_scores = (score_scale * (probs_float * (grad_probs - inner_sum))).astype(jnp.bfloat16)
        grad_query_parts.append(
            jnp.einsum(PRODUCT_1, grad_scores, key_heads, preferred_element_type=jnp.float32)
        )
        grad_keys = grad_keys + jnp.einsum(
            PRODUCT_8, grad_scores, query_block, preferred_element_type=jnp.float32
        )
        grad_values = grad_values + jnp.einsum(
            PRODUCT_8, probs, grad_block, preferred_element_type=jnp.float32
        )
    grad_key_own, grad_value_own = (
        lax.psum_scatter(
            grad_keys.astype(jnp.bfloat16), CONTEXT, scatter_dimension=0, tiled=True
        ).astype(jnp.float32),
        lax.psum_scatter(
            grad_values.astype(jnp.bfloat16), CONTEXT, scatter_dimension=0, tiled=True
        ).astype(jnp.float32),
    )
    grad_query_all = jnp.concatenate(grad_query_parts, axis=0).reshape(row_count, -1, head_size)
    grad_query_lin = rope_query_back(grad_query_all)[0].astype(jnp.bfloat16).reshape(row_count, -1)
    grad_key_lin = rope_key_back(grad_key_own)[0].astype(jnp.bfloat16).reshape(row_count, -1)
    grad_value_low = grad_value_own.astype(jnp.bfloat16).reshape(row_count, -1)
    grad_first_part = jnp.einsum(
        "tc,dc->td", grad_query_lin, query_full, preferred_element_type=jnp.float32
    )
    grad_first_part = grad_first_part + jnp.einsum(
        "tc,dc->td", grad_key_lin, key_full, preferred_element_type=jnp.float32
    )
    grad_first_part = grad_first_part + jnp.einsum(
        "tc,dc->td", grad_value_low, value_full, preferred_element_type=jnp.float32
    )
    grad_first = lax.psum(grad_first_part.astype(jnp.bfloat16), TENSOR).astype(jnp.float32)
    grad_input_norm, grad_gain_attn_local = attn_norm_back(grad_first)
    grad_input = (grad_hidden + grad_input_norm).astype(jnp.bfloat16)
    grad_query_local = jnp.einsum(
        "td,tc->dc", first_normalized, grad_query_lin, preferred_element_type=jnp.float32
    )
    grad_key_local = jnp.einsum(
        "td,tc->dc", first_normalized, grad_key_lin, preferred_element_type=jnp.float32
    )
    grad_value_local = jnp.einsum(
        "td,tc->dc", first_normalized, grad_value_low, preferred_element_type=jnp.float32
    )
    reduced = (
        lax.psum_scatter(
            grad_gain_attn_local.astype(jnp.bfloat16),
            GROUP,
            scatter_dimension=0,
            tiled=True,
        ).astype(jnp.float32),
        lax.psum_scatter(
            grad_query_local.astype(jnp.bfloat16),
            GROUP,
            scatter_dimension=0,
            tiled=True,
        ).astype(jnp.float32),
        lax.psum_scatter(
            grad_key_local.astype(jnp.bfloat16),
            GROUP,
            scatter_dimension=0,
            tiled=True,
        ).astype(jnp.float32),
        lax.psum_scatter(
            grad_value_local.astype(jnp.bfloat16),
            GROUP,
            scatter_dimension=0,
            tiled=True,
        ).astype(jnp.float32),
        lax.psum_scatter(
            grad_out_local.astype(jnp.bfloat16),
            GROUP,
            scatter_dimension=1,
            tiled=True,
        ).astype(jnp.float32),
        lax.psum_scatter(
            grad_gain_ffn_local.astype(jnp.bfloat16),
            GROUP,
            scatter_dimension=0,
            tiled=True,
        ).astype(jnp.float32),
    )
    return (
        output,
        grad_input,
        reduced[0],
        reduced[1],
        reduced[2],
        reduced[3],
        reduced[4],
        reduced[5],
        grad_gate_out,
        grad_up_out,
        grad_down_out,
    )


F32 = jnp.float32
BF16 = jnp.bfloat16
LAST_LAST = (((1,), (1,)), ((), ()))
FIRST_FIRST = (((0,), (0,)), ((), ()))


def weight_copies(own_hbm, other_hbm, weights, sems):
    sources, _, rows, lanes = own_hbm.shape
    units = lanes // 3
    return [
        pltpu.make_async_copy(
            half_hbm.at[source, :, :, pl.ds(part * units, units)],
            weights.at[
                :, pl.ds(source * rows, rows), pl.ds((2 * part + half) * units, units)
            ],
            sems.at[source, half, part],
        )
        for source in range(sources)
        for half, half_hbm in enumerate((own_hbm, other_hbm))
        for part in range(3)
    ]


def project(tokens, cotangent, weights):
    hidden_units = weights.shape[1] // 3
    gate_up = jnp.dot(tokens, weights[:, : 2 * hidden_units], preferred_element_type=F32)
    grad_inner = jnp.dot(cotangent, weights[:, 2 * hidden_units :], preferred_element_type=F32)
    return gate_up, grad_inner


def activate(gate_up, grad_inner, share):
    hidden_units = grad_inner.shape[1]
    gate, up = gate_up[:, :hidden_units], gate_up[:, hidden_units:]
    sigmoid = 1.0 / (1.0 + jnp.exp(-gate))
    silu = gate * sigmoid
    grad_inner = grad_inner * share
    inner = silu * up * share
    grad_gate = grad_inner * up * (sigmoid * (1.0 + gate * (1.0 - sigmoid)))
    grad_up = grad_inner * silu
    return inner.astype(BF16), grad_gate.astype(BF16), grad_up.astype(BF16)


MESH_ID = pl.DeviceIdType.MESH


class Place:
    def __init__(self, line):
        self.line = line
        self.z, self.y = lax.axis_index(SHARD), lax.axis_index(CONTEXT)
        self.t = lax.axis_index(TENSOR)
        self.sibling = (self.z, self.y, self.t + 1 - 2 * (self.t % 2))
        self.partner = (self.z, 1 - self.y, self.t)
        self.across = (self.z, self.y, (self.t + 2) % 4)

    def beside(self, side):
        return (self.z + side, self.y, self.t)

    def inside(self, at):
        return (at >= 0) & (at < self.line)

    def near(self, rank):
        z, line = self.z, self.line
        half = z // 2
        mirrored = z * (1 - half) + (line - 1 - z) * half
        far = rank // 2
        place = (1 - far) * (mirrored + rank - 2 * mirrored * rank) + far * rank
        return place * (1 - half) + (line - 1 - place) * half

    def block(self, order, step):
        rank, across = order[0]
        for number, (later_rank, later_across) in enumerate(order[1:], 1):
            rank = jnp.where(step == number, later_rank, rank)
            across = jnp.where(step == number, later_across, across)
        column = self.y + across - 2 * self.y * across
        return self.near(rank) * 2 + column

    def meet(self):
        z, line = self.z, self.line
        barrier = pltpu.get_barrier_semaphore()
        for device in (self.sibling, self.partner, self.across):
            pl.semaphore_signal(barrier, inc=1, device_id=device, device_id_type=MESH_ID)
        for side in (-1, 1):

            @pl.when(self.inside(z + side))
            def _():
                pl.semaphore_signal(
                    barrier, inc=1, device_id=self.beside(side), device_id_type=MESH_ID
                )

        below, above = (z + line - 1) // line, (2 * line - 2 - z) // line
        pl.semaphore_wait(barrier, 3 + below + above)


def remote(source, target, send, recv, device):
    return pltpu.make_async_remote_copy(
        src_ref=source,
        dst_ref=target,
        send_sem=send,
        recv_sem=recv,
        device_id=device,
        device_id_type=MESH_ID,
    )


class Gather:
    order = ((0, 0), (1, 0), (0, 1), (2, 0), (1, 1), (3, 0), (2, 1), (3, 1))
    rounds = (0, 2, 4)
    crossings = (1, 3, 5, 6)

    def __init__(self, place, tokens, sems):
        self.place, self.tokens = place, tokens
        self.recv, self.along, self.across, self.cores = sems

    def line_copy(self, at, side):
        here, tokens = at * 2 + self.place.y, self.tokens
        return remote(
            tokens.at[here, 0],
            tokens.at[here, 0],
            self.along.at[at, (side + 1) // 2],
            self.recv.at[here, 0],
            self.place.beside(side),
        )

    def pair_copy(self, at, column):
        here, tokens = at * 2 + column, self.tokens
        return remote(
            tokens.at[here, 0],
            tokens.at[here, 0],
            self.across.at[at],
            self.recv.at[here, 0],
            self.place.partner,
        )

    def core_copy(self, here):
        tokens = self.tokens
        return remote(
            tokens.at[here, 0],
            tokens.at[here, 1],
            self.cores.at[here],
            self.recv.at[here, 1],
            self.place.sibling,
        )

    def start(self):
        place = self.place
        for side in (-1, 1):
            pl.when(place.inside(place.z + side))(lambda: self.line_copy(place.z, side).start())
        self.pair_copy(place.z, place.y).start()
        self.core_copy(place.z * 2 + place.y).start()

    def came_along(self, at, side):
        place = self.place
        self.line_copy(at, -side).wait_recv()
        pl.when(place.inside(place.z - side))(lambda: self.line_copy(at, -side).start())
        self.pair_copy(at, place.y).start()
        self.core_copy(at * 2 + place.y).start()

    def came_across(self, at):
        column = 1 - self.place.y
        self.pair_copy(at, column).wait_recv()
        self.core_copy(at * 2 + column).start()

    def tick(self, number):
        place = self.place
        for distance, when in enumerate(self.rounds, 1):

            @pl.when(number == when)
            def _():
                for side in (-1, 1):
                    at = place.z + side * distance
                    pl.when(place.inside(at))(partial(self.came_along, at, side))

        for distance, when in enumerate(self.crossings):

            @pl.when(number == when)
            def _():
                for side in (-1, 1) if distance else (1,):
                    at = place.z + side * distance
                    pl.when(place.inside(at))(partial(self.came_across, at))

    def finish(self):
        place = self.place
        for side in (-1, 1):
            for distance in range(place.line):
                at = place.z - side * distance

                @pl.when(place.inside(at) & place.inside(place.z + side))
                def _():
                    self.line_copy(at, side).wait_send()

        for at in range(place.line):
            self.pair_copy(at, place.y).wait_send()
        for here in range(2 * place.line):
            self.core_copy(here).wait_send()


class Reduce:
    order = ((3, 1), (3, 0), (2, 1), (2, 0), (1, 1), (1, 0), (0, 1), (0, 0))

    def __init__(self, place, arrays, terms, term_sems, sums, base, sems):
        self.place, self.terms, self.term_sems = place, terms, term_sems
        self.sums, self.base = sums, base
        self.parts, self.from_core, self.from_pair, self.from_line = arrays
        self.core_send, self.core_recv, self.pair_send, self.pair_recv = sems[:4]
        self.line_send, self.line_recv = sems[4:]

    def core_copy(self, here, source):
        return remote(
            source,
            self.from_core.at[here],
            self.core_send.at[here],
            self.core_recv.at[here],
            self.place.sibling,
        )

    def core_arrived(self, here):
        self.core_copy(here, self.from_core.at[here]).wait_recv()

    def pair_copy(self, at, slot):
        return remote(
            self.sums.at[self.base + slot],
            self.from_pair.at[at],
            self.pair_send.at[at],
            self.pair_recv.at[at],
            self.place.partner,
        )

    def line_copy(self, at, side, distance):
        slot = self.place.line if distance == 1 and side == 1 else at
        return remote(
            self.sums.at[self.base + 2 + (side + 1) // 2],
            self.from_line.at[slot],
            self.line_send.at[at],
            self.line_recv.at[slot],
            self.place.beside(side),
        )

    def add_up(self, sources, slot):
        terms = self.terms
        copies = [
            pltpu.make_async_copy(source, terms.at[i], self.term_sems.at[i])
            for i, (source, _) in enumerate(sources)
        ]
        for copy, (_, there) in zip(copies, sources):
            if there is None:
                copy.start()
            else:
                pl.when(there)(copy.start)
        for i, (copy, (_, there)) in enumerate(zip(copies, sources)):
            if there is None:
                copy.wait()
            else:
                pl.when(there)(copy.wait)

                @pl.when(jnp.logical_not(there))
                def _():
                    terms[i] = jnp.zeros_like(terms[i])

        tile = 16

        @pl.loop(0, terms.shape[1] // tile)
        def _(number):
            here = pl.ds(pl.multiple_of(number * tile, tile), tile)
            total = terms[0, here, :].astype(F32)
            for i in range(1, len(sources)):
                total += terms[i, here, :].astype(F32)
            self.sums[self.base + slot, here, :] = total.astype(BF16)

    def cross(self, rank):
        place = self.place
        at = place.near(rank)
        here = at * 2 + 1 - place.y
        slot = rank % 2
        if rank + 2 < place.line:
            self.pair_copy(place.near(rank + 2), slot).wait_send()
        self.core_arrived(here)
        self.add_up([(self.parts.at[here], None), (self.from_core.at[here], None)], slot)
        self.pair_copy(at, slot).start()

    def advance(self, distance):
        place = self.place
        for side in (-1, 1):
            at = place.z + side * distance
            here = at * 2 + place.y
            farther = place.inside(place.z - side)
            if distance + 1 < place.line:

                @pl.when(place.inside(at + side))
                def _():
                    self.line_copy(at + side, side, distance + 1).wait_send()

            @pl.when(place.inside(at))
            def _():
                self.core_arrived(here)
                self.pair_copy(at, 0).wait_recv()
                sources = [
                    (self.parts.at[here], None),
                    (self.from_core.at[here], None),
                    (self.from_pair.at[at], None),
                ]
                if distance + 1 < place.line:

                    @pl.when(farther)
                    def _():
                        self.line_copy(at, side, distance + 1).wait_recv()

                    sources.append((self.from_line.at[at], farther))
                self.add_up(sources, 2 + (side + 1) // 2)
                self.line_copy(at, side, distance).start()

    def tick(self, number, late):
        line = self.place.line
        for rank in range(line):
            when = 2 * (line - rank) - 1
            pl.when(number == when)(partial(self.cross, rank))
            if rank + 1 < line:
                pl.when(number == when + late)(partial(self.advance, rank + 1))

    def finish(self, result, sem):
        place = self.place
        z, line = place.z, place.line
        here = z * 2 + place.y
        self.core_arrived(here)
        self.pair_copy(z, 0).wait_recv()
        for side in (-1, 1):
            pl.when(place.inside(z + side))(lambda: self.line_copy(z, -side, 1).wait_recv())
        for rank in (1, 0):
            self.pair_copy(place.near(rank), rank % 2).wait_send()
        self.add_up(
            [
                (self.parts.at[here], None),
                (self.from_core.at[here], None),
                (self.from_pair.at[z], None),
                (self.from_line.at[z], place.inside(z + 1)),
                (self.from_line.at[line], place.inside(z - 1)),
            ],
            0,
        )
        copy = pltpu.make_async_copy(self.sums.at[self.base], result, sem)
        copy.start()
        copy.wait()
        for side in (-1, 1):

            @pl.when(place.inside(z + side))
            def _():
                self.line_copy(z + side, side, 1).wait_send()


def expert_kernel(*refs, line, chunk, gathers):
    refs = list(refs)

    def take(count):
        taken = refs[:count]
        del refs[:count]
        return taken[0] if count == 1 else taken

    tokens_in, cotangent_own, cotangent_other, shares_ref, own_hbm, other_hbm = take(6)
    exchanged = take(1)
    if not gathers:
        before = take(1)
        grad_piece, out_piece, grad_own, grad_other, received = take(5)
        grad_arrays, out_arrays = take(4), take(4)
        tokens_hbm = tokens_in
    else:
        parts_hbm, grad_own, grad_other, tokens_hbm, received = take(5)
    weights, grads, tokens_buf, cotangent_buf, inner_low, grad_low = take(6)
    both_buf, stage, load_sems, store_sems, row_sems, part_sems, exchange_sems = take(7)

    expert_count, model_width, all_units = weights.shape
    hidden_units = all_units // 3
    units = hidden_units // 2
    steps = 2 * line
    rows = tokens_hbm.shape[2]
    place = Place(line)
    first_rows, second_rows = pl.ds(0, rows), pl.ds(rows, rows)
    if gathers:
        mover = Gather(place, tokens_hbm, take(4))
    else:
        before_buf, terms, sums, term_sems = take(4)
        movers = [
            Reduce(place, arrays, terms, term_sems, sums, 4 * number, take(6))
            for number, arrays in enumerate((grad_arrays, out_arrays))
        ]
    order = mover.order if gathers else Reduce.order

    place.meet()
    exchange = remote(
        exchanged, received, exchange_sems.at[0], exchange_sems.at[1], place.across
    )
    exchange.start()
    if gathers:
        own_block = place.z * 2 + place.y
        own_copy = pltpu.make_async_copy(tokens_in, tokens_hbm.at[own_block, 0], row_sems.at[0, 0])
        own_copy.start()
        own_copy.wait()
        mover.start()
    weight_loads = weight_copies(own_hbm, other_hbm, weights, load_sems)
    for copy in weight_loads:
        copy.start()
    grads[...] = jnp.zeros_like(grads)

    def row_copies(step, slot):
        here = place.block(order, step)
        lanes = pl.ds(0, model_width)
        pairs = [
            (tokens_hbm.at[here, 0], tokens_buf.at[slot, first_rows, :]),
            (tokens_hbm.at[here, 1], tokens_buf.at[slot, second_rows, :]),
            (cotangent_own.at[here, :, lanes], cotangent_buf.at[slot, first_rows, :]),
            (cotangent_other.at[here, :, lanes], cotangent_buf.at[slot, second_rows, :]),
        ]
        if not gathers:
            pairs.append((before.at[here], before_buf.at[slot]))
        return [
            pltpu.make_async_copy(source, target, row_sems.at[slot, i])
            for i, (source, target) in enumerate(pairs)
        ]

    def load_rows(step, slot):
        if gathers:
            mover.core_copy(place.block(order, step)).wait_recv()
        for copy in row_copies(step, slot):
            copy.start()

    load_rows(0, 0)
    for copy in weight_loads:
        copy.wait()

    halves = [pl.ds(number * model_width, model_width) for number in range(2)]

    def core_copies(step, slot):
        here = place.block(order, step)
        return [
            mover.core_copy(here, both_buf.at[slot, second_rows, lanes])
            for mover, lanes in zip(movers, halves)
        ]

    def part_copies(step, slot):
        here = place.block(order, step)
        if gathers:
            pairs = [(both_buf.at[slot], parts_hbm.at[here])]
        else:
            pairs = [
                (both_buf.at[slot, first_rows, lanes], mover.parts.at[here])
                for mover, lanes in zip(movers, halves)
            ]
        return [
            pltpu.make_async_copy(source, target, part_sems.at[slot, i])
            for i, (source, target) in enumerate(pairs)
        ]

    @pl.loop(0, steps)
    def _(step):
        slot = step % 2
        for copy in row_copies(step, slot):
            copy.wait()
        shares = shares_ref[place.block(order, step)]
        lane = lax.broadcasted_iota(jnp.int32, shares.shape, 1)

        def run(expert, gate_up, grad_inner):
            share = jnp.sum(jnp.where(lane == expert, shares, 0.0), axis=1, keepdims=True)
            inner, grad_gate, grad_up = activate(gate_up, grad_inner, share)
            inner_low[expert] = inner
            grad_low[expert, :, :hidden_units] = grad_gate
            grad_low[expert, :, hidden_units:] = grad_up

        def weight_grads(expert):
            grads[expert, :, : 2 * hidden_units] += lax.dot_general(
                tokens_buf[slot], grad_low[expert], FIRST_FIRST, preferred_element_type=F32
            )
            grads[expert, :, 2 * hidden_units :] += lax.dot_general(
                cotangent_buf[slot], inner_low[expert], FIRST_FIRST, preferred_element_type=F32
            )

        results = project(tokens_buf[slot], cotangent_buf[slot], weights[0])
        for expert in range(expert_count):
            run(expert, *results)
            if expert + 1 < expert_count:
                results = project(tokens_buf[slot], cotangent_buf[slot], weights[expert + 1])
            weight_grads(expert)

        @pl.when(step >= 1)
        def _():
            for copy in part_copies(step - 1, 1 - slot):
                copy.wait()

        if gathers:
            mover.tick(step)
        else:
            for late, reducer in enumerate(movers):
                reducer.tick(step, late)

            @pl.when(step >= 2)
            def _():
                for copy in core_copies(step - 2, slot):
                    copy.wait_send()

        @pl.loop(0, model_width // chunk)
        def _(number):
            @pl.when((number == 1) & (step + 1 < steps))
            def _():
                load_rows(step + 1, 1 - slot)

            cols = pl.ds(pl.multiple_of(number * chunk, chunk), chunk)

            def total_of(lows, lanes, target):
                if gathers:
                    total = jnp.zeros((2 * rows, chunk), F32)
                else:
                    total = before_buf[slot, :, target].astype(F32)
                for expert in range(expert_count):
                    total += lax.dot_general(
                        lows[expert],
                        weights[expert, cols, lanes],
                        LAST_LAST,
                        preferred_element_type=F32,
                    )
                both_buf[slot, :, target] = total.astype(BF16)

            beyond = pl.ds(pl.multiple_of(model_width + number * chunk, chunk), chunk)
            total_of(grad_low, pl.ds(0, 2 * hidden_units), cols)
            total_of(inner_low, pl.ds(2 * hidden_units, hidden_units), beyond)

        if not gathers:
            for copy in core_copies(step, slot):
                copy.start()
        for copy in part_copies(step, slot):
            copy.start()

    last = (steps - 1) % 2
    for copy in part_copies(steps - 1, last):
        copy.wait()
    if not gathers:
        for copy in core_copies(steps - 2, 1 - last) + core_copies(steps - 1, last):
            copy.wait_send()
        movers[1].advance(1)

    sources, _, slice_rows, _ = own_hbm.shape

    def grad_copy(expert, source, half, slot):
        return pltpu.make_async_copy(
            stage.at[slot, half],
            (grad_own, grad_other)[half].at[source, expert],
            store_sems.at[slot, half],
        )

    @pl.loop(0, expert_count * sources)
    def _(number):
        expert, source = number // sources, number % sources
        slot = number % 2

        @pl.when(number >= 2)
        def _():
            for half in range(2):
                grad_copy(expert, source, half, slot).wait()

        here = pl.ds(pl.multiple_of(source * slice_rows, slice_rows), slice_rows)
        for half in range(2):
            for part in range(3):
                first = (2 * part + half) * units
                stage[slot, half, :, part * units : (part + 1) * units] = grads[
                    expert, here, first : first + units
                ].astype(BF16)
            grad_copy(expert, source, half, slot).start()

    for slot in range(2):
        for half in range(2):
            grad_copy(0, 0, half, slot).wait()

    exchange.wait()
    if gathers:
        mover.finish()
    else:
        for number, result in enumerate((grad_piece, out_piece)):
            movers[number].finish(result, row_sems.at[0, number])


def expert_call(operands, own, shares, line, rows, model_width, gathers, collective_id, chunk=512):
    sources, expert_count, slice_rows, lanes = own.shape
    hidden_units = 2 * lanes // 3
    blocks = 2 * line
    in_place = pl.BlockSpec(memory_space=pl.ANY)
    dma = pltpu.SemaphoreType.DMA
    flops = 2 * blocks * 2 * rows * model_width * expert_count * hidden_units * 9

    def low(*shape):
        return jax.ShapeDtypeStruct(shape, BF16)

    if gathers:
        out_shape = [
            low(blocks, 2 * rows, 2 * model_width),
            low(*own.shape),
            low(*own.shape),
            low(blocks, 2, rows, model_width),
            low(*operands[6].shape),
        ]
        own_scratch = [dma((blocks, 2)), dma((line, 2)), dma((line,)), dma((blocks,))]
    else:
        out_shape = [
            low(rows, model_width),
            low(rows, model_width),
            low(*own.shape),
            low(*own.shape),
            low(*operands[6].shape),
        ]
        out_shape += 2 * [
            low(blocks, rows, model_width),
            low(blocks, rows, model_width),
            low(line, rows, model_width),
            low(line + 1, rows, model_width),
        ]
        own_scratch = [
            pltpu.VMEM((2, 2 * rows, 2 * model_width), BF16),
            pltpu.VMEM((5, rows, model_width), BF16),
            pltpu.VMEM((8, rows, model_width), BF16),
            dma((5,)),
        ]
        own_scratch += 2 * [
            dma((blocks,)),
            dma((blocks,)),
            dma((line,)),
            dma((line,)),
            dma((line,)),
            dma((line + 1,)),
        ]
    in_specs = [in_place] * len(operands)
    in_specs[3] = pl.BlockSpec(memory_space=pltpu.VMEM)
    results = pl.pallas_call(
        partial(expert_kernel, line=line, chunk=chunk, gathers=gathers),
        in_specs=in_specs,
        out_specs=[in_place] * len(out_shape),
        out_shape=out_shape,
        scratch_shapes=[
            pltpu.VMEM((expert_count, model_width, 3 * hidden_units), BF16),
            pltpu.VMEM((expert_count, model_width, 3 * hidden_units), F32),
            pltpu.VMEM((2, 2 * rows, model_width), BF16),
            pltpu.VMEM((2, 2 * rows, model_width), BF16),
            pltpu.VMEM((expert_count, 2 * rows, hidden_units), BF16),
            pltpu.VMEM((expert_count, 2 * rows, 2 * hidden_units), BF16),
            pltpu.VMEM((2, 2 * rows, 2 * model_width), BF16),
            pltpu.VMEM((2, 2, slice_rows, lanes), BF16),
            dma((sources, 2, 3)),
            dma((2, 2)),
            dma((2, 5)),
            dma((2, 2)),
            dma((2,)),
        ]
        + own_scratch,
        compiler_params=pltpu.CompilerParams(
            vmem_limit_bytes=60 * 2**20, collective_id=collective_id, has_side_effects=True
        ),
        cost_estimate=pl.CostEstimate(
            flops=flops, bytes_accessed=80 * 2**20, transcendentals=0
        ),
    )(*operands)
    return results[:5]


def experts_gathering(piece, cotangents, shares, own, other, exchanged, line):
    rows, model_width = piece.shape
    operands = (piece, *cotangents, shares, own, other, exchanged)
    return expert_call(operands, own, shares, line, rows, model_width, True, 1)


def experts_reducing(
    tokens, cotangents, shares, own, other, exchanged, parts, line
):
    _, _, rows, model_width = tokens.shape
    operands = (tokens, *cotangents, shares, own, other, exchanged, parts)
    return expert_call(operands, own, shares, line, rows, model_width, False, 2)


def attention_rows(values, kv_head, group_size):
    first = kv_head * group_size
    return jnp.concatenate(
        [values[:, (first + r) * HEAD_DIM : (first + r + 1) * HEAD_DIM] for r in range(group_size)],
        axis=0,
    )


def quarter_turn(values):
    half = HEAD_DIM // 2
    return jnp.concatenate([-values[:, half:], values[:, :half]], axis=1)


def window_mask(start, doc_start_ref, first_ref, block_rows, window):
    key_index = start + lax.broadcasted_iota(jnp.int32, (block_rows, window), 1)
    query_index = (
        first_ref[0]
        + pl.program_id(0) * block_rows
        + lax.broadcasted_iota(jnp.int32, (block_rows, window), 0)
    )
    return (key_index <= query_index) & (key_index >= doc_start_ref[...])


def window_start(first_ref, block_rows, window):
    end = first_ref[0] + (pl.program_id(0) + 1) * block_rows
    return pl.multiple_of(jnp.maximum(end - window, 0), block_rows)


def attention_forward_kernel(
    first_ref, query_ref, key_value_ref, doc_start_ref, attended_ref, lse_ref, *, group_size, window
):
    block_rows = query_ref.shape[0]
    kv_heads = key_value_ref.shape[1] // (2 * HEAD_DIM)
    start = window_start(first_ref, block_rows, window)
    allowed = window_mask(start, doc_start_ref, first_ref, block_rows, window)
    bias = jnp.where(allowed, 0.0, -1e30)
    bias = jnp.concatenate([bias] * group_size, axis=0)
    keys_values = key_value_ref[pl.ds(start, window), :]
    queries = query_ref[...]
    parts = []
    for g in range(kv_heads):
        keys = keys_values[:, g * HEAD_DIM : (g + 1) * HEAD_DIM]
        values = keys_values[:, (kv_heads + g) * HEAD_DIM : (kv_heads + g + 1) * HEAD_DIM]
        scores = lax.dot_general(
            attention_rows(queries, g, group_size), keys, LAST_LAST, preferred_element_type=F32
        )
        scores = scores * HEAD_DIM**-0.5 + bias
        row_max = jnp.max(scores, axis=1, keepdims=True)
        exponent = jnp.exp(scores - row_max)
        total = jnp.sum(exponent, axis=1, keepdims=True)
        probs = (exponent * (1.0 / total)).astype(BF16)
        mixed = jnp.dot(probs, values, preferred_element_type=F32).astype(BF16)
        lse_ref[0, g] = row_max + jnp.log(total)
        parts += [mixed[r * block_rows : (r + 1) * block_rows] for r in range(group_size)]
    attended_ref[...] = jnp.concatenate(parts, axis=1)


def attention_backward_kernel(
    first_ref,
    query_ref,
    key_value_ref,
    doc_start_ref,
    lse_ref,
    grad_ref,
    turns_ref,
    query_turns_ref,
    grad_query_ref,
    grad_key_value_ref,
    grad_keys,
    grad_values,
    *,
    group_size,
    window,
    steps,
):
    step = pl.program_id(0)
    block_rows = query_ref.shape[0]
    kv_heads = key_value_ref.shape[1] // (2 * HEAD_DIM)

    @pl.when(step == 0)
    def _():
        grad_keys[...] = jnp.zeros_like(grad_keys)
        grad_values[...] = jnp.zeros_like(grad_values)

    start = window_start(first_ref, block_rows, window)
    allowed = window_mask(start, doc_start_ref, first_ref, block_rows, window)
    bias = jnp.where(allowed, 0.0, -1e30)
    bias = jnp.concatenate([bias] * group_size, axis=0)
    rows = pl.ds(start, window)
    keys_values = key_value_ref[rows, :]
    queries = query_ref[...]
    grads = grad_ref[...]
    query_turns = jnp.concatenate([query_turns_ref[...]] * group_size, axis=0)
    parts = []
    for g in range(kv_heads):
        keys = keys_values[:, g * HEAD_DIM : (g + 1) * HEAD_DIM]
        values = keys_values[:, (kv_heads + g) * HEAD_DIM : (kv_heads + g + 1) * HEAD_DIM]
        query_rows = attention_rows(queries, g, group_size)
        grad_rows = attention_rows(grads, g, group_size)
        scores = lax.dot_general(query_rows, keys, LAST_LAST, preferred_element_type=F32)
        probs = jnp.exp(scores * HEAD_DIM**-0.5 + bias - lse_ref[0, g])
        grad_probs = lax.dot_general(grad_rows, values, LAST_LAST, preferred_element_type=F32)
        inner = jnp.sum(grad_probs * probs, axis=1, keepdims=True)
        grad_scores = (HEAD_DIM**-0.5 * (probs * (grad_probs - inner))).astype(BF16)
        grad_values[g, rows, :] += lax.dot_general(
            probs.astype(BF16), grad_rows, FIRST_FIRST, preferred_element_type=F32
        )
        both_queries = jnp.concatenate([query_rows, quarter_turn(query_rows)], axis=1)
        grad_keys[g, rows, :] += lax.dot_general(
            grad_scores, both_queries, FIRST_FIRST, preferred_element_type=F32
        )
        both_keys = jnp.concatenate([keys, quarter_turn(keys)], axis=1)
        turned = jnp.dot(grad_scores, both_keys, preferred_element_type=F32) * query_turns
        grad_query = (turned[:, :HEAD_DIM] + turned[:, HEAD_DIM:]).astype(BF16)
        parts += [grad_query[r * block_rows : (r + 1) * block_rows] for r in range(group_size)]
    grad_query_ref[...] = jnp.concatenate(parts, axis=1)

    @pl.when(step == steps - 1)
    def _():
        key_parts, value_parts = [], []
        for g in range(kv_heads):
            turned = grad_keys[g] * turns_ref[...]
            key_parts.append((turned[:, :HEAD_DIM] + turned[:, HEAD_DIM:]).astype(BF16))
            value_parts.append(grad_values[g].astype(BF16))
        grad_key_value_ref[...] = jnp.concatenate(key_parts + value_parts, axis=1)


def attention_specs(queries, keys_values, block_rows):
    return dict(
        smem=pl.BlockSpec(memory_space=pltpu.SMEM),
        rows=pl.BlockSpec((block_rows, queries.shape[1]), lambda i: (i, 0)),
        whole=pl.BlockSpec(keys_values.shape, lambda i: (0, 0)),
        column=pl.BlockSpec((block_rows, 1), lambda i: (i, 0)),
    )


def attention_forward(first, queries, keys_values, doc_start, block_rows=256, reach=1024):
    row_count, query_cols = queries.shape
    kv_heads = keys_values.shape[1] // (2 * HEAD_DIM)
    group_size = query_cols // HEAD_DIM // kv_heads
    steps = row_count // block_rows
    window = min(reach + block_rows, keys_values.shape[0])
    specs = attention_specs(queries, keys_values, block_rows)
    stacked = group_size * block_rows
    return pl.pallas_call(
        partial(attention_forward_kernel, group_size=group_size, window=window),
        grid=(steps,),
        in_specs=[specs["smem"], specs["rows"], specs["whole"], specs["column"]],
        out_specs=[
            specs["rows"],
            pl.BlockSpec((1, kv_heads, stacked, 1), lambda i: (i, 0, 0, 0)),
        ],
        out_shape=[
            jax.ShapeDtypeStruct(queries.shape, BF16),
            jax.ShapeDtypeStruct((steps, kv_heads, stacked, 1), F32),
        ],
        compiler_params=pltpu.CompilerParams(vmem_limit_bytes=48 * 2**20),
        cost_estimate=pl.CostEstimate(
            flops=4 * row_count * window * query_cols * 8, bytes_accessed=2**22, transcendentals=0
        ),
    )(first, queries, keys_values, doc_start)


def attention_backward(
    first, queries, keys_values, doc_start, lse, grads, turns, query_turns, block_rows=256, reach=1024
):
    row_count, query_cols = queries.shape
    kv_heads = keys_values.shape[1] // (2 * HEAD_DIM)
    group_size = query_cols // HEAD_DIM // kv_heads
    steps = row_count // block_rows
    window = min(reach + block_rows, keys_values.shape[0])
    specs = attention_specs(queries, keys_values, block_rows)
    stacked = group_size * block_rows
    return pl.pallas_call(
        partial(attention_backward_kernel, group_size=group_size, window=window, steps=steps),
        grid=(steps,),
        in_specs=[
            specs["smem"],
            specs["rows"],
            specs["whole"],
            specs["column"],
            pl.BlockSpec((1, kv_heads, stacked, 1), lambda i: (i, 0, 0, 0)),
            specs["rows"],
            pl.BlockSpec(turns.shape, lambda i: (0, 0)),
            pl.BlockSpec((block_rows, turns.shape[1]), lambda i: (i, 0)),
        ],
        out_specs=[specs["rows"], specs["whole"]],
        out_shape=[
            jax.ShapeDtypeStruct(queries.shape, BF16),
            jax.ShapeDtypeStruct(keys_values.shape, BF16),
        ],
        scratch_shapes=[
            pltpu.VMEM((kv_heads, keys_values.shape[0], 2 * HEAD_DIM), F32),
            pltpu.VMEM((kv_heads, keys_values.shape[0], HEAD_DIM), F32),
        ],
        compiler_params=pltpu.CompilerParams(vmem_limit_bytes=48 * 2**20),
        cost_estimate=pl.CostEstimate(
            flops=10 * row_count * window * query_cols * 8, bytes_accessed=2**23, transcendentals=0
        ),
    )(first, queries, keys_values, doc_start, lse, grads, turns, query_turns)


def rotation_tables(positions):
    half_dim = HEAD_DIM // 2
    frequencies = 10000.0 ** (-2.0 * jnp.arange(half_dim, dtype=F32) / HEAD_DIM)
    angles = positions.astype(F32)[:, None] * frequencies[None, :]
    cosine, sine = jnp.cos(angles), jnp.sin(angles)
    return jnp.concatenate([cosine, cosine, -sine, -sine], axis=1)


def turned_columns(weight):
    rows, cols = weight.shape
    halves = weight.reshape(rows, cols // HEAD_DIM, 2, HEAD_DIM // 2)
    return jnp.stack([-halves[:, :, 1], halves[:, :, 0]], axis=2).reshape(rows, cols)


def expert_plan(
    residual_in,
    gain_attn,
    query_weight,
    key_projection_weight,
    value_projection_weight,
    out_weight,
    gain_ffn,
    gate_weight,
    up_weight,
    down_weight,
    segments,
    routes,
    shares,
    cotangent,
    *,
    groups,
    tensor_size,
):
    row_count, model_width = residual_in.shape
    query_cols = query_weight.shape[1]
    kv_cols = key_projection_weight.shape[1]
    expert_count, slice_rows, unit_count = gate_weight.shape
    own_experts = expert_count // groups
    piece_rows = row_count // tensor_size
    first_count = own_experts * 2 // 5
    context_rank = lax.axis_index(CONTEXT)
    tensor_rank = lax.axis_index(TENSOR)
    group_rank = lax.axis_index(SHARD) * lax.axis_size(CONTEXT) + context_rank
    chip_half, core = tensor_rank // 2, tensor_rank % 2
    own_first = context_rank * row_count
    piece_first = tensor_rank * piece_rows
    sibling = [(i, i ^ 1) for i in range(tensor_size)]
    across = [(i, i ^ 2) for i in range(tensor_size)]
    pair = [(0, 1), (1, 0)]

    def own_piece(values):
        return lax.dynamic_slice_in_dim(values, piece_first, piece_rows)

    def pick(values, axis, index):
        return lax.dynamic_index_in_dim(values, index, axis, keepdims=False)

    def sum_over_tensor(parts):
        parts = parts.astype(BF16).reshape(2, 2, piece_rows, -1)
        received = lax.ppermute(pick(parts, 1, 1 - core), TENSOR, sibling)
        half = pick(parts, 1, core).astype(F32) + received.astype(F32)
        received = lax.ppermute(pick(half, 0, 1 - chip_half).astype(BF16), TENSOR, across)
        return pick(half, 0, chip_half) + received.astype(F32)

    def gather_over_tensor(piece):
        other = lax.ppermute(piece, TENSOR, across)
        chips = jnp.where(
            chip_half == 0, jnp.concatenate([piece, other]), jnp.concatenate([other, piece])
        ).reshape(2, 1, piece_rows, -1)
        others = lax.ppermute(chips, TENSOR, sibling)
        both = jnp.where(
            core == 0,
            jnp.concatenate([chips, others], axis=1),
            jnp.concatenate([others, chips], axis=1),
        )
        return both.reshape(row_count, -1)

    def padded_columns(*gains):
        columns = jnp.stack(gains, axis=1)
        return jnp.pad(columns, ((0, 0), (0, 128 - len(gains))))

    with jax.named_scope("weights"):
        qkv_full = lax.all_gather(
            jnp.concatenate(
                [
                    query_weight,
                    key_projection_weight,
                    value_projection_weight,
                    out_weight.T,
                    padded_columns(gain_attn, gain_ffn),
                ],
                axis=1,
            ),
            GROUP,
            axis=0,
            tiled=True,
        )
        qkv_cols = query_cols + 2 * kv_cols
        qkv_weight = qkv_full[:, :qkv_cols]
        out_transposed = qkv_full[:, qkv_cols : qkv_cols + query_cols]
        gain_attn_float = qkv_full[:, qkv_cols + query_cols].astype(F32)
        gain_ffn_float = qkv_full[:, qkv_cols + query_cols + 1].astype(F32)
        lanes = 3 * unit_count


        def expert_slices(first, count):
            slices = jnp.concatenate(
                [
                    weight.reshape((groups, own_experts) + weight.shape[1:])[:, first : first + count]
                    for weight in (gate_weight, up_weight, down_weight.transpose(0, 2, 1))
                ],
                axis=3,
            ).reshape(groups * count, slice_rows, lanes)
            owned = lax.all_to_all(slices, GROUP, 0, 0, tiled=True)
            return owned.reshape(groups, count, slice_rows, lanes)

        owned_first = expert_slices(0, first_count)
        owned_second = expert_slices(first_count, own_experts - first_count)

    with jax.named_scope("cotangents"):
        cotangent_piece = own_piece(cotangent)
        spread = jnp.sum(
            jnp.where(
                own_piece(routes)[:, :, None] == jnp.arange(expert_count, dtype=jnp.int32),
                own_piece(shares)[:, :, None],
                0.0,
            ),
            axis=1,
        )
        spread_high = spread.astype(BF16)
        spread_low = (spread - spread_high.astype(F32)).astype(BF16)
        spread_both = jnp.pad(
            jnp.concatenate([spread_high, spread_low], axis=1),
            ((0, 0), (0, 128 - 2 * expert_count)),
        )
        cotangent_own = lax.all_gather(
            jnp.concatenate([cotangent_piece, spread_both], axis=1), GROUP, axis=0, tiled=False
        )

    with jax.named_scope("attention"):
        positions = doc_positions(segments)
        turns = rotation_tables(positions)
        own_turns = lax.dynamic_slice_in_dim(turns, own_first, row_count)
        own_index = own_first + jnp.arange(row_count, dtype=jnp.int32)
        doc_start = own_index - lax.dynamic_slice_in_dim(positions, own_first, row_count)
        input_float = residual_in.astype(F32)
        first_normalized = rms_scale(input_float, gain_attn_float).astype(BF16)
        rotated_cols = query_cols + kv_cols
        projected = jnp.dot(
            first_normalized,
            jnp.concatenate([qkv_weight, turned_columns(qkv_weight[:, :rotated_cols])], axis=1),
            preferred_element_type=F32,
        )
        heads = rotated_cols // HEAD_DIM
        rotated = (
            projected[:, :rotated_cols] * jnp.tile(own_turns[:, :HEAD_DIM], (1, heads))
            - projected[:, qkv_cols:] * jnp.tile(own_turns[:, HEAD_DIM:], (1, heads))
        ).astype(BF16)
        queries = rotated[:, :query_cols]
        own_keys_values = jnp.concatenate(
            [rotated[:, query_cols:], projected[:, rotated_cols:qkv_cols].astype(BF16)], axis=1
        )
        owned_first, own_keys_values = lax.optimization_barrier((owned_first, own_keys_values))
        other_keys_values = lax.ppermute(own_keys_values, CONTEXT, pair)
        keys_values = jnp.where(
            context_rank == 0,
            jnp.concatenate([own_keys_values, other_keys_values]),
            jnp.concatenate([other_keys_values, own_keys_values]),
        )
        others_first = lax.ppermute(owned_first, TENSOR, across)
        first = own_first.reshape(1).astype(jnp.int32)
        attended, lse = attention_forward(first, queries, keys_values, doc_start[:, None])
        attn_part = lax.dot_general(
            attended, out_transposed, LAST_LAST, preferred_element_type=F32
        )
        attn_piece = sum_over_tensor(attn_part)
        others_first, owned_second, attn_piece = lax.optimization_barrier(
            (others_first, owned_second, attn_piece)
        )
        hidden = own_piece(residual_in).astype(F32) + attn_piece
        normed_ffn, ffn_norm_back = jax.vjp(rms_scale, hidden, gain_ffn_float)

    with jax.named_scope("exchange"):
        cotangent_own, normed_ffn = lax.optimization_barrier((cotangent_own, normed_ffn))
        cotangent_other = lax.ppermute(cotangent_own, TENSOR, sibling)
        spread_all = jnp.concatenate(
            [cotangent_own[:, :, model_width:], cotangent_other[:, :, model_width:]], axis=1
        )

        def shares_of(first, count):
            start = group_rank * own_experts + first
            high = lax.dynamic_slice_in_dim(spread_all, start, count, axis=2)
            low = lax.dynamic_slice_in_dim(spread_all, start + expert_count, count, axis=2)
            total = high.astype(F32) + low.astype(F32)
            return jnp.pad(total, ((0, 0), (0, 0), (0, 8 - count)))

        shares_first = shares_of(0, first_count)
        shares_second = shares_of(first_count, own_experts - first_count)

    with jax.named_scope("experts"):
        line = groups // 2
        cotangents = (cotangent_own, cotangent_other)
        parts, grad_own_first, grad_other_first, tokens, others_second = (
            experts_gathering(
                normed_ffn.astype(BF16),
                cotangents,
                shares_first,
                owned_first,
                others_first,
                owned_second,
                line,
            )
        )
        grad_second, out_piece, grad_own_second, grad_other_second, received_first = (
            experts_reducing(
                tokens,
                cotangents,
                shares_second,
                owned_second,
                others_second,
                grad_other_first,
                parts,
                line,
            )
        )

    with jax.named_scope("expert_grads"):

        def added(own, received):
            return (own.astype(F32) + received.astype(F32)).astype(BF16)

        def returned(total):
            flat = total.reshape((total.shape[0] * total.shape[1],) + total.shape[2:])
            return lax.all_to_all(flat, GROUP, 0, 0, tiled=True).reshape(total.shape)

        total_first = added(grad_own_first, received_first)
        received_second = lax.ppermute(grad_other_second, TENSOR, across)
        total_first, grad_second = lax.optimization_barrier((total_first, grad_second))
        returned_first = returned(total_first)
        grad_hidden_norm, grad_gain_ffn_local = ffn_norm_back(grad_second.astype(F32))
        grad_hidden = cotangent_piece.astype(F32) + grad_hidden_norm
        grad_hidden_low = gather_over_tensor(grad_hidden.astype(BF16))
        output = gather_over_tensor((hidden + out_piece.astype(F32)).astype(BF16))

    with jax.named_scope("attention_back"):
        grad_out_local = lax.dot_general(
            grad_hidden_low, attended, FIRST_FIRST, preferred_element_type=F32
        )
        grad_out_transposed = lax.psum_scatter(
            grad_out_local.astype(BF16), GROUP, scatter_dimension=0, tiled=True
        )
        grad_attended = jnp.dot(grad_hidden_low, out_transposed, preferred_element_type=F32)
        grad_query_lin, grad_key_value = attention_backward(
            first,
            queries,
            keys_values,
            doc_start[:, None],
            lse,
            grad_attended.astype(BF16),
            turns,
            own_turns,
        )
        total_second = added(grad_own_second, received_second)
        grad_key_value = grad_key_value.reshape(2, row_count, -1)
        received = lax.ppermute(pick(grad_key_value, 0, 1 - context_rank), CONTEXT, pair)
        grad_key_value = (
            pick(grad_key_value, 0, context_rank).astype(F32) + received.astype(F32)
        ).astype(BF16)
        grad_projected = jnp.concatenate([grad_query_lin, grad_key_value], axis=1)
        grad_first_part = lax.dot_general(
            grad_projected, qkv_weight, LAST_LAST, preferred_element_type=F32
        )
        grad_qkv_local = lax.dot_general(
            first_normalized, grad_projected, FIRST_FIRST, preferred_element_type=F32
        ).astype(BF16)
        returned_first, total_second, grad_out_transposed, grad_first_part, grad_qkv_local = (
            lax.optimization_barrier(
                (returned_first, total_second, grad_out_transposed, grad_first_part, grad_qkv_local)
            )
        )
        returned_second = returned(total_second)
        grad_first = sum_over_tensor(grad_first_part)
        _, attn_norm_back = jax.vjp(
            rms_scale, own_piece(residual_in).astype(F32), gain_attn_float
        )
        grad_input_norm, grad_gain_attn_local = attn_norm_back(grad_first)
        grad_input = gather_over_tensor((grad_hidden + grad_input_norm).astype(BF16))
        grad_qkv = lax.psum_scatter(
            grad_qkv_local, GROUP, scatter_dimension=0, tiled=True
        ).astype(F32)
        gains = jnp.stack([grad_gain_attn_local, grad_gain_ffn_local])
        for axis, step, size in (
            (TENSOR, 1, tensor_size),
            (TENSOR, 2, tensor_size),
            (CONTEXT, 1, 2),
            (SHARD, 1, groups // 2),
            (SHARD, 2, groups // 2),
        ):
            gains = gains + lax.ppermute(gains, axis, [(i, i ^ step) for i in range(size)])
        gains = lax.dynamic_slice_in_dim(gains, group_rank * slice_rows, slice_rows, axis=1)

    def whole(first, last, turned):
        parts = [
            part[..., first:last].transpose(0, 1, 3, 2) if turned else part[..., first:last]
            for part in (returned_first, returned_second)
        ]
        joined = jnp.concatenate(parts, axis=1).astype(F32)
        return joined.reshape((expert_count,) + joined.shape[2:])

    units = unit_count
    return (
        output,
        grad_input,
        gains[0],
        grad_qkv[:, :query_cols],
        grad_qkv[:, query_cols:rotated_cols],
        grad_qkv[:, rotated_cols:qkv_cols],
        grad_out_transposed.astype(F32).T,
        gains[1],
        whole(0, units, False),
        whole(units, 2 * units, False),
        whole(2 * units, 3 * units, True),
    )


def solution(mesh):
    placed = (
        P(GROUP, None),
        P(GROUP),
        P(GROUP, TENSOR),
        P(GROUP, TENSOR),
        P(GROUP, TENSOR),
        P(TENSOR, GROUP),
        P(GROUP),
        P(None, GROUP, TENSOR),
        P(None, GROUP, TENSOR),
        P(None, TENSOR, GROUP),
        P(SHARD),
        P(GROUP, None),
        P(GROUP, None),
        P(GROUP, None),
    )
    sizes = dict(mesh.shape)
    if sizes[SHARD] == 4 and sizes[CONTEXT] == 2 and sizes[TENSOR] == 4:
        plan = partial(
            expert_plan, groups=sizes[SHARD] * sizes[CONTEXT], tensor_size=sizes[TENSOR]
        )
    else:
        plan = gathered_plan
    return jax.shard_map(
        plan,
        mesh=mesh,
        in_specs=placed,
        out_specs=(
            P(GROUP, None),
            P(GROUP, None),
            P(GROUP),
            P(GROUP, TENSOR),
            P(GROUP, TENSOR),
            P(GROUP, TENSOR),
            P(TENSOR, GROUP),
            P(GROUP),
            P(None, GROUP, TENSOR),
            P(None, GROUP, TENSOR),
            P(None, TENSOR, GROUP),
        ),
        check_vma=False,
    )
```

```python
from functools import partial

import jax
import jax.numpy as jnp
from jax import lax
from jax.experimental import pallas as pl
from jax.experimental.pallas import tpu as pltpu
from jax.sharding import PartitionSpec as P

HEAD_DIM = 64
NDOCS = 5
SHARD = "shard"
CONTEXT = "context"
TENSOR = "tensor"
GROUP = (SHARD, CONTEXT)
PRODUCT_0 = "qgrd,kgd->grqk"
PRODUCT_1 = "grqk,kgd->qgrd"
PRODUCT_2 = "ecd,edf->ecf"
PRODUCT_3 = "ecf,efd->ecd"
PRODUCT_4 = "ecd,efd->ecf"
PRODUCT_5 = "ecf,edf->ecd"
PRODUCT_6 = "ecd,ecf->edf"
PRODUCT_7 = "ecf,ecd->efd"
PRODUCT_8 = "grqk,qgrd->kgd"


epsilon = 1e-06


def rms_scale(values, gain):
    return values * lax.rsqrt(jnp.mean(values * values, axis=-1, keepdims=True) + epsilon) * gain


def doc_positions(segment_ids):
    sequence_length = segment_ids.shape[-1]
    index_row = jnp.arange(sequence_length, dtype=jnp.int32)
    documents = jnp.arange(NDOCS, dtype=jnp.int32)
    doc_starts = jnp.sum((segment_ids[..., :, None] < documents).astype(jnp.int32), axis=-2)
    own_start = jnp.sum(
        jnp.where(segment_ids[..., :, None] == documents, doc_starts[..., None, :], 0), axis=-1
    )
    return index_row - own_start


def rotary(values, positions):
    half_dim = values.shape[-1] // 2
    frequencies = 10000.0 ** (-2.0 * jnp.arange(half_dim, dtype=jnp.float32) / values.shape[-1])
    angles = positions.astype(jnp.float32)[:, None] * frequencies[None, :]
    cosine = jnp.cos(angles)[:, None, :]
    sines = jnp.sin(angles)[:, None, :]
    first_half = values[..., :half_dim]
    second_half = values[..., half_dim:]
    return jnp.concatenate(
        [first_half * cosine - second_half * sines, second_half * cosine + first_half * sines],
        axis=-1,
    )


def swiglu(gate_value, up_value):
    return jax.nn.silu(gate_value) * up_value


def dispatch(routes, shares, block_rows, capacity, expert_count):
    block_count = routes.shape[0] // block_rows
    picks = routes.shape[1]
    chosen = routes.reshape(block_count, block_rows * picks)
    onehot = (chosen[:, :, None] == jnp.arange(expert_count, dtype=jnp.int32)).astype(jnp.int32)
    ranked = jnp.sum((jnp.cumsum(onehot, axis=1) - onehot) * onehot, axis=2)
    slot_index = (
        chosen * (block_count * capacity)
        + jnp.arange(block_count, dtype=jnp.int32)[:, None] * capacity
        + ranked
    )
    tokens = jnp.arange(block_count * block_rows * picks, dtype=jnp.int32) // picks
    total_slots = expert_count * block_count * capacity
    slot_rows = jnp.zeros((total_slots,), jnp.int32).at[slot_index.reshape(-1)].set(tokens)
    slot_share = (
        jnp.zeros((total_slots,), jnp.float32).at[slot_index.reshape(-1)].set(shares.reshape(-1))
    )
    return (slot_rows, slot_share)


def gathered_plan(
    residual_in,
    gain_attn,
    query_weight,
    key_projection_weight,
    value_projection_weight,
    out_weight,
    gain_ffn,
    gate_weight,
    up_weight,
    down_weight,
    segments,
    routes,
    shares,
    cotangent,
):
    row_count, model_width = residual_in.shape
    head_size = HEAD_DIM
    query_cols = query_weight.shape[1]
    kv_heads = key_projection_weight.shape[1] // head_size
    group_size = query_cols // head_size // kv_heads
    expert_count = gate_weight.shape[0]
    capacity = row_count * routes.shape[1] * 5 // (4 * expert_count)
    score_scale = head_size ** (-0.5)
    context_rank = lax.axis_index(CONTEXT)
    own_first = context_rank * row_count
    gain_attn_full, gain_ffn_full, query_full, key_full, value_full, out_full = (
        lax.all_gather(gain_attn, GROUP, axis=0, tiled=True),
        lax.all_gather(gain_ffn, GROUP, axis=0, tiled=True),
        lax.all_gather(query_weight, GROUP, axis=0, tiled=True),
        lax.all_gather(key_projection_weight, GROUP, axis=0, tiled=True),
        lax.all_gather(value_projection_weight, GROUP, axis=0, tiled=True),
        lax.all_gather(out_weight, GROUP, axis=1, tiled=True),
    )
    gain_attn_float = gain_attn_full.astype(jnp.float32)
    gain_ffn_float = gain_ffn_full.astype(jnp.float32)
    positions = doc_positions(segments)
    own_positions = lax.dynamic_slice_in_dim(positions, own_first, row_count)
    own_ids = lax.dynamic_slice_in_dim(segments, own_first, row_count)
    own_index = own_first + jnp.arange(row_count, dtype=jnp.int32)
    input_float = residual_in.astype(jnp.float32)
    normed_attn, attn_norm_back = jax.vjp(rms_scale, input_float, gain_attn_float)
    first_normalized = normed_attn.astype(jnp.bfloat16)
    query_lin = jnp.dot(first_normalized, query_full, preferred_element_type=jnp.float32).reshape(
        row_count, -1, head_size
    )
    key_linear = jnp.dot(first_normalized, key_full, preferred_element_type=jnp.float32).reshape(
        row_count, -1, head_size
    )
    value_tokens = jnp.dot(first_normalized, value_full, preferred_element_type=jnp.float32).astype(
        jnp.bfloat16
    )
    rope_local = partial(rotary, positions=own_positions)
    query_rot, rope_query_back = jax.vjp(rope_local, query_lin)
    key_rot, rope_key_back = jax.vjp(rope_local, key_linear)
    query_low = query_rot.astype(jnp.bfloat16)
    key_low = key_rot.astype(jnp.bfloat16).reshape(row_count, -1)
    key_all, value_all = (
        lax.all_gather(key_low, CONTEXT, axis=0, tiled=True),
        lax.all_gather(value_tokens, CONTEXT, axis=0, tiled=True),
    )
    key_index = jnp.arange(key_all.shape[0], dtype=jnp.int32)
    key_ids = jnp.take(segments, jnp.clip(key_index, 0, segments.shape[0] - 1))
    key_valid = key_index >= 0
    key_heads = key_all.reshape(-1, kv_heads, head_size)
    value_heads = value_all.reshape(-1, kv_heads, head_size)
    query_heads = query_low.reshape(row_count, kv_heads, group_size, head_size)
    block_rows = min(512, row_count)
    block_starts = list(range(0, row_count, block_rows))

    def block_scores(block_first):
        query_block = query_heads[block_first : block_first + block_rows]
        raw_scores = jnp.einsum(
            PRODUCT_0, query_block, key_heads, preferred_element_type=jnp.float32
        )
        block_ids = own_ids[block_first : block_first + block_rows]
        block_index = own_index[block_first : block_first + block_rows]
        allowed = (
            key_valid[None, :]
            & (key_ids[None, :] == block_ids[:, None])
            & (key_index[None, :] <= block_index[:, None])
        )
        return (query_block, jnp.where(allowed, raw_scores * score_scale, -1e30))

    mixed_parts = []
    lse_parts = []
    for block_first in block_starts:
        query_block, scores = block_scores(block_first)
        row_max = jnp.max(scores, axis=-1, keepdims=True)
        exponent = jnp.exp(scores - row_max)
        row_total = jnp.sum(exponent, axis=-1, keepdims=True)
        probs = (exponent / row_total).astype(jnp.bfloat16)
        mixed_parts.append(
            jnp.einsum(PRODUCT_1, probs, value_heads, preferred_element_type=jnp.float32)
        )
        lse_parts.append(row_max + jnp.log(row_total))
    attended = (
        jnp.concatenate(mixed_parts, axis=0).reshape(row_count, query_cols).astype(jnp.bfloat16)
    )
    attn_part = jnp.dot(attended, out_full, preferred_element_type=jnp.float32)
    hidden = input_float + lax.psum(attn_part.astype(jnp.bfloat16), TENSOR).astype(jnp.float32)
    normed_ffn, ffn_norm_back = jax.vjp(rms_scale, hidden, gain_ffn_float)
    normed_second = normed_ffn.astype(jnp.bfloat16)
    slot_rows, slot_share = dispatch(routes, shares, row_count, capacity, expert_count)
    per_turn = expert_count // 5
    turn_count = expert_count // per_turn
    turn_slots = per_turn * capacity

    def local_experts(turn_index):
        gate_part = lax.dynamic_slice_in_dim(gate_weight, turn_index * per_turn, per_turn, 0)
        up_part = lax.dynamic_slice_in_dim(up_weight, turn_index * per_turn, per_turn, 0)
        down_part = lax.dynamic_slice_in_dim(down_weight, turn_index * per_turn, per_turn, 0)
        return (gate_part, up_part, down_part)

    def turn_inputs(turn_index):
        token_rows = lax.dynamic_slice_in_dim(slot_rows, turn_index * turn_slots, turn_slots)
        share_rows = lax.dynamic_slice_in_dim(slot_share, turn_index * turn_slots, turn_slots)
        picked = normed_second[token_rows].reshape(per_turn, capacity, model_width)
        return (token_rows, share_rows, picked)

    def forward_turn(running, turn_index):
        gate_part, up_part, down_part = local_experts(turn_index)
        gate_full, up_full, down_full = (
            lax.all_gather(gate_part, GROUP, axis=1, tiled=True),
            lax.all_gather(up_part, GROUP, axis=1, tiled=True),
            lax.all_gather(down_part, GROUP, axis=2, tiled=True),
        )
        token_rows, share_rows, picked = turn_inputs(turn_index)
        gate_value = jnp.einsum(
            PRODUCT_2, picked, gate_full, preferred_element_type=jnp.float32
        )
        up_value = jnp.einsum(PRODUCT_2, picked, up_full, preferred_element_type=jnp.float32)
        inner = swiglu(gate_value, up_value).astype(jnp.bfloat16)
        expert_result = jnp.einsum(
            PRODUCT_3, inner, down_full, preferred_element_type=jnp.float32
        ).reshape(turn_slots, model_width)
        return (running.at[token_rows].add(expert_result * share_rows[:, None]), None)

    turn_ids = jnp.arange(turn_count, dtype=jnp.int32)
    expert_part, _ = lax.scan(
        forward_turn, jnp.zeros((row_count, model_width), jnp.float32), turn_ids
    )
    expert_total = lax.psum(expert_part.astype(jnp.bfloat16), TENSOR).astype(jnp.float32)
    output = (hidden + expert_total).astype(jnp.bfloat16)
    upstream = cotangent.astype(jnp.float32)

    def backward_turn(running, turn_index):
        gate_part, up_part, down_part = local_experts(turn_index)
        gate_full, up_full, down_full = (
            lax.all_gather(gate_part, GROUP, axis=1, tiled=True),
            lax.all_gather(up_part, GROUP, axis=1, tiled=True),
            lax.all_gather(down_part, GROUP, axis=2, tiled=True),
        )
        token_rows, share_rows, picked = turn_inputs(turn_index)
        gate_value = jnp.einsum(
            PRODUCT_2, picked, gate_full, preferred_element_type=jnp.float32
        )
        up_value = jnp.einsum(PRODUCT_2, picked, up_full, preferred_element_type=jnp.float32)
        inner_float, swiglu_back = jax.vjp(swiglu, gate_value, up_value)
        inner = inner_float.astype(jnp.bfloat16)
        grad_slot = (
            (upstream[token_rows] * share_rows[:, None])
            .astype(jnp.bfloat16)
            .reshape(per_turn, capacity, model_width)
        )
        grad_inner = jnp.einsum(
            PRODUCT_4, grad_slot, down_full, preferred_element_type=jnp.float32
        )
        grad_gate_value, grad_up_value = swiglu_back(grad_inner)
        grad_gate_low = grad_gate_value.astype(jnp.bfloat16)
        grad_up_low = grad_up_value.astype(jnp.bfloat16)
        grad_picked = jnp.einsum(
            PRODUCT_5, grad_gate_low, gate_full, preferred_element_type=jnp.float32
        )
        grad_picked = grad_picked + jnp.einsum(
            PRODUCT_5, grad_up_low, up_full, preferred_element_type=jnp.float32
        )
        running = running.at[token_rows].add(grad_picked.reshape(turn_slots, model_width))
        shard_grads = (
            lax.psum_scatter(
                jnp.einsum(
                    PRODUCT_6, picked, grad_gate_low, preferred_element_type=jnp.float32
                ).astype(jnp.bfloat16),
                GROUP,
                scatter_dimension=1,
                tiled=True,
            ).astype(jnp.float32),
            lax.psum_scatter(
                jnp.einsum(
                    PRODUCT_6, picked, grad_up_low, preferred_element_type=jnp.float32
                ).astype(jnp.bfloat16),
                GROUP,
                scatter_dimension=1,
                tiled=True,
            ).astype(jnp.float32),
            lax.psum_scatter(
                jnp.einsum(
                    PRODUCT_7, inner, grad_slot, preferred_element_type=jnp.float32
                ).astype(jnp.bfloat16),
                GROUP,
                scatter_dimension=2,
                tiled=True,
            ).astype(jnp.float32),
        )
        return (running, shard_grads)

    grad_second_part, stacked_grads = lax.scan(
        backward_turn, jnp.zeros((row_count, model_width), jnp.float32), turn_ids
    )
    grad_gate_out = stacked_grads[0].reshape(gate_weight.shape)
    grad_up_out = stacked_grads[1].reshape(up_weight.shape)
    grad_down_out = stacked_grads[2].reshape(down_weight.shape)
    grad_second = lax.psum(grad_second_part.astype(jnp.bfloat16), TENSOR).astype(jnp.float32)
    grad_hidden_norm, grad_gain_ffn_local = ffn_norm_back(grad_second)
    grad_hidden = upstream + grad_hidden_norm
    grad_hidden_low = grad_hidden.astype(jnp.bfloat16)
    grad_out_local = jnp.einsum(
        "tc,td->cd", attended, grad_hidden_low, preferred_element_type=jnp.float32
    )
    grad_attended = jnp.einsum(
        "td,cd->tc", grad_hidden_low, out_full, preferred_element_type=jnp.float32
    )
    grad_attended = grad_attended.astype(jnp.bfloat16).reshape(
        row_count, kv_heads, group_size, head_size
    )
    grad_query_parts = []
    grad_keys = jnp.zeros(key_heads.shape, jnp.float32)
    grad_values = jnp.zeros(value_heads.shape, jnp.float32)
    for block_number in range(len(block_starts)):
        block_first = block_starts[block_number]
        query_block, scores = block_scores(block_first)
        probs_float = jnp.exp(scores - lse_parts[block_number])
        probs = probs_float.astype(jnp.bfloat16)
        grad_block = grad_attended[block_first : block_first + block_rows]
        grad_probs = jnp.einsum(
            PRODUCT_0, grad_block, value_heads, preferred_element_type=jnp.float32
        )
        inner_sum = jnp.sum(grad_probs * probs_float, axis=-1, keepdims=True)
        grad_scores = (score_scale * (probs_float * (grad_probs - inner_sum))).astype(jnp.bfloat16)
        grad_query_parts.append(
            jnp.einsum(PRODUCT_1, grad_scores, key_heads, preferred_element_type=jnp.float32)
        )
        grad_keys = grad_keys + jnp.einsum(
            PRODUCT_8, grad_scores, query_block, preferred_element_type=jnp.float32
        )
        grad_values = grad_values + jnp.einsum(
            PRODUCT_8, probs, grad_block, preferred_element_type=jnp.float32
        )
    grad_key_own, grad_value_own = (
        lax.psum_scatter(
            grad_keys.astype(jnp.bfloat16), CONTEXT, scatter_dimension=0, tiled=True
        ).astype(jnp.float32),
        lax.psum_scatter(
            grad_values.astype(jnp.bfloat16), CONTEXT, scatter_dimension=0, tiled=True
        ).astype(jnp.float32),
    )
    grad_query_all = jnp.concatenate(grad_query_parts, axis=0).reshape(row_count, -1, head_size)
    grad_query_lin = rope_query_back(grad_query_all)[0].astype(jnp.bfloat16).reshape(row_count, -1)
    grad_key_lin = rope_key_back(grad_key_own)[0].astype(jnp.bfloat16).reshape(row_count, -1)
    grad_value_low = grad_value_own.astype(jnp.bfloat16).reshape(row_count, -1)
    grad_first_part = jnp.einsum(
        "tc,dc->td", grad_query_lin, query_full, preferred_element_type=jnp.float32
    )
    grad_first_part = grad_first_part + jnp.einsum(
        "tc,dc->td", grad_key_lin, key_full, preferred_element_type=jnp.float32
    )
    grad_first_part = grad_first_part + jnp.einsum(
        "tc,dc->td", grad_value_low, value_full, preferred_element_type=jnp.float32
    )
    grad_first = lax.psum(grad_first_part.astype(jnp.bfloat16), TENSOR).astype(jnp.float32)
    grad_input_norm, grad_gain_attn_local = attn_norm_back(grad_first)
    grad_input = (grad_hidden + grad_input_norm).astype(jnp.bfloat16)
    grad_query_local = jnp.einsum(
        "td,tc->dc", first_normalized, grad_query_lin, preferred_element_type=jnp.float32
    )
    grad_key_local = jnp.einsum(
        "td,tc->dc", first_normalized, grad_key_lin, preferred_element_type=jnp.float32
    )
    grad_value_local = jnp.einsum(
        "td,tc->dc", first_normalized, grad_value_low, preferred_element_type=jnp.float32
    )
    reduced = (
        lax.psum_scatter(
            grad_gain_attn_local.astype(jnp.bfloat16),
            GROUP,
            scatter_dimension=0,
            tiled=True,
        ).astype(jnp.float32),
        lax.psum_scatter(
            grad_query_local.astype(jnp.bfloat16),
            GROUP,
            scatter_dimension=0,
            tiled=True,
        ).astype(jnp.float32),
        lax.psum_scatter(
            grad_key_local.astype(jnp.bfloat16),
            GROUP,
            scatter_dimension=0,
            tiled=True,
        ).astype(jnp.float32),
        lax.psum_scatter(
            grad_value_local.astype(jnp.bfloat16),
            GROUP,
            scatter_dimension=0,
            tiled=True,
        ).astype(jnp.float32),
        lax.psum_scatter(
            grad_out_local.astype(jnp.bfloat16),
            GROUP,
            scatter_dimension=1,
            tiled=True,
        ).astype(jnp.float32),
        lax.psum_scatter(
            grad_gain_ffn_local.astype(jnp.bfloat16),
            GROUP,
            scatter_dimension=0,
            tiled=True,
        ).astype(jnp.float32),
    )
    return (
        output,
        grad_input,
        reduced[0],
        reduced[1],
        reduced[2],
        reduced[3],
        reduced[4],
        reduced[5],
        grad_gate_out,
        grad_up_out,
        grad_down_out,
    )


F32 = jnp.float32
BF16 = jnp.bfloat16
LAST_LAST = (((1,), (1,)), ((), ()))
FIRST_FIRST = (((0,), (0,)), ((), ()))


def weight_copies(own_hbm, other_hbm, weights, sems):
    sources, _, rows, lanes = own_hbm.shape
    units = lanes // 3
    return [
        pltpu.make_async_copy(
            half_hbm.at[source, :, :, pl.ds(part * units, units)],
            weights.at[
                :, pl.ds(source * rows, rows), pl.ds((2 * part + half) * units, units)
            ],
            sems.at[source, half, part],
        )
        for source in range(sources)
        for half, half_hbm in enumerate((own_hbm, other_hbm))
        for part in range(3)
    ]


def project(tokens, cotangent, weights):
    hidden_units = weights.shape[1] // 3
    gate_up = jnp.dot(tokens, weights[:, : 2 * hidden_units], preferred_element_type=F32)
    grad_inner = jnp.dot(cotangent, weights[:, 2 * hidden_units :], preferred_element_type=F32)
    return gate_up, grad_inner


def activate(gate_up, grad_inner, share):
    hidden_units = grad_inner.shape[1]
    gate, up = gate_up[:, :hidden_units], gate_up[:, hidden_units:]
    sigmoid = 1.0 / (1.0 + jnp.exp(-gate))
    silu = gate * sigmoid
    grad_inner = grad_inner * share
    inner = silu * up * share
    grad_gate = grad_inner * up * (sigmoid * (1.0 + gate * (1.0 - sigmoid)))
    grad_up = grad_inner * silu
    return inner.astype(BF16), grad_gate.astype(BF16), grad_up.astype(BF16)


MESH_ID = pl.DeviceIdType.MESH


class Place:
    def __init__(self, line):
        self.line = line
        self.z, self.y = lax.axis_index(SHARD), lax.axis_index(CONTEXT)
        self.t = lax.axis_index(TENSOR)
        self.sibling = (self.z, self.y, self.t + 1 - 2 * (self.t % 2))
        self.partner = (self.z, 1 - self.y, self.t)
        self.across = (self.z, self.y, (self.t + 2) % 4)

    def beside(self, side):
        return (self.z + side, self.y, self.t)

    def inside(self, at):
        return (at >= 0) & (at < self.line)

    def near(self, rank):
        z, line = self.z, self.line
        half = z // 2
        mirrored = z * (1 - half) + (line - 1 - z) * half
        far = rank // 2
        place = (1 - far) * (mirrored + rank - 2 * mirrored * rank) + far * rank
        return place * (1 - half) + (line - 1 - place) * half

    def block(self, order, step):
        rank, across = order[0]
        for number, (later_rank, later_across) in enumerate(order[1:], 1):
            rank = jnp.where(step == number, later_rank, rank)
            across = jnp.where(step == number, later_across, across)
        column = self.y + across - 2 * self.y * across
        return self.near(rank) * 2 + column

    def meet(self):
        z, line = self.z, self.line
        barrier = pltpu.get_barrier_semaphore()
        for device in (self.sibling, self.partner, self.across):
            pl.semaphore_signal(barrier, inc=1, device_id=device, device_id_type=MESH_ID)
        for side in (-1, 1):

            @pl.when(self.inside(z + side))
            def _():
                pl.semaphore_signal(
                    barrier, inc=1, device_id=self.beside(side), device_id_type=MESH_ID
                )

        below, above = (z + line - 1) // line, (2 * line - 2 - z) // line
        pl.semaphore_wait(barrier, 3 + below + above)


def remote(source, target, send, recv, device):
    return pltpu.make_async_remote_copy(
        src_ref=source,
        dst_ref=target,
        send_sem=send,
        recv_sem=recv,
        device_id=device,
        device_id_type=MESH_ID,
    )


class Gather:
    order = ((0, 0), (1, 0), (0, 1), (2, 0), (1, 1), (3, 0), (2, 1), (3, 1))
    rounds = (0, 2, 4)
    crossings = (1, 3, 5, 6)

    def __init__(self, place, tokens, sems):
        self.place, self.tokens = place, tokens
        self.recv, self.along, self.across, self.cores = sems

    def line_copy(self, at, side):
        here, tokens = at * 2 + self.place.y, self.tokens
        return remote(
            tokens.at[here, 0],
            tokens.at[here, 0],
            self.along.at[at, (side + 1) // 2],
            self.recv.at[here, 0],
            self.place.beside(side),
        )

    def pair_copy(self, at, column):
        here, tokens = at * 2 + column, self.tokens
        return remote(
            tokens.at[here, 0],
            tokens.at[here, 0],
            self.across.at[at],
            self.recv.at[here, 0],
            self.place.partner,
        )

    def core_copy(self, here):
        tokens = self.tokens
        return remote(
            tokens.at[here, 0],
            tokens.at[here, 1],
            self.cores.at[here],
            self.recv.at[here, 1],
            self.place.sibling,
        )

    def start(self):
        place = self.place
        for side in (-1, 1):
            pl.when(place.inside(place.z + side))(lambda: self.line_copy(place.z, side).start())
        self.pair_copy(place.z, place.y).start()
        self.core_copy(place.z * 2 + place.y).start()

    def came_along(self, at, side):
        place = self.place
        self.line_copy(at, -side).wait_recv()
        pl.when(place.inside(place.z - side))(lambda: self.line_copy(at, -side).start())
        self.pair_copy(at, place.y).start()
        self.core_copy(at * 2 + place.y).start()

    def came_across(self, at):
        column = 1 - self.place.y
        self.pair_copy(at, column).wait_recv()
        self.core_copy(at * 2 + column).start()

    def tick(self, number):
        place = self.place
        for distance, when in enumerate(self.rounds, 1):

            @pl.when(number == when)
            def _():
                for side in (-1, 1):
                    at = place.z + side * distance
                    pl.when(place.inside(at))(partial(self.came_along, at, side))

        for distance, when in enumerate(self.crossings):

            @pl.when(number == when)
            def _():
                for side in (-1, 1) if distance else (1,):
                    at = place.z + side * distance
                    pl.when(place.inside(at))(partial(self.came_across, at))

    def finish(self):
        place = self.place
        for side in (-1, 1):
            for distance in range(place.line):
                at = place.z - side * distance

                @pl.when(place.inside(at) & place.inside(place.z + side))
                def _():
                    self.line_copy(at, side).wait_send()

        for at in range(place.line):
            self.pair_copy(at, place.y).wait_send()
        for here in range(2 * place.line):
            self.core_copy(here).wait_send()


class Reduce:
    order = ((3, 1), (3, 0), (2, 1), (2, 0), (1, 1), (1, 0), (0, 1), (0, 0))

    def __init__(self, place, arrays, terms, term_sems, sums, base, sems):
        self.place, self.terms, self.term_sems = place, terms, term_sems
        self.sums, self.base = sums, base
        self.parts, self.from_core, self.from_pair, self.from_line = arrays
        self.core_send, self.core_recv, self.pair_send, self.pair_recv = sems[:4]
        self.line_send, self.line_recv = sems[4:]

    def core_copy(self, here, source):
        return remote(
            source,
            self.from_core.at[here],
            self.core_send.at[here],
            self.core_recv.at[here],
            self.place.sibling,
        )

    def core_arrived(self, here):
        self.core_copy(here, self.from_core.at[here]).wait_recv()

    def pair_copy(self, at, slot):
        return remote(
            self.sums.at[self.base + slot],
            self.from_pair.at[at],
            self.pair_send.at[at],
            self.pair_recv.at[at],
            self.place.partner,
        )

    def line_copy(self, at, side, distance):
        slot = self.place.line if distance == 1 and side == 1 else at
        return remote(
            self.sums.at[self.base + 2 + (side + 1) // 2],
            self.from_line.at[slot],
            self.line_send.at[at],
            self.line_recv.at[slot],
            self.place.beside(side),
        )

    def add_up(self, sources, slot):
        terms = self.terms
        copies = [
            pltpu.make_async_copy(source, terms.at[i], self.term_sems.at[i])
            for i, (source, _) in enumerate(sources)
        ]
        for copy, (_, there) in zip(copies, sources):
            if there is None:
                copy.start()
            else:
                pl.when(there)(copy.start)
        for i, (copy, (_, there)) in enumerate(zip(copies, sources)):
            if there is None:
                copy.wait()
            else:
                pl.when(there)(copy.wait)

                @pl.when(jnp.logical_not(there))
                def _():
                    terms[i] = jnp.zeros_like(terms[i])

        tile = 16

        @pl.loop(0, terms.shape[1] // tile)
        def _(number):
            here = pl.ds(pl.multiple_of(number * tile, tile), tile)
            total = terms[0, here, :].astype(F32)
            for i in range(1, len(sources)):
                total += terms[i, here, :].astype(F32)
            self.sums[self.base + slot, here, :] = total.astype(BF16)

    def cross(self, rank):
        place = self.place
        at = place.near(rank)
        here = at * 2 + 1 - place.y
        slot = rank % 2
        if rank + 2 < place.line:
            self.pair_copy(place.near(rank + 2), slot).wait_send()
        self.core_arrived(here)
        self.add_up([(self.parts.at[here], None), (self.from_core.at[here], None)], slot)
        self.pair_copy(at, slot).start()

    def advance(self, distance):
        place = self.place
        for side in (-1, 1):
            at = place.z + side * distance
            here = at * 2 + place.y
            farther = place.inside(place.z - side)
            if distance + 1 < place.line:

                @pl.when(place.inside(at + side))
                def _():
                    self.line_copy(at + side, side, distance + 1).wait_send()

            @pl.when(place.inside(at))
            def _():
                self.core_arrived(here)
                self.pair_copy(at, 0).wait_recv()
                sources = [
                    (self.parts.at[here], None),
                    (self.from_core.at[here], None),
                    (self.from_pair.at[at], None),
                ]
                if distance + 1 < place.line:

                    @pl.when(farther)
                    def _():
                        self.line_copy(at, side, distance + 1).wait_recv()

                    sources.append((self.from_line.at[at], farther))
                self.add_up(sources, 2 + (side + 1) // 2)
                self.line_copy(at, side, distance).start()

    def tick(self, number, late):
        line = self.place.line
        for rank in range(line):
            when = 2 * (line - rank) - 1
            pl.when(number == when)(partial(self.cross, rank))
            if rank + 1 < line:
                pl.when(number == when + late)(partial(self.advance, rank + 1))

    def finish(self, result, sem):
        place = self.place
        z, line = place.z, place.line
        here = z * 2 + place.y
        self.core_arrived(here)
        self.pair_copy(z, 0).wait_recv()
        for side in (-1, 1):
            pl.when(place.inside(z + side))(lambda: self.line_copy(z, -side, 1).wait_recv())
        for rank in (1, 0):
            self.pair_copy(place.near(rank), rank % 2).wait_send()
        self.add_up(
            [
                (self.parts.at[here], None),
                (self.from_core.at[here], None),
                (self.from_pair.at[z], None),
                (self.from_line.at[z], place.inside(z + 1)),
                (self.from_line.at[line], place.inside(z - 1)),
            ],
            0,
        )
        copy = pltpu.make_async_copy(self.sums.at[self.base], result, sem)
        copy.start()
        copy.wait()
        for side in (-1, 1):

            @pl.when(place.inside(z + side))
            def _():
                self.line_copy(z + side, side, 1).wait_send()


def expert_kernel(*refs, line, chunk, gathers):
    refs = list(refs)

    def take(count):
        taken = refs[:count]
        del refs[:count]
        return taken[0] if count == 1 else taken

    tokens_in, cotangent_own = take(2)
    if not gathers:
        cotangent_other = take(1)
    shares_ref, own_hbm, other_hbm, exchanged = take(4)
    if not gathers:
        before = take(1)
        grad_piece, out_piece, grad_own, grad_other, received = take(5)
        grad_arrays, out_arrays = take(4), take(4)
        tokens_hbm = tokens_in
    else:
        parts_hbm, grad_own, grad_other, tokens_hbm, received, cotangent_other = take(6)
    weights, grads, tokens_buf, cotangent_buf, inner_low, grad_low = take(6)
    both_buf, stage, load_sems, store_sems, row_sems, part_sems, exchange_sems = take(7)

    expert_count, model_width, all_units = weights.shape
    hidden_units = all_units // 3
    units = hidden_units // 2
    steps = 2 * line
    rows = tokens_hbm.shape[2]
    place = Place(line)
    first_rows, second_rows = pl.ds(0, rows), pl.ds(rows, rows)
    if gathers:
        mover = Gather(place, tokens_hbm, take(4))
        cotangent_send, cotangent_recv = take(2)
    else:
        before_buf, terms, sums, term_sems = take(4)
        movers = [
            Reduce(place, arrays, terms, term_sems, sums, 4 * number, take(6))
            for number, arrays in enumerate((grad_arrays, out_arrays))
        ]
    order = mover.order if gathers else Reduce.order

    def cotangent_copy(step):
        here = place.block(order, step)
        return remote(
            cotangent_own.at[here],
            cotangent_other.at[here],
            cotangent_send.at[here],
            cotangent_recv.at[here],
            place.sibling,
        )

    place.meet()
    exchange = remote(
        exchanged, received, exchange_sems.at[0], exchange_sems.at[1], place.across
    )
    exchange.start()
    if gathers:
        own_block = place.z * 2 + place.y
        own_copy = pltpu.make_async_copy(tokens_in, tokens_hbm.at[own_block, 0], row_sems.at[0, 0])
        own_copy.start()
        own_copy.wait()
        mover.start()
        for step in range(steps):
            cotangent_copy(step).start()
    weight_loads = weight_copies(own_hbm, other_hbm, weights, load_sems)
    for copy in weight_loads:
        copy.start()
    grads[...] = jnp.zeros_like(grads)

    def row_copies(step, slot):
        here = place.block(order, step)
        lanes = pl.ds(0, model_width)
        pairs = [
            (tokens_hbm.at[here, 0], tokens_buf.at[slot, first_rows, :]),
            (tokens_hbm.at[here, 1], tokens_buf.at[slot, second_rows, :]),
            (cotangent_own.at[here, :, lanes], cotangent_buf.at[slot, first_rows, :]),
            (cotangent_other.at[here, :, lanes], cotangent_buf.at[slot, second_rows, :]),
        ]
        if not gathers:
            pairs.append((before.at[here], before_buf.at[slot]))
        return [
            pltpu.make_async_copy(source, target, row_sems.at[slot, i])
            for i, (source, target) in enumerate(pairs)
        ]

    def load_rows(step, slot):
        if gathers:
            mover.core_copy(place.block(order, step)).wait_recv()
            cotangent_copy(step).wait_recv()
        for copy in row_copies(step, slot):
            copy.start()

    load_rows(0, 0)
    for copy in weight_loads:
        copy.wait()

    halves = [pl.ds(number * model_width, model_width) for number in range(2)]

    def core_copies(step, slot):
        here = place.block(order, step)
        return [
            mover.core_copy(here, both_buf.at[slot, second_rows, lanes])
            for mover, lanes in zip(movers, halves)
        ]

    def part_copies(step, slot):
        here = place.block(order, step)
        if gathers:
            pairs = [(both_buf.at[slot], parts_hbm.at[here])]
        else:
            pairs = [
                (both_buf.at[slot, first_rows, lanes], mover.parts.at[here])
                for mover, lanes in zip(movers, halves)
            ]
        return [
            pltpu.make_async_copy(source, target, part_sems.at[slot, i])
            for i, (source, target) in enumerate(pairs)
        ]

    @pl.loop(0, steps)
    def _(step):
        slot = step % 2
        for copy in row_copies(step, slot):
            copy.wait()
        shares = shares_ref[place.block(order, step)]
        lane = lax.broadcasted_iota(jnp.int32, shares.shape, 1)

        def run(expert, gate_up, grad_inner):
            share = jnp.sum(jnp.where(lane == expert, shares, 0.0), axis=1, keepdims=True)
            inner, grad_gate, grad_up = activate(gate_up, grad_inner, share)
            inner_low[expert] = inner
            grad_low[expert, :, :hidden_units] = grad_gate
            grad_low[expert, :, hidden_units:] = grad_up

        def weight_grads(expert):
            grads[expert, :, : 2 * hidden_units] += lax.dot_general(
                tokens_buf[slot], grad_low[expert], FIRST_FIRST, preferred_element_type=F32
            )
            grads[expert, :, 2 * hidden_units :] += lax.dot_general(
                cotangent_buf[slot], inner_low[expert], FIRST_FIRST, preferred_element_type=F32
            )

        results = project(tokens_buf[slot], cotangent_buf[slot], weights[0])
        for expert in range(expert_count):
            run(expert, *results)
            if expert + 1 < expert_count:
                results = project(tokens_buf[slot], cotangent_buf[slot], weights[expert + 1])
            weight_grads(expert)

        @pl.when(step >= 1)
        def _():
            for copy in part_copies(step - 1, 1 - slot):
                copy.wait()

        if gathers:
            mover.tick(step)
        else:
            for late, reducer in enumerate(movers):
                reducer.tick(step, late)

            @pl.when(step >= 2)
            def _():
                for copy in core_copies(step - 2, slot):
                    copy.wait_send()

        @pl.loop(0, model_width // chunk)
        def _(number):
            @pl.when((number == 1) & (step + 1 < steps))
            def _():
                load_rows(step + 1, 1 - slot)

            cols = pl.ds(pl.multiple_of(number * chunk, chunk), chunk)

            def total_of(lows, lanes, target):
                if gathers:
                    total = jnp.zeros((2 * rows, chunk), F32)
                else:
                    total = before_buf[slot, :, target].astype(F32)
                for expert in range(expert_count):
                    total += lax.dot_general(
                        lows[expert],
                        weights[expert, cols, lanes],
                        LAST_LAST,
                        preferred_element_type=F32,
                    )
                both_buf[slot, :, target] = total.astype(BF16)

            beyond = pl.ds(pl.multiple_of(model_width + number * chunk, chunk), chunk)
            total_of(grad_low, pl.ds(0, 2 * hidden_units), cols)
            total_of(inner_low, pl.ds(2 * hidden_units, hidden_units), beyond)

        if not gathers:
            for copy in core_copies(step, slot):
                copy.start()
        for copy in part_copies(step, slot):
            copy.start()

    last = (steps - 1) % 2
    for copy in part_copies(steps - 1, last):
        copy.wait()
    if not gathers:
        for copy in core_copies(steps - 2, 1 - last) + core_copies(steps - 1, last):
            copy.wait_send()
        movers[1].advance(1)

    sources, _, slice_rows, _ = own_hbm.shape

    def grad_copy(expert, source, half, slot):
        return pltpu.make_async_copy(
            stage.at[slot, half],
            (grad_own, grad_other)[half].at[source, expert],
            store_sems.at[slot, half],
        )

    @pl.loop(0, expert_count * sources)
    def _(number):
        expert, source = number // sources, number % sources
        slot = number % 2

        @pl.when(number >= 2)
        def _():
            for half in range(2):
                grad_copy(expert, source, half, slot).wait()

        here = pl.ds(pl.multiple_of(source * slice_rows, slice_rows), slice_rows)
        for half in range(2):
            for part in range(3):
                first = (2 * part + half) * units
                stage[slot, half, :, part * units : (part + 1) * units] = grads[
                    expert, here, first : first + units
                ].astype(BF16)
            grad_copy(expert, source, half, slot).start()

    for slot in range(2):
        for half in range(2):
            grad_copy(0, 0, half, slot).wait()

    exchange.wait()
    if gathers:
        mover.finish()
        for step in range(steps):
            cotangent_copy(step).wait_send()
    else:
        for number, result in enumerate((grad_piece, out_piece)):
            movers[number].finish(result, row_sems.at[0, number])


def expert_call(operands, own, shares, line, rows, model_width, gathers, collective_id, chunk=512):
    sources, expert_count, slice_rows, lanes = own.shape
    hidden_units = 2 * lanes // 3
    blocks = 2 * line
    in_place = pl.BlockSpec(memory_space=pl.ANY)
    dma = pltpu.SemaphoreType.DMA
    flops = 2 * blocks * 2 * rows * model_width * expert_count * hidden_units * 9

    def low(*shape):
        return jax.ShapeDtypeStruct(shape, BF16)

    if gathers:
        out_shape = [
            low(blocks, 2 * rows, 2 * model_width),
            low(*own.shape),
            low(*own.shape),
            low(blocks, 2, rows, model_width),
            low(*operands[5].shape),
            low(*operands[1].shape),
        ]
        own_scratch = [dma((blocks, 2)), dma((line, 2)), dma((line,)), dma((blocks,))]
        own_scratch += [dma((blocks,)), dma((blocks,))]
    else:
        out_shape = [
            low(rows, model_width),
            low(rows, model_width),
            low(*own.shape),
            low(*own.shape),
            low(*operands[6].shape),
        ]
        out_shape += 2 * [
            low(blocks, rows, model_width),
            low(blocks, rows, model_width),
            low(line, rows, model_width),
            low(line + 1, rows, model_width),
        ]
        own_scratch = [
            pltpu.VMEM((2, 2 * rows, 2 * model_width), BF16),
            pltpu.VMEM((5, rows, model_width), BF16),
            pltpu.VMEM((8, rows, model_width), BF16),
            dma((5,)),
        ]
        own_scratch += 2 * [
            dma((blocks,)),
            dma((blocks,)),
            dma((line,)),
            dma((line,)),
            dma((line,)),
            dma((line + 1,)),
        ]
    in_specs = [in_place] * len(operands)
    in_specs[2 if gathers else 3] = pl.BlockSpec(memory_space=pltpu.VMEM)
    results = pl.pallas_call(
        partial(expert_kernel, line=line, chunk=chunk, gathers=gathers),
        in_specs=in_specs,
        out_specs=[in_place] * len(out_shape),
        out_shape=out_shape,
        scratch_shapes=[
            pltpu.VMEM((expert_count, model_width, 3 * hidden_units), BF16),
            pltpu.VMEM((expert_count, model_width, 3 * hidden_units), F32),
            pltpu.VMEM((2, 2 * rows, model_width), BF16),
            pltpu.VMEM((2, 2 * rows, model_width), BF16),
            pltpu.VMEM((expert_count, 2 * rows, hidden_units), BF16),
            pltpu.VMEM((expert_count, 2 * rows, 2 * hidden_units), BF16),
            pltpu.VMEM((2, 2 * rows, 2 * model_width), BF16),
            pltpu.VMEM((2, 2, slice_rows, lanes), BF16),
            dma((sources, 2, 3)),
            dma((2, 2)),
            dma((2, 5)),
            dma((2, 2)),
            dma((2,)),
        ]
        + own_scratch,
        compiler_params=pltpu.CompilerParams(
            vmem_limit_bytes=60 * 2**20, collective_id=collective_id, has_side_effects=True
        ),
        cost_estimate=pl.CostEstimate(
            flops=flops, bytes_accessed=80 * 2**20, transcendentals=0
        ),
    )(*operands)
    return results[: 6 if gathers else 5]


def experts_gathering(piece, cotangent, shares, own, other, exchanged, line):
    rows, model_width = piece.shape
    operands = (piece, cotangent, shares, own, other, exchanged)
    return expert_call(operands, own, shares, line, rows, model_width, True, 1)


def experts_reducing(
    tokens, cotangents, shares, own, other, exchanged, parts, line
):
    _, _, rows, model_width = tokens.shape
    operands = (tokens, *cotangents, shares, own, other, exchanged, parts)
    return expert_call(operands, own, shares, line, rows, model_width, False, 2)


def attention_rows(values, kv_head, group_size):
    first = kv_head * group_size
    return jnp.concatenate(
        [values[:, (first + r) * HEAD_DIM : (first + r + 1) * HEAD_DIM] for r in range(group_size)],
        axis=0,
    )


def quarter_turn(values):
    half = HEAD_DIM // 2
    return jnp.concatenate([-values[:, half:], values[:, :half]], axis=1)


def window_mask(start, doc_start_ref, first_ref, block_rows, window):
    key_index = start + lax.broadcasted_iota(jnp.int32, (block_rows, window), 1)
    query_index = (
        first_ref[0]
        + pl.program_id(0) * block_rows
        + lax.broadcasted_iota(jnp.int32, (block_rows, window), 0)
    )
    return (key_index <= query_index) & (key_index >= doc_start_ref[...])


def window_start(first_ref, block_rows, window):
    end = first_ref[0] + (pl.program_id(0) + 1) * block_rows
    return pl.multiple_of(jnp.maximum(end - window, 0), block_rows)


def attention_forward_kernel(
    first_ref, query_ref, key_value_ref, doc_start_ref, attended_ref, lse_ref, *, group_size, window
):
    block_rows = query_ref.shape[0]
    kv_heads = key_value_ref.shape[1] // (2 * HEAD_DIM)
    start = window_start(first_ref, block_rows, window)
    allowed = window_mask(start, doc_start_ref, first_ref, block_rows, window)
    bias = jnp.where(allowed, 0.0, -1e30)
    bias = jnp.concatenate([bias] * group_size, axis=0)
    keys_values = key_value_ref[pl.ds(start, window), :]
    queries = query_ref[...]
    parts = []
    for g in range(kv_heads):
        keys = keys_values[:, g * HEAD_DIM : (g + 1) * HEAD_DIM]
        values = keys_values[:, (kv_heads + g) * HEAD_DIM : (kv_heads + g + 1) * HEAD_DIM]
        scores = lax.dot_general(
            attention_rows(queries, g, group_size), keys, LAST_LAST, preferred_element_type=F32
        )
        scores = scores * HEAD_DIM**-0.5 + bias
        row_max = jnp.max(scores, axis=1, keepdims=True)
        exponent = jnp.exp(scores - row_max)
        total = jnp.sum(exponent, axis=1, keepdims=True)
        probs = (exponent * (1.0 / total)).astype(BF16)
        mixed = jnp.dot(probs, values, preferred_element_type=F32).astype(BF16)
        lse_ref[0, g] = row_max + jnp.log(total)
        parts += [mixed[r * block_rows : (r + 1) * block_rows] for r in range(group_size)]
    attended_ref[...] = jnp.concatenate(parts, axis=1)


def attention_backward_kernel(
    first_ref,
    query_ref,
    key_value_ref,
    doc_start_ref,
    lse_ref,
    grad_ref,
    turns_ref,
    query_turns_ref,
    grad_query_ref,
    grad_key_value_ref,
    grad_keys,
    grad_values,
    *,
    group_size,
    window,
    steps,
):
    step = pl.program_id(0)
    block_rows = query_ref.shape[0]
    kv_heads = key_value_ref.shape[1] // (2 * HEAD_DIM)

    @pl.when(step == 0)
    def _():
        grad_keys[...] = jnp.zeros_like(grad_keys)
        grad_values[...] = jnp.zeros_like(grad_values)

    start = window_start(first_ref, block_rows, window)
    allowed = window_mask(start, doc_start_ref, first_ref, block_rows, window)
    bias = jnp.where(allowed, 0.0, -1e30)
    bias = jnp.concatenate([bias] * group_size, axis=0)
    rows = pl.ds(start, window)
    keys_values = key_value_ref[rows, :]
    queries = query_ref[...]
    grads = grad_ref[...]
    query_turns = jnp.concatenate([query_turns_ref[...]] * group_size, axis=0)
    parts = []
    for g in range(kv_heads):
        keys = keys_values[:, g * HEAD_DIM : (g + 1) * HEAD_DIM]
        values = keys_values[:, (kv_heads + g) * HEAD_DIM : (kv_heads + g + 1) * HEAD_DIM]
        query_rows = attention_rows(queries, g, group_size)
        grad_rows = attention_rows(grads, g, group_size)
        scores = lax.dot_general(query_rows, keys, LAST_LAST, preferred_element_type=F32)
        probs = jnp.exp(scores * HEAD_DIM**-0.5 + bias - lse_ref[0, g])
        grad_probs = lax.dot_general(grad_rows, values, LAST_LAST, preferred_element_type=F32)
        inner = jnp.sum(grad_probs * probs, axis=1, keepdims=True)
        grad_scores = (HEAD_DIM**-0.5 * (probs * (grad_probs - inner))).astype(BF16)
        grad_values[g, rows, :] += lax.dot_general(
            probs.astype(BF16), grad_rows, FIRST_FIRST, preferred_element_type=F32
        )
        both_queries = jnp.concatenate([query_rows, quarter_turn(query_rows)], axis=1)
        grad_keys[g, rows, :] += lax.dot_general(
            grad_scores, both_queries, FIRST_FIRST, preferred_element_type=F32
        )
        both_keys = jnp.concatenate([keys, quarter_turn(keys)], axis=1)
        turned = jnp.dot(grad_scores, both_keys, preferred_element_type=F32) * query_turns
        grad_query = (turned[:, :HEAD_DIM] + turned[:, HEAD_DIM:]).astype(BF16)
        parts += [grad_query[r * block_rows : (r + 1) * block_rows] for r in range(group_size)]
    grad_query_ref[...] = jnp.concatenate(parts, axis=1)

    @pl.when(step == steps - 1)
    def _():
        key_parts, value_parts = [], []
        for g in range(kv_heads):
            turned = grad_keys[g] * turns_ref[...]
            key_parts.append((turned[:, :HEAD_DIM] + turned[:, HEAD_DIM:]).astype(BF16))
            value_parts.append(grad_values[g].astype(BF16))
        grad_key_value_ref[...] = jnp.concatenate(key_parts + value_parts, axis=1)


def attention_specs(queries, keys_values, block_rows):
    return dict(
        smem=pl.BlockSpec(memory_space=pltpu.SMEM),
        rows=pl.BlockSpec((block_rows, queries.shape[1]), lambda i: (i, 0)),
        whole=pl.BlockSpec(keys_values.shape, lambda i: (0, 0)),
        column=pl.BlockSpec((block_rows, 1), lambda i: (i, 0)),
    )


def attention_forward(first, queries, keys_values, doc_start, block_rows=256, reach=1024):
    row_count, query_cols = queries.shape
    kv_heads = keys_values.shape[1] // (2 * HEAD_DIM)
    group_size = query_cols // HEAD_DIM // kv_heads
    steps = row_count // block_rows
    window = min(reach + block_rows, keys_values.shape[0])
    specs = attention_specs(queries, keys_values, block_rows)
    stacked = group_size * block_rows
    return pl.pallas_call(
        partial(attention_forward_kernel, group_size=group_size, window=window),
        grid=(steps,),
        in_specs=[specs["smem"], specs["rows"], specs["whole"], specs["column"]],
        out_specs=[
            specs["rows"],
            pl.BlockSpec((1, kv_heads, stacked, 1), lambda i: (i, 0, 0, 0)),
        ],
        out_shape=[
            jax.ShapeDtypeStruct(queries.shape, BF16),
            jax.ShapeDtypeStruct((steps, kv_heads, stacked, 1), F32),
        ],
        compiler_params=pltpu.CompilerParams(vmem_limit_bytes=48 * 2**20),
        cost_estimate=pl.CostEstimate(
            flops=4 * row_count * window * query_cols * 8, bytes_accessed=2**22, transcendentals=0
        ),
    )(first, queries, keys_values, doc_start)


def attention_backward(
    first, queries, keys_values, doc_start, lse, grads, turns, query_turns, block_rows=256, reach=1024
):
    row_count, query_cols = queries.shape
    kv_heads = keys_values.shape[1] // (2 * HEAD_DIM)
    group_size = query_cols // HEAD_DIM // kv_heads
    steps = row_count // block_rows
    window = min(reach + block_rows, keys_values.shape[0])
    specs = attention_specs(queries, keys_values, block_rows)
    stacked = group_size * block_rows
    return pl.pallas_call(
        partial(attention_backward_kernel, group_size=group_size, window=window, steps=steps),
        grid=(steps,),
        in_specs=[
            specs["smem"],
            specs["rows"],
            specs["whole"],
            specs["column"],
            pl.BlockSpec((1, kv_heads, stacked, 1), lambda i: (i, 0, 0, 0)),
            specs["rows"],
            pl.BlockSpec(turns.shape, lambda i: (0, 0)),
            pl.BlockSpec((block_rows, turns.shape[1]), lambda i: (i, 0)),
        ],
        out_specs=[specs["rows"], specs["whole"]],
        out_shape=[
            jax.ShapeDtypeStruct(queries.shape, BF16),
            jax.ShapeDtypeStruct(keys_values.shape, BF16),
        ],
        scratch_shapes=[
            pltpu.VMEM((kv_heads, keys_values.shape[0], 2 * HEAD_DIM), F32),
            pltpu.VMEM((kv_heads, keys_values.shape[0], HEAD_DIM), F32),
        ],
        compiler_params=pltpu.CompilerParams(vmem_limit_bytes=48 * 2**20),
        cost_estimate=pl.CostEstimate(
            flops=10 * row_count * window * query_cols * 8, bytes_accessed=2**23, transcendentals=0
        ),
    )(first, queries, keys_values, doc_start, lse, grads, turns, query_turns)


def rotation_tables(positions):
    half_dim = HEAD_DIM // 2
    frequencies = 10000.0 ** (-2.0 * jnp.arange(half_dim, dtype=F32) / HEAD_DIM)
    angles = positions.astype(F32)[:, None] * frequencies[None, :]
    cosine, sine = jnp.cos(angles), jnp.sin(angles)
    return jnp.concatenate([cosine, cosine, -sine, -sine], axis=1)


def turned_columns(weight):
    rows, cols = weight.shape
    halves = weight.reshape(rows, cols // HEAD_DIM, 2, HEAD_DIM // 2)
    return jnp.stack([-halves[:, :, 1], halves[:, :, 0]], axis=2).reshape(rows, cols)


def expert_plan(
    residual_in,
    gain_attn,
    query_weight,
    key_projection_weight,
    value_projection_weight,
    out_weight,
    gain_ffn,
    gate_weight,
    up_weight,
    down_weight,
    segments,
    routes,
    shares,
    cotangent,
    *,
    groups,
    tensor_size,
):
    row_count, model_width = residual_in.shape
    query_cols = query_weight.shape[1]
    kv_cols = key_projection_weight.shape[1]
    expert_count, slice_rows, unit_count = gate_weight.shape
    own_experts = expert_count // groups
    piece_rows = row_count // tensor_size
    first_count = own_experts * 2 // 5
    context_rank = lax.axis_index(CONTEXT)
    tensor_rank = lax.axis_index(TENSOR)
    group_rank = lax.axis_index(SHARD) * lax.axis_size(CONTEXT) + context_rank
    chip_half, core = tensor_rank // 2, tensor_rank % 2
    own_first = context_rank * row_count
    piece_first = tensor_rank * piece_rows
    sibling = [(i, i ^ 1) for i in range(tensor_size)]
    across = [(i, i ^ 2) for i in range(tensor_size)]
    pair = [(0, 1), (1, 0)]

    def own_piece(values):
        return lax.dynamic_slice_in_dim(values, piece_first, piece_rows)

    def pick(values, axis, index):
        return lax.dynamic_index_in_dim(values, index, axis, keepdims=False)

    def sum_over_tensor(parts):
        parts = parts.astype(BF16).reshape(2, 2, piece_rows, -1)
        received = lax.ppermute(pick(parts, 1, 1 - core), TENSOR, sibling)
        half = pick(parts, 1, core).astype(F32) + received.astype(F32)
        received = lax.ppermute(pick(half, 0, 1 - chip_half).astype(BF16), TENSOR, across)
        return pick(half, 0, chip_half) + received.astype(F32)

    def gather_over_tensor(piece):
        other = lax.ppermute(piece, TENSOR, across)
        chips = jnp.where(
            chip_half == 0, jnp.concatenate([piece, other]), jnp.concatenate([other, piece])
        ).reshape(2, 1, piece_rows, -1)
        others = lax.ppermute(chips, TENSOR, sibling)
        both = jnp.where(
            core == 0,
            jnp.concatenate([chips, others], axis=1),
            jnp.concatenate([others, chips], axis=1),
        )
        return both.reshape(row_count, -1)

    def padded_columns(*gains):
        columns = jnp.stack(gains, axis=1)
        return jnp.pad(columns, ((0, 0), (0, 128 - len(gains))))

    with jax.named_scope("weights"):
        lanes = 3 * unit_count

        def slices(first, count):
            return jnp.concatenate(
                [
                    weight.reshape((groups, own_experts) + weight.shape[1:])[:, first : first + count]
                    for weight in (gate_weight, up_weight, down_weight.transpose(0, 2, 1))
                ],
                axis=3,
            ).reshape(groups * count, slice_rows, lanes)

        def to_groups(values):
            owned = lax.all_to_all(values, GROUP, 0, 0, tiled=True)
            return owned.reshape(groups, -1, slice_rows, lanes)

        slices_first, slices_second = lax.optimization_barrier(
            (slices(0, first_count), slices(first_count, own_experts - first_count))
        )
        owned_first, owned_second = to_groups(slices_first), to_groups(slices_second)

        qkv_full = lax.all_gather(
            jnp.concatenate(
                [
                    query_weight,
                    key_projection_weight,
                    value_projection_weight,
                    out_weight.T,
                    padded_columns(gain_attn, gain_ffn),
                ],
                axis=1,
            ),
            GROUP,
            axis=0,
            tiled=True,
        )
        qkv_cols = query_cols + 2 * kv_cols
        owned_first, qkv_full = lax.optimization_barrier((owned_first, qkv_full))
        others_first = lax.ppermute(owned_first, TENSOR, across)
        qkv_weight = qkv_full[:, :qkv_cols]
        out_transposed = qkv_full[:, qkv_cols : qkv_cols + query_cols]
        gain_attn_float = qkv_full[:, qkv_cols + query_cols].astype(F32)
        gain_ffn_float = qkv_full[:, qkv_cols + query_cols + 1].astype(F32)


    with jax.named_scope("cotangents"):
        cotangent_piece = own_piece(cotangent)
        spread = jnp.sum(
            jnp.where(
                own_piece(routes)[:, :, None] == jnp.arange(expert_count, dtype=jnp.int32),
                own_piece(shares)[:, :, None],
                0.0,
            ),
            axis=1,
        )
        spread_high = spread.astype(BF16)
        spread_low = (spread - spread_high.astype(F32)).astype(BF16)
        spread_both = jnp.pad(
            jnp.concatenate([spread_high, spread_low], axis=1),
            ((0, 0), (0, 128 - 2 * expert_count)),
        )
        cotangent_own = lax.all_gather(
            jnp.concatenate([cotangent_piece, spread_both], axis=1), GROUP, axis=0, tiled=False
        )

    with jax.named_scope("attention"):
        positions = doc_positions(segments)
        turns = rotation_tables(positions)
        own_turns = lax.dynamic_slice_in_dim(turns, own_first, row_count)
        own_index = own_first + jnp.arange(row_count, dtype=jnp.int32)
        doc_start = own_index - lax.dynamic_slice_in_dim(positions, own_first, row_count)
        input_float = residual_in.astype(F32)
        first_normalized = rms_scale(input_float, gain_attn_float).astype(BF16)
        rotated_cols = query_cols + kv_cols
        projected = jnp.dot(
            first_normalized,
            jnp.concatenate([qkv_weight, turned_columns(qkv_weight[:, :rotated_cols])], axis=1),
            preferred_element_type=F32,
        )
        heads = rotated_cols // HEAD_DIM
        rotated = (
            projected[:, :rotated_cols] * jnp.tile(own_turns[:, :HEAD_DIM], (1, heads))
            - projected[:, qkv_cols:] * jnp.tile(own_turns[:, HEAD_DIM:], (1, heads))
        ).astype(BF16)
        queries = rotated[:, :query_cols]
        own_keys_values = jnp.concatenate(
            [rotated[:, query_cols:], projected[:, rotated_cols:qkv_cols].astype(BF16)], axis=1
        )
        other_keys_values = lax.ppermute(own_keys_values, CONTEXT, pair)
        keys_values = jnp.where(
            context_rank == 0,
            jnp.concatenate([own_keys_values, other_keys_values]),
            jnp.concatenate([other_keys_values, own_keys_values]),
        )
        first = own_first.reshape(1).astype(jnp.int32)
        attended, lse = attention_forward(first, queries, keys_values, doc_start[:, None])
        attn_part = lax.dot_general(
            attended, out_transposed, LAST_LAST, preferred_element_type=F32
        )
        attn_piece = sum_over_tensor(attn_part)
        others_first, owned_second, attn_piece = lax.optimization_barrier(
            (others_first, owned_second, attn_piece)
        )
        hidden = own_piece(residual_in).astype(F32) + attn_piece
        normed_ffn, ffn_norm_back = jax.vjp(rms_scale, hidden, gain_ffn_float)

    with jax.named_scope("exchange"):
        cotangent_own, normed_ffn = lax.optimization_barrier((cotangent_own, normed_ffn))
        spread_own = cotangent_own[:, :, model_width:]
        spread_all = jnp.concatenate(
            [spread_own, lax.ppermute(spread_own, TENSOR, sibling)], axis=1
        )

        def shares_of(first, count):
            start = group_rank * own_experts + first
            high = lax.dynamic_slice_in_dim(spread_all, start, count, axis=2)
            low = lax.dynamic_slice_in_dim(spread_all, start + expert_count, count, axis=2)
            total = high.astype(F32) + low.astype(F32)
            return jnp.pad(total, ((0, 0), (0, 0), (0, 8 - count)))

        shares_first = shares_of(0, first_count)
        shares_second = shares_of(first_count, own_experts - first_count)

    with jax.named_scope("experts"):
        line = groups // 2
        parts, grad_own_first, grad_other_first, tokens, others_second, cotangent_other = (
            experts_gathering(
                normed_ffn.astype(BF16),
                cotangent_own,
                shares_first,
                owned_first,
                others_first,
                owned_second,
                line,
            )
        )
        grad_second, out_piece, grad_own_second, grad_other_second, received_first = (
            experts_reducing(
                tokens,
                (cotangent_own, cotangent_other),
                shares_second,
                owned_second,
                others_second,
                grad_other_first,
                parts,
                line,
            )
        )

    with jax.named_scope("expert_grads"):

        def added(own, received):
            return (own.astype(F32) + received.astype(F32)).astype(BF16)

        def returned(total):
            flat = total.reshape((total.shape[0] * total.shape[1],) + total.shape[2:])
            return lax.all_to_all(flat, GROUP, 0, 0, tiled=True).reshape(total.shape)

        total_first = added(grad_own_first, received_first)
        received_second = lax.ppermute(grad_other_second, TENSOR, across)
        total_first, grad_second = lax.optimization_barrier((total_first, grad_second))
        returned_first = returned(total_first)
        grad_hidden_norm, grad_gain_ffn_local = ffn_norm_back(grad_second.astype(F32))
        grad_hidden = cotangent_piece.astype(F32) + grad_hidden_norm
        grad_hidden_low = gather_over_tensor(grad_hidden.astype(BF16))
        output = gather_over_tensor((hidden + out_piece.astype(F32)).astype(BF16))

    with jax.named_scope("attention_back"):
        grad_out_local = lax.dot_general(
            grad_hidden_low, attended, FIRST_FIRST, preferred_element_type=F32
        )
        grad_out_transposed = lax.psum_scatter(
            grad_out_local.astype(BF16), GROUP, scatter_dimension=0, tiled=True
        )
        grad_attended = jnp.dot(grad_hidden_low, out_transposed, preferred_element_type=F32)
        returned_first, grad_attended = lax.optimization_barrier((returned_first, grad_attended))
        grad_query_lin, grad_key_value = attention_backward(
            first,
            queries,
            keys_values,
            doc_start[:, None],
            lse,
            grad_attended.astype(BF16),
            turns,
            own_turns,
        )
        total_second = added(grad_own_second, received_second)
        grad_key_value = grad_key_value.reshape(2, row_count, -1)
        received = lax.ppermute(pick(grad_key_value, 0, 1 - context_rank), CONTEXT, pair)
        grad_key_value = (
            pick(grad_key_value, 0, context_rank).astype(F32) + received.astype(F32)
        ).astype(BF16)
        grad_projected = jnp.concatenate([grad_query_lin, grad_key_value], axis=1)
        grad_first_part = lax.dot_general(
            grad_projected, qkv_weight, LAST_LAST, preferred_element_type=F32
        )
        grad_qkv_local = lax.dot_general(
            first_normalized, grad_projected, FIRST_FIRST, preferred_element_type=F32
        ).astype(BF16)
        total_second, grad_out_transposed, grad_first_part, grad_qkv_local = (
            lax.optimization_barrier(
                (total_second, grad_out_transposed, grad_first_part, grad_qkv_local)
            )
        )
        returned_second = returned(total_second)
        grad_first = sum_over_tensor(grad_first_part)
        _, attn_norm_back = jax.vjp(
            rms_scale, own_piece(residual_in).astype(F32), gain_attn_float
        )
        grad_input_norm, grad_gain_attn_local = attn_norm_back(grad_first)
        grad_input = gather_over_tensor((grad_hidden + grad_input_norm).astype(BF16))
        grad_qkv = lax.psum_scatter(grad_qkv_local, GROUP, scatter_dimension=0, tiled=True)
        gains = jnp.stack([grad_gain_attn_local, grad_gain_ffn_local])
        for axis, step, size in (
            (TENSOR, 1, tensor_size),
            (TENSOR, 2, tensor_size),
            (CONTEXT, 1, 2),
            (SHARD, 1, groups // 2),
            (SHARD, 2, groups // 2),
        ):
            gains = gains + lax.ppermute(gains, axis, [(i, i ^ step) for i in range(size)])
        gains = lax.dynamic_slice_in_dim(gains, group_rank * slice_rows, slice_rows, axis=1)

    returned_second, grad_qkv, gains, grad_input, output = lax.optimization_barrier(
        (returned_second, grad_qkv, gains, grad_input, output)
    )
    grad_qkv = grad_qkv.astype(F32)

    def whole(first, last, turned):
        parts = [
            part[..., first:last].transpose(0, 1, 3, 2) if turned else part[..., first:last]
            for part in (returned_first, returned_second)
        ]
        joined = jnp.concatenate(parts, axis=1).astype(F32)
        return joined.reshape((expert_count,) + joined.shape[2:])

    units = unit_count
    return (
        output,
        grad_input,
        gains[0],
        grad_qkv[:, :query_cols],
        grad_qkv[:, query_cols:rotated_cols],
        grad_qkv[:, rotated_cols:qkv_cols],
        grad_out_transposed.astype(F32).T,
        gains[1],
        whole(0, units, False),
        whole(units, 2 * units, False),
        whole(2 * units, 3 * units, True),
    )


def solution(mesh):
    placed = (
        P(GROUP, None),
        P(GROUP),
        P(GROUP, TENSOR),
        P(GROUP, TENSOR),
        P(GROUP, TENSOR),
        P(TENSOR, GROUP),
        P(GROUP),
        P(None, GROUP, TENSOR),
        P(None, GROUP, TENSOR),
        P(None, TENSOR, GROUP),
        P(SHARD),
        P(GROUP, None),
        P(GROUP, None),
        P(GROUP, None),
    )
    sizes = dict(mesh.shape)
    if sizes[SHARD] == 4 and sizes[CONTEXT] == 2 and sizes[TENSOR] == 4:
        plan = partial(
            expert_plan, groups=sizes[SHARD] * sizes[CONTEXT], tensor_size=sizes[TENSOR]
        )
    else:
        plan = gathered_plan
    return jax.shard_map(
        plan,
        mesh=mesh,
        in_specs=placed,
        out_specs=(
            P(GROUP, None),
            P(GROUP, None),
            P(GROUP),
            P(GROUP, TENSOR),
            P(GROUP, TENSOR),
            P(GROUP, TENSOR),
            P(TENSOR, GROUP),
            P(GROUP),
            P(None, GROUP, TENSOR),
            P(None, GROUP, TENSOR),
            P(None, TENSOR, GROUP),
        ),
        check_vma=False,
    )
```

```python
from functools import partial

import jax
import jax.numpy as jnp
from jax import lax
from jax.experimental import pallas as pl
from jax.experimental.pallas import tpu as pltpu
from jax.sharding import PartitionSpec as P

HEAD_DIM = 64
NDOCS = 5
SHARD = "shard"
CONTEXT = "context"
TENSOR = "tensor"
GROUP = (SHARD, CONTEXT)
PRODUCT_0 = "qgrd,kgd->grqk"
PRODUCT_1 = "grqk,kgd->qgrd"
PRODUCT_2 = "ecd,edf->ecf"
PRODUCT_3 = "ecf,efd->ecd"
PRODUCT_4 = "ecd,efd->ecf"
PRODUCT_5 = "ecf,edf->ecd"
PRODUCT_6 = "ecd,ecf->edf"
PRODUCT_7 = "ecf,ecd->efd"
PRODUCT_8 = "grqk,qgrd->kgd"


epsilon = 1e-06


def rms_scale(values, gain):
    return values * lax.rsqrt(jnp.mean(values * values, axis=-1, keepdims=True) + epsilon) * gain


def doc_positions(segment_ids):
    sequence_length = segment_ids.shape[-1]
    index_row = jnp.arange(sequence_length, dtype=jnp.int32)
    documents = jnp.arange(NDOCS, dtype=jnp.int32)
    doc_starts = jnp.sum((segment_ids[..., :, None] < documents).astype(jnp.int32), axis=-2)
    own_start = jnp.sum(
        jnp.where(segment_ids[..., :, None] == documents, doc_starts[..., None, :], 0), axis=-1
    )
    return index_row - own_start


def rotary(values, positions):
    half_dim = values.shape[-1] // 2
    frequencies = 10000.0 ** (-2.0 * jnp.arange(half_dim, dtype=jnp.float32) / values.shape[-1])
    angles = positions.astype(jnp.float32)[:, None] * frequencies[None, :]
    cosine = jnp.cos(angles)[:, None, :]
    sines = jnp.sin(angles)[:, None, :]
    first_half = values[..., :half_dim]
    second_half = values[..., half_dim:]
    return jnp.concatenate(
        [first_half * cosine - second_half * sines, second_half * cosine + first_half * sines],
        axis=-1,
    )


def swiglu(gate_value, up_value):
    return jax.nn.silu(gate_value) * up_value


def dispatch(routes, shares, block_rows, capacity, expert_count):
    block_count = routes.shape[0] // block_rows
    picks = routes.shape[1]
    chosen = routes.reshape(block_count, block_rows * picks)
    onehot = (chosen[:, :, None] == jnp.arange(expert_count, dtype=jnp.int32)).astype(jnp.int32)
    ranked = jnp.sum((jnp.cumsum(onehot, axis=1) - onehot) * onehot, axis=2)
    slot_index = (
        chosen * (block_count * capacity)
        + jnp.arange(block_count, dtype=jnp.int32)[:, None] * capacity
        + ranked
    )
    tokens = jnp.arange(block_count * block_rows * picks, dtype=jnp.int32) // picks
    total_slots = expert_count * block_count * capacity
    slot_rows = jnp.zeros((total_slots,), jnp.int32).at[slot_index.reshape(-1)].set(tokens)
    slot_share = (
        jnp.zeros((total_slots,), jnp.float32).at[slot_index.reshape(-1)].set(shares.reshape(-1))
    )
    return (slot_rows, slot_share)


def gathered_plan(
    residual_in,
    gain_attn,
    query_weight,
    key_projection_weight,
    value_projection_weight,
    out_weight,
    gain_ffn,
    gate_weight,
    up_weight,
    down_weight,
    segments,
    routes,
    shares,
    cotangent,
):
    row_count, model_width = residual_in.shape
    head_size = HEAD_DIM
    query_cols = query_weight.shape[1]
    kv_heads = key_projection_weight.shape[1] // head_size
    group_size = query_cols // head_size // kv_heads
    expert_count = gate_weight.shape[0]
    capacity = row_count * routes.shape[1] * 5 // (4 * expert_count)
    score_scale = head_size ** (-0.5)
    context_rank = lax.axis_index(CONTEXT)
    own_first = context_rank * row_count
    gain_attn_full, gain_ffn_full, query_full, key_full, value_full, out_full = (
        lax.all_gather(gain_attn, GROUP, axis=0, tiled=True),
        lax.all_gather(gain_ffn, GROUP, axis=0, tiled=True),
        lax.all_gather(query_weight, GROUP, axis=0, tiled=True),
        lax.all_gather(key_projection_weight, GROUP, axis=0, tiled=True),
        lax.all_gather(value_projection_weight, GROUP, axis=0, tiled=True),
        lax.all_gather(out_weight, GROUP, axis=1, tiled=True),
    )
    gain_attn_float = gain_attn_full.astype(jnp.float32)
    gain_ffn_float = gain_ffn_full.astype(jnp.float32)
    positions = doc_positions(segments)
    own_positions = lax.dynamic_slice_in_dim(positions, own_first, row_count)
    own_ids = lax.dynamic_slice_in_dim(segments, own_first, row_count)
    own_index = own_first + jnp.arange(row_count, dtype=jnp.int32)
    input_float = residual_in.astype(jnp.float32)
    normed_attn, attn_norm_back = jax.vjp(rms_scale, input_float, gain_attn_float)
    first_normalized = normed_attn.astype(jnp.bfloat16)
    query_lin = jnp.dot(first_normalized, query_full, preferred_element_type=jnp.float32).reshape(
        row_count, -1, head_size
    )
    key_linear = jnp.dot(first_normalized, key_full, preferred_element_type=jnp.float32).reshape(
        row_count, -1, head_size
    )
    value_tokens = jnp.dot(first_normalized, value_full, preferred_element_type=jnp.float32).astype(
        jnp.bfloat16
    )
    rope_local = partial(rotary, positions=own_positions)
    query_rot, rope_query_back = jax.vjp(rope_local, query_lin)
    key_rot, rope_key_back = jax.vjp(rope_local, key_linear)
    query_low = query_rot.astype(jnp.bfloat16)
    key_low = key_rot.astype(jnp.bfloat16).reshape(row_count, -1)
    key_all, value_all = (
        lax.all_gather(key_low, CONTEXT, axis=0, tiled=True),
        lax.all_gather(value_tokens, CONTEXT, axis=0, tiled=True),
    )
    key_index = jnp.arange(key_all.shape[0], dtype=jnp.int32)
    key_ids = jnp.take(segments, jnp.clip(key_index, 0, segments.shape[0] - 1))
    key_valid = key_index >= 0
    key_heads = key_all.reshape(-1, kv_heads, head_size)
    value_heads = value_all.reshape(-1, kv_heads, head_size)
    query_heads = query_low.reshape(row_count, kv_heads, group_size, head_size)
    block_rows = min(512, row_count)
    block_starts = list(range(0, row_count, block_rows))

    def block_scores(block_first):
        query_block = query_heads[block_first : block_first + block_rows]
        raw_scores = jnp.einsum(
            PRODUCT_0, query_block, key_heads, preferred_element_type=jnp.float32
        )
        block_ids = own_ids[block_first : block_first + block_rows]
        block_index = own_index[block_first : block_first + block_rows]
        allowed = (
            key_valid[None, :]
            & (key_ids[None, :] == block_ids[:, None])
            & (key_index[None, :] <= block_index[:, None])
        )
        return (query_block, jnp.where(allowed, raw_scores * score_scale, -1e30))

    mixed_parts = []
    lse_parts = []
    for block_first in block_starts:
        query_block, scores = block_scores(block_first)
        row_max = jnp.max(scores, axis=-1, keepdims=True)
        exponent = jnp.exp(scores - row_max)
        row_total = jnp.sum(exponent, axis=-1, keepdims=True)
        probs = (exponent / row_total).astype(jnp.bfloat16)
        mixed_parts.append(
            jnp.einsum(PRODUCT_1, probs, value_heads, preferred_element_type=jnp.float32)
        )
        lse_parts.append(row_max + jnp.log(row_total))
    attended = (
        jnp.concatenate(mixed_parts, axis=0).reshape(row_count, query_cols).astype(jnp.bfloat16)
    )
    attn_part = jnp.dot(attended, out_full, preferred_element_type=jnp.float32)
    hidden = input_float + lax.psum(attn_part.astype(jnp.bfloat16), TENSOR).astype(jnp.float32)
    normed_ffn, ffn_norm_back = jax.vjp(rms_scale, hidden, gain_ffn_float)
    normed_second = normed_ffn.astype(jnp.bfloat16)
    slot_rows, slot_share = dispatch(routes, shares, row_count, capacity, expert_count)
    per_turn = expert_count // 5
    turn_count = expert_count // per_turn
    turn_slots = per_turn * capacity

    def local_experts(turn_index):
        gate_part = lax.dynamic_slice_in_dim(gate_weight, turn_index * per_turn, per_turn, 0)
        up_part = lax.dynamic_slice_in_dim(up_weight, turn_index * per_turn, per_turn, 0)
        down_part = lax.dynamic_slice_in_dim(down_weight, turn_index * per_turn, per_turn, 0)
        return (gate_part, up_part, down_part)

    def turn_inputs(turn_index):
        token_rows = lax.dynamic_slice_in_dim(slot_rows, turn_index * turn_slots, turn_slots)
        share_rows = lax.dynamic_slice_in_dim(slot_share, turn_index * turn_slots, turn_slots)
        picked = normed_second[token_rows].reshape(per_turn, capacity, model_width)
        return (token_rows, share_rows, picked)

    def forward_turn(running, turn_index):
        gate_part, up_part, down_part = local_experts(turn_index)
        gate_full, up_full, down_full = (
            lax.all_gather(gate_part, GROUP, axis=1, tiled=True),
            lax.all_gather(up_part, GROUP, axis=1, tiled=True),
            lax.all_gather(down_part, GROUP, axis=2, tiled=True),
        )
        token_rows, share_rows, picked = turn_inputs(turn_index)
        gate_value = jnp.einsum(
            PRODUCT_2, picked, gate_full, preferred_element_type=jnp.float32
        )
        up_value = jnp.einsum(PRODUCT_2, picked, up_full, preferred_element_type=jnp.float32)
        inner = swiglu(gate_value, up_value).astype(jnp.bfloat16)
        expert_result = jnp.einsum(
            PRODUCT_3, inner, down_full, preferred_element_type=jnp.float32
        ).reshape(turn_slots, model_width)
        return (running.at[token_rows].add(expert_result * share_rows[:, None]), None)

    turn_ids = jnp.arange(turn_count, dtype=jnp.int32)
    expert_part, _ = lax.scan(
        forward_turn, jnp.zeros((row_count, model_width), jnp.float32), turn_ids
    )
    expert_total = lax.psum(expert_part.astype(jnp.bfloat16), TENSOR).astype(jnp.float32)
    output = (hidden + expert_total).astype(jnp.bfloat16)
    upstream = cotangent.astype(jnp.float32)

    def backward_turn(running, turn_index):
        gate_part, up_part, down_part = local_experts(turn_index)
        gate_full, up_full, down_full = (
            lax.all_gather(gate_part, GROUP, axis=1, tiled=True),
            lax.all_gather(up_part, GROUP, axis=1, tiled=True),
            lax.all_gather(down_part, GROUP, axis=2, tiled=True),
        )
        token_rows, share_rows, picked = turn_inputs(turn_index)
        gate_value = jnp.einsum(
            PRODUCT_2, picked, gate_full, preferred_element_type=jnp.float32
        )
        up_value = jnp.einsum(PRODUCT_2, picked, up_full, preferred_element_type=jnp.float32)
        inner_float, swiglu_back = jax.vjp(swiglu, gate_value, up_value)
        inner = inner_float.astype(jnp.bfloat16)
        grad_slot = (
            (upstream[token_rows] * share_rows[:, None])
            .astype(jnp.bfloat16)
            .reshape(per_turn, capacity, model_width)
        )
        grad_inner = jnp.einsum(
            PRODUCT_4, grad_slot, down_full, preferred_element_type=jnp.float32
        )
        grad_gate_value, grad_up_value = swiglu_back(grad_inner)
        grad_gate_low = grad_gate_value.astype(jnp.bfloat16)
        grad_up_low = grad_up_value.astype(jnp.bfloat16)
        grad_picked = jnp.einsum(
            PRODUCT_5, grad_gate_low, gate_full, preferred_element_type=jnp.float32
        )
        grad_picked = grad_picked + jnp.einsum(
            PRODUCT_5, grad_up_low, up_full, preferred_element_type=jnp.float32
        )
        running = running.at[token_rows].add(grad_picked.reshape(turn_slots, model_width))
        shard_grads = (
            lax.psum_scatter(
                jnp.einsum(
                    PRODUCT_6, picked, grad_gate_low, preferred_element_type=jnp.float32
                ).astype(jnp.bfloat16),
                GROUP,
                scatter_dimension=1,
                tiled=True,
            ).astype(jnp.float32),
            lax.psum_scatter(
                jnp.einsum(
                    PRODUCT_6, picked, grad_up_low, preferred_element_type=jnp.float32
                ).astype(jnp.bfloat16),
                GROUP,
                scatter_dimension=1,
                tiled=True,
            ).astype(jnp.float32),
            lax.psum_scatter(
                jnp.einsum(
                    PRODUCT_7, inner, grad_slot, preferred_element_type=jnp.float32
                ).astype(jnp.bfloat16),
                GROUP,
                scatter_dimension=2,
                tiled=True,
            ).astype(jnp.float32),
        )
        return (running, shard_grads)

    grad_second_part, stacked_grads = lax.scan(
        backward_turn, jnp.zeros((row_count, model_width), jnp.float32), turn_ids
    )
    grad_gate_out = stacked_grads[0].reshape(gate_weight.shape)
    grad_up_out = stacked_grads[1].reshape(up_weight.shape)
    grad_down_out = stacked_grads[2].reshape(down_weight.shape)
    grad_second = lax.psum(grad_second_part.astype(jnp.bfloat16), TENSOR).astype(jnp.float32)
    grad_hidden_norm, grad_gain_ffn_local = ffn_norm_back(grad_second)
    grad_hidden = upstream + grad_hidden_norm
    grad_hidden_low = grad_hidden.astype(jnp.bfloat16)
    grad_out_local = jnp.einsum(
        "tc,td->cd", attended, grad_hidden_low, preferred_element_type=jnp.float32
    )
    grad_attended = jnp.einsum(
        "td,cd->tc", grad_hidden_low, out_full, preferred_element_type=jnp.float32
    )
    grad_attended = grad_attended.astype(jnp.bfloat16).reshape(
        row_count, kv_heads, group_size, head_size
    )
    grad_query_parts = []
    grad_keys = jnp.zeros(key_heads.shape, jnp.float32)
    grad_values = jnp.zeros(value_heads.shape, jnp.float32)
    for block_number in range(len(block_starts)):
        block_first = block_starts[block_number]
        query_block, scores = block_scores(block_first)
        probs_float = jnp.exp(scores - lse_parts[block_number])
        probs = probs_float.astype(jnp.bfloat16)
        grad_block = grad_attended[block_first : block_first + block_rows]
        grad_probs = jnp.einsum(
            PRODUCT_0, grad_block, value_heads, preferred_element_type=jnp.float32
        )
        inner_sum = jnp.sum(grad_probs * probs_float, axis=-1, keepdims=True)
        grad_scores = (score_scale * (probs_float * (grad_probs - inner_sum))).astype(jnp.bfloat16)
        grad_query_parts.append(
            jnp.einsum(PRODUCT_1, grad_scores, key_heads, preferred_element_type=jnp.float32)
        )
        grad_keys = grad_keys + jnp.einsum(
            PRODUCT_8, grad_scores, query_block, preferred_element_type=jnp.float32
        )
        grad_values = grad_values + jnp.einsum(
            PRODUCT_8, probs, grad_block, preferred_element_type=jnp.float32
        )
    grad_key_own, grad_value_own = (
        lax.psum_scatter(
            grad_keys.astype(jnp.bfloat16), CONTEXT, scatter_dimension=0, tiled=True
        ).astype(jnp.float32),
        lax.psum_scatter(
            grad_values.astype(jnp.bfloat16), CONTEXT, scatter_dimension=0, tiled=True
        ).astype(jnp.float32),
    )
    grad_query_all = jnp.concatenate(grad_query_parts, axis=0).reshape(row_count, -1, head_size)
    grad_query_lin = rope_query_back(grad_query_all)[0].astype(jnp.bfloat16).reshape(row_count, -1)
    grad_key_lin = rope_key_back(grad_key_own)[0].astype(jnp.bfloat16).reshape(row_count, -1)
    grad_value_low = grad_value_own.astype(jnp.bfloat16).reshape(row_count, -1)
    grad_first_part = jnp.einsum(
        "tc,dc->td", grad_query_lin, query_full, preferred_element_type=jnp.float32
    )
    grad_first_part = grad_first_part + jnp.einsum(
        "tc,dc->td", grad_key_lin, key_full, preferred_element_type=jnp.float32
    )
    grad_first_part = grad_first_part + jnp.einsum(
        "tc,dc->td", grad_value_low, value_full, preferred_element_type=jnp.float32
    )
    grad_first = lax.psum(grad_first_part.astype(jnp.bfloat16), TENSOR).astype(jnp.float32)
    grad_input_norm, grad_gain_attn_local = attn_norm_back(grad_first)
    grad_input = (grad_hidden + grad_input_norm).astype(jnp.bfloat16)
    grad_query_local = jnp.einsum(
        "td,tc->dc", first_normalized, grad_query_lin, preferred_element_type=jnp.float32
    )
    grad_key_local = jnp.einsum(
        "td,tc->dc", first_normalized, grad_key_lin, preferred_element_type=jnp.float32
    )
    grad_value_local = jnp.einsum(
        "td,tc->dc", first_normalized, grad_value_low, preferred_element_type=jnp.float32
    )
    reduced = (
        lax.psum_scatter(
            grad_gain_attn_local.astype(jnp.bfloat16),
            GROUP,
            scatter_dimension=0,
            tiled=True,
        ).astype(jnp.float32),
        lax.psum_scatter(
            grad_query_local.astype(jnp.bfloat16),
            GROUP,
            scatter_dimension=0,
            tiled=True,
        ).astype(jnp.float32),
        lax.psum_scatter(
            grad_key_local.astype(jnp.bfloat16),
            GROUP,
            scatter_dimension=0,
            tiled=True,
        ).astype(jnp.float32),
        lax.psum_scatter(
            grad_value_local.astype(jnp.bfloat16),
            GROUP,
            scatter_dimension=0,
            tiled=True,
        ).astype(jnp.float32),
        lax.psum_scatter(
            grad_out_local.astype(jnp.bfloat16),
            GROUP,
            scatter_dimension=1,
            tiled=True,
        ).astype(jnp.float32),
        lax.psum_scatter(
            grad_gain_ffn_local.astype(jnp.bfloat16),
            GROUP,
            scatter_dimension=0,
            tiled=True,
        ).astype(jnp.float32),
    )
    return (
        output,
        grad_input,
        reduced[0],
        reduced[1],
        reduced[2],
        reduced[3],
        reduced[4],
        reduced[5],
        grad_gate_out,
        grad_up_out,
        grad_down_out,
    )


F32 = jnp.float32
BF16 = jnp.bfloat16
LAST_LAST = (((1,), (1,)), ((), ()))
FIRST_FIRST = (((0,), (0,)), ((), ()))


def weight_copies(own_hbm, other_hbm, weights, sems):
    sources, _, rows, lanes = own_hbm.shape
    units = lanes // 3
    return [
        pltpu.make_async_copy(
            half_hbm.at[source, :, :, pl.ds(part * units, units)],
            weights.at[
                :, pl.ds(source * rows, rows), pl.ds((2 * part + half) * units, units)
            ],
            sems.at[source, half, part],
        )
        for source in range(sources)
        for half, half_hbm in enumerate((own_hbm, other_hbm))
        for part in range(3)
    ]


def project(tokens, cotangent, weights):
    hidden_units = weights.shape[1] // 3
    gate_up = jnp.dot(tokens, weights[:, : 2 * hidden_units], preferred_element_type=F32)
    grad_inner = jnp.dot(cotangent, weights[:, 2 * hidden_units :], preferred_element_type=F32)
    return gate_up, grad_inner


def activate(gate_up, grad_inner, share):
    hidden_units = grad_inner.shape[1]
    gate, up = gate_up[:, :hidden_units], gate_up[:, hidden_units:]
    sigmoid = 1.0 / (1.0 + jnp.exp(-gate))
    silu = gate * sigmoid
    grad_inner = grad_inner * share
    inner = silu * up * share
    grad_gate = grad_inner * up * (sigmoid * (1.0 + gate * (1.0 - sigmoid)))
    grad_up = grad_inner * silu
    return inner.astype(BF16), grad_gate.astype(BF16), grad_up.astype(BF16)


MESH_ID = pl.DeviceIdType.MESH


class Place:
    def __init__(self, line):
        self.line = line
        self.z, self.y = lax.axis_index(SHARD), lax.axis_index(CONTEXT)
        self.t = lax.axis_index(TENSOR)
        self.sibling = (self.z, self.y, self.t + 1 - 2 * (self.t % 2))
        self.partner = (self.z, 1 - self.y, self.t)
        self.across = (self.z, self.y, (self.t + 2) % 4)

    def beside(self, side):
        return (self.z + side, self.y, self.t)

    def inside(self, at):
        return (at >= 0) & (at < self.line)

    def near(self, rank):
        z, line = self.z, self.line
        half = z // 2
        mirrored = z * (1 - half) + (line - 1 - z) * half
        far = rank // 2
        place = (1 - far) * (mirrored + rank - 2 * mirrored * rank) + far * rank
        return place * (1 - half) + (line - 1 - place) * half

    def block(self, order, step):
        rank, across = order[0]
        for number, (later_rank, later_across) in enumerate(order[1:], 1):
            rank = jnp.where(step == number, later_rank, rank)
            across = jnp.where(step == number, later_across, across)
        column = self.y + across - 2 * self.y * across
        return self.near(rank) * 2 + column

    def meet(self):
        z, line = self.z, self.line
        barrier = pltpu.get_barrier_semaphore()
        for device in (self.sibling, self.partner, self.across):
            pl.semaphore_signal(barrier, inc=1, device_id=device, device_id_type=MESH_ID)
        for side in (-1, 1):

            @pl.when(self.inside(z + side))
            def _():
                pl.semaphore_signal(
                    barrier, inc=1, device_id=self.beside(side), device_id_type=MESH_ID
                )

        below, above = (z + line - 1) // line, (2 * line - 2 - z) // line
        pl.semaphore_wait(barrier, 3 + below + above)


def remote(source, target, send, recv, device):
    return pltpu.make_async_remote_copy(
        src_ref=source,
        dst_ref=target,
        send_sem=send,
        recv_sem=recv,
        device_id=device,
        device_id_type=MESH_ID,
    )


class Gather:
    order = ((0, 0), (1, 0), (0, 1), (2, 0), (1, 1), (3, 0), (2, 1), (3, 1))
    rounds = (0, 2, 4)
    crossings = (1, 3, 5, 6)

    def __init__(self, place, tokens, sems):
        self.place, self.tokens = place, tokens
        self.recv, self.along, self.across, self.cores = sems

    def line_copy(self, at, side):
        here, tokens = at * 2 + self.place.y, self.tokens
        return remote(
            tokens.at[here, 0],
            tokens.at[here, 0],
            self.along.at[at, (side + 1) // 2],
            self.recv.at[here, 0],
            self.place.beside(side),
        )

    def pair_copy(self, at, column):
        here, tokens = at * 2 + column, self.tokens
        return remote(
            tokens.at[here, 0],
            tokens.at[here, 0],
            self.across.at[at],
            self.recv.at[here, 0],
            self.place.partner,
        )

    def core_copy(self, here):
        tokens = self.tokens
        return remote(
            tokens.at[here, 0],
            tokens.at[here, 1],
            self.cores.at[here],
            self.recv.at[here, 1],
            self.place.sibling,
        )

    def start(self):
        place = self.place
        for side in (-1, 1):
            pl.when(place.inside(place.z + side))(lambda: self.line_copy(place.z, side).start())
        self.pair_copy(place.z, place.y).start()
        self.core_copy(place.z * 2 + place.y).start()

    def came_along(self, at, side):
        place = self.place
        self.line_copy(at, -side).wait_recv()
        pl.when(place.inside(place.z - side))(lambda: self.line_copy(at, -side).start())
        self.pair_copy(at, place.y).start()
        self.core_copy(at * 2 + place.y).start()

    def came_across(self, at):
        column = 1 - self.place.y
        self.pair_copy(at, column).wait_recv()
        self.core_copy(at * 2 + column).start()

    def tick(self, number):
        place = self.place
        for distance, when in enumerate(self.rounds, 1):

            @pl.when(number == when)
            def _():
                for side in (-1, 1):
                    at = place.z + side * distance
                    pl.when(place.inside(at))(partial(self.came_along, at, side))

        for distance, when in enumerate(self.crossings):

            @pl.when(number == when)
            def _():
                for side in (-1, 1) if distance else (1,):
                    at = place.z + side * distance
                    pl.when(place.inside(at))(partial(self.came_across, at))

    def finish(self):
        place = self.place
        for side in (-1, 1):
            for distance in range(place.line):
                at = place.z - side * distance

                @pl.when(place.inside(at) & place.inside(place.z + side))
                def _():
                    self.line_copy(at, side).wait_send()

        for at in range(place.line):
            self.pair_copy(at, place.y).wait_send()
        for here in range(2 * place.line):
            self.core_copy(here).wait_send()


class Reduce:
    order = ((3, 1), (3, 0), (2, 1), (2, 0), (1, 1), (1, 0), (0, 1), (0, 0))

    def __init__(self, place, arrays, terms, term_sems, sums, base, sems):
        self.place, self.terms, self.term_sems = place, terms, term_sems
        self.sums, self.base = sums, base
        self.parts, self.from_core, self.from_pair, self.from_line = arrays
        self.core_send, self.core_recv, self.pair_send, self.pair_recv = sems[:4]
        self.line_send, self.line_recv = sems[4:]

    def core_copy(self, here, source):
        return remote(
            source,
            self.from_core.at[here],
            self.core_send.at[here],
            self.core_recv.at[here],
            self.place.sibling,
        )

    def core_arrived(self, here):
        self.core_copy(here, self.from_core.at[here]).wait_recv()

    def pair_copy(self, at, slot):
        return remote(
            self.sums.at[self.base + slot],
            self.from_pair.at[at],
            self.pair_send.at[at],
            self.pair_recv.at[at],
            self.place.partner,
        )

    def line_copy(self, at, side, distance):
        slot = self.place.line if distance == 1 and side == 1 else at
        return remote(
            self.sums.at[self.base + 2 + (side + 1) // 2],
            self.from_line.at[slot],
            self.line_send.at[at],
            self.line_recv.at[slot],
            self.place.beside(side),
        )

    def add_up(self, sources, slot):
        terms = self.terms
        copies = [
            pltpu.make_async_copy(source, terms.at[i], self.term_sems.at[i])
            for i, (source, _) in enumerate(sources)
        ]
        for copy, (_, there) in zip(copies, sources):
            if there is None:
                copy.start()
            else:
                pl.when(there)(copy.start)
        for i, (copy, (_, there)) in enumerate(zip(copies, sources)):
            if there is None:
                copy.wait()
            else:
                pl.when(there)(copy.wait)

                @pl.when(jnp.logical_not(there))
                def _():
                    terms[i] = jnp.zeros_like(terms[i])

        tile = 16

        @pl.loop(0, terms.shape[1] // tile)
        def _(number):
            here = pl.ds(pl.multiple_of(number * tile, tile), tile)
            total = terms[0, here, :].astype(F32)
            for i in range(1, len(sources)):
                total += terms[i, here, :].astype(F32)
            self.sums[self.base + slot, here, :] = total.astype(BF16)

    def cross(self, rank):
        place = self.place
        at = place.near(rank)
        here = at * 2 + 1 - place.y
        slot = rank % 2
        if rank + 2 < place.line:
            self.pair_copy(place.near(rank + 2), slot).wait_send()
        self.core_arrived(here)
        self.add_up([(self.parts.at[here], None), (self.from_core.at[here], None)], slot)
        self.pair_copy(at, slot).start()

    def advance(self, distance):
        place = self.place
        for side in (-1, 1):
            at = place.z + side * distance
            here = at * 2 + place.y
            farther = place.inside(place.z - side)
            if distance + 1 < place.line:

                @pl.when(place.inside(at + side))
                def _():
                    self.line_copy(at + side, side, distance + 1).wait_send()

            @pl.when(place.inside(at))
            def _():
                self.core_arrived(here)
                self.pair_copy(at, 0).wait_recv()
                sources = [
                    (self.parts.at[here], None),
                    (self.from_core.at[here], None),
                    (self.from_pair.at[at], None),
                ]
                if distance + 1 < place.line:

                    @pl.when(farther)
                    def _():
                        self.line_copy(at, side, distance + 1).wait_recv()

                    sources.append((self.from_line.at[at], farther))
                self.add_up(sources, 2 + (side + 1) // 2)
                self.line_copy(at, side, distance).start()

    def tick(self, number, late):
        line = self.place.line
        for rank in range(line):
            when = 2 * (line - rank) - 1
            pl.when(number == when)(partial(self.cross, rank))
            if rank + 1 < line:
                pl.when(number == when + late)(partial(self.advance, rank + 1))

    def finish(self, result, sem):
        place = self.place
        z, line = place.z, place.line
        here = z * 2 + place.y
        self.core_arrived(here)
        self.pair_copy(z, 0).wait_recv()
        for side in (-1, 1):
            pl.when(place.inside(z + side))(lambda: self.line_copy(z, -side, 1).wait_recv())
        for rank in (1, 0):
            self.pair_copy(place.near(rank), rank % 2).wait_send()
        self.add_up(
            [
                (self.parts.at[here], None),
                (self.from_core.at[here], None),
                (self.from_pair.at[z], None),
                (self.from_line.at[z], place.inside(z + 1)),
                (self.from_line.at[line], place.inside(z - 1)),
            ],
            0,
        )
        copy = pltpu.make_async_copy(self.sums.at[self.base], result, sem)
        copy.start()
        copy.wait()
        for side in (-1, 1):

            @pl.when(place.inside(z + side))
            def _():
                self.line_copy(z + side, side, 1).wait_send()


def expert_kernel(*refs, line, chunk, gathers):
    refs = list(refs)

    def take(count):
        taken = refs[:count]
        del refs[:count]
        return taken[0] if count == 1 else taken

    tokens_in, cotangent_own = take(2)
    if not gathers:
        cotangent_other = take(1)
    shares_ref, own_hbm, other_hbm, exchanged = take(4)
    if not gathers:
        before = take(1)
        grad_piece, out_piece, grad_own, grad_other, received = take(5)
        grad_arrays, out_arrays = take(4), take(4)
        tokens_hbm = tokens_in
    else:
        parts_hbm, grad_own, grad_other, tokens_hbm, received, cotangent_other = take(6)
    weights, grads, tokens_buf, cotangent_buf, inner_low, grad_low = take(6)
    both_buf, stage, load_sems, store_sems, row_sems, part_sems, exchange_sems = take(7)

    expert_count, model_width, all_units = weights.shape
    hidden_units = all_units // 3
    units = hidden_units // 2
    steps = 2 * line
    rows = tokens_hbm.shape[2]
    place = Place(line)
    first_rows, second_rows = pl.ds(0, rows), pl.ds(rows, rows)
    if gathers:
        mover = Gather(place, tokens_hbm, take(4))
        cotangent_send, cotangent_recv = take(2)
    else:
        before_buf, terms, sums, term_sems = take(4)
        movers = [
            Reduce(place, arrays, terms, term_sems, sums, 4 * number, take(6))
            for number, arrays in enumerate((grad_arrays, out_arrays))
        ]
    order = mover.order if gathers else Reduce.order

    def cotangent_copy(step):
        here = place.block(order, step)
        return remote(
            cotangent_own.at[here],
            cotangent_other.at[here],
            cotangent_send.at[here],
            cotangent_recv.at[here],
            place.sibling,
        )

    place.meet()
    exchange = remote(
        exchanged, received, exchange_sems.at[0], exchange_sems.at[1], place.across
    )
    exchange.start()
    if gathers:
        own_block = place.z * 2 + place.y
        own_copy = pltpu.make_async_copy(tokens_in, tokens_hbm.at[own_block, 0], row_sems.at[0, 0])
        own_copy.start()
        own_copy.wait()
        mover.start()
        for step in range(steps):
            cotangent_copy(step).start()
    weight_loads = weight_copies(own_hbm, other_hbm, weights, load_sems)
    for copy in weight_loads:
        copy.start()
    grads[...] = jnp.zeros_like(grads)

    def row_copies(step, slot):
        here = place.block(order, step)
        lanes = pl.ds(0, model_width)
        pairs = [
            (tokens_hbm.at[here, 0], tokens_buf.at[slot, first_rows, :]),
            (tokens_hbm.at[here, 1], tokens_buf.at[slot, second_rows, :]),
            (cotangent_own.at[here, :, lanes], cotangent_buf.at[slot, first_rows, :]),
            (cotangent_other.at[here, :, lanes], cotangent_buf.at[slot, second_rows, :]),
        ]
        if not gathers:
            pairs.append((before.at[here], before_buf.at[slot]))
        return [
            pltpu.make_async_copy(source, target, row_sems.at[slot, i])
            for i, (source, target) in enumerate(pairs)
        ]

    def load_rows(step, slot):
        if gathers:
            mover.core_copy(place.block(order, step)).wait_recv()
            cotangent_copy(step).wait_recv()
        for copy in row_copies(step, slot):
            copy.start()

    load_rows(0, 0)
    for copy in weight_loads:
        copy.wait()

    halves = [pl.ds(number * model_width, model_width) for number in range(2)]

    def core_copies(step, slot):
        here = place.block(order, step)
        return [
            mover.core_copy(here, both_buf.at[slot, second_rows, lanes])
            for mover, lanes in zip(movers, halves)
        ]

    def part_copies(step, slot):
        here = place.block(order, step)
        if gathers:
            pairs = [(both_buf.at[slot], parts_hbm.at[here])]
        else:
            pairs = [
                (both_buf.at[slot, first_rows, lanes], mover.parts.at[here])
                for mover, lanes in zip(movers, halves)
            ]
        return [
            pltpu.make_async_copy(source, target, part_sems.at[slot, i])
            for i, (source, target) in enumerate(pairs)
        ]

    @pl.loop(0, steps)
    def _(step):
        slot = step % 2
        for copy in row_copies(step, slot):
            copy.wait()
        shares = shares_ref[place.block(order, step)]
        lane = lax.broadcasted_iota(jnp.int32, shares.shape, 1)

        def run(expert, gate_up, grad_inner):
            share = jnp.sum(jnp.where(lane == expert, shares, 0.0), axis=1, keepdims=True)
            inner, grad_gate, grad_up = activate(gate_up, grad_inner, share)
            inner_low[expert] = inner
            grad_low[expert, :, :hidden_units] = grad_gate
            grad_low[expert, :, hidden_units:] = grad_up

        def weight_grads(expert):
            grads[expert, :, : 2 * hidden_units] += lax.dot_general(
                tokens_buf[slot], grad_low[expert], FIRST_FIRST, preferred_element_type=F32
            )
            grads[expert, :, 2 * hidden_units :] += lax.dot_general(
                cotangent_buf[slot], inner_low[expert], FIRST_FIRST, preferred_element_type=F32
            )

        results = project(tokens_buf[slot], cotangent_buf[slot], weights[0])
        for expert in range(expert_count):
            run(expert, *results)
            if expert + 1 < expert_count:
                results = project(tokens_buf[slot], cotangent_buf[slot], weights[expert + 1])
            weight_grads(expert)

        @pl.when(step >= 1)
        def _():
            for copy in part_copies(step - 1, 1 - slot):
                copy.wait()

        if gathers:
            mover.tick(step)
        else:
            for late, reducer in enumerate(movers):
                reducer.tick(step, late)

            @pl.when(step >= 2)
            def _():
                for copy in core_copies(step - 2, slot):
                    copy.wait_send()

        @pl.loop(0, model_width // chunk)
        def _(number):
            @pl.when((number == 1) & (step + 1 < steps))
            def _():
                load_rows(step + 1, 1 - slot)

            cols = pl.ds(pl.multiple_of(number * chunk, chunk), chunk)

            def total_of(lows, lanes, target):
                if gathers:
                    total = jnp.zeros((2 * rows, chunk), F32)
                else:
                    total = before_buf[slot, :, target].astype(F32)
                for expert in range(expert_count):
                    total += lax.dot_general(
                        lows[expert],
                        weights[expert, cols, lanes],
                        LAST_LAST,
                        preferred_element_type=F32,
                    )
                both_buf[slot, :, target] = total.astype(BF16)

            beyond = pl.ds(pl.multiple_of(model_width + number * chunk, chunk), chunk)
            total_of(grad_low, pl.ds(0, 2 * hidden_units), cols)
            total_of(inner_low, pl.ds(2 * hidden_units, hidden_units), beyond)

        if not gathers:
            for copy in core_copies(step, slot):
                copy.start()
        for copy in part_copies(step, slot):
            copy.start()

    last = (steps - 1) % 2
    for copy in part_copies(steps - 1, last):
        copy.wait()
    if not gathers:
        for copy in core_copies(steps - 2, 1 - last) + core_copies(steps - 1, last):
            copy.wait_send()
        movers[1].advance(1)

    sources, _, slice_rows, _ = own_hbm.shape

    def grad_copy(expert, source, half, slot):
        return pltpu.make_async_copy(
            stage.at[slot, half],
            (grad_own, grad_other)[half].at[source, expert],
            store_sems.at[slot, half],
        )

    @pl.loop(0, expert_count * sources)
    def _(number):
        expert, source = number // sources, number % sources
        slot = number % 2

        @pl.when(number >= 2)
        def _():
            for half in range(2):
                grad_copy(expert, source, half, slot).wait()

        here = pl.ds(pl.multiple_of(source * slice_rows, slice_rows), slice_rows)
        for half in range(2):
            for part in range(3):
                first = (2 * part + half) * units
                stage[slot, half, :, part * units : (part + 1) * units] = grads[
                    expert, here, first : first + units
                ].astype(BF16)
            grad_copy(expert, source, half, slot).start()

    for slot in range(2):
        for half in range(2):
            grad_copy(0, 0, half, slot).wait()

    exchange.wait()
    if gathers:
        mover.finish()
        for step in range(steps):
            cotangent_copy(step).wait_send()
    else:
        for number, result in enumerate((grad_piece, out_piece)):
            movers[number].finish(result, row_sems.at[0, number])


def expert_call(operands, own, shares, line, rows, model_width, gathers, collective_id, chunk=512):
    sources, expert_count, slice_rows, lanes = own.shape
    hidden_units = 2 * lanes // 3
    blocks = 2 * line
    in_place = pl.BlockSpec(memory_space=pl.ANY)
    dma = pltpu.SemaphoreType.DMA
    flops = 2 * blocks * 2 * rows * model_width * expert_count * hidden_units * 9

    def low(*shape):
        return jax.ShapeDtypeStruct(shape, BF16)

    if gathers:
        out_shape = [
            low(blocks, 2 * rows, 2 * model_width),
            low(*own.shape),
            low(*own.shape),
            low(blocks, 2, rows, model_width),
            low(*operands[5].shape),
            low(*operands[1].shape),
        ]
        own_scratch = [dma((blocks, 2)), dma((line, 2)), dma((line,)), dma((blocks,))]
        own_scratch += [dma((blocks,)), dma((blocks,))]
    else:
        out_shape = [
            low(rows, model_width),
            low(rows, model_width),
            low(*own.shape),
            low(*own.shape),
            low(*operands[6].shape),
        ]
        out_shape += 2 * [
            low(blocks, rows, model_width),
            low(blocks, rows, model_width),
            low(line, rows, model_width),
            low(line + 1, rows, model_width),
        ]
        own_scratch = [
            pltpu.VMEM((2, 2 * rows, 2 * model_width), BF16),
            pltpu.VMEM((5, rows, model_width), BF16),
            pltpu.VMEM((8, rows, model_width), BF16),
            dma((5,)),
        ]
        own_scratch += 2 * [
            dma((blocks,)),
            dma((blocks,)),
            dma((line,)),
            dma((line,)),
            dma((line,)),
            dma((line + 1,)),
        ]
    in_specs = [in_place] * len(operands)
    in_specs[2 if gathers else 3] = pl.BlockSpec(memory_space=pltpu.VMEM)
    results = pl.pallas_call(
        partial(expert_kernel, line=line, chunk=chunk, gathers=gathers),
        in_specs=in_specs,
        out_specs=[in_place] * len(out_shape),
        out_shape=out_shape,
        scratch_shapes=[
            pltpu.VMEM((expert_count, model_width, 3 * hidden_units), BF16),
            pltpu.VMEM((expert_count, model_width, 3 * hidden_units), F32),
            pltpu.VMEM((2, 2 * rows, model_width), BF16),
            pltpu.VMEM((2, 2 * rows, model_width), BF16),
            pltpu.VMEM((expert_count, 2 * rows, hidden_units), BF16),
            pltpu.VMEM((expert_count, 2 * rows, 2 * hidden_units), BF16),
            pltpu.VMEM((2, 2 * rows, 2 * model_width), BF16),
            pltpu.VMEM((2, 2, slice_rows, lanes), BF16),
            dma((sources, 2, 3)),
            dma((2, 2)),
            dma((2, 5)),
            dma((2, 2)),
            dma((2,)),
        ]
        + own_scratch,
        compiler_params=pltpu.CompilerParams(
            vmem_limit_bytes=60 * 2**20, collective_id=collective_id, has_side_effects=True
        ),
        cost_estimate=pl.CostEstimate(
            flops=flops, bytes_accessed=80 * 2**20, transcendentals=0
        ),
    )(*operands)
    return results[: 6 if gathers else 5]


def experts_gathering(piece, cotangent, shares, own, other, exchanged, line):
    rows, model_width = piece.shape
    operands = (piece, cotangent, shares, own, other, exchanged)
    return expert_call(operands, own, shares, line, rows, model_width, True, 1)


def experts_reducing(
    tokens, cotangents, shares, own, other, exchanged, parts, line
):
    _, _, rows, model_width = tokens.shape
    operands = (tokens, *cotangents, shares, own, other, exchanged, parts)
    return expert_call(operands, own, shares, line, rows, model_width, False, 2)


def attention_rows(values, kv_head, group_size):
    first = kv_head * group_size
    return jnp.concatenate(
        [values[:, (first + r) * HEAD_DIM : (first + r + 1) * HEAD_DIM] for r in range(group_size)],
        axis=0,
    )


def quarter_turn(values):
    half = HEAD_DIM // 2
    return jnp.concatenate([-values[:, half:], values[:, :half]], axis=1)


def window_mask(start, doc_start_ref, first_ref, block_rows, window):
    key_index = start + lax.broadcasted_iota(jnp.int32, (block_rows, window), 1)
    query_index = (
        first_ref[0]
        + pl.program_id(0) * block_rows
        + lax.broadcasted_iota(jnp.int32, (block_rows, window), 0)
    )
    return (key_index <= query_index) & (key_index >= doc_start_ref[...])


def window_start(first_ref, block_rows, window):
    end = first_ref[0] + (pl.program_id(0) + 1) * block_rows
    return pl.multiple_of(jnp.maximum(end - window, 0), block_rows)


def attention_forward_kernel(
    first_ref, query_ref, key_value_ref, doc_start_ref, attended_ref, lse_ref, *, group_size, window
):
    block_rows = query_ref.shape[0]
    kv_heads = key_value_ref.shape[1] // (2 * HEAD_DIM)
    start = window_start(first_ref, block_rows, window)
    allowed = window_mask(start, doc_start_ref, first_ref, block_rows, window)
    bias = jnp.where(allowed, 0.0, -1e30)
    bias = jnp.concatenate([bias] * group_size, axis=0)
    keys_values = key_value_ref[pl.ds(start, window), :]
    queries = query_ref[...]
    parts = []
    for g in range(kv_heads):
        keys = keys_values[:, g * HEAD_DIM : (g + 1) * HEAD_DIM]
        values = keys_values[:, (kv_heads + g) * HEAD_DIM : (kv_heads + g + 1) * HEAD_DIM]
        scores = lax.dot_general(
            attention_rows(queries, g, group_size), keys, LAST_LAST, preferred_element_type=F32
        )
        scores = scores * HEAD_DIM**-0.5 + bias
        row_max = jnp.max(scores, axis=1, keepdims=True)
        exponent = jnp.exp(scores - row_max)
        total = jnp.sum(exponent, axis=1, keepdims=True)
        probs = (exponent * (1.0 / total)).astype(BF16)
        mixed = jnp.dot(probs, values, preferred_element_type=F32).astype(BF16)
        lse_ref[0, g] = row_max + jnp.log(total)
        parts += [mixed[r * block_rows : (r + 1) * block_rows] for r in range(group_size)]
    attended_ref[...] = jnp.concatenate(parts, axis=1)


def attention_backward_kernel(
    first_ref,
    query_ref,
    key_value_ref,
    doc_start_ref,
    lse_ref,
    grad_ref,
    turns_ref,
    query_turns_ref,
    grad_query_ref,
    grad_key_value_ref,
    grad_keys,
    grad_values,
    *,
    group_size,
    window,
    steps,
):
    step = pl.program_id(0)
    block_rows = query_ref.shape[0]
    kv_heads = key_value_ref.shape[1] // (2 * HEAD_DIM)

    @pl.when(step == 0)
    def _():
        grad_keys[...] = jnp.zeros_like(grad_keys)
        grad_values[...] = jnp.zeros_like(grad_values)

    start = window_start(first_ref, block_rows, window)
    allowed = window_mask(start, doc_start_ref, first_ref, block_rows, window)
    bias = jnp.where(allowed, 0.0, -1e30)
    bias = jnp.concatenate([bias] * group_size, axis=0)
    rows = pl.ds(start, window)
    keys_values = key_value_ref[rows, :]
    queries = query_ref[...]
    grads = grad_ref[...]
    query_turns = jnp.concatenate([query_turns_ref[...]] * group_size, axis=0)
    parts = []
    for g in range(kv_heads):
        keys = keys_values[:, g * HEAD_DIM : (g + 1) * HEAD_DIM]
        values = keys_values[:, (kv_heads + g) * HEAD_DIM : (kv_heads + g + 1) * HEAD_DIM]
        query_rows = attention_rows(queries, g, group_size)
        grad_rows = attention_rows(grads, g, group_size)
        scores = lax.dot_general(query_rows, keys, LAST_LAST, preferred_element_type=F32)
        probs = jnp.exp(scores * HEAD_DIM**-0.5 + bias - lse_ref[0, g])
        grad_probs = lax.dot_general(grad_rows, values, LAST_LAST, preferred_element_type=F32)
        inner = jnp.sum(grad_probs * probs, axis=1, keepdims=True)
        grad_scores = (HEAD_DIM**-0.5 * (probs * (grad_probs - inner))).astype(BF16)
        grad_values[g, rows, :] += lax.dot_general(
            probs.astype(BF16), grad_rows, FIRST_FIRST, preferred_element_type=F32
        )
        both_queries = jnp.concatenate([query_rows, quarter_turn(query_rows)], axis=1)
        grad_keys[g, rows, :] += lax.dot_general(
            grad_scores, both_queries, FIRST_FIRST, preferred_element_type=F32
        )
        both_keys = jnp.concatenate([keys, quarter_turn(keys)], axis=1)
        turned = jnp.dot(grad_scores, both_keys, preferred_element_type=F32) * query_turns
        grad_query = (turned[:, :HEAD_DIM] + turned[:, HEAD_DIM:]).astype(BF16)
        parts += [grad_query[r * block_rows : (r + 1) * block_rows] for r in range(group_size)]
    grad_query_ref[...] = jnp.concatenate(parts, axis=1)

    @pl.when(step == steps - 1)
    def _():
        key_parts, value_parts = [], []
        for g in range(kv_heads):
            turned = grad_keys[g] * turns_ref[...]
            key_parts.append((turned[:, :HEAD_DIM] + turned[:, HEAD_DIM:]).astype(BF16))
            value_parts.append(grad_values[g].astype(BF16))
        grad_key_value_ref[...] = jnp.concatenate(key_parts + value_parts, axis=1)


def attention_specs(queries, keys_values, block_rows):
    return dict(
        smem=pl.BlockSpec(memory_space=pltpu.SMEM),
        rows=pl.BlockSpec((block_rows, queries.shape[1]), lambda i: (i, 0)),
        whole=pl.BlockSpec(keys_values.shape, lambda i: (0, 0)),
        column=pl.BlockSpec((block_rows, 1), lambda i: (i, 0)),
    )


def attention_forward(first, queries, keys_values, doc_start, block_rows=256, reach=1024):
    row_count, query_cols = queries.shape
    kv_heads = keys_values.shape[1] // (2 * HEAD_DIM)
    group_size = query_cols // HEAD_DIM // kv_heads
    steps = row_count // block_rows
    window = min(reach + block_rows, keys_values.shape[0])
    specs = attention_specs(queries, keys_values, block_rows)
    stacked = group_size * block_rows
    return pl.pallas_call(
        partial(attention_forward_kernel, group_size=group_size, window=window),
        grid=(steps,),
        in_specs=[specs["smem"], specs["rows"], specs["whole"], specs["column"]],
        out_specs=[
            specs["rows"],
            pl.BlockSpec((1, kv_heads, stacked, 1), lambda i: (i, 0, 0, 0)),
        ],
        out_shape=[
            jax.ShapeDtypeStruct(queries.shape, BF16),
            jax.ShapeDtypeStruct((steps, kv_heads, stacked, 1), F32),
        ],
        compiler_params=pltpu.CompilerParams(vmem_limit_bytes=48 * 2**20),
        cost_estimate=pl.CostEstimate(
            flops=4 * row_count * window * query_cols * 8, bytes_accessed=2**22, transcendentals=0
        ),
    )(first, queries, keys_values, doc_start)


def attention_backward(
    first, queries, keys_values, doc_start, lse, grads, turns, query_turns, block_rows=256, reach=1024
):
    row_count, query_cols = queries.shape
    kv_heads = keys_values.shape[1] // (2 * HEAD_DIM)
    group_size = query_cols // HEAD_DIM // kv_heads
    steps = row_count // block_rows
    window = min(reach + block_rows, keys_values.shape[0])
    specs = attention_specs(queries, keys_values, block_rows)
    stacked = group_size * block_rows
    return pl.pallas_call(
        partial(attention_backward_kernel, group_size=group_size, window=window, steps=steps),
        grid=(steps,),
        in_specs=[
            specs["smem"],
            specs["rows"],
            specs["whole"],
            specs["column"],
            pl.BlockSpec((1, kv_heads, stacked, 1), lambda i: (i, 0, 0, 0)),
            specs["rows"],
            pl.BlockSpec(turns.shape, lambda i: (0, 0)),
            pl.BlockSpec((block_rows, turns.shape[1]), lambda i: (i, 0)),
        ],
        out_specs=[specs["rows"], specs["whole"]],
        out_shape=[
            jax.ShapeDtypeStruct(queries.shape, BF16),
            jax.ShapeDtypeStruct(keys_values.shape, BF16),
        ],
        scratch_shapes=[
            pltpu.VMEM((kv_heads, keys_values.shape[0], 2 * HEAD_DIM), F32),
            pltpu.VMEM((kv_heads, keys_values.shape[0], HEAD_DIM), F32),
        ],
        compiler_params=pltpu.CompilerParams(vmem_limit_bytes=48 * 2**20),
        cost_estimate=pl.CostEstimate(
            flops=10 * row_count * window * query_cols * 8, bytes_accessed=2**23, transcendentals=0
        ),
    )(first, queries, keys_values, doc_start, lse, grads, turns, query_turns)


def rotation_tables(positions):
    half_dim = HEAD_DIM // 2
    frequencies = 10000.0 ** (-2.0 * jnp.arange(half_dim, dtype=F32) / HEAD_DIM)
    angles = positions.astype(F32)[:, None] * frequencies[None, :]
    cosine, sine = jnp.cos(angles), jnp.sin(angles)
    return jnp.concatenate([cosine, cosine, -sine, -sine], axis=1)


def turned_columns(weight):
    rows, cols = weight.shape
    halves = weight.reshape(rows, cols // HEAD_DIM, 2, HEAD_DIM // 2)
    return jnp.stack([-halves[:, :, 1], halves[:, :, 0]], axis=2).reshape(rows, cols)


def expert_plan(
    residual_in,
    gain_attn,
    query_weight,
    key_projection_weight,
    value_projection_weight,
    out_weight,
    gain_ffn,
    gate_weight,
    up_weight,
    down_weight,
    segments,
    routes,
    shares,
    cotangent,
    *,
    groups,
    tensor_size,
):
    row_count, model_width = residual_in.shape
    query_cols = query_weight.shape[1]
    kv_cols = key_projection_weight.shape[1]
    expert_count, slice_rows, unit_count = gate_weight.shape
    own_experts = expert_count // groups
    piece_rows = row_count // tensor_size
    first_count = own_experts * 2 // 5
    context_rank = lax.axis_index(CONTEXT)
    tensor_rank = lax.axis_index(TENSOR)
    group_rank = lax.axis_index(SHARD) * lax.axis_size(CONTEXT) + context_rank
    chip_half, core = tensor_rank // 2, tensor_rank % 2
    own_first = context_rank * row_count
    piece_first = tensor_rank * piece_rows
    sibling = [(i, i ^ 1) for i in range(tensor_size)]
    across = [(i, i ^ 2) for i in range(tensor_size)]
    pair = [(0, 1), (1, 0)]

    def own_piece(values):
        return lax.dynamic_slice_in_dim(values, piece_first, piece_rows)

    def pick(values, axis, index):
        return lax.dynamic_index_in_dim(values, index, axis, keepdims=False)

    def sum_over_tensor(parts):
        parts = parts.astype(BF16).reshape(2, 2, piece_rows, -1)
        received = lax.ppermute(pick(parts, 1, 1 - core), TENSOR, sibling)
        half = pick(parts, 1, core).astype(F32) + received.astype(F32)
        received = lax.ppermute(pick(half, 0, 1 - chip_half).astype(BF16), TENSOR, across)
        return pick(half, 0, chip_half) + received.astype(F32)

    def gather_over_tensor(piece):
        other = lax.ppermute(piece, TENSOR, across)
        chips = jnp.where(
            chip_half == 0, jnp.concatenate([piece, other]), jnp.concatenate([other, piece])
        ).reshape(2, 1, piece_rows, -1)
        others = lax.ppermute(chips, TENSOR, sibling)
        both = jnp.where(
            core == 0,
            jnp.concatenate([chips, others], axis=1),
            jnp.concatenate([others, chips], axis=1),
        )
        return both.reshape(row_count, -1)

    def padded_columns(*gains):
        columns = jnp.stack(gains, axis=1)
        return jnp.pad(columns, ((0, 0), (0, 128 - len(gains))))

    with jax.named_scope("weights"):
        lanes = 3 * unit_count

        def slices(first, count):
            return jnp.concatenate(
                [
                    weight.reshape((groups, own_experts) + weight.shape[1:])[:, first : first + count]
                    for weight in (gate_weight, up_weight, down_weight.transpose(0, 2, 1))
                ],
                axis=3,
            ).reshape(groups * count, slice_rows, lanes)

        def to_groups(values):
            owned = lax.all_to_all(values, GROUP, 0, 0, tiled=True)
            return owned.reshape(groups, -1, slice_rows, lanes)

        slices_first, slices_second = lax.optimization_barrier(
            (slices(0, first_count), slices(first_count, own_experts - first_count))
        )
        owned_first, owned_second = to_groups(slices_first), to_groups(slices_second)

        spread_lanes = slice_rows * 128 // piece_rows
        spread = jnp.sum(
            jnp.where(
                own_piece(routes)[:, :, None] == jnp.arange(expert_count, dtype=jnp.int32),
                own_piece(shares)[:, :, None],
                0.0,
            ),
            axis=1,
        )
        spread_high = spread.astype(BF16)
        spread_low = (spread - spread_high.astype(F32)).astype(BF16)
        spread_both = jnp.pad(
            jnp.concatenate([spread_high, spread_low], axis=1),
            ((0, 0), (0, spread_lanes - 2 * expert_count)),
        )
        qkv_full = lax.all_gather(
            jnp.concatenate(
                [
                    query_weight,
                    key_projection_weight,
                    value_projection_weight,
                    out_weight.T,
                    padded_columns(gain_attn, gain_ffn),
                    spread_both.reshape(slice_rows, 128),
                ],
                axis=1,
            ),
            GROUP,
            axis=0,
            tiled=True,
        )
        qkv_cols = query_cols + 2 * kv_cols
        owned_first, qkv_full = lax.optimization_barrier((owned_first, qkv_full))
        others_first = lax.ppermute(owned_first, TENSOR, across)
        qkv_weight = qkv_full[:, :qkv_cols]
        out_transposed = qkv_full[:, qkv_cols : qkv_cols + query_cols]
        gain_attn_float = qkv_full[:, qkv_cols + query_cols].astype(F32)
        gain_ffn_float = qkv_full[:, qkv_cols + query_cols + 1].astype(F32)


    with jax.named_scope("cotangents"):
        cotangent_piece = own_piece(cotangent)
        cotangent_own = lax.all_gather(cotangent_piece, GROUP, axis=0, tiled=False)

    with jax.named_scope("attention"):
        positions = doc_positions(segments)
        turns = rotation_tables(positions)
        own_turns = lax.dynamic_slice_in_dim(turns, own_first, row_count)
        own_index = own_first + jnp.arange(row_count, dtype=jnp.int32)
        doc_start = own_index - lax.dynamic_slice_in_dim(positions, own_first, row_count)
        input_float = residual_in.astype(F32)
        first_normalized = rms_scale(input_float, gain_attn_float).astype(BF16)
        rotated_cols = query_cols + kv_cols
        projected = jnp.dot(
            first_normalized,
            jnp.concatenate([qkv_weight, turned_columns(qkv_weight[:, :rotated_cols])], axis=1),
            preferred_element_type=F32,
        )
        heads = rotated_cols // HEAD_DIM
        rotated = (
            projected[:, :rotated_cols] * jnp.tile(own_turns[:, :HEAD_DIM], (1, heads))
            - projected[:, qkv_cols:] * jnp.tile(own_turns[:, HEAD_DIM:], (1, heads))
        ).astype(BF16)
        queries = rotated[:, :query_cols]
        own_keys_values = jnp.concatenate(
            [rotated[:, query_cols:], projected[:, rotated_cols:qkv_cols].astype(BF16)], axis=1
        )
        other_keys_values = lax.ppermute(own_keys_values, CONTEXT, pair)
        keys_values = jnp.where(
            context_rank == 0,
            jnp.concatenate([own_keys_values, other_keys_values]),
            jnp.concatenate([other_keys_values, own_keys_values]),
        )
        first = own_first.reshape(1).astype(jnp.int32)
        attended, lse = attention_forward(first, queries, keys_values, doc_start[:, None])
        attn_part = lax.dot_general(
            attended, out_transposed, LAST_LAST, preferred_element_type=F32
        )
        attn_piece = sum_over_tensor(attn_part)
        others_first, owned_second, attn_piece = lax.optimization_barrier(
            (others_first, owned_second, attn_piece)
        )
        hidden = own_piece(residual_in).astype(F32) + attn_piece
        normed_ffn, ffn_norm_back = jax.vjp(rms_scale, hidden, gain_ffn_float)

    with jax.named_scope("exchange"):
        cotangent_own, normed_ffn = lax.optimization_barrier((cotangent_own, normed_ffn))
        spread_own = qkv_full[:, qkv_cols + query_cols + 128 :]
        spread_own = spread_own.reshape(groups, piece_rows, spread_lanes)
        spread_all = jnp.concatenate(
            [spread_own, lax.ppermute(spread_own, TENSOR, sibling)], axis=1
        )

        def shares_of(first, count):
            start = group_rank * own_experts + first
            high = lax.dynamic_slice_in_dim(spread_all, start, count, axis=2)
            low = lax.dynamic_slice_in_dim(spread_all, start + expert_count, count, axis=2)
            total = high.astype(F32) + low.astype(F32)
            return jnp.pad(total, ((0, 0), (0, 0), (0, 8 - count)))

        shares_first = shares_of(0, first_count)
        shares_second = shares_of(first_count, own_experts - first_count)

    with jax.named_scope("experts"):
        line = groups // 2
        parts, grad_own_first, grad_other_first, tokens, others_second, cotangent_other = (
            experts_gathering(
                normed_ffn.astype(BF16),
                cotangent_own,
                shares_first,
                owned_first,
                others_first,
                owned_second,
                line,
            )
        )
        grad_second, out_piece, grad_own_second, grad_other_second, received_first = (
            experts_reducing(
                tokens,
                (cotangent_own, cotangent_other),
                shares_second,
                owned_second,
                others_second,
                grad_other_first,
                parts,
                line,
            )
        )

    with jax.named_scope("expert_grads"):

        def added(own, received):
            return (own.astype(F32) + received.astype(F32)).astype(BF16)

        def returned(total):
            flat = total.reshape((total.shape[0] * total.shape[1],) + total.shape[2:])
            return lax.all_to_all(flat, GROUP, 0, 0, tiled=True).reshape(total.shape)

        total_first = added(grad_own_first, received_first)
        received_second = lax.ppermute(grad_other_second, TENSOR, across)
        total_first, grad_second = lax.optimization_barrier((total_first, grad_second))
        returned_first = returned(total_first)
        grad_hidden_norm, grad_gain_ffn_local = ffn_norm_back(grad_second.astype(F32))
        grad_hidden = cotangent_piece.astype(F32) + grad_hidden_norm
        grad_hidden_low = gather_over_tensor(grad_hidden.astype(BF16))
        output = gather_over_tensor((hidden + out_piece.astype(F32)).astype(BF16))

    with jax.named_scope("attention_back"):
        grad_out_local = lax.dot_general(
            grad_hidden_low, attended, FIRST_FIRST, preferred_element_type=F32
        )
        grad_out_transposed = lax.psum_scatter(
            grad_out_local.astype(BF16), GROUP, scatter_dimension=0, tiled=True
        )
        grad_attended = jnp.dot(grad_hidden_low, out_transposed, preferred_element_type=F32)
        returned_first, grad_attended = lax.optimization_barrier((returned_first, grad_attended))
        grad_query_lin, grad_key_value = attention_backward(
            first,
            queries,
            keys_values,
            doc_start[:, None],
            lse,
            grad_attended.astype(BF16),
            turns,
            own_turns,
        )
        total_second = added(grad_own_second, received_second)
        grad_key_value = grad_key_value.reshape(2, row_count, -1)
        received = lax.ppermute(pick(grad_key_value, 0, 1 - context_rank), CONTEXT, pair)
        grad_key_value = (
            pick(grad_key_value, 0, context_rank).astype(F32) + received.astype(F32)
        ).astype(BF16)
        grad_projected = jnp.concatenate([grad_query_lin, grad_key_value], axis=1)
        grad_first_part = lax.dot_general(
            grad_projected, qkv_weight, LAST_LAST, preferred_element_type=F32
        )
        grad_qkv_local = lax.dot_general(
            first_normalized, grad_projected, FIRST_FIRST, preferred_element_type=F32
        ).astype(BF16)
        total_second, grad_out_transposed, grad_first_part, grad_qkv_local = (
            lax.optimization_barrier(
                (total_second, grad_out_transposed, grad_first_part, grad_qkv_local)
            )
        )
        returned_second = returned(total_second)
        grad_first = sum_over_tensor(grad_first_part)
        _, attn_norm_back = jax.vjp(
            rms_scale, own_piece(residual_in).astype(F32), gain_attn_float
        )
        grad_input_norm, grad_gain_attn_local = attn_norm_back(grad_first)
        grad_input = gather_over_tensor((grad_hidden + grad_input_norm).astype(BF16))
        grad_qkv = lax.psum_scatter(grad_qkv_local, GROUP, scatter_dimension=0, tiled=True)
        gains = jnp.stack([grad_gain_attn_local, grad_gain_ffn_local])
        for axis, step, size in (
            (TENSOR, 1, tensor_size),
            (TENSOR, 2, tensor_size),
            (CONTEXT, 1, 2),
            (SHARD, 1, groups // 2),
            (SHARD, 2, groups // 2),
        ):
            gains = gains + lax.ppermute(gains, axis, [(i, i ^ step) for i in range(size)])
        gains = lax.dynamic_slice_in_dim(gains, group_rank * slice_rows, slice_rows, axis=1)

    returned_second, grad_qkv, gains, grad_input, output = lax.optimization_barrier(
        (returned_second, grad_qkv, gains, grad_input, output)
    )
    grad_qkv = grad_qkv.astype(F32)

    def whole(first, last, turned):
        parts = [
            part[..., first:last].transpose(0, 1, 3, 2) if turned else part[..., first:last]
            for part in (returned_first, returned_second)
        ]
        joined = jnp.concatenate(parts, axis=1).astype(F32)
        return joined.reshape((expert_count,) + joined.shape[2:])

    units = unit_count
    return (
        output,
        grad_input,
        gains[0],
        grad_qkv[:, :query_cols],
        grad_qkv[:, query_cols:rotated_cols],
        grad_qkv[:, rotated_cols:qkv_cols],
        grad_out_transposed.astype(F32).T,
        gains[1],
        whole(0, units, False),
        whole(units, 2 * units, False),
        whole(2 * units, 3 * units, True),
    )


def solution(mesh):
    placed = (
        P(GROUP, None),
        P(GROUP),
        P(GROUP, TENSOR),
        P(GROUP, TENSOR),
        P(GROUP, TENSOR),
        P(TENSOR, GROUP),
        P(GROUP),
        P(None, GROUP, TENSOR),
        P(None, GROUP, TENSOR),
        P(None, TENSOR, GROUP),
        P(SHARD),
        P(GROUP, None),
        P(GROUP, None),
        P(GROUP, None),
    )
    sizes = dict(mesh.shape)
    if sizes[SHARD] == 4 and sizes[CONTEXT] == 2 and sizes[TENSOR] == 4:
        plan = partial(
            expert_plan, groups=sizes[SHARD] * sizes[CONTEXT], tensor_size=sizes[TENSOR]
        )
    else:
        plan = gathered_plan
    return jax.shard_map(
        plan,
        mesh=mesh,
        in_specs=placed,
        out_specs=(
            P(GROUP, None),
            P(GROUP, None),
            P(GROUP),
            P(GROUP, TENSOR),
            P(GROUP, TENSOR),
            P(GROUP, TENSOR),
            P(TENSOR, GROUP),
            P(GROUP),
            P(None, GROUP, TENSOR),
            P(None, GROUP, TENSOR),
            P(None, TENSOR, GROUP),
        ),
        check_vma=False,
    )
```

```python
from functools import partial

import jax
import jax.numpy as jnp
from jax import lax
from jax.experimental import pallas as pl
from jax.experimental.pallas import tpu as pltpu
from jax.sharding import PartitionSpec as P

HEAD_DIM = 64
NDOCS = 5
SHARD = "shard"
CONTEXT = "context"
TENSOR = "tensor"
GROUP = (SHARD, CONTEXT)
PRODUCT_0 = "qgrd,kgd->grqk"
PRODUCT_1 = "grqk,kgd->qgrd"
PRODUCT_2 = "ecd,edf->ecf"
PRODUCT_3 = "ecf,efd->ecd"
PRODUCT_4 = "ecd,efd->ecf"
PRODUCT_5 = "ecf,edf->ecd"
PRODUCT_6 = "ecd,ecf->edf"
PRODUCT_7 = "ecf,ecd->efd"
PRODUCT_8 = "grqk,qgrd->kgd"


epsilon = 1e-06


def rms_scale(values, gain):
    return values * lax.rsqrt(jnp.mean(values * values, axis=-1, keepdims=True) + epsilon) * gain


def doc_positions(segment_ids):
    sequence_length = segment_ids.shape[-1]
    index_row = jnp.arange(sequence_length, dtype=jnp.int32)
    documents = jnp.arange(NDOCS, dtype=jnp.int32)
    doc_starts = jnp.sum((segment_ids[..., :, None] < documents).astype(jnp.int32), axis=-2)
    own_start = jnp.sum(
        jnp.where(segment_ids[..., :, None] == documents, doc_starts[..., None, :], 0), axis=-1
    )
    return index_row - own_start


def rotary(values, positions):
    half_dim = values.shape[-1] // 2
    frequencies = 10000.0 ** (-2.0 * jnp.arange(half_dim, dtype=jnp.float32) / values.shape[-1])
    angles = positions.astype(jnp.float32)[:, None] * frequencies[None, :]
    cosine = jnp.cos(angles)[:, None, :]
    sines = jnp.sin(angles)[:, None, :]
    first_half = values[..., :half_dim]
    second_half = values[..., half_dim:]
    return jnp.concatenate(
        [first_half * cosine - second_half * sines, second_half * cosine + first_half * sines],
        axis=-1,
    )


def swiglu(gate_value, up_value):
    return jax.nn.silu(gate_value) * up_value


def dispatch(routes, shares, block_rows, capacity, expert_count):
    block_count = routes.shape[0] // block_rows
    picks = routes.shape[1]
    chosen = routes.reshape(block_count, block_rows * picks)
    onehot = (chosen[:, :, None] == jnp.arange(expert_count, dtype=jnp.int32)).astype(jnp.int32)
    ranked = jnp.sum((jnp.cumsum(onehot, axis=1) - onehot) * onehot, axis=2)
    slot_index = (
        chosen * (block_count * capacity)
        + jnp.arange(block_count, dtype=jnp.int32)[:, None] * capacity
        + ranked
    )
    tokens = jnp.arange(block_count * block_rows * picks, dtype=jnp.int32) // picks
    total_slots = expert_count * block_count * capacity
    slot_rows = jnp.zeros((total_slots,), jnp.int32).at[slot_index.reshape(-1)].set(tokens)
    slot_share = (
        jnp.zeros((total_slots,), jnp.float32).at[slot_index.reshape(-1)].set(shares.reshape(-1))
    )
    return (slot_rows, slot_share)


def gathered_plan(
    residual_in,
    gain_attn,
    query_weight,
    key_projection_weight,
    value_projection_weight,
    out_weight,
    gain_ffn,
    gate_weight,
    up_weight,
    down_weight,
    segments,
    routes,
    shares,
    cotangent,
):
    row_count, model_width = residual_in.shape
    head_size = HEAD_DIM
    query_cols = query_weight.shape[1]
    kv_heads = key_projection_weight.shape[1] // head_size
    group_size = query_cols // head_size // kv_heads
    expert_count = gate_weight.shape[0]
    capacity = row_count * routes.shape[1] * 5 // (4 * expert_count)
    score_scale = head_size ** (-0.5)
    context_rank = lax.axis_index(CONTEXT)
    own_first = context_rank * row_count
    gain_attn_full, gain_ffn_full, query_full, key_full, value_full, out_full = (
        lax.all_gather(gain_attn, GROUP, axis=0, tiled=True),
        lax.all_gather(gain_ffn, GROUP, axis=0, tiled=True),
        lax.all_gather(query_weight, GROUP, axis=0, tiled=True),
        lax.all_gather(key_projection_weight, GROUP, axis=0, tiled=True),
        lax.all_gather(value_projection_weight, GROUP, axis=0, tiled=True),
        lax.all_gather(out_weight, GROUP, axis=1, tiled=True),
    )
    gain_attn_float = gain_attn_full.astype(jnp.float32)
    gain_ffn_float = gain_ffn_full.astype(jnp.float32)
    positions = doc_positions(segments)
    own_positions = lax.dynamic_slice_in_dim(positions, own_first, row_count)
    own_ids = lax.dynamic_slice_in_dim(segments, own_first, row_count)
    own_index = own_first + jnp.arange(row_count, dtype=jnp.int32)
    input_float = residual_in.astype(jnp.float32)
    normed_attn, attn_norm_back = jax.vjp(rms_scale, input_float, gain_attn_float)
    first_normalized = normed_attn.astype(jnp.bfloat16)
    query_lin = jnp.dot(first_normalized, query_full, preferred_element_type=jnp.float32).reshape(
        row_count, -1, head_size
    )
    key_linear = jnp.dot(first_normalized, key_full, preferred_element_type=jnp.float32).reshape(
        row_count, -1, head_size
    )
    value_tokens = jnp.dot(first_normalized, value_full, preferred_element_type=jnp.float32).astype(
        jnp.bfloat16
    )
    rope_local = partial(rotary, positions=own_positions)
    query_rot, rope_query_back = jax.vjp(rope_local, query_lin)
    key_rot, rope_key_back = jax.vjp(rope_local, key_linear)
    query_low = query_rot.astype(jnp.bfloat16)
    key_low = key_rot.astype(jnp.bfloat16).reshape(row_count, -1)
    key_all, value_all = (
        lax.all_gather(key_low, CONTEXT, axis=0, tiled=True),
        lax.all_gather(value_tokens, CONTEXT, axis=0, tiled=True),
    )
    key_index = jnp.arange(key_all.shape[0], dtype=jnp.int32)
    key_ids = jnp.take(segments, jnp.clip(key_index, 0, segments.shape[0] - 1))
    key_valid = key_index >= 0
    key_heads = key_all.reshape(-1, kv_heads, head_size)
    value_heads = value_all.reshape(-1, kv_heads, head_size)
    query_heads = query_low.reshape(row_count, kv_heads, group_size, head_size)
    block_rows = min(512, row_count)
    block_starts = list(range(0, row_count, block_rows))

    def block_scores(block_first):
        query_block = query_heads[block_first : block_first + block_rows]
        raw_scores = jnp.einsum(
            PRODUCT_0, query_block, key_heads, preferred_element_type=jnp.float32
        )
        block_ids = own_ids[block_first : block_first + block_rows]
        block_index = own_index[block_first : block_first + block_rows]
        allowed = (
            key_valid[None, :]
            & (key_ids[None, :] == block_ids[:, None])
            & (key_index[None, :] <= block_index[:, None])
        )
        return (query_block, jnp.where(allowed, raw_scores * score_scale, -1e30))

    mixed_parts = []
    lse_parts = []
    for block_first in block_starts:
        query_block, scores = block_scores(block_first)
        row_max = jnp.max(scores, axis=-1, keepdims=True)
        exponent = jnp.exp(scores - row_max)
        row_total = jnp.sum(exponent, axis=-1, keepdims=True)
        probs = (exponent / row_total).astype(jnp.bfloat16)
        mixed_parts.append(
            jnp.einsum(PRODUCT_1, probs, value_heads, preferred_element_type=jnp.float32)
        )
        lse_parts.append(row_max + jnp.log(row_total))
    attended = (
        jnp.concatenate(mixed_parts, axis=0).reshape(row_count, query_cols).astype(jnp.bfloat16)
    )
    attn_part = jnp.dot(attended, out_full, preferred_element_type=jnp.float32)
    hidden = input_float + lax.psum(attn_part.astype(jnp.bfloat16), TENSOR).astype(jnp.float32)
    normed_ffn, ffn_norm_back = jax.vjp(rms_scale, hidden, gain_ffn_float)
    normed_second = normed_ffn.astype(jnp.bfloat16)
    slot_rows, slot_share = dispatch(routes, shares, row_count, capacity, expert_count)
    per_turn = expert_count // 5
    turn_count = expert_count // per_turn
    turn_slots = per_turn * capacity

    def local_experts(turn_index):
        gate_part = lax.dynamic_slice_in_dim(gate_weight, turn_index * per_turn, per_turn, 0)
        up_part = lax.dynamic_slice_in_dim(up_weight, turn_index * per_turn, per_turn, 0)
        down_part = lax.dynamic_slice_in_dim(down_weight, turn_index * per_turn, per_turn, 0)
        return (gate_part, up_part, down_part)

    def turn_inputs(turn_index):
        token_rows = lax.dynamic_slice_in_dim(slot_rows, turn_index * turn_slots, turn_slots)
        share_rows = lax.dynamic_slice_in_dim(slot_share, turn_index * turn_slots, turn_slots)
        picked = normed_second[token_rows].reshape(per_turn, capacity, model_width)
        return (token_rows, share_rows, picked)

    def forward_turn(running, turn_index):
        gate_part, up_part, down_part = local_experts(turn_index)
        gate_full, up_full, down_full = (
            lax.all_gather(gate_part, GROUP, axis=1, tiled=True),
            lax.all_gather(up_part, GROUP, axis=1, tiled=True),
            lax.all_gather(down_part, GROUP, axis=2, tiled=True),
        )
        token_rows, share_rows, picked = turn_inputs(turn_index)
        gate_value = jnp.einsum(
            PRODUCT_2, picked, gate_full, preferred_element_type=jnp.float32
        )
        up_value = jnp.einsum(PRODUCT_2, picked, up_full, preferred_element_type=jnp.float32)
        inner = swiglu(gate_value, up_value).astype(jnp.bfloat16)
        expert_result = jnp.einsum(
            PRODUCT_3, inner, down_full, preferred_element_type=jnp.float32
        ).reshape(turn_slots, model_width)
        return (running.at[token_rows].add(expert_result * share_rows[:, None]), None)

    turn_ids = jnp.arange(turn_count, dtype=jnp.int32)
    expert_part, _ = lax.scan(
        forward_turn, jnp.zeros((row_count, model_width), jnp.float32), turn_ids
    )
    expert_total = lax.psum(expert_part.astype(jnp.bfloat16), TENSOR).astype(jnp.float32)
    output = (hidden + expert_total).astype(jnp.bfloat16)
    upstream = cotangent.astype(jnp.float32)

    def backward_turn(running, turn_index):
        gate_part, up_part, down_part = local_experts(turn_index)
        gate_full, up_full, down_full = (
            lax.all_gather(gate_part, GROUP, axis=1, tiled=True),
            lax.all_gather(up_part, GROUP, axis=1, tiled=True),
            lax.all_gather(down_part, GROUP, axis=2, tiled=True),
        )
        token_rows, share_rows, picked = turn_inputs(turn_index)
        gate_value = jnp.einsum(
            PRODUCT_2, picked, gate_full, preferred_element_type=jnp.float32
        )
        up_value = jnp.einsum(PRODUCT_2, picked, up_full, preferred_element_type=jnp.float32)
        inner_float, swiglu_back = jax.vjp(swiglu, gate_value, up_value)
        inner = inner_float.astype(jnp.bfloat16)
        grad_slot = (
            (upstream[token_rows] * share_rows[:, None])
            .astype(jnp.bfloat16)
            .reshape(per_turn, capacity, model_width)
        )
        grad_inner = jnp.einsum(
            PRODUCT_4, grad_slot, down_full, preferred_element_type=jnp.float32
        )
        grad_gate_value, grad_up_value = swiglu_back(grad_inner)
        grad_gate_low = grad_gate_value.astype(jnp.bfloat16)
        grad_up_low = grad_up_value.astype(jnp.bfloat16)
        grad_picked = jnp.einsum(
            PRODUCT_5, grad_gate_low, gate_full, preferred_element_type=jnp.float32
        )
        grad_picked = grad_picked + jnp.einsum(
            PRODUCT_5, grad_up_low, up_full, preferred_element_type=jnp.float32
        )
        running = running.at[token_rows].add(grad_picked.reshape(turn_slots, model_width))
        shard_grads = (
            lax.psum_scatter(
                jnp.einsum(
                    PRODUCT_6, picked, grad_gate_low, preferred_element_type=jnp.float32
                ).astype(jnp.bfloat16),
                GROUP,
                scatter_dimension=1,
                tiled=True,
            ).astype(jnp.float32),
            lax.psum_scatter(
                jnp.einsum(
                    PRODUCT_6, picked, grad_up_low, preferred_element_type=jnp.float32
                ).astype(jnp.bfloat16),
                GROUP,
                scatter_dimension=1,
                tiled=True,
            ).astype(jnp.float32),
            lax.psum_scatter(
                jnp.einsum(
                    PRODUCT_7, inner, grad_slot, preferred_element_type=jnp.float32
                ).astype(jnp.bfloat16),
                GROUP,
                scatter_dimension=2,
                tiled=True,
            ).astype(jnp.float32),
        )
        return (running, shard_grads)

    grad_second_part, stacked_grads = lax.scan(
        backward_turn, jnp.zeros((row_count, model_width), jnp.float32), turn_ids
    )
    grad_gate_out = stacked_grads[0].reshape(gate_weight.shape)
    grad_up_out = stacked_grads[1].reshape(up_weight.shape)
    grad_down_out = stacked_grads[2].reshape(down_weight.shape)
    grad_second = lax.psum(grad_second_part.astype(jnp.bfloat16), TENSOR).astype(jnp.float32)
    grad_hidden_norm, grad_gain_ffn_local = ffn_norm_back(grad_second)
    grad_hidden = upstream + grad_hidden_norm
    grad_hidden_low = grad_hidden.astype(jnp.bfloat16)
    grad_out_local = jnp.einsum(
        "tc,td->cd", attended, grad_hidden_low, preferred_element_type=jnp.float32
    )
    grad_attended = jnp.einsum(
        "td,cd->tc", grad_hidden_low, out_full, preferred_element_type=jnp.float32
    )
    grad_attended = grad_attended.astype(jnp.bfloat16).reshape(
        row_count, kv_heads, group_size, head_size
    )
    grad_query_parts = []
    grad_keys = jnp.zeros(key_heads.shape, jnp.float32)
    grad_values = jnp.zeros(value_heads.shape, jnp.float32)
    for block_number in range(len(block_starts)):
        block_first = block_starts[block_number]
        query_block, scores = block_scores(block_first)
        probs_float = jnp.exp(scores - lse_parts[block_number])
        probs = probs_float.astype(jnp.bfloat16)
        grad_block = grad_attended[block_first : block_first + block_rows]
        grad_probs = jnp.einsum(
            PRODUCT_0, grad_block, value_heads, preferred_element_type=jnp.float32
        )
        inner_sum = jnp.sum(grad_probs * probs_float, axis=-1, keepdims=True)
        grad_scores = (score_scale * (probs_float * (grad_probs - inner_sum))).astype(jnp.bfloat16)
        grad_query_parts.append(
            jnp.einsum(PRODUCT_1, grad_scores, key_heads, preferred_element_type=jnp.float32)
        )
        grad_keys = grad_keys + jnp.einsum(
            PRODUCT_8, grad_scores, query_block, preferred_element_type=jnp.float32
        )
        grad_values = grad_values + jnp.einsum(
            PRODUCT_8, probs, grad_block, preferred_element_type=jnp.float32
        )
    grad_key_own, grad_value_own = (
        lax.psum_scatter(
            grad_keys.astype(jnp.bfloat16), CONTEXT, scatter_dimension=0, tiled=True
        ).astype(jnp.float32),
        lax.psum_scatter(
            grad_values.astype(jnp.bfloat16), CONTEXT, scatter_dimension=0, tiled=True
        ).astype(jnp.float32),
    )
    grad_query_all = jnp.concatenate(grad_query_parts, axis=0).reshape(row_count, -1, head_size)
    grad_query_lin = rope_query_back(grad_query_all)[0].astype(jnp.bfloat16).reshape(row_count, -1)
    grad_key_lin = rope_key_back(grad_key_own)[0].astype(jnp.bfloat16).reshape(row_count, -1)
    grad_value_low = grad_value_own.astype(jnp.bfloat16).reshape(row_count, -1)
    grad_first_part = jnp.einsum(
        "tc,dc->td", grad_query_lin, query_full, preferred_element_type=jnp.float32
    )
    grad_first_part = grad_first_part + jnp.einsum(
        "tc,dc->td", grad_key_lin, key_full, preferred_element_type=jnp.float32
    )
    grad_first_part = grad_first_part + jnp.einsum(
        "tc,dc->td", grad_value_low, value_full, preferred_element_type=jnp.float32
    )
    grad_first = lax.psum(grad_first_part.astype(jnp.bfloat16), TENSOR).astype(jnp.float32)
    grad_input_norm, grad_gain_attn_local = attn_norm_back(grad_first)
    grad_input = (grad_hidden + grad_input_norm).astype(jnp.bfloat16)
    grad_query_local = jnp.einsum(
        "td,tc->dc", first_normalized, grad_query_lin, preferred_element_type=jnp.float32
    )
    grad_key_local = jnp.einsum(
        "td,tc->dc", first_normalized, grad_key_lin, preferred_element_type=jnp.float32
    )
    grad_value_local = jnp.einsum(
        "td,tc->dc", first_normalized, grad_value_low, preferred_element_type=jnp.float32
    )
    reduced = (
        lax.psum_scatter(
            grad_gain_attn_local.astype(jnp.bfloat16),
            GROUP,
            scatter_dimension=0,
            tiled=True,
        ).astype(jnp.float32),
        lax.psum_scatter(
            grad_query_local.astype(jnp.bfloat16),
            GROUP,
            scatter_dimension=0,
            tiled=True,
        ).astype(jnp.float32),
        lax.psum_scatter(
            grad_key_local.astype(jnp.bfloat16),
            GROUP,
            scatter_dimension=0,
            tiled=True,
        ).astype(jnp.float32),
        lax.psum_scatter(
            grad_value_local.astype(jnp.bfloat16),
            GROUP,
            scatter_dimension=0,
            tiled=True,
        ).astype(jnp.float32),
        lax.psum_scatter(
            grad_out_local.astype(jnp.bfloat16),
            GROUP,
            scatter_dimension=1,
            tiled=True,
        ).astype(jnp.float32),
        lax.psum_scatter(
            grad_gain_ffn_local.astype(jnp.bfloat16),
            GROUP,
            scatter_dimension=0,
            tiled=True,
        ).astype(jnp.float32),
    )
    return (
        output,
        grad_input,
        reduced[0],
        reduced[1],
        reduced[2],
        reduced[3],
        reduced[4],
        reduced[5],
        grad_gate_out,
        grad_up_out,
        grad_down_out,
    )


F32 = jnp.float32
BF16 = jnp.bfloat16
LAST_LAST = (((1,), (1,)), ((), ()))
FIRST_FIRST = (((0,), (0,)), ((), ()))


def weight_copies(own_hbm, other_hbm, weights, sems):
    sources, _, rows, lanes = own_hbm.shape
    units = lanes // 3
    return [
        pltpu.make_async_copy(
            half_hbm.at[source, :, :, pl.ds(part * units, units)],
            weights.at[
                :, pl.ds(source * rows, rows), pl.ds((2 * part + half) * units, units)
            ],
            sems.at[source, half, part],
        )
        for source in range(sources)
        for half, half_hbm in enumerate((own_hbm, other_hbm))
        for part in range(3)
    ]


def project(tokens, cotangent, weights):
    hidden_units = weights.shape[1] // 3
    gate_up = jnp.dot(tokens, weights[:, : 2 * hidden_units], preferred_element_type=F32)
    grad_inner = jnp.dot(cotangent, weights[:, 2 * hidden_units :], preferred_element_type=F32)
    return gate_up, grad_inner


def activate(gate_up, grad_inner, share):
    hidden_units = grad_inner.shape[1]
    gate, up = gate_up[:, :hidden_units], gate_up[:, hidden_units:]
    sigmoid = 1.0 / (1.0 + jnp.exp(-gate))
    silu = gate * sigmoid
    grad_inner = grad_inner * share
    inner = silu * up * share
    grad_gate = grad_inner * up * (sigmoid * (1.0 + gate * (1.0 - sigmoid)))
    grad_up = grad_inner * silu
    return inner.astype(BF16), grad_gate.astype(BF16), grad_up.astype(BF16)


MESH_ID = pl.DeviceIdType.MESH


class Place:
    def __init__(self, line):
        self.line = line
        self.z, self.y = lax.axis_index(SHARD), lax.axis_index(CONTEXT)
        self.t = lax.axis_index(TENSOR)
        self.sibling = (self.z, self.y, self.t + 1 - 2 * (self.t % 2))
        self.partner = (self.z, 1 - self.y, self.t)
        self.across = (self.z, self.y, (self.t + 2) % 4)

    def beside(self, side):
        return (self.z + side, self.y, self.t)

    def inside(self, at):
        return (at >= 0) & (at < self.line)

    def near(self, rank):
        z, line = self.z, self.line
        half = z // 2
        mirrored = z * (1 - half) + (line - 1 - z) * half
        far = rank // 2
        place = (1 - far) * (mirrored + rank - 2 * mirrored * rank) + far * rank
        return place * (1 - half) + (line - 1 - place) * half

    def block(self, order, step):
        rank, across = order[0]
        for number, (later_rank, later_across) in enumerate(order[1:], 1):
            rank = jnp.where(step == number, later_rank, rank)
            across = jnp.where(step == number, later_across, across)
        column = self.y + across - 2 * self.y * across
        return self.near(rank) * 2 + column

    def meet(self):
        z, line = self.z, self.line
        barrier = pltpu.get_barrier_semaphore()
        for device in (self.sibling, self.partner, self.across):
            pl.semaphore_signal(barrier, inc=1, device_id=device, device_id_type=MESH_ID)
        for side in (-1, 1):

            @pl.when(self.inside(z + side))
            def _():
                pl.semaphore_signal(
                    barrier, inc=1, device_id=self.beside(side), device_id_type=MESH_ID
                )

        below, above = (z + line - 1) // line, (2 * line - 2 - z) // line
        pl.semaphore_wait(barrier, 3 + below + above)


def remote(source, target, send, recv, device):
    return pltpu.make_async_remote_copy(
        src_ref=source,
        dst_ref=target,
        send_sem=send,
        recv_sem=recv,
        device_id=device,
        device_id_type=MESH_ID,
    )


class Gather:
    order = ((0, 0), (1, 0), (0, 1), (2, 0), (1, 1), (3, 0), (2, 1), (3, 1))
    rounds = (0, 2, 4)
    crossings = (1, 3, 5, 6)

    def __init__(self, place, tokens, sems):
        self.place, self.tokens = place, tokens
        self.recv, self.along, self.across, self.cores = sems

    def line_copy(self, at, side, source=None):
        here, tokens = at * 2 + self.place.y, self.tokens
        return remote(
            tokens.at[here, 0] if source is None else source,
            tokens.at[here, 0],
            self.along.at[at, (side + 1) // 2],
            self.recv.at[here, 0],
            self.place.beside(side),
        )

    def pair_copy(self, at, column, source=None):
        here, tokens = at * 2 + column, self.tokens
        return remote(
            tokens.at[here, 0] if source is None else source,
            tokens.at[here, 0],
            self.across.at[at],
            self.recv.at[here, 0],
            self.place.partner,
        )

    def core_copy(self, here, source=None):
        tokens = self.tokens
        return remote(
            tokens.at[here, 0] if source is None else source,
            tokens.at[here, 1],
            self.cores.at[here],
            self.recv.at[here, 1],
            self.place.sibling,
        )

    def start(self, piece):
        place = self.place
        for side in (-1, 1):
            pl.when(place.inside(place.z + side))(
                lambda: self.line_copy(place.z, side, piece).start()
            )
        self.pair_copy(place.z, place.y, piece).start()
        self.core_copy(place.z * 2 + place.y, piece).start()

    def came_along(self, at, side):
        place = self.place
        self.line_copy(at, -side).wait_recv()
        pl.when(place.inside(place.z - side))(lambda: self.line_copy(at, -side).start())
        self.pair_copy(at, place.y).start()
        self.core_copy(at * 2 + place.y).start()

    def came_across(self, at):
        column = 1 - self.place.y
        self.pair_copy(at, column).wait_recv()
        self.core_copy(at * 2 + column).start()

    def tick(self, number):
        place = self.place
        for distance, when in enumerate(self.rounds, 1):

            @pl.when(number == when)
            def _():
                for side in (-1, 1):
                    at = place.z + side * distance
                    pl.when(place.inside(at))(partial(self.came_along, at, side))

        for distance, when in enumerate(self.crossings):

            @pl.when(number == when)
            def _():
                for side in (-1, 1) if distance else (1,):
                    at = place.z + side * distance
                    pl.when(place.inside(at))(partial(self.came_across, at))

    def finish(self):
        place = self.place
        for side in (-1, 1):
            for distance in range(place.line):
                at = place.z - side * distance

                @pl.when(place.inside(at) & place.inside(place.z + side))
                def _():
                    self.line_copy(at, side).wait_send()

        for at in range(place.line):
            self.pair_copy(at, place.y).wait_send()
        for here in range(2 * place.line):
            self.core_copy(here).wait_send()


class Reduce:
    order = ((3, 1), (3, 0), (2, 1), (2, 0), (1, 1), (1, 0), (0, 1), (0, 0))

    def __init__(self, place, arrays, terms, term_sems, sums, base, sems):
        self.place, self.terms, self.term_sems = place, terms, term_sems
        self.sums, self.base = sums, base
        self.parts, self.from_core, self.from_pair, self.from_line = arrays
        self.core_send, self.core_recv, self.pair_send, self.pair_recv = sems[:4]
        self.line_send, self.line_recv = sems[4:]

    def core_copy(self, here, source):
        return remote(
            source,
            self.from_core.at[here],
            self.core_send.at[here],
            self.core_recv.at[here],
            self.place.sibling,
        )

    def core_arrived(self, here):
        self.core_copy(here, self.from_core.at[here]).wait_recv()

    def pair_copy(self, at, slot):
        return remote(
            self.sums.at[self.base + slot],
            self.from_pair.at[at],
            self.pair_send.at[at],
            self.pair_recv.at[at],
            self.place.partner,
        )

    def line_copy(self, at, side, distance):
        slot = self.place.line if distance == 1 and side == 1 else at
        return remote(
            self.sums.at[self.base + 2 + (side + 1) // 2],
            self.from_line.at[slot],
            self.line_send.at[at],
            self.line_recv.at[slot],
            self.place.beside(side),
        )

    def add_up(self, sources, slot):
        terms = self.terms
        copies = [
            pltpu.make_async_copy(source, terms.at[i], self.term_sems.at[i])
            for i, (source, _) in enumerate(sources)
        ]
        for copy, (_, there) in zip(copies, sources):
            if there is None:
                copy.start()
            else:
                pl.when(there)(copy.start)
        for i, (copy, (_, there)) in enumerate(zip(copies, sources)):
            if there is None:
                copy.wait()
            else:
                pl.when(there)(copy.wait)

                @pl.when(jnp.logical_not(there))
                def _():
                    terms[i] = jnp.zeros_like(terms[i])

        tile = 16

        @pl.loop(0, terms.shape[1] // tile)
        def _(number):
            here = pl.ds(pl.multiple_of(number * tile, tile), tile)
            total = terms[0, here, :].astype(F32)
            for i in range(1, len(sources)):
                total += terms[i, here, :].astype(F32)
            self.sums[self.base + slot, here, :] = total.astype(BF16)

    def cross(self, rank):
        place = self.place
        at = place.near(rank)
        here = at * 2 + 1 - place.y
        slot = rank % 2
        if rank + 2 < place.line:
            self.pair_copy(place.near(rank + 2), slot).wait_send()
        self.core_arrived(here)
        self.add_up([(self.parts.at[here], None), (self.from_core.at[here], None)], slot)
        self.pair_copy(at, slot).start()

    def advance(self, distance):
        place = self.place
        for side in (-1, 1):
            at = place.z + side * distance
            here = at * 2 + place.y
            farther = place.inside(place.z - side)
            if distance + 1 < place.line:

                @pl.when(place.inside(at + side))
                def _():
                    self.line_copy(at + side, side, distance + 1).wait_send()

            @pl.when(place.inside(at))
            def _():
                self.core_arrived(here)
                self.pair_copy(at, 0).wait_recv()
                sources = [
                    (self.parts.at[here], None),
                    (self.from_core.at[here], None),
                    (self.from_pair.at[at], None),
                ]
                if distance + 1 < place.line:

                    @pl.when(farther)
                    def _():
                        self.line_copy(at, side, distance + 1).wait_recv()

                    sources.append((self.from_line.at[at], farther))
                self.add_up(sources, 2 + (side + 1) // 2)
                self.line_copy(at, side, distance).start()

    def tick(self, number, late):
        line = self.place.line
        for rank in range(line):
            when = 2 * (line - rank) - 1
            pl.when(number == when)(partial(self.cross, rank))
            if rank + 1 < line:
                pl.when(number == when + late)(partial(self.advance, rank + 1))

    def finish(self, result, sem):
        place = self.place
        z, line = place.z, place.line
        here = z * 2 + place.y
        self.core_arrived(here)
        self.pair_copy(z, 0).wait_recv()
        for side in (-1, 1):
            pl.when(place.inside(z + side))(lambda: self.line_copy(z, -side, 1).wait_recv())
        for rank in (1, 0):
            self.pair_copy(place.near(rank), rank % 2).wait_send()
        self.add_up(
            [
                (self.parts.at[here], None),
                (self.from_core.at[here], None),
                (self.from_pair.at[z], None),
                (self.from_line.at[z], place.inside(z + 1)),
                (self.from_line.at[line], place.inside(z - 1)),
            ],
            0,
        )
        copy = pltpu.make_async_copy(self.sums.at[self.base], result, sem)
        copy.start()
        copy.wait()
        for side in (-1, 1):

            @pl.when(place.inside(z + side))
            def _():
                self.line_copy(z + side, side, 1).wait_send()


def expert_kernel(*refs, line, chunk, gathers):
    refs = list(refs)

    def take(count):
        taken = refs[:count]
        del refs[:count]
        return taken[0] if count == 1 else taken

    tokens_in, cotangent_own = take(2)
    if not gathers:
        cotangent_other = take(1)
    shares_ref, own_hbm, other_hbm, exchanged = take(4)
    if not gathers:
        before = take(1)
        grad_piece, out_piece, grad_own, grad_other, received = take(5)
        grad_arrays, out_arrays = take(4), take(4)
        tokens_hbm = tokens_in
    else:
        parts_hbm, grad_own, grad_other, tokens_hbm, received, cotangent_other = take(6)
    weights, grads, tokens_buf, cotangent_buf, inner_low, grad_low = take(6)
    both_buf, stage, load_sems, store_sems, row_sems, part_sems, exchange_sems = take(7)

    expert_count, model_width, all_units = weights.shape
    hidden_units = all_units // 3
    units = hidden_units // 2
    steps = 2 * line
    rows = tokens_hbm.shape[2]
    place = Place(line)
    first_rows, second_rows = pl.ds(0, rows), pl.ds(rows, rows)
    if gathers:
        mover = Gather(place, tokens_hbm, take(4))
        cotangent_send, cotangent_recv = take(2)
    else:
        before_buf, terms, sums, term_sems = take(4)
        movers = [
            Reduce(place, arrays, terms, term_sems, sums, 4 * number, take(6))
            for number, arrays in enumerate((grad_arrays, out_arrays))
        ]
    order = mover.order if gathers else Reduce.order

    def cotangent_copy(step):
        here = place.block(order, step)
        return remote(
            cotangent_own.at[here],
            cotangent_other.at[here],
            cotangent_send.at[here],
            cotangent_recv.at[here],
            place.sibling,
        )

    place.meet()
    exchange = remote(
        exchanged, received, exchange_sems.at[0], exchange_sems.at[1], place.across
    )
    exchange.start()
    if gathers:
        own_block = place.z * 2 + place.y
        own_copy = pltpu.make_async_copy(tokens_in, tokens_hbm.at[own_block, 0], row_sems.at[0, 0])
        mover.start(tokens_in)
        own_copy.start()
        for step in range(steps):
            cotangent_copy(step).start()
    weight_loads = weight_copies(own_hbm, other_hbm, weights, load_sems)
    for copy in weight_loads:
        copy.start()
    grads[...] = jnp.zeros_like(grads)

    def row_copies(step, slot):
        here = place.block(order, step)
        lanes = pl.ds(0, model_width)
        pairs = [
            (tokens_hbm.at[here, 0], tokens_buf.at[slot, first_rows, :]),
            (tokens_hbm.at[here, 1], tokens_buf.at[slot, second_rows, :]),
            (cotangent_own.at[here, :, lanes], cotangent_buf.at[slot, first_rows, :]),
            (cotangent_other.at[here, :, lanes], cotangent_buf.at[slot, second_rows, :]),
        ]
        if not gathers:
            pairs.append((before.at[here], before_buf.at[slot]))
        return [
            pltpu.make_async_copy(source, target, row_sems.at[slot, i])
            for i, (source, target) in enumerate(pairs)
        ]

    def load_rows(step, slot):
        if gathers:
            mover.core_copy(place.block(order, step)).wait_recv()
            cotangent_copy(step).wait_recv()
        for copy in row_copies(step, slot):
            copy.start()

    if gathers:
        own_copy.wait()
    load_rows(0, 0)
    for copy in weight_loads:
        copy.wait()

    halves = [pl.ds(number * model_width, model_width) for number in range(2)]

    def core_copies(step, slot):
        here = place.block(order, step)
        return [
            mover.core_copy(here, both_buf.at[slot, second_rows, lanes])
            for mover, lanes in zip(movers, halves)
        ]

    def part_copies(step, slot):
        here = place.block(order, step)
        if gathers:
            pairs = [(both_buf.at[slot], parts_hbm.at[here])]
        else:
            pairs = [
                (both_buf.at[slot, first_rows, lanes], mover.parts.at[here])
                for mover, lanes in zip(movers, halves)
            ]
        return [
            pltpu.make_async_copy(source, target, part_sems.at[slot, i])
            for i, (source, target) in enumerate(pairs)
        ]

    @pl.loop(0, steps)
    def _(step):
        slot = step % 2
        for copy in row_copies(step, slot):
            copy.wait()
        shares = shares_ref[place.block(order, step)]
        lane = lax.broadcasted_iota(jnp.int32, shares.shape, 1)

        def run(expert, gate_up, grad_inner):
            share = jnp.sum(jnp.where(lane == expert, shares, 0.0), axis=1, keepdims=True)
            inner, grad_gate, grad_up = activate(gate_up, grad_inner, share)
            inner_low[expert] = inner
            grad_low[expert, :, :hidden_units] = grad_gate
            grad_low[expert, :, hidden_units:] = grad_up

        def weight_grads(expert):
            grads[expert, :, : 2 * hidden_units] += lax.dot_general(
                tokens_buf[slot], grad_low[expert], FIRST_FIRST, preferred_element_type=F32
            )
            grads[expert, :, 2 * hidden_units :] += lax.dot_general(
                cotangent_buf[slot], inner_low[expert], FIRST_FIRST, preferred_element_type=F32
            )

        results = project(tokens_buf[slot], cotangent_buf[slot], weights[0])
        for expert in range(expert_count):
            run(expert, *results)
            if expert + 1 < expert_count:
                results = project(tokens_buf[slot], cotangent_buf[slot], weights[expert + 1])
            weight_grads(expert)

        @pl.when(step >= 1)
        def _():
            for copy in part_copies(step - 1, 1 - slot):
                copy.wait()

        if gathers:
            mover.tick(step)
        else:
            for late, reducer in enumerate(movers):
                reducer.tick(step, late)

            @pl.when(step >= 2)
            def _():
                for copy in core_copies(step - 2, slot):
                    copy.wait_send()

        @pl.loop(0, model_width // chunk)
        def _(number):
            @pl.when((number == 1) & (step + 1 < steps))
            def _():
                load_rows(step + 1, 1 - slot)

            cols = pl.ds(pl.multiple_of(number * chunk, chunk), chunk)

            def total_of(lows, lanes, target):
                if gathers:
                    total = jnp.zeros((2 * rows, chunk), F32)
                else:
                    total = before_buf[slot, :, target].astype(F32)
                for expert in range(expert_count):
                    total += lax.dot_general(
                        lows[expert],
                        weights[expert, cols, lanes],
                        LAST_LAST,
                        preferred_element_type=F32,
                    )
                both_buf[slot, :, target] = total.astype(BF16)

            beyond = pl.ds(pl.multiple_of(model_width + number * chunk, chunk), chunk)
            total_of(grad_low, pl.ds(0, 2 * hidden_units), cols)
            total_of(inner_low, pl.ds(2 * hidden_units, hidden_units), beyond)

        if not gathers:
            for copy in core_copies(step, slot):
                copy.start()
        for copy in part_copies(step, slot):
            copy.start()

    last = (steps - 1) % 2
    for copy in part_copies(steps - 1, last):
        copy.wait()
    if not gathers:
        for copy in core_copies(steps - 2, 1 - last) + core_copies(steps - 1, last):
            copy.wait_send()
        movers[1].advance(1)

    sources, _, slice_rows, _ = own_hbm.shape

    def grad_copy(expert, source, half, slot):
        return pltpu.make_async_copy(
            stage.at[slot, half],
            (grad_own, grad_other)[half].at[source, expert],
            store_sems.at[slot, half],
        )

    @pl.loop(0, expert_count * sources)
    def _(number):
        expert, source = number // sources, number % sources
        slot = number % 2

        @pl.when(number >= 2)
        def _():
            for half in range(2):
                grad_copy(expert, source, half, slot).wait()

        here = pl.ds(pl.multiple_of(source * slice_rows, slice_rows), slice_rows)
        for half in range(2):
            for part in range(3):
                first = (2 * part + half) * units
                stage[slot, half, :, part * units : (part + 1) * units] = grads[
                    expert, here, first : first + units
                ].astype(BF16)
            grad_copy(expert, source, half, slot).start()

    for slot in range(2):
        for half in range(2):
            grad_copy(0, 0, half, slot).wait()

    exchange.wait()
    if gathers:
        mover.finish()
        for step in range(steps):
            cotangent_copy(step).wait_send()
    else:
        for number, result in enumerate((grad_piece, out_piece)):
            movers[number].finish(result, row_sems.at[0, number])


def expert_call(operands, own, shares, line, rows, model_width, gathers, collective_id, chunk=512):
    sources, expert_count, slice_rows, lanes = own.shape
    hidden_units = 2 * lanes // 3
    blocks = 2 * line
    in_place = pl.BlockSpec(memory_space=pl.ANY)
    dma = pltpu.SemaphoreType.DMA
    flops = 2 * blocks * 2 * rows * model_width * expert_count * hidden_units * 9

    def low(*shape):
        return jax.ShapeDtypeStruct(shape, BF16)

    if gathers:
        out_shape = [
            low(blocks, 2 * rows, 2 * model_width),
            low(*own.shape),
            low(*own.shape),
            low(blocks, 2, rows, model_width),
            low(*operands[5].shape),
            low(*operands[1].shape),
        ]
        own_scratch = [dma((blocks, 2)), dma((line, 2)), dma((line,)), dma((blocks,))]
        own_scratch += [dma((blocks,)), dma((blocks,))]
    else:
        out_shape = [
            low(rows, model_width),
            low(rows, model_width),
            low(*own.shape),
            low(*own.shape),
            low(*operands[6].shape),
        ]
        out_shape += 2 * [
            low(blocks, rows, model_width),
            low(blocks, rows, model_width),
            low(line, rows, model_width),
            low(line + 1, rows, model_width),
        ]
        own_scratch = [
            pltpu.VMEM((2, 2 * rows, 2 * model_width), BF16),
            pltpu.VMEM((5, rows, model_width), BF16),
            pltpu.VMEM((8, rows, model_width), BF16),
            dma((5,)),
        ]
        own_scratch += 2 * [
            dma((blocks,)),
            dma((blocks,)),
            dma((line,)),
            dma((line,)),
            dma((line,)),
            dma((line + 1,)),
        ]
    in_specs = [in_place] * len(operands)
    in_specs[2 if gathers else 3] = pl.BlockSpec(memory_space=pltpu.VMEM)
    results = pl.pallas_call(
        partial(expert_kernel, line=line, chunk=chunk, gathers=gathers),
        in_specs=in_specs,
        out_specs=[in_place] * len(out_shape),
        out_shape=out_shape,
        scratch_shapes=[
            pltpu.VMEM((expert_count, model_width, 3 * hidden_units), BF16),
            pltpu.VMEM((expert_count, model_width, 3 * hidden_units), F32),
            pltpu.VMEM((2, 2 * rows, model_width), BF16),
            pltpu.VMEM((2, 2 * rows, model_width), BF16),
            pltpu.VMEM((expert_count, 2 * rows, hidden_units), BF16),
            pltpu.VMEM((expert_count, 2 * rows, 2 * hidden_units), BF16),
            pltpu.VMEM((2, 2 * rows, 2 * model_width), BF16),
            pltpu.VMEM((2, 2, slice_rows, lanes), BF16),
            dma((sources, 2, 3)),
            dma((2, 2)),
            dma((2, 5)),
            dma((2, 2)),
            dma((2,)),
        ]
        + own_scratch,
        compiler_params=pltpu.CompilerParams(
            vmem_limit_bytes=60 * 2**20, collective_id=collective_id, has_side_effects=True
        ),
        cost_estimate=pl.CostEstimate(
            flops=flops, bytes_accessed=80 * 2**20, transcendentals=0
        ),
    )(*operands)
    return results[: 6 if gathers else 5]


def experts_gathering(piece, cotangent, shares, own, other, exchanged, line):
    rows, model_width = piece.shape
    operands = (piece, cotangent, shares, own, other, exchanged)
    return expert_call(operands, own, shares, line, rows, model_width, True, 1)


def experts_reducing(
    tokens, cotangents, shares, own, other, exchanged, parts, line
):
    _, _, rows, model_width = tokens.shape
    operands = (tokens, *cotangents, shares, own, other, exchanged, parts)
    return expert_call(operands, own, shares, line, rows, model_width, False, 2)


def attention_rows(values, kv_head, group_size):
    first = kv_head * group_size
    return jnp.concatenate(
        [values[:, (first + r) * HEAD_DIM : (first + r + 1) * HEAD_DIM] for r in range(group_size)],
        axis=0,
    )


def quarter_turn(values):
    half = HEAD_DIM // 2
    return jnp.concatenate([-values[:, half:], values[:, :half]], axis=1)


def window_mask(start, doc_start_ref, first_ref, block_rows, window):
    key_index = start + lax.broadcasted_iota(jnp.int32, (block_rows, window), 1)
    query_index = (
        first_ref[0]
        + pl.program_id(0) * block_rows
        + lax.broadcasted_iota(jnp.int32, (block_rows, window), 0)
    )
    return (key_index <= query_index) & (key_index >= doc_start_ref[...])


def window_start(first_ref, block_rows, window):
    end = first_ref[0] + (pl.program_id(0) + 1) * block_rows
    return pl.multiple_of(jnp.maximum(end - window, 0), block_rows)


def attention_forward_kernel(
    first_ref, query_ref, key_value_ref, doc_start_ref, attended_ref, lse_ref, *, group_size, window
):
    block_rows = query_ref.shape[0]
    kv_heads = key_value_ref.shape[1] // (2 * HEAD_DIM)
    start = window_start(first_ref, block_rows, window)
    allowed = window_mask(start, doc_start_ref, first_ref, block_rows, window)
    bias = jnp.where(allowed, 0.0, -1e30)
    bias = jnp.concatenate([bias] * group_size, axis=0)
    keys_values = key_value_ref[pl.ds(start, window), :]
    queries = query_ref[...]
    parts = []
    for g in range(kv_heads):
        keys = keys_values[:, g * HEAD_DIM : (g + 1) * HEAD_DIM]
        values = keys_values[:, (kv_heads + g) * HEAD_DIM : (kv_heads + g + 1) * HEAD_DIM]
        scores = lax.dot_general(
            attention_rows(queries, g, group_size), keys, LAST_LAST, preferred_element_type=F32
        )
        scores = scores * HEAD_DIM**-0.5 + bias
        row_max = jnp.max(scores, axis=1, keepdims=True)
        exponent = jnp.exp(scores - row_max)
        total = jnp.sum(exponent, axis=1, keepdims=True)
        probs = (exponent * (1.0 / total)).astype(BF16)
        mixed = jnp.dot(probs, values, preferred_element_type=F32).astype(BF16)
        lse_ref[0, g] = row_max + jnp.log(total)
        parts += [mixed[r * block_rows : (r + 1) * block_rows] for r in range(group_size)]
    attended_ref[...] = jnp.concatenate(parts, axis=1)


def attention_backward_kernel(
    first_ref,
    query_ref,
    key_value_ref,
    doc_start_ref,
    lse_ref,
    grad_ref,
    turns_ref,
    query_turns_ref,
    grad_query_ref,
    grad_key_value_ref,
    grad_keys,
    grad_values,
    *,
    group_size,
    window,
    steps,
):
    step = pl.program_id(0)
    block_rows = query_ref.shape[0]
    kv_heads = key_value_ref.shape[1] // (2 * HEAD_DIM)

    @pl.when(step == 0)
    def _():
        grad_keys[...] = jnp.zeros_like(grad_keys)
        grad_values[...] = jnp.zeros_like(grad_values)

    start = window_start(first_ref, block_rows, window)
    allowed = window_mask(start, doc_start_ref, first_ref, block_rows, window)
    bias = jnp.where(allowed, 0.0, -1e30)
    bias = jnp.concatenate([bias] * group_size, axis=0)
    rows = pl.ds(start, window)
    keys_values = key_value_ref[rows, :]
    queries = query_ref[...]
    grads = grad_ref[...]
    query_turns = jnp.concatenate([query_turns_ref[...]] * group_size, axis=0)
    parts = []
    for g in range(kv_heads):
        keys = keys_values[:, g * HEAD_DIM : (g + 1) * HEAD_DIM]
        values = keys_values[:, (kv_heads + g) * HEAD_DIM : (kv_heads + g + 1) * HEAD_DIM]
        query_rows = attention_rows(queries, g, group_size)
        grad_rows = attention_rows(grads, g, group_size)
        scores = lax.dot_general(query_rows, keys, LAST_LAST, preferred_element_type=F32)
        probs = jnp.exp(scores * HEAD_DIM**-0.5 + bias - lse_ref[0, g])
        grad_probs = lax.dot_general(grad_rows, values, LAST_LAST, preferred_element_type=F32)
        inner = jnp.sum(grad_probs * probs, axis=1, keepdims=True)
        grad_scores = (HEAD_DIM**-0.5 * (probs * (grad_probs - inner))).astype(BF16)
        grad_values[g, rows, :] += lax.dot_general(
            probs.astype(BF16), grad_rows, FIRST_FIRST, preferred_element_type=F32
        )
        both_queries = jnp.concatenate([query_rows, quarter_turn(query_rows)], axis=1)
        grad_keys[g, rows, :] += lax.dot_general(
            grad_scores, both_queries, FIRST_FIRST, preferred_element_type=F32
        )
        both_keys = jnp.concatenate([keys, quarter_turn(keys)], axis=1)
        turned = jnp.dot(grad_scores, both_keys, preferred_element_type=F32) * query_turns
        grad_query = (turned[:, :HEAD_DIM] + turned[:, HEAD_DIM:]).astype(BF16)
        parts += [grad_query[r * block_rows : (r + 1) * block_rows] for r in range(group_size)]
    grad_query_ref[...] = jnp.concatenate(parts, axis=1)

    @pl.when(step == steps - 1)
    def _():
        key_parts, value_parts = [], []
        for g in range(kv_heads):
            turned = grad_keys[g] * turns_ref[...]
            key_parts.append((turned[:, :HEAD_DIM] + turned[:, HEAD_DIM:]).astype(BF16))
            value_parts.append(grad_values[g].astype(BF16))
        grad_key_value_ref[...] = jnp.concatenate(key_parts + value_parts, axis=1)


def attention_specs(queries, keys_values, block_rows):
    return dict(
        smem=pl.BlockSpec(memory_space=pltpu.SMEM),
        rows=pl.BlockSpec((block_rows, queries.shape[1]), lambda i: (i, 0)),
        whole=pl.BlockSpec(keys_values.shape, lambda i: (0, 0)),
        column=pl.BlockSpec((block_rows, 1), lambda i: (i, 0)),
    )


def attention_forward(first, queries, keys_values, doc_start, block_rows=256, reach=1024):
    row_count, query_cols = queries.shape
    kv_heads = keys_values.shape[1] // (2 * HEAD_DIM)
    group_size = query_cols // HEAD_DIM // kv_heads
    steps = row_count // block_rows
    window = min(reach + block_rows, keys_values.shape[0])
    specs = attention_specs(queries, keys_values, block_rows)
    stacked = group_size * block_rows
    return pl.pallas_call(
        partial(attention_forward_kernel, group_size=group_size, window=window),
        grid=(steps,),
        in_specs=[specs["smem"], specs["rows"], specs["whole"], specs["column"]],
        out_specs=[
            specs["rows"],
            pl.BlockSpec((1, kv_heads, stacked, 1), lambda i: (i, 0, 0, 0)),
        ],
        out_shape=[
            jax.ShapeDtypeStruct(queries.shape, BF16),
            jax.ShapeDtypeStruct((steps, kv_heads, stacked, 1), F32),
        ],
        compiler_params=pltpu.CompilerParams(vmem_limit_bytes=48 * 2**20),
        cost_estimate=pl.CostEstimate(
            flops=4 * row_count * window * query_cols * 8, bytes_accessed=2**22, transcendentals=0
        ),
    )(first, queries, keys_values, doc_start)


def attention_backward(
    first, queries, keys_values, doc_start, lse, grads, turns, query_turns, block_rows=256, reach=1024
):
    row_count, query_cols = queries.shape
    kv_heads = keys_values.shape[1] // (2 * HEAD_DIM)
    group_size = query_cols // HEAD_DIM // kv_heads
    steps = row_count // block_rows
    window = min(reach + block_rows, keys_values.shape[0])
    specs = attention_specs(queries, keys_values, block_rows)
    stacked = group_size * block_rows
    return pl.pallas_call(
        partial(attention_backward_kernel, group_size=group_size, window=window, steps=steps),
        grid=(steps,),
        in_specs=[
            specs["smem"],
            specs["rows"],
            specs["whole"],
            specs["column"],
            pl.BlockSpec((1, kv_heads, stacked, 1), lambda i: (i, 0, 0, 0)),
            specs["rows"],
            pl.BlockSpec(turns.shape, lambda i: (0, 0)),
            pl.BlockSpec((block_rows, turns.shape[1]), lambda i: (i, 0)),
        ],
        out_specs=[specs["rows"], specs["whole"]],
        out_shape=[
            jax.ShapeDtypeStruct(queries.shape, BF16),
            jax.ShapeDtypeStruct(keys_values.shape, BF16),
        ],
        scratch_shapes=[
            pltpu.VMEM((kv_heads, keys_values.shape[0], 2 * HEAD_DIM), F32),
            pltpu.VMEM((kv_heads, keys_values.shape[0], HEAD_DIM), F32),
        ],
        compiler_params=pltpu.CompilerParams(vmem_limit_bytes=48 * 2**20),
        cost_estimate=pl.CostEstimate(
            flops=10 * row_count * window * query_cols * 8, bytes_accessed=2**23, transcendentals=0
        ),
    )(first, queries, keys_values, doc_start, lse, grads, turns, query_turns)


def rotation_tables(positions):
    half_dim = HEAD_DIM // 2
    frequencies = 10000.0 ** (-2.0 * jnp.arange(half_dim, dtype=F32) / HEAD_DIM)
    angles = positions.astype(F32)[:, None] * frequencies[None, :]
    cosine, sine = jnp.cos(angles), jnp.sin(angles)
    return jnp.concatenate([cosine, cosine, -sine, -sine], axis=1)


def turned_columns(weight):
    rows, cols = weight.shape
    halves = weight.reshape(rows, cols // HEAD_DIM, 2, HEAD_DIM // 2)
    return jnp.stack([-halves[:, :, 1], halves[:, :, 0]], axis=2).reshape(rows, cols)


def expert_plan(
    residual_in,
    gain_attn,
    query_weight,
    key_projection_weight,
    value_projection_weight,
    out_weight,
    gain_ffn,
    gate_weight,
    up_weight,
    down_weight,
    segments,
    routes,
    shares,
    cotangent,
    *,
    groups,
    tensor_size,
):
    row_count, model_width = residual_in.shape
    query_cols = query_weight.shape[1]
    kv_cols = key_projection_weight.shape[1]
    expert_count, slice_rows, unit_count = gate_weight.shape
    own_experts = expert_count // groups
    piece_rows = row_count // tensor_size
    first_count = own_experts * 2 // 5
    context_rank = lax.axis_index(CONTEXT)
    tensor_rank = lax.axis_index(TENSOR)
    group_rank = lax.axis_index(SHARD) * lax.axis_size(CONTEXT) + context_rank
    chip_half, core = tensor_rank // 2, tensor_rank % 2
    own_first = context_rank * row_count
    piece_first = tensor_rank * piece_rows
    sibling = [(i, i ^ 1) for i in range(tensor_size)]
    across = [(i, i ^ 2) for i in range(tensor_size)]
    pair = [(0, 1), (1, 0)]

    def own_piece(values):
        return lax.dynamic_slice_in_dim(values, piece_first, piece_rows)

    def pick(values, axis, index):
        return lax.dynamic_index_in_dim(values, index, axis, keepdims=False)

    def sum_over_tensor(parts):
        parts = parts.astype(BF16).reshape(2, 2, piece_rows, -1)
        received = lax.ppermute(pick(parts, 1, 1 - core), TENSOR, sibling)
        half = pick(parts, 1, core).astype(F32) + received.astype(F32)
        received = lax.ppermute(pick(half, 0, 1 - chip_half).astype(BF16), TENSOR, across)
        return pick(half, 0, chip_half) + received.astype(F32)

    def gather_over_tensor(piece):
        other = lax.ppermute(piece, TENSOR, across)
        chips = jnp.where(
            chip_half == 0, jnp.concatenate([piece, other]), jnp.concatenate([other, piece])
        ).reshape(2, 1, piece_rows, -1)
        others = lax.ppermute(chips, TENSOR, sibling)
        both = jnp.where(
            core == 0,
            jnp.concatenate([chips, others], axis=1),
            jnp.concatenate([others, chips], axis=1),
        )
        return both.reshape(row_count, -1)

    def padded_columns(*gains):
        columns = jnp.stack(gains, axis=1)
        return jnp.pad(columns, ((0, 0), (0, 128 - len(gains))))

    with jax.named_scope("weights"):
        lanes = 3 * unit_count

        def slices(first, count):
            return jnp.concatenate(
                [
                    weight.reshape((groups, own_experts) + weight.shape[1:])[:, first : first + count]
                    for weight in (gate_weight, up_weight, down_weight.transpose(0, 2, 1))
                ],
                axis=3,
            ).reshape(groups * count, slice_rows, lanes)

        def to_groups(values):
            owned = lax.all_to_all(values, GROUP, 0, 0, tiled=True)
            return owned.reshape(groups, -1, slice_rows, lanes)

        slices_first, slices_second = lax.optimization_barrier(
            (slices(0, first_count), slices(first_count, own_experts - first_count))
        )
        owned_first, owned_second = to_groups(slices_first), to_groups(slices_second)

        qkv_full = lax.all_gather(
            jnp.concatenate(
                [
                    query_weight,
                    key_projection_weight,
                    value_projection_weight,
                    out_weight.T,
                    padded_columns(gain_attn, gain_ffn),
                ],
                axis=1,
            ),
            GROUP,
            axis=0,
            tiled=True,
        )
        qkv_cols = query_cols + 2 * kv_cols
        owned_first, qkv_full = lax.optimization_barrier((owned_first, qkv_full))
        others_first = lax.ppermute(owned_first, TENSOR, across)
        qkv_weight = qkv_full[:, :qkv_cols]
        out_transposed = qkv_full[:, qkv_cols : qkv_cols + query_cols]
        gain_attn_float = qkv_full[:, qkv_cols + query_cols].astype(F32)
        gain_ffn_float = qkv_full[:, qkv_cols + query_cols + 1].astype(F32)


    with jax.named_scope("cotangents"):
        cotangent_piece = own_piece(cotangent)
        spread = jnp.sum(
            jnp.where(
                own_piece(routes)[:, :, None] == jnp.arange(expert_count, dtype=jnp.int32),
                own_piece(shares)[:, :, None],
                0.0,
            ),
            axis=1,
        )
        spread_high = spread.astype(BF16)
        spread_low = (spread - spread_high.astype(F32)).astype(BF16)
        spread_both = jnp.pad(
            jnp.concatenate([spread_high, spread_low], axis=1),
            ((0, 0), (0, 128 - 2 * expert_count)),
        )
        cotangent_own = lax.all_gather(
            jnp.concatenate([cotangent_piece, spread_both], axis=1), GROUP, axis=0, tiled=False
        )

    with jax.named_scope("attention"):
        positions = doc_positions(segments)
        turns = rotation_tables(positions)
        own_turns = lax.dynamic_slice_in_dim(turns, own_first, row_count)
        own_index = own_first + jnp.arange(row_count, dtype=jnp.int32)
        doc_start = own_index - lax.dynamic_slice_in_dim(positions, own_first, row_count)
        input_float = residual_in.astype(F32)
        first_normalized = rms_scale(input_float, gain_attn_float).astype(BF16)
        rotated_cols = query_cols + kv_cols
        projected = jnp.dot(
            first_normalized,
            jnp.concatenate([qkv_weight, turned_columns(qkv_weight[:, :rotated_cols])], axis=1),
            preferred_element_type=F32,
        )
        heads = rotated_cols // HEAD_DIM
        rotated = (
            projected[:, :rotated_cols] * jnp.tile(own_turns[:, :HEAD_DIM], (1, heads))
            - projected[:, qkv_cols:] * jnp.tile(own_turns[:, HEAD_DIM:], (1, heads))
        ).astype(BF16)
        queries = rotated[:, :query_cols]
        own_keys_values = jnp.concatenate(
            [rotated[:, query_cols:], projected[:, rotated_cols:qkv_cols].astype(BF16)], axis=1
        )
        other_keys_values = lax.ppermute(own_keys_values, CONTEXT, pair)
        keys_values = jnp.where(
            context_rank == 0,
            jnp.concatenate([own_keys_values, other_keys_values]),
            jnp.concatenate([other_keys_values, own_keys_values]),
        )
        first = own_first.reshape(1).astype(jnp.int32)
        attended, lse = attention_forward(first, queries, keys_values, doc_start[:, None])
        attn_part = lax.dot_general(
            attended, out_transposed, LAST_LAST, preferred_element_type=F32
        )
        attn_piece = sum_over_tensor(attn_part)
        others_first, owned_second, attn_piece = lax.optimization_barrier(
            (others_first, owned_second, attn_piece)
        )
        hidden = own_piece(residual_in).astype(F32) + attn_piece
        normed_ffn, ffn_norm_back = jax.vjp(rms_scale, hidden, gain_ffn_float)

    with jax.named_scope("exchange"):
        cotangent_own, normed_ffn = lax.optimization_barrier((cotangent_own, normed_ffn))
        spread_own = cotangent_own[:, :, model_width:]
        spread_all = jnp.concatenate(
            [spread_own, lax.ppermute(spread_own, TENSOR, sibling)], axis=1
        )

        def shares_of(first, count):
            start = group_rank * own_experts + first
            high = lax.dynamic_slice_in_dim(spread_all, start, count, axis=2)
            low = lax.dynamic_slice_in_dim(spread_all, start + expert_count, count, axis=2)
            total = high.astype(F32) + low.astype(F32)
            return jnp.pad(total, ((0, 0), (0, 0), (0, 8 - count)))

        shares_first = shares_of(0, first_count)
        shares_second = shares_of(first_count, own_experts - first_count)

    with jax.named_scope("experts"):
        line = groups // 2
        parts, grad_own_first, grad_other_first, tokens, others_second, cotangent_other = (
            experts_gathering(
                normed_ffn.astype(BF16),
                cotangent_own,
                shares_first,
                owned_first,
                others_first,
                owned_second,
                line,
            )
        )
        grad_second, out_piece, grad_own_second, grad_other_second, received_first = (
            experts_reducing(
                tokens,
                (cotangent_own, cotangent_other),
                shares_second,
                owned_second,
                others_second,
                grad_other_first,
                parts,
                line,
            )
        )

    with jax.named_scope("expert_grads"):

        def added(own, received):
            return (own.astype(F32) + received.astype(F32)).astype(BF16)

        def returned(total):
            flat = total.reshape((total.shape[0] * total.shape[1],) + total.shape[2:])
            return lax.all_to_all(flat, GROUP, 0, 0, tiled=True).reshape(total.shape)

        total_first = added(grad_own_first, received_first)
        received_second = lax.ppermute(grad_other_second, TENSOR, across)
        total_first, grad_second = lax.optimization_barrier((total_first, grad_second))
        returned_first = returned(total_first)
        grad_hidden_norm, grad_gain_ffn_local = ffn_norm_back(grad_second.astype(F32))
        grad_hidden = cotangent_piece.astype(F32) + grad_hidden_norm
        grad_hidden_low = gather_over_tensor(grad_hidden.astype(BF16))
        output = gather_over_tensor((hidden + out_piece.astype(F32)).astype(BF16))

    with jax.named_scope("attention_back"):
        grad_out_local = lax.dot_general(
            grad_hidden_low, attended, FIRST_FIRST, preferred_element_type=F32
        )
        grad_out_transposed = lax.psum_scatter(
            grad_out_local.astype(BF16), GROUP, scatter_dimension=0, tiled=True
        )
        grad_attended = jnp.dot(grad_hidden_low, out_transposed, preferred_element_type=F32)
        returned_first, grad_attended = lax.optimization_barrier((returned_first, grad_attended))
        grad_query_lin, grad_key_value = attention_backward(
            first,
            queries,
            keys_values,
            doc_start[:, None],
            lse,
            grad_attended.astype(BF16),
            turns,
            own_turns,
        )
        total_second = added(grad_own_second, received_second)
        grad_key_value = grad_key_value.reshape(2, row_count, -1)
        received = lax.ppermute(pick(grad_key_value, 0, 1 - context_rank), CONTEXT, pair)
        grad_key_value = (
            pick(grad_key_value, 0, context_rank).astype(F32) + received.astype(F32)
        ).astype(BF16)
        grad_projected = jnp.concatenate([grad_query_lin, grad_key_value], axis=1)
        grad_first_part = lax.dot_general(
            grad_projected, qkv_weight, LAST_LAST, preferred_element_type=F32
        )
        grad_qkv_local = lax.dot_general(
            first_normalized, grad_projected, FIRST_FIRST, preferred_element_type=F32
        ).astype(BF16)
        total_second, grad_out_transposed, grad_first_part, grad_qkv_local = (
            lax.optimization_barrier(
                (total_second, grad_out_transposed, grad_first_part, grad_qkv_local)
            )
        )
        returned_second = returned(total_second)
        grad_first = sum_over_tensor(grad_first_part)
        _, attn_norm_back = jax.vjp(
            rms_scale, own_piece(residual_in).astype(F32), gain_attn_float
        )
        grad_input_norm, grad_gain_attn_local = attn_norm_back(grad_first)
        grad_input = gather_over_tensor((grad_hidden + grad_input_norm).astype(BF16))
        grad_qkv = lax.psum_scatter(grad_qkv_local, GROUP, scatter_dimension=0, tiled=True)
        gains = jnp.stack([grad_gain_attn_local, grad_gain_ffn_local])
        for axis, step, size in (
            (TENSOR, 1, tensor_size),
            (TENSOR, 2, tensor_size),
            (CONTEXT, 1, 2),
            (SHARD, 1, groups // 2),
            (SHARD, 2, groups // 2),
        ):
            gains = gains + lax.ppermute(gains, axis, [(i, i ^ step) for i in range(size)])
        gains = lax.dynamic_slice_in_dim(gains, group_rank * slice_rows, slice_rows, axis=1)

    returned_second, grad_qkv, gains, grad_input, output = lax.optimization_barrier(
        (returned_second, grad_qkv, gains, grad_input, output)
    )
    grad_qkv = grad_qkv.astype(F32)

    def whole(first, last, turned):
        parts = [
            part[..., first:last].transpose(0, 1, 3, 2) if turned else part[..., first:last]
            for part in (returned_first, returned_second)
        ]
        joined = jnp.concatenate(parts, axis=1).astype(F32)
        return joined.reshape((expert_count,) + joined.shape[2:])

    units = unit_count
    return (
        output,
        grad_input,
        gains[0],
        grad_qkv[:, :query_cols],
        grad_qkv[:, query_cols:rotated_cols],
        grad_qkv[:, rotated_cols:qkv_cols],
        grad_out_transposed.astype(F32).T,
        gains[1],
        whole(0, units, False),
        whole(units, 2 * units, False),
        whole(2 * units, 3 * units, True),
    )


def solution(mesh):
    placed = (
        P(GROUP, None),
        P(GROUP),
        P(GROUP, TENSOR),
        P(GROUP, TENSOR),
        P(GROUP, TENSOR),
        P(TENSOR, GROUP),
        P(GROUP),
        P(None, GROUP, TENSOR),
        P(None, GROUP, TENSOR),
        P(None, TENSOR, GROUP),
        P(SHARD),
        P(GROUP, None),
        P(GROUP, None),
        P(GROUP, None),
    )
    sizes = dict(mesh.shape)
    if sizes[SHARD] == 4 and sizes[CONTEXT] == 2 and sizes[TENSOR] == 4:
        plan = partial(
            expert_plan, groups=sizes[SHARD] * sizes[CONTEXT], tensor_size=sizes[TENSOR]
        )
    else:
        plan = gathered_plan
    return jax.shard_map(
        plan,
        mesh=mesh,
        in_specs=placed,
        out_specs=(
            P(GROUP, None),
            P(GROUP, None),
            P(GROUP),
            P(GROUP, TENSOR),
            P(GROUP, TENSOR),
            P(GROUP, TENSOR),
            P(TENSOR, GROUP),
            P(GROUP),
            P(None, GROUP, TENSOR),
            P(None, GROUP, TENSOR),
            P(None, TENSOR, GROUP),
        ),
        check_vma=False,
    )
```
